32 devices in a mesh: lat: 8 (over y, x, core), lon: 4 (over z).
Axes of the slice: x: 2, y: 2, z: 4, core: 2. Of those that a mesh axis runs over, the one named last changes fastest.
Arguments:
- control: float32 [128, 32, 512], P('lat', None, 'lon'), may hold values from -6 to 6
- background: float32 [128, 32, 512], P('lat', None, 'lon'), may hold values from -6 to 6
- lon_width: int32 [128], P('lat'), may hold values from 2 to 16
- block_cells: int32 [512, 4], P('lat', 'lon'), may hold values from 0 to 255, as said below
- block_owner: int32 [512, 4], P('lat', 'lon'), may hold values from -1 to 7, as said below
- channel_count: int32 [288, 4], P('lat', 'lon'), may hold values from 1 to 256
- radiance: bfloat16 [2048, 1152], P('lat', 'lon'), may hold values from -6 to 6
- in_weight: bfloat16 [32, 1024], replicated, may hold values from -1 to 1
- in_bias: float32 [1024], replicated, may hold values from -3 to 3
- mid_weight: bfloat16 [1024, 1024], replicated, may hold values from -0.1875 to 0.1875
- mid_bias: float32 [1024], replicated, may hold values from -3 to 3
- out_weight: bfloat16 [1024, 256], replicated, may hold values from -0.1875 to 0.1875
- out_bias: float32 [256], replicated, may hold values from -3 to 3
Outputs:
- gradient: float32 [128, 32, 512], P('lat', None, 'lon')
The draws below stay inside these ranges and needn't reach their ends.
Inputs may be any that keep to these rules, and one draw needn't show every extreme that they name: `block_owner`: the live slots of a device come first, unused ones hold -1. Every device has at least 16 observed blocks, some device of every lon index has 64. One device sends at most 8 blocks to one owner, and an owner receives at most 36 blocks from its lon index; both bounds are reached in every draw. `block_cells`: the live slots of one device name distinct blocks.
All inputs are finite; a program needn't handle non-finite values.
Results may differ from the reference program's by a relative error of at most 0.0023.
Values may be sent and summed in bfloat16 or wider, within the bound.
No kernel may reach another device: no remote copies, remote signals or barrier semaphores. Data moves between devices by JAX's collectives and lax.ppermute only.
A program may use at most 64 MiB of HBM per device.

```python
import jax
import jax.numpy as jnp
from jax import lax

LAT_DEV = 16
LON_DEV = 128
LEVELS = 32
NET_HIDDEN = 1024
CHANNELS = 256
REACH = 16
BLOCK_COLS = 8
OBS_MOST = 64
OBS_LOW = 32
RECV_MOST = 36
LAT_ROWS = 128
LON_COLS = 512
N_LAT = 8
N_LON = 4


def routing_tables(key):
    folded = jax.random.fold_in(key, 4711)
    key_count, key_busy, key_full, key_cells = jax.random.split(folded, 4)
    counts = jax.random.randint(key_count, (N_LAT, N_LON), OBS_LOW // 2, OBS_LOW + 1)
    busiest = jax.random.randint(key_busy, (N_LON,), 0, N_LAT)
    full_col = jax.random.randint(key_full, (), 0, N_LON)
    lat_ids = jnp.arange(N_LAT)[:, None]
    lon_ids = jnp.arange(N_LON)[None, :]
    counts = jnp.where(lon_ids == full_col, OBS_LOW, counts)
    counts = jnp.where(lat_ids == busiest[None, :], OBS_MOST, counts)
    starts = jnp.cumsum(counts, axis=0) - counts
    slot_ids = jnp.arange(OBS_MOST)[None, :, None]
    owners = jnp.where(slot_ids < counts[:, None, :], (starts[:, None, :] + slot_ids) % N_LAT, -1)
    cell_keys = jax.random.split(key_cells, N_LAT * N_LON)
    cell_total = LAT_DEV * (LON_DEV // BLOCK_COLS)
    shuffled = jax.vmap(lambda cell_key: jax.random.permutation(cell_key, cell_total)[:OBS_MOST])(cell_keys)
    cell_ids = jnp.transpose(shuffled.reshape(N_LAT, N_LON, OBS_MOST), (0, 2, 1))
    return (cell_ids.reshape(N_LAT * OBS_MOST, N_LON).astype(jnp.int32), owners.reshape(N_LAT * OBS_MOST, N_LON).astype(jnp.int32))


def draw_block_cells(key, part):
    return routing_tables(key)[0]


def draw_block_owner(key, part):
    return routing_tables(key)[1]


def place_ends(drawn, rng, smallest, largest):
    spot = [jax.random.randint(jax.random.fold_in(rng, axis), (), 0, length) for axis, length in enumerate(drawn.shape)]
    main_axis = drawn.shape.index(max(drawn.shape))
    beside = spot[:main_axis] + [(spot[main_axis] + 1) % drawn.shape[main_axis]] + spot[main_axis + 1:]
    return drawn.at[tuple(spot)].set(smallest).at[tuple(beside)].set(largest)


def levels(stream_key, dims, cuts, least, largest):
    gain, own = 1.0, jax.random.fold_in(stream_key, 6)
    for dim, parts in cuts:
        steps = jnp.exp(jax.random.uniform(jax.random.fold_in(own, dim), (parts,), jnp.float32, least / len(cuts), largest / len(cuts)))
        gain = gain * jnp.repeat(steps, dims[dim] // parts).reshape([-1 if axis == dim else 1 for axis in range(len(dims))])
    return gain


def bell_draw(own_key, shape, deviation, bound, pieces=(), kind=jnp.bfloat16):
    level = levels(own_key, shape, pieces, -0.22, 0.18) if pieces else 1.0
    values = jax.random.normal(own_key, shape, jnp.float32) * deviation * level
    return jnp.minimum(jnp.maximum(values, -bound), bound).astype(kind)


def setup_inputs(seed: int = 0) -> dict:
    streams_of = jax.random.split(jax.random.key(seed), 14)
    return {
        "control": bell_draw(streams_of[0], (LAT_ROWS, LEVELS, LON_COLS), 1.0, 6.0, ((0, 8), (2, 4)), jnp.float32),
        "background": bell_draw(streams_of[1], (LAT_ROWS, LEVELS, LON_COLS), 1.0, 6.0, ((0, 8), (2, 4)), jnp.float32),
        "lon_width": place_ends(jax.random.randint(streams_of[2], (LAT_ROWS,), 2, 17), jax.random.fold_in(streams_of[2], 1), 2, 16).astype(jnp.int32),
        "block_cells": draw_block_cells(jax.random.fold_in(streams_of[13], 71), 0),
        "block_owner": draw_block_owner(jax.random.fold_in(streams_of[13], 71), 0),
        "channel_count": place_ends(jax.random.randint(streams_of[5], (RECV_MOST * N_LAT, N_LON), 1, CHANNELS + 1), jax.random.fold_in(streams_of[5], 1), 1, CHANNELS).astype(jnp.int32),
        "radiance": bell_draw(streams_of[6], (N_LAT * CHANNELS, N_LON * RECV_MOST * BLOCK_COLS), 1.0, 6.0, ((0, 8), (1, 4))),
        "in_weight": bell_draw(streams_of[7], (LEVELS, NET_HIDDEN), LEVELS ** -0.5, 1.0),
        "in_bias": bell_draw(streams_of[8], (NET_HIDDEN,), 0.5, 3.0, (), jnp.float32),
        "mid_weight": bell_draw(streams_of[9], (NET_HIDDEN, NET_HIDDEN), NET_HIDDEN ** -0.5, 0.1875),
        "mid_bias": bell_draw(streams_of[10], (NET_HIDDEN,), 0.5, 3.0, (), jnp.float32),
        "out_weight": bell_draw(streams_of[11], (NET_HIDDEN, CHANNELS), NET_HIDDEN ** -0.5, 0.1875),
        "out_bias": bell_draw(streams_of[12], (CHANNELS,), 0.5, 3.0, (), jnp.float32),
    }


lat_sigma = 8.0

def tap_offsets():
    return jnp.arange(-REACH, REACH + 1).astype(jnp.float32)

def lat_taps():
    offsets = tap_offsets()
    raw_taps = jnp.exp(-offsets * offsets / (2.0 * lat_sigma * lat_sigma))
    return raw_taps / jnp.sqrt(jnp.sum(raw_taps * raw_taps))

def lon_taps(lon_width):
    offsets = tap_offsets()[None, :]
    spread = lon_width.astype(jnp.float32)[:, None]
    raw_taps = jnp.exp(-offsets * offsets / (2.0 * spread * spread))
    return raw_taps / jnp.sqrt(lax.optimization_barrier(jnp.sum(raw_taps * raw_taps, axis=1, keepdims=True)))

def smooth_lat(values):
    weights = lat_taps()
    padded = jnp.pad(values, ((REACH, REACH), (0, 0)))
    height = values.shape[0]
    summed = jnp.zeros_like(values)
    for offset in range(2 * REACH + 1):
        summed = summed + weights[offset] * padded[offset:offset + height]
    return summed

def smooth_lon(values, weights):
    summed = jnp.zeros_like(values)
    for offset in range(2 * REACH + 1):
        summed = summed + weights[:, offset][:, None] * jnp.roll(values, REACH - offset, axis=1)
    return summed

def per_level(values, plane_fn):

    def one_level(level):
        plane = lax.dynamic_index_in_dim(values, level, 1, keepdims=False)
        return plane_fn(plane)
    stacked = lax.map(one_level, jnp.arange(LEVELS).astype(jnp.int32))
    return jnp.transpose(stacked, (1, 0, 2))

def radiate(inputs, observed, kept_mask, in_weight, in_bias, mid_weight, mid_bias, out_weight, out_bias):
    first_pre = jnp.einsum('lh,lm->hm', in_weight.astype(jnp.float32), inputs.astype(jnp.float32)) + in_bias[:, None]
    act_one = lax.optimization_barrier(jnp.tanh(first_pre).astype(jnp.bfloat16))
    second_pre = jnp.einsum('hk,hm->km', mid_weight.astype(jnp.float32), act_one.astype(jnp.float32)) + mid_bias[:, None]
    act_two = lax.optimization_barrier(jnp.tanh(second_pre).astype(jnp.bfloat16))
    emitted = jnp.einsum('kn,km->nm', out_weight.astype(jnp.float32), act_two.astype(jnp.float32)) + out_bias[:, None]
    misfit = jnp.where(kept_mask, emitted - observed.astype(jnp.float32), 0.0)
    misfit = lax.optimization_barrier(misfit.astype(jnp.bfloat16))
    back_two = jnp.einsum('kn,nm->km', out_weight.astype(jnp.float32), misfit.astype(jnp.float32))
    two_val = act_two.astype(jnp.float32)
    grad_two = lax.optimization_barrier((back_two * (1.0 - two_val * two_val)).astype(jnp.bfloat16))
    back_one = jnp.einsum('hk,km->hm', mid_weight.astype(jnp.float32), grad_two.astype(jnp.float32))
    one_val = act_one.astype(jnp.float32)
    grad_one = lax.optimization_barrier((back_one * (1.0 - one_val * one_val)).astype(jnp.bfloat16))
    summed = jnp.einsum('lh,hm->lm', in_weight.astype(jnp.float32), grad_one.astype(jnp.float32))
    return lax.optimization_barrier(summed.astype(jnp.bfloat16))

def reference(control, background, lon_width, block_cells, block_owner, channel_count, radiance, in_weight, in_bias, mid_weight, mid_bias, out_weight, out_bias):
    lon_weights = lon_taps(lon_width)
    increment = per_level(control, lambda plane: smooth_lon(smooth_lat(plane), lon_weights))
    profile = lax.optimization_barrier((background + increment).astype(jnp.bfloat16))
    groups = LON_DEV // BLOCK_COLS
    entries = N_LAT * OBS_MOST
    slots_all = N_LAT * RECV_MOST
    entry_ids = jnp.arange(entries).astype(jnp.int32)
    slot_ids = jnp.arange(slots_all).astype(jnp.int32)
    channel_ids = jnp.arange(CHANNELS).astype(jnp.int32)

    def one_column(lon_index):
        owners = lax.dynamic_index_in_dim(block_owner, lon_index, 1, keepdims=False)
        picked_all = lax.dynamic_index_in_dim(block_cells, lon_index, 1, keepdims=False)
        counts = lax.dynamic_index_in_dim(channel_count, lon_index, 1, keepdims=False)
        start_col = (lon_index * LON_DEV).astype(jnp.int32)
        columns = lax.dynamic_slice_in_dim(profile, start_col, LON_DEV, 2)
        cells = columns.reshape(LAT_ROWS, LEVELS, groups, BLOCK_COLS)
        obs_start = (lon_index * RECV_MOST * BLOCK_COLS).astype(jnp.int32)
        observed = lax.dynamic_slice_in_dim(radiance, obs_start, RECV_MOST * BLOCK_COLS, 1)
        observed = jnp.transpose(observed.reshape(N_LAT, CHANNELS, RECV_MOST * BLOCK_COLS), (1, 0, 2)).reshape(CHANNELS, slots_all * BLOCK_COLS)
        is_live = owners >= 0
        same_owner = (owners[:, None] == owners[None, :]) & (entry_ids[None, :] < entry_ids[:, None])
        arrival = lax.optimization_barrier(jnp.sum(same_owner.astype(jnp.int32), axis=1)).astype(jnp.int32)
        target = jnp.where(is_live, owners * RECV_MOST + arrival, -1).astype(jnp.int32)
        matches = target[None, :] == slot_ids[:, None]
        filled = jnp.any(matches, axis=1)
        source = lax.optimization_barrier(jnp.sum(jnp.where(matches, entry_ids[None, :], 0), axis=1)).astype(jnp.int32)
        picked = picked_all[source]
        grid_row = (source // OBS_MOST * LAT_DEV + picked // groups).astype(jnp.int32)
        group = (picked % groups).astype(jnp.int32)
        blocks = cells[grid_row, :, group, :]
        blocks = jnp.where(filled[:, None, None], blocks, jnp.zeros((), jnp.bfloat16))
        inputs = jnp.transpose(blocks, (1, 0, 2)).reshape(LEVELS, slots_all * BLOCK_COLS)
        col_counts = jnp.broadcast_to(counts[:, None], (slots_all, BLOCK_COLS)).reshape(-1)
        col_filled = jnp.broadcast_to(filled[:, None], (slots_all, BLOCK_COLS)).reshape(-1)
        kept_mask = (channel_ids[:, None] < col_counts[None, :]) & col_filled[None, :]
        sensitivity = radiate(inputs, observed, kept_mask, in_weight, in_bias, mid_weight, mid_bias, out_weight, out_bias)
        sens_blocks = jnp.transpose(sensitivity.reshape(LEVELS, slots_all, BLOCK_COLS), (1, 0, 2)).astype(jnp.float32)
        landing = jnp.zeros((LAT_ROWS, LEVELS, groups, BLOCK_COLS), jnp.float32)
        drop_row = jnp.where(filled, grid_row, LAT_ROWS).astype(jnp.int32)
        landing = landing.at[drop_row, :, group, :].add(sens_blocks, mode='drop')
        return landing.reshape(LAT_ROWS, LEVELS, LON_DEV)
    landed = lax.map(one_column, jnp.arange(N_LON).astype(jnp.int32))
    landing = jnp.transpose(landed, (1, 2, 0, 3)).reshape(LAT_ROWS, LEVELS, LON_COLS)
    return control + per_level(landing, lambda plane: smooth_lat(smooth_lon(plane, lon_weights)))
```

```python
import functools

import jax
import jax.numpy as jnp
import numpy as np
from jax import lax
from jax.experimental import pallas as pl
from jax.experimental.pallas import tpu as pltpu
from jax.sharding import PartitionSpec as P

REACH = 16
BLOCK_COLS = 8
LANES = 128
LAT_SIGMA = 8.0
VMEM_BYTES = 40 * 1024 * 1024

VMEM = pl.BlockSpec(memory_space=pltpu.VMEM)
SMEM = pl.BlockSpec(memory_space=pltpu.SMEM)
ANY = pl.BlockSpec(memory_space=pl.ANY)


def lat_taps():
    offsets = np.arange(-REACH, REACH + 1, dtype=np.float64)
    raw = np.exp(-offsets * offsets / (2.0 * LAT_SIGMA * LAT_SIGMA))
    return [float(v) for v in (raw / np.sqrt(np.sum(raw * raw))).astype(np.float32)]


def call(kernel, out_shape, in_specs, out_specs, flops, bytes_moved, scratch=(), name=None):
    return pl.pallas_call(
        kernel,
        out_shape=out_shape,
        in_specs=in_specs,
        out_specs=out_specs,
        scratch_shapes=list(scratch),
        compiler_params=pltpu.CompilerParams(vmem_limit_bytes=VMEM_BYTES),
        cost_estimate=pl.CostEstimate(flops=flops, bytes_accessed=bytes_moved, transcendentals=0),
        name=name,
    )


def lat_conv_row(row, low, own, high):
    taps = lat_taps()
    height = own.shape[0]
    acc = None
    for j in range(-REACH, REACH + 1):
        source = row + j
        if source < 0:
            part = low[source + REACH]
        elif source < height:
            part = own[source]
        else:
            part = high[source - height]
        term = taps[j + REACH] * part
        acc = term if acc is None else acc + term
    return acc


def lon_conv(padded, taps, tile, width):
    acc = taps[tile, 0:1, :] * padded[tile, pl.ds(REACH, width), :]
    for j in range(1, REACH + 1):
        both = padded[tile, pl.ds(REACH + j, width), :] + padded[tile, pl.ds(REACH - j, width), :]
        acc = acc + taps[tile, j : j + 1, :] * both
    return acc


def owner_kernel(radiance, block_owner, channel_count, slabs, meta):
    channels, columns = radiance.shape
    slots = columns // BLOCK_COLS
    halves = channels // LANES
    parts = []
    for half in range(halves):
        block = radiance[half * LANES : (half + 1) * LANES, :].astype(jnp.float32)
        parts.append(jnp.transpose(block).reshape(slots, BLOCK_COLS, LANES))
    slabs[...] = jnp.concatenate(parts, axis=1).astype(jnp.bfloat16)
    meta[...] = jnp.zeros_like(meta)
    meta[0:1, :] = jnp.full((1, LANES), -1, jnp.int32)
    meta[0:1, 0 : block_owner.shape[1]] = block_owner[...]
    meta[1:2, 0 : channel_count.shape[1]] = channel_count[...]


def prepare_kernel(lon_width, background, taps, turned):
    tiles = turned.shape[0]
    height, levels, width = background.shape
    per_tile = height // tiles
    lane_row = lax.broadcasted_iota(jnp.int32, (1, LANES), 1) // levels
    steps = lax.broadcasted_iota(jnp.int32, (taps.shape[1], LANES), 0)
    dist = steps.astype(jnp.float32)
    weight = jnp.where(steps == 0, 1.0, jnp.where(steps <= REACH, 2.0, 0.0))
    for tile in range(tiles):
        spread = jnp.zeros((1, LANES), jnp.int32)
        for sub in range(per_tile):
            spread = jnp.where(lane_row == sub, lon_width[tile * per_tile + sub], spread)
        spread = spread.astype(jnp.float32)
        raw = jnp.exp(-dist * dist / (2.0 * spread * spread))
        norm = jnp.sum(weight * raw * raw, axis=0, keepdims=True)
        taps[tile] = raw / jnp.sqrt(norm)
        rows = background[tile * per_tile : (tile + 1) * per_tile].reshape(per_tile * levels, width)
        turned[tile] = jnp.transpose(rows)


def routing_kernel(recv_most, slot_count, mine, everyone, table):
    count = everyone.shape[0]
    here = lax.axis_index("lat")
    rows = lax.broadcasted_iota(jnp.int32, (slot_count, LANES), 0)
    lanes = lax.broadcasted_iota(jnp.int32, (slot_count, LANES), 1)
    diagonal = rows == lanes
    owner = jnp.sum(jnp.where(diagonal, mine[0:1, :], 0), axis=1, keepdims=True)

    def rank(device, acc):
        before = (device < here) | ((device == here) & (lanes < rows))
        same = everyone[device, 0:1, :] == owner
        return acc + jnp.where(same & before, 1, 0)

    zero = jnp.zeros((slot_count, LANES), jnp.int32)
    arrival = jnp.sum(lax.fori_loop(0, count, rank, zero, unroll=count <= 8), axis=1, keepdims=True)

    def counted(device, acc):
        hit = (owner == device) & (lanes == arrival)
        return acc + jnp.where(hit, everyone[device, 1:2, :], 0)

    kept = jnp.sum(lax.fori_loop(0, count, counted, zero, unroll=count <= 8), axis=1, keepdims=True)
    target = jnp.where(owner >= 0, owner * recv_most + arrival, 0)
    table[...] = jnp.zeros_like(table)
    table[0:1, :] = jnp.sum(jnp.where(diagonal, target, 0), axis=0, keepdims=True)
    table[1:2, :] = jnp.sum(jnp.where(diagonal, kept, 0), axis=0, keepdims=True)


def lat_smooth_kernel(low, own, high, smoothed, edge_low, edge_high):
    tiles = smoothed.shape[0]
    height, levels, width = own.shape
    per_tile = height // tiles
    for tile in range(tiles):
        rows = [lat_conv_row(tile * per_tile + sub, low, own, high) for sub in range(per_tile)]
        turned = jnp.transpose(jnp.concatenate(rows, axis=0))
        smoothed[tile] = turned
        edge_low[tile] = turned[0:REACH]
        edge_high[tile] = turned[width - REACH : width]


def block_place(cells, slot, groups, per_tile, width):
    block = cells[slot]
    row = block // groups
    start = (row // per_tile) * width + (block % groups) * BLOCK_COLS
    return pl.multiple_of(start, BLOCK_COLS), row % per_tile


def net_kernel(
    cells,
    table,
    low,
    own,
    high,
    turned,
    taps,
    slabs,
    in_weight,
    in_bias,
    mid_weight,
    mid_bias,
    out_weight,
    out_bias,
    landing,
    edge_low,
    edge_high,
    padded,
    profile,
    picked,
    wide_in,
    emitted,
    misfit,
    observed,
    act_one,
    act_two,
    sem,
):
    tiles, width, _ = own.shape
    levels = in_weight.shape[0]
    per_tile = LANES // levels
    groups = width // BLOCK_COLS
    slot_count = cells.shape[0]
    channels = out_weight.shape[1]

    def fetch(slot, carry):
        pltpu.make_async_copy(slabs.at[table[0, slot]], observed.at[slot], sem).start()
        return carry

    lax.fori_loop(0, slot_count, fetch, 0, unroll=8)

    padded[:, 0:REACH, :] = low[...]
    padded[:, REACH : REACH + width, :] = own[...]
    padded[:, REACH + width :, :] = high[...]
    for tile in range(tiles):
        total = turned[tile] + lon_conv(padded, taps, tile, width)
        profile[tile * width : (tile + 1) * width, :] = total.astype(jnp.bfloat16).astype(jnp.float32)
    for sub in range(per_tile):
        wide_in[sub * levels : (sub + 1) * levels, :] = in_weight[...]

    lane_row = lax.broadcasted_iota(jnp.int32, (BLOCK_COLS, LANES), 1) // levels
    for slot in range(slot_count):
        start, sub = block_place(cells, slot, groups, per_tile, width)
        block = profile[pl.ds(start, BLOCK_COLS), :]
        picked[slot * BLOCK_COLS : (slot + 1) * BLOCK_COLS, :] = jnp.where(lane_row == sub, block, 0.0)

    def dot(a, b):
        return jnp.dot(a, b, preferred_element_type=jnp.float32)

    def dot_t(a, b):
        return lax.dot_general(a, b, (((1,), (1,)), ((), ())), preferred_element_type=jnp.float32)

    inputs = picked[...].astype(jnp.bfloat16)
    act_one[...] = jnp.tanh(dot(inputs, wide_in[...]) + in_bias[...]).astype(jnp.bfloat16)
    act_two[...] = jnp.tanh(dot(act_one[...], mid_weight[...]) + mid_bias[...]).astype(jnp.bfloat16)
    emitted[...] = dot(act_two[...], out_weight[...]) + out_bias[...]

    pltpu.make_async_copy(slabs.at[pl.ds(0, slot_count)], observed, sem).wait()
    channel = lax.broadcasted_iota(jnp.int32, (BLOCK_COLS, channels), 1)
    for slot in range(0, slot_count, 2):
        pair = []
        for at in (slot, slot + 1):
            slab = observed[at].astype(jnp.float32)
            seen = jnp.concatenate(
                [slab[h * BLOCK_COLS : (h + 1) * BLOCK_COLS] for h in range(channels // LANES)], axis=1
            )
            gap = emitted[at * BLOCK_COLS : (at + 1) * BLOCK_COLS, :] - seen
            pair.append(jnp.where(channel < table[1, at], gap, 0.0))
        misfit[slot * BLOCK_COLS : (slot + 2) * BLOCK_COLS, :] = jnp.concatenate(pair, axis=0).astype(
            jnp.bfloat16
        )

    two = act_two[...].astype(jnp.float32)
    grad_two = (dot_t(misfit[...], out_weight[...]) * (1.0 - two * two)).astype(jnp.bfloat16)
    one = act_one[...].astype(jnp.float32)
    grad_one = (dot_t(grad_two, mid_weight[...]) * (1.0 - one * one)).astype(jnp.bfloat16)
    picked[...] = dot_t(grad_one, wide_in[...]).astype(jnp.bfloat16).astype(jnp.float32)

    profile[...] = jnp.zeros_like(profile)
    for slot in range(slot_count):
        start, sub = block_place(cells, slot, groups, per_tile, width)
        block = picked[slot * BLOCK_COLS : (slot + 1) * BLOCK_COLS, :]
        profile[pl.ds(start, BLOCK_COLS), :] += jnp.where(lane_row == sub, block, 0.0)
    for tile in range(tiles):
        landing[tile] = profile[tile * width : (tile + 1) * width, :]
        edge_low[tile] = profile[tile * width : tile * width + REACH, :].astype(jnp.bfloat16)
        edge_high[tile] = profile[(tile + 1) * width - REACH : (tile + 1) * width, :].astype(jnp.bfloat16)


def lon_back_kernel(low, own, high, taps, back, padded):
    tiles, width, _ = own.shape
    height, levels, _ = back.shape
    per_tile = height // tiles
    padded[:, 0:REACH, :] = low[...].astype(jnp.float32)
    padded[:, REACH : REACH + width, :] = own[...]
    padded[:, REACH + width :, :] = high[...].astype(jnp.float32)
    for tile in range(tiles):
        rows = jnp.transpose(lon_conv(padded, taps, tile, width))
        back[tile * per_tile : (tile + 1) * per_tile] = rows.reshape(per_tile, levels, width)


def lat_back_kernel(low, own, high, control, gradient):
    for row in range(own.shape[0]):
        gradient[row] = control[row] + lat_conv_row(row, low, own, high)


def swap(forward_value, backward_value, axis, periodic):
    count = lax.axis_size(axis)
    forward = [(i, i + 1) for i in range(count - 1)]
    if periodic:
        forward.append((count - 1, 0))
    backward = [(target, source) for source, target in forward]
    return lax.ppermute(forward_value, axis, forward), lax.ppermute(backward_value, axis, backward)


def shards(
    control,
    background,
    lon_width,
    block_cells,
    block_owner,
    channel_count,
    radiance,
    in_weight,
    in_bias,
    mid_weight,
    mid_bias,
    out_weight,
    out_bias,
):
    height, levels, width = control.shape
    hidden = mid_weight.shape[0]
    channels, columns = radiance.shape
    slot_count = block_owner.shape[0]
    recv_most = channel_count.shape[0]
    per_tile = LANES // levels
    tiles = height // per_tile
    slab_rows = BLOCK_COLS * channels // LANES
    f32, bf16, i32 = jnp.float32, jnp.bfloat16, jnp.int32
    shape = jax.ShapeDtypeStruct
    field = height * levels * width
    conv_flops = 2 * 33 * field

    low, high = swap(control, control, "lat", False)

    slabs, meta = call(
        owner_kernel,
        (shape((recv_most, slab_rows, LANES), bf16), shape((8, LANES), i32)),
        [VMEM] * 3,
        (VMEM, VMEM),
        0,
        4 * channels * columns,
        name="owner_slabs",
    )(radiance, block_owner.reshape(1, slot_count), channel_count.reshape(1, recv_most))
    all_meta = lax.all_gather(meta, "lat", axis=0, tiled=False)
    all_slabs = lax.all_gather(slabs, "lat", axis=0, tiled=True)

    taps, turned = call(
        prepare_kernel,
        (shape((tiles, 24, LANES), f32), shape((tiles, width, LANES), f32)),
        [SMEM, VMEM],
        (VMEM, VMEM),
        0,
        8 * field,
        name="taps_background",
    )(lon_width, background)

    table = call(
        functools.partial(routing_kernel, recv_most, slot_count),
        shape((8, LANES), i32),
        [VMEM, VMEM],
        VMEM,
        0,
        32768,
        name="routing",
    )(meta, all_meta)

    smoothed, edge_low, edge_high = call(
        lat_smooth_kernel,
        (shape((tiles, width, LANES), f32),) + (shape((tiles, REACH, LANES), f32),) * 2,
        [VMEM] * 3,
        (VMEM,) * 3,
        conv_flops,
        16 * field,
        name="lat_smooth",
    )(low, control, high)
    low, high = swap(edge_high, edge_low, "lon", True)

    x_rows = slot_count * BLOCK_COLS
    landing, edge_low, edge_high = call(
        net_kernel,
        (shape((tiles, width, LANES), f32),) + (shape((tiles, REACH, LANES), bf16),) * 2,
        [SMEM, SMEM] + [VMEM] * 5 + [ANY] + [VMEM] * 6,
        (VMEM,) * 3,
        4 * x_rows * hidden * (LANES + hidden + channels),
        6 * 1024 * 1024,
        scratch=(
            pltpu.VMEM((tiles, width + 2 * REACH, LANES), f32),
            pltpu.VMEM((tiles * width, LANES), f32),
            pltpu.VMEM((x_rows, LANES), f32),
            pltpu.VMEM((LANES, hidden), bf16),
            pltpu.VMEM((x_rows, channels), f32),
            pltpu.VMEM((x_rows, channels), bf16),
            pltpu.VMEM((slot_count, slab_rows, LANES), bf16),
            pltpu.VMEM((x_rows, hidden), bf16),
            pltpu.VMEM((x_rows, hidden), bf16),
            pltpu.SemaphoreType.DMA,
        ),
        name="net",
    )(
        block_cells.reshape(slot_count),
        table,
        low,
        smoothed,
        high,
        turned,
        taps,
        all_slabs,
        in_weight,
        in_bias.reshape(1, hidden),
        mid_weight,
        mid_bias.reshape(1, hidden),
        out_weight,
        out_bias.reshape(1, channels),
    )
    low, high = swap(edge_high, edge_low, "lon", True)

    back = call(
        lon_back_kernel,
        shape((height, levels, width), f32),
        [VMEM] * 4,
        VMEM,
        conv_flops,
        8 * field,
        scratch=(pltpu.VMEM((tiles, width + 2 * REACH, LANES), f32),),
        name="lon_back",
    )(low, landing, high, taps)
    low, high = swap(back, back, "lat", False)

    return call(
        lat_back_kernel,
        shape((height, levels, width), f32),
        [VMEM] * 4,
        VMEM,
        conv_flops,
        20 * field,
        name="lat_back",
    )(low, back, high, control)


def solution(mesh):
    return jax.shard_map(
        shards,
        mesh=mesh,
        in_specs=(
            P("lat", None, "lon"),
            P("lat", None, "lon"),
            P("lat"),
            P("lat", "lon"),
            P("lat", "lon"),
            P("lat", "lon"),
            P("lat", "lon"),
            P(),
            P(),
            P(),
            P(),
            P(),
            P(),
        ),
        out_specs=P("lat", None, "lon"),
        check_vma=False,
    )
```

```python
import functools

import jax
import jax.numpy as jnp
import numpy as np
from jax import lax
from jax.experimental import pallas as pl
from jax.experimental.pallas import tpu as pltpu
from jax.sharding import PartitionSpec as P

REACH = 16
BLOCK_COLS = 8
LANES = 128
LAT_SIGMA = 8.0
VMEM_BYTES = 40 * 1024 * 1024

VMEM = pl.BlockSpec(memory_space=pltpu.VMEM)
SMEM = pl.BlockSpec(memory_space=pltpu.SMEM)
HBM = pl.BlockSpec(memory_space=pltpu.HBM)
ANY = pl.BlockSpec(memory_space=pl.ANY)


def lat_taps():
    offsets = np.arange(-REACH, REACH + 1, dtype=np.float64)
    raw = np.exp(-offsets * offsets / (2.0 * LAT_SIGMA * LAT_SIGMA))
    return [float(v) for v in (raw / np.sqrt(np.sum(raw * raw))).astype(np.float32)]


def call(kernel, out_shape, in_specs, out_specs, flops, bytes_moved, scratch=(), name=None):
    return pl.pallas_call(
        kernel,
        out_shape=out_shape,
        in_specs=in_specs,
        out_specs=out_specs,
        scratch_shapes=list(scratch),
        compiler_params=pltpu.CompilerParams(vmem_limit_bytes=VMEM_BYTES),
        cost_estimate=pl.CostEstimate(flops=flops, bytes_accessed=bytes_moved, transcendentals=0),
        name=name,
    )


def pinned(*values):
    return [pltpu.with_memory_space_constraint(value, pltpu.HBM) for value in values]


def lat_conv_row(row, low, own, high):
    taps = lat_taps()
    height = own.shape[0]
    acc = None
    for j in range(-REACH, REACH + 1):
        source = row + j
        if source < 0:
            part = low[source + REACH].astype(jnp.float32)
        elif source < height:
            part = own[source]
        else:
            part = high[source - height].astype(jnp.float32)
        term = taps[j + REACH] * part
        acc = term if acc is None else acc + term
    return acc


def lon_conv(padded, taps, tile, width):
    acc = taps[tile, 0:1, :] * padded[tile, pl.ds(REACH, width), :]
    for j in range(1, REACH + 1):
        both = padded[tile, pl.ds(REACH + j, width), :] + padded[tile, pl.ds(REACH - j, width), :]
        acc = acc + taps[tile, j : j + 1, :] * both
    return acc


def first_kernel(
    radiance, block_owner, channel_count, control, slabs, held, halved, owners, counts, rows, tables, sems
):
    recv_most = radiance.shape[0]
    moves = [
        pltpu.make_async_copy(radiance, slabs.at[pl.ds(0, recv_most)], sems.at[0]),
        pltpu.make_async_copy(block_owner, owners, sems.at[1]),
        pltpu.make_async_copy(channel_count, counts, sems.at[2]),
        pltpu.make_async_copy(control, held, sems.at[3]),
    ]
    for move in moves:
        move.start()
    rows[...] = jnp.full(rows.shape, -1.0, jnp.float32)
    moves[1].wait()
    moves[2].wait()
    rows[0:1, 0 : owners.shape[1]] = owners[...].astype(jnp.float32)
    rows[1:2, 0 : counts.shape[1]] = counts[...].astype(jnp.float32)
    tables[...] = rows[...].astype(jnp.bfloat16)
    last = pltpu.make_async_copy(tables, slabs.at[recv_most], sems.at[4])
    last.start()
    moves[3].wait()
    halved[...] = held[...].astype(jnp.bfloat16)
    moves[0].wait()
    last.wait()


def prepare_kernel(lon_width, background, taps, turned, widths, field, sems):
    moves = [
        pltpu.make_async_copy(lon_width, widths, sems.at[0]),
        pltpu.make_async_copy(background, field, sems.at[1]),
    ]
    for move in moves:
        move.start()
    tiles = turned.shape[0]
    height, levels, width = background.shape
    per_tile = height // tiles
    lane_row = lax.broadcasted_iota(jnp.int32, (1, LANES), 1) // levels
    steps = lax.broadcasted_iota(jnp.int32, (taps.shape[1], LANES), 0)
    dist = steps.astype(jnp.float32)
    weight = jnp.where(steps == 0, 1.0, jnp.where(steps <= REACH, 2.0, 0.0))
    moves[0].wait()
    for tile in range(tiles):
        spread = jnp.zeros((1, LANES), jnp.int32)
        for sub in range(per_tile):
            spread = jnp.where(lane_row == sub, widths[tile * per_tile + sub], spread)
        spread = spread.astype(jnp.float32)
        raw = jnp.exp(-dist * dist / (2.0 * spread * spread))
        norm = jnp.sum(weight * raw * raw, axis=0, keepdims=True)
        taps[tile] = raw / jnp.sqrt(norm)
    moves[1].wait()
    for tile in range(tiles):
        rows = field[tile * per_tile : (tile + 1) * per_tile].reshape(per_tile * levels, width)
        turned[tile] = jnp.transpose(rows)


def routing(recv_most, slot_count, near, far, table):
    half = near.shape[0]
    here = lax.axis_index("lat")
    parity = here % 2
    rows = lax.broadcasted_iota(jnp.int32, (slot_count, LANES), 0)
    lanes = lax.broadcasted_iota(jnp.int32, (slot_count, LANES), 1)
    diagonal = rows == lanes
    zero = jnp.zeros((slot_count, LANES), jnp.int32)

    def line(ref, k, row):
        return ref[k].astype(jnp.float32)[row : row + 1].astype(jnp.int32)

    mine = line(near, here // 2, 0)
    owner = jnp.sum(jnp.where(diagonal, mine, 0), axis=1, keepdims=True)

    def rank(k, acc):
        for ref, device in ((near, 2 * k + parity), (far, 2 * k + 1 - parity)):
            before = (device < here) | ((device == here) & (lanes < rows))
            acc = acc + jnp.where((line(ref, k, 0) == owner) & before, 1, 0)
        return acc

    unroll = half <= 4
    arrival = jnp.sum(lax.fori_loop(0, half, rank, zero, unroll=unroll), axis=1, keepdims=True)

    def counted(k, acc):
        for ref, device in ((near, 2 * k + parity), (far, 2 * k + 1 - parity)):
            hit = (owner == device) & (lanes == arrival)
            acc = acc + jnp.where(hit, line(ref, k, 1), 0)
        return acc

    kept = jnp.sum(lax.fori_loop(0, half, counted, zero, unroll=unroll), axis=1, keepdims=True)
    live = owner >= 0
    target = jnp.where(live, (owner // 2) * (recv_most + 1) + arrival, 0)
    close = jnp.where(live & (owner % 2 != parity), 0, 1)
    table[...] = jnp.zeros_like(table)
    for row, column in enumerate((target, kept, close)):
        table[row : row + 1, :] = jnp.sum(jnp.where(diagonal, column, 0), axis=0, keepdims=True)


def lat_smooth_kernel(low, own, high, smoothed, edge_low, edge_high):
    tiles = smoothed.shape[0]
    height, levels, width = own.shape
    per_tile = height // tiles
    for tile in range(tiles):
        rows = [lat_conv_row(tile * per_tile + sub, low, own, high) for sub in range(per_tile)]
        turned = jnp.transpose(jnp.concatenate(rows, axis=0))
        smoothed[tile] = turned
        edge_low[tile] = turned[0:REACH]
        edge_high[tile] = turned[width - REACH : width]


def block_place(cells, slot, groups, per_tile, width):
    block = cells[slot]
    row = block // groups
    start = (row // per_tile) * width + (block % groups) * BLOCK_COLS
    return pl.multiple_of(start, BLOCK_COLS), row % per_tile


def dot(a, b):
    return jnp.dot(a, b, preferred_element_type=jnp.float32)


def dot_t(a, b):
    return lax.dot_general(a, b, (((1,), (1,)), ((), ())), preferred_element_type=jnp.float32)


def forward_kernel(
    block_cells,
    low,
    own,
    high,
    turned,
    taps,
    in_weight,
    in_bias,
    mid_weight,
    mid_bias,
    out_weight,
    out_bias,
    act_one,
    act_two,
    emitted,
    wide_in,
    weight_two,
    weight_out,
    cells,
    padded,
    profile,
    picked,
    bias_one,
    bias_two,
    bias_out,
    sems,
):
    tiles, width, _ = own.shape
    levels = in_weight.shape[0]
    per_tile = LANES // levels
    groups = width // BLOCK_COLS
    slot_count = block_cells.shape[0]

    cells_in = pltpu.make_async_copy(block_cells, cells, sems.at[0])
    first_in = [
        pltpu.make_async_copy(in_weight, wide_in.at[pl.ds(sub * levels, levels)], sems.at[1 + sub])
        for sub in range(per_tile)
    ] + [pltpu.make_async_copy(in_bias, bias_one, sems.at[1 + per_tile])]
    mid_in = [
        pltpu.make_async_copy(mid_weight, weight_two, sems.at[2 + per_tile]),
        pltpu.make_async_copy(mid_bias, bias_two, sems.at[3 + per_tile]),
    ]
    out_in = [
        pltpu.make_async_copy(out_weight, weight_out, sems.at[4 + per_tile]),
        pltpu.make_async_copy(out_bias, bias_out, sems.at[5 + per_tile]),
    ]
    for move in [cells_in] + first_in + mid_in + out_in:
        move.start()

    padded[:, 0:REACH, :] = low[...]
    padded[:, REACH : REACH + width, :] = own[...]
    padded[:, REACH + width :, :] = high[...]
    for tile in range(tiles):
        total = turned[tile] + lon_conv(padded, taps, tile, width)
        profile[tile * width : (tile + 1) * width, :] = total.astype(jnp.bfloat16).astype(jnp.float32)

    lane_row = lax.broadcasted_iota(jnp.int32, (BLOCK_COLS, LANES), 1) // levels
    cells_in.wait()
    for slot in range(slot_count):
        start, sub = block_place(cells, slot, groups, per_tile, width)
        block = profile[pl.ds(start, BLOCK_COLS), :]
        picked[slot * BLOCK_COLS : (slot + 1) * BLOCK_COLS, :] = jnp.where(lane_row == sub, block, 0.0)

    for move in first_in:
        move.wait()
    inputs = picked[...].astype(jnp.bfloat16)
    act_one[...] = jnp.tanh(dot(inputs, wide_in[...]) + bias_one[...]).astype(jnp.bfloat16)
    for move in mid_in:
        move.wait()
    act_two[...] = jnp.tanh(dot(act_one[...], weight_two[...]) + bias_two[...]).astype(jnp.bfloat16)
    for move in out_in:
        move.wait()
    emitted[...] = dot(act_two[...], weight_out[...]) + bias_out[...]


def backward_kernel(
    per_tile,
    block_cells,
    near,
    far,
    act_one,
    act_two,
    emitted,
    wide_in,
    weight_two,
    weight_out,
    landing,
    edge_low,
    edge_high,
    cells,
    near_tables,
    far_tables,
    table_rows,
    table,
    field,
    picked,
    misfit,
    observed,
    sems,
):
    tiles, width, _ = landing.shape
    half = near_tables.shape[0]
    per_owner = near.shape[0] // half
    slot_count = block_cells.shape[0]
    channels = weight_out.shape[1]
    groups = width // BLOCK_COLS
    levels = LANES // per_tile

    def tables_in(ref, rows, sem):
        return [
            pltpu.make_async_copy(ref.at[k * per_owner + per_owner - 1], rows.at[k], sem.at[k])
            for k in range(half)
        ]

    routes = tables_in(near, near_tables, sems.at[0]) + tables_in(far, far_tables, sems.at[1])
    cells_in = pltpu.make_async_copy(block_cells, cells, sems.at[2, 0])
    for move in routes + [cells_in]:
        move.start()
    field[...] = jnp.zeros_like(field)
    for move in routes:
        move.wait()
    routing(per_owner - 1, slot_count, near_tables, far_tables, table_rows)
    table_in = pltpu.make_async_copy(table_rows, table, sems.at[2, 1])
    table_in.start()
    table_in.wait()

    def fetch(slot, carry):
        for ref, close in ((near, 1), (far, 0)):

            @pl.when(table[2, slot] == close)
            def _():
                pltpu.make_async_copy(ref.at[table[0, slot]], observed.at[slot], sems.at[2, 2]).start()

        return carry

    lax.fori_loop(0, slot_count, fetch, 0, unroll=8)
    pltpu.make_async_copy(near.at[pl.ds(0, slot_count)], observed, sems.at[2, 2]).wait()

    channel = lax.broadcasted_iota(jnp.int32, (BLOCK_COLS, channels), 1)
    for slot in range(0, slot_count, 2):
        pair = []
        for at in (slot, slot + 1):
            slab = observed[at].astype(jnp.float32)
            seen = jnp.concatenate(
                [slab[h * BLOCK_COLS : (h + 1) * BLOCK_COLS] for h in range(channels // LANES)], axis=1
            )
            gap = emitted[at * BLOCK_COLS : (at + 1) * BLOCK_COLS, :] - seen
            pair.append(jnp.where(channel < table[1, at], gap, 0.0))
        misfit[slot * BLOCK_COLS : (slot + 2) * BLOCK_COLS, :] = jnp.concatenate(pair, axis=0).astype(
            jnp.bfloat16
        )

    two = act_two[...].astype(jnp.float32)
    grad_two = (dot_t(misfit[...], weight_out[...]) * (1.0 - two * two)).astype(jnp.bfloat16)
    one = act_one[...].astype(jnp.float32)
    grad_one = (dot_t(grad_two, weight_two[...]) * (1.0 - one * one)).astype(jnp.bfloat16)
    picked[...] = dot_t(grad_one, wide_in[...]).astype(jnp.bfloat16).astype(jnp.float32)

    lane_row = lax.broadcasted_iota(jnp.int32, (BLOCK_COLS, LANES), 1) // levels
    cells_in.wait()
    for slot in range(slot_count):
        start, sub = block_place(cells, slot, groups, per_tile, width)
        block = picked[slot * BLOCK_COLS : (slot + 1) * BLOCK_COLS, :]
        field[pl.ds(start, BLOCK_COLS), :] += jnp.where(lane_row == sub, block, 0.0)
    for tile in range(tiles):
        landing[tile] = field[tile * width : (tile + 1) * width, :]
        edge_low[tile] = field[tile * width : tile * width + REACH, :].astype(jnp.bfloat16)
        edge_high[tile] = field[(tile + 1) * width - REACH : (tile + 1) * width, :].astype(jnp.bfloat16)


def lon_back_kernel(low, own, high, taps, back, halved, padded):
    tiles, width, _ = own.shape
    height, levels, _ = back.shape
    per_tile = height // tiles
    padded[:, 0:REACH, :] = low[...].astype(jnp.float32)
    padded[:, REACH : REACH + width, :] = own[...]
    padded[:, REACH + width :, :] = high[...].astype(jnp.float32)
    for tile in range(tiles):
        rows = jnp.transpose(lon_conv(padded, taps, tile, width))
        rows = rows.reshape(per_tile, levels, width)
        back[tile * per_tile : (tile + 1) * per_tile] = rows
        halved[tile * per_tile : (tile + 1) * per_tile] = rows.astype(jnp.bfloat16)


def lat_back_kernel(low, own, high, control, gradient):
    for row in range(own.shape[0]):
        gradient[row] = control[row] + lat_conv_row(row, low, own, high)


def swap(forward_value, backward_value, axis, periodic):
    count = lax.axis_size(axis)
    forward = [(i, i + 1) for i in range(count - 1)]
    if periodic:
        forward.append((count - 1, 0))
    backward = [(target, source) for source, target in forward]
    return lax.ppermute(forward_value, axis, forward), lax.ppermute(backward_value, axis, backward)


def shards(
    control,
    background,
    lon_width,
    block_cells,
    block_owner,
    channel_count,
    radiance,
    in_weight,
    in_bias,
    mid_weight,
    mid_bias,
    out_weight,
    out_bias,
):
    height, levels, width = control.shape
    hidden = mid_weight.shape[0]
    channels, columns = radiance.shape
    slot_count = block_owner.shape[0]
    recv_most = channel_count.shape[0]
    per_tile = LANES // levels
    tiles = height // per_tile
    slab_rows = BLOCK_COLS * channels // LANES
    f32, bf16, i32 = jnp.float32, jnp.bfloat16, jnp.int32
    shape = jax.ShapeDtypeStruct
    field = height * levels * width
    conv_flops = 2 * 33 * field

    halves = channels // LANES
    radiance = radiance.T.reshape(recv_most, BLOCK_COLS, halves, LANES)
    radiance = jnp.swapaxes(radiance, 1, 2).reshape(recv_most, slab_rows, LANES)
    slabs, held, halved = call(
        first_kernel,
        (
            shape((recv_most + 1, slab_rows, LANES), bf16),
            shape(control.shape, f32),
            shape(control.shape, bf16),
        ),
        [HBM] * 4,
        (HBM, VMEM, VMEM),
        0,
        16 * field,
        scratch=(
            pltpu.VMEM((1, slot_count), i32),
            pltpu.VMEM((1, recv_most), i32),
            pltpu.VMEM((slab_rows, LANES), f32),
            pltpu.VMEM((slab_rows, LANES), bf16),
            pltpu.SemaphoreType.DMA((5,)),
        ),
        name="slabs_halves",
    )(*pinned(radiance, block_owner.reshape(1, slot_count), channel_count.reshape(1, recv_most), control))

    lat_count = lax.axis_size("lat")
    parities = [list(range(start, lat_count, 2)) for start in range(2)]
    near = lax.all_gather(slabs, "lat", axis=0, tiled=True, axis_index_groups=parities)
    low, high = swap(halved, halved, "lat", False)

    taps, turned = call(
        prepare_kernel,
        (shape((tiles, 24, LANES), f32), shape((tiles, width, LANES), f32)),
        [HBM, HBM],
        (VMEM, VMEM),
        0,
        8 * field,
        scratch=(
            pltpu.SMEM((height,), i32),
            pltpu.VMEM((height, levels, width), f32),
            pltpu.SemaphoreType.DMA((2,)),
        ),
        name="taps_background",
    )(*pinned(lon_width, background))

    smoothed, edge_low, edge_high = call(
        lat_smooth_kernel,
        (shape((tiles, width, LANES), f32),) + (shape((tiles, REACH, LANES), f32),) * 2,
        [VMEM] * 3,
        (VMEM,) * 3,
        conv_flops,
        16 * field,
        name="lat_smooth",
    )(low, held, high)
    low, high = swap(edge_high, edge_low, "lon", True)
    near, low, high = lax.optimization_barrier((near, low, high))
    far = lax.ppermute(near, "lat", [(i, i ^ 1) for i in range(lat_count)])

    x_rows = slot_count * BLOCK_COLS
    net_flops = 2 * x_rows * hidden * (LANES + hidden + channels)
    cells = block_cells.reshape(slot_count)
    states = call(
        forward_kernel,
        (
            shape((x_rows, hidden), bf16),
            shape((x_rows, hidden), bf16),
            shape((x_rows, channels), f32),
            shape((LANES, hidden), bf16),
            shape((hidden, hidden), bf16),
            shape((hidden, channels), bf16),
        ),
        [HBM] + [VMEM] * 5 + [HBM] * 6,
        (VMEM,) * 6,
        net_flops,
        6 * 1024 * 1024,
        scratch=(
            pltpu.SMEM((slot_count,), i32),
            pltpu.VMEM((tiles, width + 2 * REACH, LANES), f32),
            pltpu.VMEM((tiles * width, LANES), f32),
            pltpu.VMEM((x_rows, LANES), f32),
            pltpu.VMEM((1, hidden), f32),
            pltpu.VMEM((1, hidden), f32),
            pltpu.VMEM((1, channels), f32),
            pltpu.SemaphoreType.DMA((6 + per_tile,)),
        ),
        name="net_forward",
    )(
        *pinned(cells),
        low,
        smoothed,
        high,
        turned,
        taps,
        *pinned(
            in_weight,
            in_bias.reshape(1, hidden),
            mid_weight,
            mid_bias.reshape(1, hidden),
            out_weight,
            out_bias.reshape(1, channels),
        ),
    )

    landing, edge_low, edge_high = call(
        functools.partial(backward_kernel, per_tile),
        (shape((tiles, width, LANES), f32),) + (shape((tiles, REACH, LANES), bf16),) * 2,
        [HBM, HBM, ANY] + [VMEM] * 6,
        (VMEM,) * 3,
        net_flops,
        6 * 1024 * 1024,
        scratch=(
            pltpu.SMEM((slot_count,), i32),
            pltpu.VMEM((lat_count // 2, slab_rows, LANES), bf16),
            pltpu.VMEM((lat_count // 2, slab_rows, LANES), bf16),
            pltpu.VMEM((8, LANES), i32),
            pltpu.SMEM((8, LANES), i32),
            pltpu.VMEM((tiles * width, LANES), f32),
            pltpu.VMEM((x_rows, LANES), f32),
            pltpu.VMEM((x_rows, channels), bf16),
            pltpu.VMEM((slot_count, slab_rows, LANES), bf16),
            pltpu.SemaphoreType.DMA((3, max(4, lat_count // 2))),
        ),
        name="net_backward",
    )(*pinned(cells, near), far, *states)
    low, high = swap(edge_high, edge_low, "lon", True)

    back, halved = call(
        lon_back_kernel,
        (shape((height, levels, width), f32), shape((height, levels, width), bf16)),
        [VMEM] * 4,
        (VMEM, VMEM),
        conv_flops,
        8 * field,
        scratch=(pltpu.VMEM((tiles, width + 2 * REACH, LANES), f32),),
        name="lon_back",
    )(low, landing, high, taps)
    low, high = swap(halved, halved, "lat", False)

    return call(
        lat_back_kernel,
        shape((height, levels, width), f32),
        [VMEM] * 4,
        VMEM,
        conv_flops,
        20 * field,
        name="lat_back",
    )(low, back, high, held)


def solution(mesh):
    return jax.shard_map(
        shards,
        mesh=mesh,
        in_specs=(
            P("lat", None, "lon"),
            P("lat", None, "lon"),
            P("lat"),
            P("lat", "lon"),
            P("lat", "lon"),
            P("lat", "lon"),
            P("lat", "lon"),
            P(),
            P(),
            P(),
            P(),
            P(),
            P(),
        ),
        out_specs=P("lat", None, "lon"),
        check_vma=False,
    )
```

```python
import functools

import jax
import jax.numpy as jnp
import numpy as np
from jax import lax
from jax.experimental import pallas as pl
from jax.experimental.pallas import tpu as pltpu
from jax.sharding import PartitionSpec as P

REACH = 16
BLOCK_COLS = 8
LANES = 128
LAT_SIGMA = 8.0
VMEM_BYTES = 40 * 1024 * 1024

VMEM = pl.BlockSpec(memory_space=pltpu.VMEM)
SMEM = pl.BlockSpec(memory_space=pltpu.SMEM)
HBM = pl.BlockSpec(memory_space=pltpu.HBM)
ANY = pl.BlockSpec(memory_space=pl.ANY)


def lat_taps():
    offsets = np.arange(-REACH, REACH + 1, dtype=np.float64)
    raw = np.exp(-offsets * offsets / (2.0 * LAT_SIGMA * LAT_SIGMA))
    return [float(v) for v in (raw / np.sqrt(np.sum(raw * raw))).astype(np.float32)]


def call(kernel, out_shape, in_specs, out_specs, flops, bytes_moved, scratch=(), name=None):
    return pl.pallas_call(
        kernel,
        out_shape=out_shape,
        in_specs=in_specs,
        out_specs=out_specs,
        scratch_shapes=list(scratch),
        compiler_params=pltpu.CompilerParams(vmem_limit_bytes=VMEM_BYTES),
        cost_estimate=pl.CostEstimate(flops=flops, bytes_accessed=bytes_moved, transcendentals=0),
        name=name,
    )


def pinned(*values):
    return [pltpu.with_memory_space_constraint(value, pltpu.HBM) for value in values]


def lat_conv_row(row, low, own, high):
    taps = lat_taps()
    height = own.shape[0]
    acc = None
    for j in range(-REACH, REACH + 1):
        source = row + j
        if source < 0:
            part = low[source + REACH]
        elif source < height:
            part = own[source]
        else:
            part = high[source - height]
        term = taps[j + REACH] * part
        acc = term if acc is None else acc + term
    return acc


def fill_padded(padded, far, own, close):
    width = own.shape[1]
    low, high = sides(far[...], close[...], "lon")
    padded[:, 0:REACH, :] = low
    padded[:, REACH : REACH + width, :] = own[...]
    padded[:, REACH + width :, :] = high


def lon_conv(padded, taps, tile, width):
    acc = taps[tile, 0:1, :] * padded[tile, pl.ds(REACH, width), :]
    for j in range(1, REACH + 1):
        both = padded[tile, pl.ds(REACH + j, width), :] + padded[tile, pl.ds(REACH - j, width), :]
        acc = acc + taps[tile, j : j + 1, :] * both
    return acc


def first_kernel(
    radiance, block_owner, channel_count, control, slabs, held, halved, owners, counts, rows, tables, sems
):
    recv_most = radiance.shape[0]
    moves = [
        pltpu.make_async_copy(radiance, slabs.at[pl.ds(0, recv_most)], sems.at[0]),
        pltpu.make_async_copy(block_owner, owners, sems.at[1]),
        pltpu.make_async_copy(channel_count, counts, sems.at[2]),
        pltpu.make_async_copy(control, held, sems.at[3]),
    ]
    for move in moves:
        move.start()
    rows[...] = jnp.full(rows.shape, -1.0, jnp.float32)
    moves[1].wait()
    moves[2].wait()
    rows[0:1, 0 : owners.shape[1]] = owners[...].astype(jnp.float32)
    rows[1:2, 0 : counts.shape[1]] = counts[...].astype(jnp.float32)
    tables[...] = rows[...].astype(jnp.bfloat16)
    last = pltpu.make_async_copy(tables, slabs.at[recv_most], sems.at[4])
    last.start()
    moves[3].wait()
    halved[...] = held[...].astype(jnp.bfloat16)
    moves[0].wait()
    last.wait()


def prepare_kernel(lon_width, background, taps, turned, widths, field, sems):
    moves = [
        pltpu.make_async_copy(lon_width, widths, sems.at[0]),
        pltpu.make_async_copy(background, field, sems.at[1]),
    ]
    for move in moves:
        move.start()
    tiles = turned.shape[0]
    height, levels, width = background.shape
    per_tile = height // tiles
    lane_row = lax.broadcasted_iota(jnp.int32, (1, LANES), 1) // levels
    steps = lax.broadcasted_iota(jnp.int32, (taps.shape[1], LANES), 0)
    dist = steps.astype(jnp.float32)
    weight = jnp.where(steps == 0, 1.0, jnp.where(steps <= REACH, 2.0, 0.0))
    moves[0].wait()
    for tile in range(tiles):
        spread = jnp.zeros((1, LANES), jnp.int32)
        for sub in range(per_tile):
            spread = jnp.where(lane_row == sub, widths[tile * per_tile + sub], spread)
        spread = spread.astype(jnp.float32)
        raw = jnp.exp(-dist * dist / (2.0 * spread * spread))
        norm = jnp.sum(weight * raw * raw, axis=0, keepdims=True)
        taps[tile] = raw / jnp.sqrt(norm)
    moves[1].wait()
    for tile in range(tiles):
        rows = field[tile * per_tile : (tile + 1) * per_tile].reshape(per_tile * levels, width)
        turned[tile] = jnp.transpose(rows)


def routing(recv_most, slot_count, tables, table):
    count = tables.shape[0]
    half = count // 2
    here = lax.axis_index("lat")
    rows = lax.broadcasted_iota(jnp.int32, (slot_count, LANES), 0)
    lanes = lax.broadcasted_iota(jnp.int32, (slot_count, LANES), 1)
    diagonal = rows == lanes
    zero = jnp.zeros((slot_count, LANES), jnp.int32)

    def device_of(k):
        return here ^ jnp.where(k < half, 2 * k, 2 * (k - half) + 1)

    def line(k, row):
        return tables[k].astype(jnp.float32)[row : row + 1].astype(jnp.int32)

    owner = jnp.sum(jnp.where(diagonal, line(0, 0), 0), axis=1, keepdims=True)

    def rank(k, acc):
        device = device_of(k)
        before = (device < here) | ((device == here) & (lanes < rows))
        return acc + jnp.where((line(k, 0) == owner) & before, 1, 0)

    unroll = count <= 8
    arrival = jnp.sum(lax.fori_loop(0, count, rank, zero, unroll=unroll), axis=1, keepdims=True)

    def counted(k, acc):
        hit = (owner == device_of(k)) & (lanes == arrival)
        return acc + jnp.where(hit, line(k, 1), 0)

    kept = jnp.sum(lax.fori_loop(0, count, counted, zero, unroll=unroll), axis=1, keepdims=True)
    apart = owner ^ here
    place = (apart >> 1) + (apart & 1) * half
    target = jnp.where(owner >= 0, place * (recv_most + 1) + arrival, 0)
    table[...] = jnp.zeros_like(table)
    for row, column in enumerate((target, kept)):
        table[row : row + 1, :] = jnp.sum(jnp.where(diagonal, column, 0), axis=0, keepdims=True)


def odd_index(axis):
    return lax.axis_index(axis) % 2 == 1


def sides(far, close, axis):
    odd = odd_index(axis)
    far, close = far.astype(jnp.float32), close.astype(jnp.float32)
    return jnp.where(odd, close, far), jnp.where(odd, far, close)


def split_sides(low, high, axis):
    odd = odd_index(axis)
    return jnp.where(odd, high, low), jnp.where(odd, low, high)


def lat_smooth_kernel(far, close, own, smoothed, to_far, to_close, halos):
    tiles = smoothed.shape[0]
    height, levels, width = own.shape
    per_tile = height // tiles
    halos[0], halos[1] = sides(far[...], close[...], "lat")
    for tile in range(tiles):
        rows = [
            lat_conv_row(tile * per_tile + sub, halos.at[0], own, halos.at[1]) for sub in range(per_tile)
        ]
        turned = jnp.transpose(jnp.concatenate(rows, axis=0))
        smoothed[tile] = turned
        to_far[tile], to_close[tile] = split_sides(turned[0:REACH], turned[width - REACH : width], "lon")


def block_place(cells, slot, groups, per_tile, width):
    block = cells[slot]
    row = block // groups
    start = (row // per_tile) * width + (block % groups) * BLOCK_COLS
    return pl.multiple_of(start, BLOCK_COLS), row % per_tile


def dot(a, b):
    return jnp.dot(a, b, preferred_element_type=jnp.float32)


def dot_t(a, b):
    return lax.dot_general(a, b, (((1,), (1,)), ((), ())), preferred_element_type=jnp.float32)


def forward_kernel(
    block_cells,
    far,
    close,
    own,
    turned,
    taps,
    in_weight,
    in_bias,
    mid_weight,
    mid_bias,
    out_weight,
    out_bias,
    act_one,
    act_two,
    emitted,
    wide_in,
    weight_two,
    weight_out,
    cells,
    padded,
    profile,
    picked,
    bias_one,
    bias_two,
    bias_out,
    sems,
):
    tiles, width, _ = own.shape
    levels = in_weight.shape[0]
    per_tile = LANES // levels
    groups = width // BLOCK_COLS
    slot_count = block_cells.shape[0]

    cells_in = pltpu.make_async_copy(block_cells, cells, sems.at[0])
    first_in = [
        pltpu.make_async_copy(in_weight, wide_in.at[pl.ds(sub * levels, levels)], sems.at[1 + sub])
        for sub in range(per_tile)
    ] + [pltpu.make_async_copy(in_bias, bias_one, sems.at[1 + per_tile])]
    mid_in = [
        pltpu.make_async_copy(mid_weight, weight_two, sems.at[2 + per_tile]),
        pltpu.make_async_copy(mid_bias, bias_two, sems.at[3 + per_tile]),
    ]
    out_in = [
        pltpu.make_async_copy(out_weight, weight_out, sems.at[4 + per_tile]),
        pltpu.make_async_copy(out_bias, bias_out, sems.at[5 + per_tile]),
    ]
    for move in [cells_in] + first_in + mid_in + out_in:
        move.start()

    fill_padded(padded, far, own, close)
    for tile in range(tiles):
        total = turned[tile] + lon_conv(padded, taps, tile, width)
        profile[tile * width : (tile + 1) * width, :] = total.astype(jnp.bfloat16).astype(jnp.float32)

    lane_row = lax.broadcasted_iota(jnp.int32, (BLOCK_COLS, LANES), 1) // levels
    cells_in.wait()
    for slot in range(slot_count):
        start, sub = block_place(cells, slot, groups, per_tile, width)
        block = profile[pl.ds(start, BLOCK_COLS), :]
        picked[slot * BLOCK_COLS : (slot + 1) * BLOCK_COLS, :] = jnp.where(lane_row == sub, block, 0.0)

    for move in first_in:
        move.wait()
    inputs = picked[...].astype(jnp.bfloat16)
    act_one[...] = jnp.tanh(dot(inputs, wide_in[...]) + bias_one[...]).astype(jnp.bfloat16)
    for move in mid_in:
        move.wait()
    act_two[...] = jnp.tanh(dot(act_one[...], weight_two[...]) + bias_two[...]).astype(jnp.bfloat16)
    for move in out_in:
        move.wait()
    emitted[...] = dot(act_two[...], weight_out[...]) + bias_out[...]


def backward_kernel(
    per_tile,
    parts,
    block_cells,
    *refs,
):
    slabs, refs = refs[:parts], refs[parts:]
    (act_one, act_two, emitted, wide_in, weight_two, weight_out) = refs[:6]
    (landing, to_far, to_close) = refs[6:9]
    (cells, tables, table_rows, table, held, observed, field, picked, sems) = refs[9:]
    tiles, width, _ = landing.shape
    owners = tables.shape[0]
    per_owner = held.shape[0] // owners
    slot_count = block_cells.shape[0]
    channels = weight_out.shape[1]
    groups = width // BLOCK_COLS
    levels = LANES // per_tile

    routes, bulk = [], []
    for part, ref in enumerate(slabs):
        sets = ref.shape[0] // per_owner
        for k in range(sets):
            entry = len(routes)
            source = ref.at[k * per_owner + per_owner - 1]
            routes.append(pltpu.make_async_copy(source, tables.at[entry], sems.at[entry]))
        start = len(routes) - sets
        bulk.append(
            pltpu.make_async_copy(
                ref, held.at[pl.ds(start * per_owner, ref.shape[0])], sems.at[owners + part]
            )
        )
    cells_in = pltpu.make_async_copy(block_cells, cells, sems.at[owners + parts])
    for move in routes + [cells_in] + bulk:
        move.start()
    field[...] = jnp.zeros_like(field)
    for move in routes:
        move.wait()
    routing(per_owner - 1, slot_count, tables, table_rows)
    table_in = pltpu.make_async_copy(table_rows, table, sems.at[owners + parts + 1])
    table_in.start()
    for move in bulk + [table_in]:
        move.wait()

    channel = lax.broadcasted_iota(jnp.int32, (BLOCK_COLS, LANES), 1)
    for slot in range(slot_count):
        slab = held[table[0, slot]].astype(jnp.float32)
        for h in range(channels // LANES):
            part = slab[h * BLOCK_COLS : (h + 1) * BLOCK_COLS]
            kept = channel + h * LANES < table[1, slot]
            observed[slot * BLOCK_COLS : (slot + 1) * BLOCK_COLS, h * LANES : (h + 1) * LANES] = jnp.where(
                kept, part, jnp.inf
            )

    seen = observed[...]
    misfit = jnp.where(seen < jnp.inf, emitted[...] - seen, 0.0).astype(jnp.bfloat16)
    two = act_two[...].astype(jnp.float32)
    grad_two = (dot_t(misfit, weight_out[...]) * (1.0 - two * two)).astype(jnp.bfloat16)
    one = act_one[...].astype(jnp.float32)
    grad_one = (dot_t(grad_two, weight_two[...]) * (1.0 - one * one)).astype(jnp.bfloat16)
    picked[...] = dot_t(grad_one, wide_in[...]).astype(jnp.bfloat16).astype(jnp.float32)

    lane_row = lax.broadcasted_iota(jnp.int32, (BLOCK_COLS, LANES), 1) // levels
    cells_in.wait()
    for slot in range(slot_count):
        start, sub = block_place(cells, slot, groups, per_tile, width)
        block = picked[slot * BLOCK_COLS : (slot + 1) * BLOCK_COLS, :]
        field[pl.ds(start, BLOCK_COLS), :] += jnp.where(lane_row == sub, block, 0.0)
    for tile in range(tiles):
        landing[tile] = field[tile * width : (tile + 1) * width, :]
        low = field[tile * width : tile * width + REACH, :]
        high = field[(tile + 1) * width - REACH : (tile + 1) * width, :]
        low, high = split_sides(low, high, "lon")
        to_far[tile], to_close[tile] = low.astype(jnp.bfloat16), high.astype(jnp.bfloat16)


def lon_back_kernel(far, close, own, taps, back, halved, padded):
    tiles, width, _ = own.shape
    height, levels, _ = back.shape
    per_tile = height // tiles
    fill_padded(padded, far, own, close)
    for tile in range(tiles):
        rows = jnp.transpose(lon_conv(padded, taps, tile, width))
        rows = rows.reshape(per_tile, levels, width)
        back[tile * per_tile : (tile + 1) * per_tile] = rows
        halved[tile * per_tile : (tile + 1) * per_tile] = rows.astype(jnp.bfloat16)


def lat_back_kernel(far, close, own, control, gradient, halos):
    halos[0], halos[1] = sides(far[...], close[...], "lat")
    for row in range(own.shape[0]):
        gradient[row] = control[row] + lat_conv_row(row, halos.at[0], own, halos.at[1])


def exchange(to_far, to_close, axis, periodic):
    count = lax.axis_size(axis)
    far = []
    for odd in range(1, count, 2):
        if odd + 1 < count or periodic:
            far += [(odd, (odd + 1) % count), ((odd + 1) % count, odd)]
    close = [(i, i ^ 1) for i in range(count)]
    return lax.ppermute(to_far, axis, far), lax.ppermute(to_close, axis, close)


def shards(
    control,
    background,
    lon_width,
    block_cells,
    block_owner,
    channel_count,
    radiance,
    in_weight,
    in_bias,
    mid_weight,
    mid_bias,
    out_weight,
    out_bias,
):
    height, levels, width = control.shape
    hidden = mid_weight.shape[0]
    channels, columns = radiance.shape
    slot_count = block_owner.shape[0]
    recv_most = channel_count.shape[0]
    per_tile = LANES // levels
    tiles = height // per_tile
    slab_rows = BLOCK_COLS * channels // LANES
    f32, bf16, i32 = jnp.float32, jnp.bfloat16, jnp.int32
    shape = jax.ShapeDtypeStruct
    field = height * levels * width
    conv_flops = 2 * 33 * field

    halves = channels // LANES
    radiance = radiance.T.reshape(recv_most, BLOCK_COLS, halves, LANES)
    radiance = jnp.swapaxes(radiance, 1, 2).reshape(recv_most, slab_rows, LANES)
    slabs, held, halved = call(
        first_kernel,
        (
            shape((recv_most + 1, slab_rows, LANES), bf16),
            shape(control.shape, f32),
            shape(control.shape, bf16),
        ),
        [HBM] * 4,
        (HBM, VMEM, VMEM),
        0,
        16 * field,
        scratch=(
            pltpu.VMEM((1, slot_count), i32),
            pltpu.VMEM((1, recv_most), i32),
            pltpu.VMEM((slab_rows, LANES), f32),
            pltpu.VMEM((slab_rows, LANES), bf16),
            pltpu.SemaphoreType.DMA((5,)),
        ),
        name="slabs_halves",
    )(*pinned(radiance, block_owner.reshape(1, slot_count), channel_count.reshape(1, recv_most), control))

    lat_count = lax.axis_size("lat")
    near = [slabs]
    for bit in range(1, lat_count.bit_length() - 1):
        held_sets = near[0] if len(near) == 1 else jnp.concatenate(near, axis=0)
        near = [held_sets, lax.ppermute(held_sets, "lat", [(i, i ^ (1 << bit)) for i in range(lat_count)])]
        if bit == 1:
            far, close = exchange(halved, halved, "lat", False)
            near[1], far, close = lax.optimization_barrier((near[1], far, close))

    taps, turned = call(
        prepare_kernel,
        (shape((tiles, 24, LANES), f32), shape((tiles, width, LANES), f32)),
        [HBM, HBM],
        (VMEM, VMEM),
        0,
        8 * field,
        scratch=(
            pltpu.SMEM((height,), i32),
            pltpu.VMEM((height, levels, width), f32),
            pltpu.SemaphoreType.DMA((2,)),
        ),
        name="taps_background",
    )(*pinned(lon_width, background))

    halos = pltpu.VMEM((2, REACH, levels, width), f32)
    smoothed, to_far, to_close = call(
        lat_smooth_kernel,
        (shape((tiles, width, LANES), f32),) + (shape((tiles, REACH, LANES), f32),) * 2,
        [VMEM] * 3,
        (VMEM,) * 3,
        conv_flops,
        16 * field,
        scratch=(halos,),
        name="lat_smooth",
    )(far, close, held)
    far, close = exchange(to_far, to_close, "lon", True)
    near, far, close = lax.optimization_barrier((near, far, close))
    across = [lax.ppermute(part, "lat", [(i, i ^ 1) for i in range(lat_count)]) for part in near]

    x_rows = slot_count * BLOCK_COLS
    net_flops = 2 * x_rows * hidden * (LANES + hidden + channels)
    cells = block_cells.reshape(slot_count)
    states = call(
        forward_kernel,
        (
            shape((x_rows, hidden), bf16),
            shape((x_rows, hidden), bf16),
            shape((x_rows, channels), f32),
            shape((LANES, hidden), bf16),
            shape((hidden, hidden), bf16),
            shape((hidden, channels), bf16),
        ),
        [HBM] + [VMEM] * 5 + [HBM] * 6,
        (VMEM,) * 6,
        net_flops,
        6 * 1024 * 1024,
        scratch=(
            pltpu.SMEM((slot_count,), i32),
            pltpu.VMEM((tiles, width + 2 * REACH, LANES), f32),
            pltpu.VMEM((tiles * width, LANES), f32),
            pltpu.VMEM((x_rows, LANES), f32),
            pltpu.VMEM((1, hidden), f32),
            pltpu.VMEM((1, hidden), f32),
            pltpu.VMEM((1, channels), f32),
            pltpu.SemaphoreType.DMA((6 + per_tile,)),
        ),
        name="net_forward",
    )(
        *pinned(cells),
        far,
        close,
        smoothed,
        turned,
        taps,
        *pinned(
            in_weight,
            in_bias.reshape(1, hidden),
            mid_weight,
            mid_bias.reshape(1, hidden),
            out_weight,
            out_bias.reshape(1, channels),
        ),
    )

    slabs = [*near, *across]
    landing, to_far, to_close = call(
        functools.partial(backward_kernel, per_tile, len(slabs)),
        (shape((tiles, width, LANES), f32),) + (shape((tiles, REACH, LANES), bf16),) * 2,
        [HBM] + [ANY] * len(slabs) + [VMEM] * 6,
        (VMEM,) * 3,
        net_flops,
        6 * 1024 * 1024,
        scratch=(
            pltpu.SMEM((slot_count,), i32),
            pltpu.VMEM((lat_count, slab_rows, LANES), bf16),
            pltpu.VMEM((8, LANES), i32),
            pltpu.SMEM((8, LANES), i32),
            pltpu.VMEM((lat_count * (recv_most + 1), slab_rows, LANES), bf16),
            pltpu.VMEM((x_rows, channels), f32),
            pltpu.VMEM((tiles * width, LANES), f32),
            pltpu.VMEM((x_rows, LANES), f32),
            pltpu.SemaphoreType.DMA((lat_count + len(slabs) + 2,)),
        ),
        name="net_backward",
    )(*pinned(cells), *slabs, *states)
    far, close = exchange(to_far, to_close, "lon", True)

    back, halved = call(
        lon_back_kernel,
        (shape((height, levels, width), f32), shape((height, levels, width), bf16)),
        [VMEM] * 4,
        (VMEM, VMEM),
        conv_flops,
        8 * field,
        scratch=(pltpu.VMEM((tiles, width + 2 * REACH, LANES), f32),),
        name="lon_back",
    )(far, close, landing, taps)
    far, close = exchange(halved, halved, "lat", False)

    return call(
        lat_back_kernel,
        shape((height, levels, width), f32),
        [VMEM] * 4,
        VMEM,
        conv_flops,
        20 * field,
        scratch=(halos,),
        name="lat_back",
    )(far, close, back, held)


def solution(mesh):
    return jax.shard_map(
        shards,
        mesh=mesh,
        in_specs=(
            P("lat", None, "lon"),
            P("lat", None, "lon"),
            P("lat"),
            P("lat", "lon"),
            P("lat", "lon"),
            P("lat", "lon"),
            P("lat", "lon"),
            P(),
            P(),
            P(),
            P(),
            P(),
            P(),
        ),
        out_specs=P("lat", None, "lon"),
        check_vma=False,
    )
```

```python
import functools

import jax
import jax.numpy as jnp
import numpy as np
from jax import lax
from jax.experimental import pallas as pl
from jax.experimental.pallas import tpu as pltpu
from jax.sharding import PartitionSpec as P

REACH = 16
BLOCK_COLS = 8
LANES = 128
LAT_SIGMA = 8.0
VMEM_BYTES = 40 * 1024 * 1024

VMEM = pl.BlockSpec(memory_space=pltpu.VMEM)
SMEM = pl.BlockSpec(memory_space=pltpu.SMEM)
HBM = pl.BlockSpec(memory_space=pltpu.HBM)
ANY = pl.BlockSpec(memory_space=pl.ANY)


def lat_taps():
    offsets = np.arange(-REACH, REACH + 1, dtype=np.float64)
    raw = np.exp(-offsets * offsets / (2.0 * LAT_SIGMA * LAT_SIGMA))
    return [float(v) for v in (raw / np.sqrt(np.sum(raw * raw))).astype(np.float32)]


def call(kernel, out_shape, in_specs, out_specs, flops, bytes_moved, scratch=(), name=None):
    return pl.pallas_call(
        kernel,
        out_shape=out_shape,
        in_specs=in_specs,
        out_specs=out_specs,
        scratch_shapes=list(scratch),
        compiler_params=pltpu.CompilerParams(vmem_limit_bytes=VMEM_BYTES),
        cost_estimate=pl.CostEstimate(flops=flops, bytes_accessed=bytes_moved, transcendentals=0),
        name=name,
    )


def pinned(*values):
    return [pltpu.with_memory_space_constraint(value, pltpu.HBM) for value in values]


def lat_conv_row(row, low, own, high):
    taps = lat_taps()
    height = own.shape[0]
    acc = None
    for j in range(-REACH, REACH + 1):
        source = row + j
        if source < 0:
            part = low[source + REACH]
        elif source < height:
            part = own[source]
        else:
            part = high[source - height]
        term = taps[j + REACH] * part
        acc = term if acc is None else acc + term
    return acc


def fill_padded(padded, far, own, close):
    width = own.shape[1]
    low, high = sides(far[...], close[...], "lon")
    padded[:, 0:REACH, :] = low
    padded[:, REACH : REACH + width, :] = own[...]
    padded[:, REACH + width :, :] = high


def lon_conv(padded, taps, tile, start, width):
    middle = REACH + start
    acc = taps[tile, 0:1, :] * padded[tile, pl.ds(middle, width), :]
    for j in range(1, REACH + 1):
        both = padded[tile, pl.ds(middle + j, width), :] + padded[tile, pl.ds(middle - j, width), :]
        acc = acc + taps[tile, j : j + 1, :] * both
    return acc


def rounded(value):
    return value.astype(jnp.bfloat16).astype(jnp.float32)


def first_kernel(
    radiance, block_owner, channel_count, control, slabs, held, halved, owners, counts, rows, tables, sems
):
    recv_most = radiance.shape[0]
    moves = [
        pltpu.make_async_copy(radiance, slabs.at[pl.ds(0, recv_most)], sems.at[0]),
        pltpu.make_async_copy(block_owner, owners, sems.at[1]),
        pltpu.make_async_copy(channel_count, counts, sems.at[2]),
        pltpu.make_async_copy(control, held, sems.at[3]),
    ]
    for move in moves:
        move.start()
    rows[...] = jnp.full(rows.shape, -1.0, jnp.float32)
    moves[1].wait()
    moves[2].wait()
    rows[0:1, 0 : owners.shape[1]] = owners[...].astype(jnp.float32)
    rows[1:2, 0 : counts.shape[1]] = counts[...].astype(jnp.float32)
    tables[...] = rows[...].astype(jnp.bfloat16)
    last = pltpu.make_async_copy(tables, slabs.at[recv_most], sems.at[4])
    last.start()
    moves[3].wait()
    halved[...] = held[...].astype(jnp.bfloat16)
    moves[0].wait()
    last.wait()


def prepare_kernel(
    lon_width, background, block_cells, block_owner, taps, turned, plan, widths, cells, owners, rows, field, sems
):
    moves = [
        pltpu.make_async_copy(lon_width, widths, sems.at[0]),
        pltpu.make_async_copy(block_cells, cells, sems.at[1]),
        pltpu.make_async_copy(block_owner, owners, sems.at[2]),
        pltpu.make_async_copy(background, field, sems.at[3]),
    ]
    for move in moves:
        move.start()
    tiles = turned.shape[0]
    height, levels, width = background.shape
    per_tile = height // tiles
    groups = width // BLOCK_COLS
    rim = REACH // BLOCK_COLS
    slot_count = cells.shape[0]

    moves[1].wait()
    moves[2].wait()

    def outer(slot):
        group = cells[slot] % groups
        return ((group < rim) | (group >= groups - rim)) & (owners[slot] >= 0)

    outer_count = lax.fori_loop(
        0, slot_count, lambda slot, total: total + jnp.where(outer(slot), 1, 0), 0, unroll=8
    )

    def place(slot, nexts):
        first, second = nexts
        hit = outer(slot)
        position = jnp.where(hit, first, second)
        rows[0, position] = cells[slot]
        rows[1, position] = slot
        return first + jnp.where(hit, 1, 0), second + jnp.where(hit, 0, 1)

    lax.fori_loop(0, slot_count, place, (0, outer_count), unroll=8)
    rows[2, 0] = outer_count
    plan_out = pltpu.make_async_copy(rows, plan, sems.at[4])
    plan_out.start()

    lane_row = lax.broadcasted_iota(jnp.int32, (1, LANES), 1) // levels
    steps = lax.broadcasted_iota(jnp.int32, (taps.shape[1], LANES), 0)
    dist = steps.astype(jnp.float32)
    weight = jnp.where(steps == 0, 1.0, jnp.where(steps <= REACH, 2.0, 0.0))
    moves[0].wait()
    for tile in range(tiles):
        spread = jnp.zeros((1, LANES), jnp.int32)
        for sub in range(per_tile):
            spread = jnp.where(lane_row == sub, widths[tile * per_tile + sub], spread)
        spread = spread.astype(jnp.float32)
        raw = jnp.exp(-dist * dist / (2.0 * spread * spread))
        norm = jnp.sum(weight * raw * raw, axis=0, keepdims=True)
        taps[tile] = raw / jnp.sqrt(norm)
    moves[3].wait()
    for tile in range(tiles):
        block = field[tile * per_tile : (tile + 1) * per_tile].reshape(per_tile * levels, width)
        turned[tile] = jnp.transpose(block)
    plan_out.wait()


def routing(recv_most, slot_count, tables, table):
    count = tables.shape[0]
    half = count // 2
    here = lax.axis_index("lat")
    rows = lax.broadcasted_iota(jnp.int32, (slot_count, LANES), 0)
    lanes = lax.broadcasted_iota(jnp.int32, (slot_count, LANES), 1)
    diagonal = rows == lanes
    zero = jnp.zeros((slot_count, LANES), jnp.int32)

    def device_of(k):
        return here ^ jnp.where(k < half, 2 * k, 2 * (k - half) + 1)

    def line(k, row):
        return tables[k].astype(jnp.float32)[row : row + 1].astype(jnp.int32)

    owner = jnp.sum(jnp.where(diagonal, line(0, 0), 0), axis=1, keepdims=True)

    def rank(k, acc):
        device = device_of(k)
        before = (device < here) | ((device == here) & (lanes < rows))
        return acc + jnp.where((line(k, 0) == owner) & before, 1, 0)

    unroll = count <= 8
    arrival = jnp.sum(lax.fori_loop(0, count, rank, zero, unroll=unroll), axis=1, keepdims=True)

    def counted(k, acc):
        hit = (owner == device_of(k)) & (lanes == arrival)
        return acc + jnp.where(hit, line(k, 1), 0)

    kept = jnp.sum(lax.fori_loop(0, count, counted, zero, unroll=unroll), axis=1, keepdims=True)
    apart = owner ^ here
    place = (apart >> 1) + (apart & 1) * half
    target = jnp.where(owner >= 0, place * (recv_most + 1) + arrival, 0)
    table[...] = jnp.zeros_like(table)
    for row, column in enumerate((target, kept)):
        table[row : row + 1, :] = jnp.sum(jnp.where(diagonal, column, 0), axis=0, keepdims=True)


def odd_index(axis):
    return lax.axis_index(axis) % 2 == 1


def sides(far, close, axis):
    odd = odd_index(axis)
    far, close = far.astype(jnp.float32), close.astype(jnp.float32)
    return jnp.where(odd, close, far), jnp.where(odd, far, close)


def split_sides(low, high, axis):
    odd = odd_index(axis)
    return jnp.where(odd, high, low), jnp.where(odd, low, high)


def lat_smooth_kernel(far, close, own, smoothed, to_far, to_close, halos):
    tiles = smoothed.shape[0]
    height, levels, width = own.shape
    per_tile = height // tiles
    halos[0], halos[1] = sides(far[...], close[...], "lat")
    for tile in range(tiles):
        rows = [
            lat_conv_row(tile * per_tile + sub, halos.at[0], own, halos.at[1]) for sub in range(per_tile)
        ]
        turned = jnp.transpose(jnp.concatenate(rows, axis=0))
        smoothed[tile] = turned
        to_far[tile], to_close[tile] = split_sides(turned[0:REACH], turned[width - REACH : width], "lon")


def block_place(plan, position, groups, per_tile, width):
    block = plan[0, position]
    row = block // groups
    start = (row // per_tile) * width + (block % groups) * BLOCK_COLS
    return pl.multiple_of(start, BLOCK_COLS), row % per_tile


def take_blocks(plan, profile, picked, first, count, per_tile, width):
    groups = width // BLOCK_COLS
    lane_row = lax.broadcasted_iota(jnp.int32, (BLOCK_COLS, LANES), 1) // (LANES // per_tile)
    for k in range(count):
        start, sub = block_place(plan, first + k, groups, per_tile, width)
        block = profile[pl.ds(start, BLOCK_COLS), :]
        picked[k * BLOCK_COLS : (k + 1) * BLOCK_COLS, :] = jnp.where(lane_row == sub, block, 0.0)


def land_blocks(plan, field, sens, first, count, per_tile, width):
    groups = width // BLOCK_COLS
    lane_row = lax.broadcasted_iota(jnp.int32, (BLOCK_COLS, LANES), 1) // (LANES // per_tile)
    for k in range(first, first + count):
        start, sub = block_place(plan, k, groups, per_tile, width)
        block = sens[k * BLOCK_COLS : (k + 1) * BLOCK_COLS, :]
        field[pl.ds(start, BLOCK_COLS), :] += jnp.where(lane_row == sub, block, 0.0)


def take_observed(plan, table, held, observed, first, count):
    channels = observed.shape[1]
    channel = lax.broadcasted_iota(jnp.int32, (BLOCK_COLS, LANES), 1)
    for k in range(count):
        slot = plan[1, first + k]
        slab = held[table[0, slot]].astype(jnp.float32)
        kept = table[1, slot]
        for h in range(channels // LANES):
            part = slab[h * BLOCK_COLS : (h + 1) * BLOCK_COLS]
            observed[k * BLOCK_COLS : (k + 1) * BLOCK_COLS, h * LANES : (h + 1) * LANES] = jnp.where(
                channel + h * LANES < kept, part, jnp.inf
            )


def dot(a, b):
    return jnp.dot(a, b, preferred_element_type=jnp.float32)


def dot_t(a, b):
    return lax.dot_general(a, b, (((1,), (1,)), ((), ())), preferred_element_type=jnp.float32)


def net_forward(picked, weights, states):
    wide_in, weight_two, weight_out, bias_one, bias_two, bias_out = weights
    act_one, act_two, emitted = states
    inputs = picked[...].astype(jnp.bfloat16)
    act_one[...] = jnp.tanh(dot(inputs, wide_in[...]) + bias_one[...]).astype(jnp.bfloat16)
    act_two[...] = jnp.tanh(dot(act_one[...], weight_two[...]) + bias_two[...]).astype(jnp.bfloat16)
    emitted[...] = dot(act_two[...], weight_out[...]) + bias_out[...]


def net_backward(observed, states, weights):
    wide_in, weight_two, weight_out = weights[:3]
    act_one, act_two, emitted = states
    seen = observed[...]
    misfit = jnp.where(seen < jnp.inf, emitted[...] - seen, 0.0).astype(jnp.bfloat16)
    two = act_two[...].astype(jnp.float32)
    grad_two = (dot_t(misfit, weight_out[...]) * (1.0 - two * two)).astype(jnp.bfloat16)
    one = act_one[...].astype(jnp.float32)
    grad_one = (dot_t(grad_two, weight_two[...]) * (1.0 - one * one)).astype(jnp.bfloat16)
    return rounded(dot_t(grad_one, wide_in[...]))


def inner_forward_kernel(
    outer_slots,
    plan,
    own,
    turned,
    taps,
    in_weight,
    in_bias,
    mid_weight,
    mid_bias,
    out_weight,
    out_bias,
    profile,
    act_one,
    act_two,
    emitted,
    wide_in,
    weight_two,
    weight_out,
    bias_one,
    bias_two,
    bias_out,
    rows,
    padded,
    picked,
    sems,
):
    tiles, width, _ = own.shape
    levels = in_weight.shape[0]
    per_tile = LANES // levels
    count = picked.shape[0] // BLOCK_COLS

    moves = [
        pltpu.make_async_copy(plan, rows, sems.at[0]),
        pltpu.make_async_copy(in_bias, bias_one, sems.at[1]),
        pltpu.make_async_copy(mid_weight, weight_two, sems.at[2]),
        pltpu.make_async_copy(mid_bias, bias_two, sems.at[3]),
        pltpu.make_async_copy(out_weight, weight_out, sems.at[4]),
        pltpu.make_async_copy(out_bias, bias_out, sems.at[5]),
    ] + [
        pltpu.make_async_copy(in_weight, wide_in.at[pl.ds(sub * levels, levels)], sems.at[6 + sub])
        for sub in range(per_tile)
    ]
    for move in moves:
        move.start()
    zeros = jnp.zeros((tiles, REACH, LANES), jnp.float32)
    padded[:, 0:REACH, :] = zeros
    padded[:, REACH : REACH + width, :] = own[...]
    padded[:, REACH + width :, :] = zeros
    for tile in range(tiles):
        total = turned[tile] + lon_conv(padded, taps, tile, 0, width)
        profile[tile * width : (tile + 1) * width, :] = rounded(total)
    for move in moves:
        move.wait()

    @pl.when(rows[2, 0] <= outer_slots)
    def _():
        take_blocks(rows, profile, picked, outer_slots, count, per_tile, width)
        weights = (wide_in, weight_two, weight_out, bias_one, bias_two, bias_out)
        net_forward(picked, weights, (act_one, act_two, emitted))


def outer_forward_kernel(
    per_tile,
    plan,
    far,
    close,
    own,
    turned,
    taps,
    inner_profile,
    *refs,
):
    weights, states, late_states, (rows, padded, profile, picked, late_picked, sem) = (
        refs[:6],
        refs[6:9],
        refs[9:12],
        refs[12:],
    )
    tiles, width, _ = own.shape
    outer_slots = picked.shape[0] // BLOCK_COLS
    late_slots = late_picked.shape[0] // BLOCK_COLS
    plan_in = pltpu.make_async_copy(plan, rows, sem)
    plan_in.start()
    fill_padded(padded, far, own, close)
    profile[...] = inner_profile[...]
    for tile in range(tiles):
        for start in (0, width - REACH):
            total = turned[tile, start : start + REACH, :] + lon_conv(padded, taps, tile, start, REACH)
            profile[tile * width + start : tile * width + start + REACH, :] = rounded(total)
    plan_in.wait()
    take_blocks(rows, profile, picked, 0, outer_slots, per_tile, width)
    net_forward(picked, weights, states)

    @pl.when(rows[2, 0] > outer_slots)
    def _():
        take_blocks(rows, profile, late_picked, outer_slots, late_slots, per_tile, width)
        net_forward(late_picked, weights, late_states)


def outer_backward_kernel(per_tile, parts, plan, *refs):
    slabs, refs = refs[:parts], refs[parts:]
    weights, states, late_states, refs = refs[:3], refs[3:6], refs[6:9], refs[9:]
    (held, table_rows, sens, to_far, to_close) = refs[:5]
    (rows, tables, table, observed, late_observed, field, sems) = refs[5:]
    tiles = to_far.shape[0]
    width = field.shape[0] // tiles
    owners = tables.shape[0]
    per_owner = held.shape[0] // owners
    outer_slots = observed.shape[0] // BLOCK_COLS
    late_slots = late_observed.shape[0] // BLOCK_COLS

    routes, bulk = [], []
    for part, ref in enumerate(slabs):
        sets = ref.shape[0] // per_owner
        for k in range(sets):
            entry = len(routes)
            source = ref.at[k * per_owner + per_owner - 1]
            routes.append(pltpu.make_async_copy(source, tables.at[entry], sems.at[entry]))
        start = len(routes) - sets
        bulk.append(
            pltpu.make_async_copy(
                ref, held.at[pl.ds(start * per_owner, ref.shape[0])], sems.at[owners + part]
            )
        )
    plan_in = pltpu.make_async_copy(plan, rows, sems.at[owners + parts])
    for move in routes + [plan_in] + bulk:
        move.start()
    field[...] = jnp.zeros_like(field)
    for move in routes:
        move.wait()
    routing(per_owner - 1, outer_slots + late_slots, tables, table_rows)
    table_in = pltpu.make_async_copy(table_rows, table, sems.at[owners + parts + 1])
    table_in.start()
    for move in bulk + [plan_in, table_in]:
        move.wait()

    take_observed(rows, table, held, observed, 0, outer_slots)
    sens[0 : outer_slots * BLOCK_COLS, :] = net_backward(observed, states, weights)
    land_blocks(rows, field, sens, 0, outer_slots, per_tile, width)

    @pl.when(rows[2, 0] > outer_slots)
    def _():
        take_observed(rows, table, held, late_observed, outer_slots, late_slots)
        sens[outer_slots * BLOCK_COLS :, :] = net_backward(late_observed, late_states, weights)
        land_blocks(rows, field, sens, outer_slots, late_slots, per_tile, width)

    for tile in range(tiles):
        low = field[tile * width : tile * width + REACH, :]
        high = field[(tile + 1) * width - REACH : (tile + 1) * width, :]
        low, high = split_sides(low, high, "lon")
        to_far[tile], to_close[tile] = low.astype(jnp.bfloat16), high.astype(jnp.bfloat16)


def inner_backward_kernel(per_tile, outer_slots, plan, held, table_rows, sens, *refs):
    weights, states, refs = refs[:3], refs[3:6], refs[6:]
    landing, rows, table, observed, inner, field, sems = refs
    tiles, width, _ = landing.shape
    late_slots = observed.shape[0] // BLOCK_COLS
    split = outer_slots * BLOCK_COLS
    moves = [
        pltpu.make_async_copy(plan, rows, sems.at[0]),
        pltpu.make_async_copy(table_rows, table, sems.at[1]),
    ]
    for move in moves:
        move.start()
    field[...] = jnp.zeros_like(field)
    inner[...] = sens[...]
    for move in moves:
        move.wait()

    @pl.when(rows[2, 0] <= outer_slots)
    def _():
        take_observed(rows, table, held, observed, outer_slots, late_slots)
        inner[split:, :] = net_backward(observed, states, weights)

    land_blocks(rows, field, inner, 0, outer_slots + late_slots, per_tile, width)
    for tile in range(tiles):
        landing[tile] = field[tile * width : (tile + 1) * width, :]


def lon_back_kernel(far, close, own, taps, back, halved, padded):
    tiles, width, _ = own.shape
    height, levels, _ = back.shape
    per_tile = height // tiles
    fill_padded(padded, far, own, close)
    for tile in range(tiles):
        rows = jnp.transpose(lon_conv(padded, taps, tile, 0, width))
        rows = rows.reshape(per_tile, levels, width)
        back[tile * per_tile : (tile + 1) * per_tile] = rows
        halved[tile * per_tile : (tile + 1) * per_tile] = rows.astype(jnp.bfloat16)


def lat_back_kernel(far, close, own, control, gradient, halos):
    halos[0], halos[1] = sides(far[...], close[...], "lat")
    for row in range(own.shape[0]):
        gradient[row] = control[row] + lat_conv_row(row, halos.at[0], own, halos.at[1])


def exchange(to_far, to_close, axis, periodic):
    count = lax.axis_size(axis)
    far = []
    for odd in range(1, count, 2):
        if odd + 1 < count or periodic:
            far += [(odd, (odd + 1) % count), ((odd + 1) % count, odd)]
    close = [(i, i ^ 1) for i in range(count)]
    return lax.ppermute(to_far, axis, far), lax.ppermute(to_close, axis, close)


def shards(
    control,
    background,
    lon_width,
    block_cells,
    block_owner,
    channel_count,
    radiance,
    in_weight,
    in_bias,
    mid_weight,
    mid_bias,
    out_weight,
    out_bias,
):
    height, levels, width = control.shape
    hidden = mid_weight.shape[0]
    channels, columns = radiance.shape
    slot_count = block_owner.shape[0]
    recv_most = channel_count.shape[0]
    per_tile = LANES // levels
    tiles = height // per_tile
    slab_rows = BLOCK_COLS * channels // LANES
    f32, bf16, i32 = jnp.float32, jnp.bfloat16, jnp.int32
    shape = jax.ShapeDtypeStruct
    field = height * levels * width
    conv_flops = 2 * 33 * field

    halves = channels // LANES
    radiance = radiance.T.reshape(recv_most, BLOCK_COLS, halves, LANES)
    radiance = jnp.swapaxes(radiance, 1, 2).reshape(recv_most, slab_rows, LANES)
    slabs, held, halved = call(
        first_kernel,
        (
            shape((recv_most + 1, slab_rows, LANES), bf16),
            shape(control.shape, f32),
            shape(control.shape, bf16),
        ),
        [HBM] * 4,
        (HBM, VMEM, VMEM),
        0,
        16 * field,
        scratch=(
            pltpu.VMEM((1, slot_count), i32),
            pltpu.VMEM((1, recv_most), i32),
            pltpu.VMEM((slab_rows, LANES), f32),
            pltpu.VMEM((slab_rows, LANES), bf16),
            pltpu.SemaphoreType.DMA((5,)),
        ),
        name="slabs_halves",
    )(*pinned(radiance, block_owner.reshape(1, slot_count), channel_count.reshape(1, recv_most), control))

    cells = block_cells.reshape(slot_count)
    taps, turned, plan = call(
        prepare_kernel,
        (
            shape((tiles, 24, LANES), f32),
            shape((tiles, width, LANES), f32),
            shape((8, LANES), i32),
        ),
        [HBM] * 4,
        (VMEM, VMEM, HBM),
        0,
        8 * field,
        scratch=(
            pltpu.SMEM((height,), i32),
            pltpu.SMEM((slot_count,), i32),
            pltpu.SMEM((slot_count,), i32),
            pltpu.SMEM((8, LANES), i32),
            pltpu.VMEM((height, levels, width), f32),
            pltpu.SemaphoreType.DMA((5,)),
        ),
        name="taps_background",
    )(*pinned(lon_width, background, cells, block_owner.reshape(slot_count)))
    lat_count = lax.axis_size("lat")
    near = [slabs]
    for bit in range(1, lat_count.bit_length() - 1):
        held_sets = near[0] if len(near) == 1 else jnp.concatenate(near, axis=0)
        near = [held_sets, lax.ppermute(held_sets, "lat", [(i, i ^ (1 << bit)) for i in range(lat_count)])]
        if bit == 1:
            far, close = exchange(halved, halved, "lat", False)
            near[1], far, close, taps = lax.optimization_barrier((near[1], far, close, taps))

    halos = pltpu.VMEM((2, REACH, levels, width), f32)
    smoothed, to_far, to_close = call(
        lat_smooth_kernel,
        (shape((tiles, width, LANES), f32),) + (shape((tiles, REACH, LANES), f32),) * 2,
        [VMEM] * 3,
        (VMEM,) * 3,
        conv_flops,
        16 * field,
        scratch=(halos,),
        name="lat_smooth",
    )(far, close, held)
    far, close = exchange(to_far, to_close, "lon", True)

    outer_slots = 3 * slot_count // 8
    late_slots = slot_count - outer_slots
    x_rows = slot_count * BLOCK_COLS
    outer_rows, late_rows = outer_slots * BLOCK_COLS, late_slots * BLOCK_COLS
    row_flops = 2 * hidden * (LANES + hidden + channels)
    weight_shapes = (
        shape((LANES, hidden), bf16),
        shape((hidden, hidden), bf16),
        shape((hidden, channels), bf16),
        shape((1, hidden), f32),
        shape((1, hidden), f32),
        shape((1, channels), f32),
    )

    def state_shapes(rows):
        return (shape((rows, hidden), bf16), shape((rows, hidden), bf16), shape((rows, channels), f32))

    plan_rows = pltpu.SMEM((8, LANES), i32)
    padded = pltpu.VMEM((tiles, width + 2 * REACH, LANES), f32)
    flat = pltpu.VMEM((tiles * width, LANES), f32)

    profile, *rest = call(
        functools.partial(inner_forward_kernel, outer_slots),
        (shape((tiles * width, LANES), f32),) + state_shapes(late_rows) + weight_shapes,
        [HBM] + [VMEM] * 3 + [HBM] * 6,
        (VMEM,) * 10,
        late_rows * row_flops,
        4 * 1024 * 1024,
        scratch=(
            plan_rows,
            padded,
            pltpu.VMEM((late_rows, LANES), f32),
            pltpu.SemaphoreType.DMA((6 + per_tile,)),
        ),
        name="inner_forward",
    )(
        *pinned(plan),
        smoothed,
        turned,
        taps,
        *pinned(
            in_weight,
            in_bias.reshape(1, hidden),
            mid_weight,
            mid_bias.reshape(1, hidden),
            out_weight,
            out_bias.reshape(1, channels),
        ),
    )
    inner_states, weights = rest[:3], rest[3:]
    near, far, close, profile = lax.optimization_barrier((near, far, close, profile))
    across = [lax.ppermute(part, "lat", [(i, i ^ 1) for i in range(lat_count)]) for part in near]

    states = call(
        functools.partial(outer_forward_kernel, per_tile),
        state_shapes(outer_rows) + state_shapes(late_rows),
        [HBM] + [VMEM] * 12,
        (VMEM,) * 6,
        outer_rows * row_flops,
        4 * 1024 * 1024,
        scratch=(
            plan_rows,
            padded,
            flat,
            pltpu.VMEM((outer_rows, LANES), f32),
            pltpu.VMEM((late_rows, LANES), f32),
            pltpu.SemaphoreType.DMA,
        ),
        name="outer_forward",
    )(*pinned(plan), far, close, smoothed, turned, taps, profile, *weights)

    slabs = [*near, *across]
    held_slabs, table, sens, to_far, to_close = call(
        functools.partial(outer_backward_kernel, per_tile, len(slabs)),
        (
            shape((lat_count * (recv_most + 1), slab_rows, LANES), bf16),
            shape((8, LANES), i32),
            shape((x_rows, LANES), f32),
            shape((tiles, REACH, LANES), bf16),
            shape((tiles, REACH, LANES), bf16),
        ),
        [HBM] + [ANY] * len(slabs) + [VMEM] * 9,
        (VMEM,) * 5,
        outer_rows * row_flops,
        4 * 1024 * 1024,
        scratch=(
            plan_rows,
            pltpu.VMEM((lat_count, slab_rows, LANES), bf16),
            pltpu.SMEM((8, LANES), i32),
            pltpu.VMEM((outer_rows, channels), f32),
            pltpu.VMEM((late_rows, channels), f32),
            flat,
            pltpu.SemaphoreType.DMA((lat_count + len(slabs) + 2,)),
        ),
        name="outer_backward",
    )(*pinned(plan), *slabs, *weights[:3], *states)
    far, close = exchange(to_far, to_close, "lon", True)

    landing = call(
        functools.partial(inner_backward_kernel, per_tile, outer_slots),
        shape((tiles, width, LANES), f32),
        [HBM, VMEM, ANY] + [VMEM] * 7,
        VMEM,
        late_rows * row_flops,
        4 * 1024 * 1024,
        scratch=(
            plan_rows,
            pltpu.SMEM((8, LANES), i32),
            pltpu.VMEM((late_rows, channels), f32),
            pltpu.VMEM((x_rows, LANES), f32),
            flat,
            pltpu.SemaphoreType.DMA((2,)),
        ),
        name="inner_backward",
    )(*pinned(plan), held_slabs, table, sens, *weights[:3], *inner_states)

    back, halved = call(
        lon_back_kernel,
        (shape((height, levels, width), f32), shape((height, levels, width), bf16)),
        [VMEM] * 4,
        (VMEM, VMEM),
        conv_flops,
        8 * field,
        scratch=(pltpu.VMEM((tiles, width + 2 * REACH, LANES), f32),),
        name="lon_back",
    )(far, close, landing, taps)
    far, close = exchange(halved, halved, "lat", False)

    return call(
        lat_back_kernel,
        shape((height, levels, width), f32),
        [VMEM] * 4,
        VMEM,
        conv_flops,
        20 * field,
        scratch=(halos,),
        name="lat_back",
    )(far, close, back, held)


def solution(mesh):
    return jax.shard_map(
        shards,
        mesh=mesh,
        in_specs=(
            P("lat", None, "lon"),
            P("lat", None, "lon"),
            P("lat"),
            P("lat", "lon"),
            P("lat", "lon"),
            P("lat", "lon"),
            P("lat", "lon"),
            P(),
            P(),
            P(),
            P(),
            P(),
            P(),
        ),
        out_specs=P("lat", None, "lon"),
        check_vma=False,
    )
```

```python
import functools

import jax
import jax.numpy as jnp
import numpy as np
from jax import lax
from jax.experimental import pallas as pl
from jax.experimental.pallas import tpu as pltpu
from jax.sharding import PartitionSpec as P

REACH = 16
BLOCK_COLS = 8
LANES = 128
LAT_SIGMA = 8.0
VMEM_BYTES = 40 * 1024 * 1024

VMEM = pl.BlockSpec(memory_space=pltpu.VMEM)
SMEM = pl.BlockSpec(memory_space=pltpu.SMEM)
HBM = pl.BlockSpec(memory_space=pltpu.HBM)
ANY = pl.BlockSpec(memory_space=pl.ANY)


def lat_taps():
    offsets = np.arange(-REACH, REACH + 1, dtype=np.float64)
    raw = np.exp(-offsets * offsets / (2.0 * LAT_SIGMA * LAT_SIGMA))
    return [float(v) for v in (raw / np.sqrt(np.sum(raw * raw))).astype(np.float32)]


def call(kernel, out_shape, in_specs, out_specs, flops, bytes_moved, scratch=(), name=None):
    return pl.pallas_call(
        kernel,
        out_shape=out_shape,
        in_specs=in_specs,
        out_specs=out_specs,
        scratch_shapes=list(scratch),
        compiler_params=pltpu.CompilerParams(vmem_limit_bytes=VMEM_BYTES),
        cost_estimate=pl.CostEstimate(flops=flops, bytes_accessed=bytes_moved, transcendentals=0),
        name=name,
    )


def pinned(*values):
    return [pltpu.with_memory_space_constraint(value, pltpu.HBM) for value in values]


def lat_sum(parts, row, first, height, start=None):
    taps = lat_taps()
    acc = start
    for k in range(height):
        j = first + k - row
        if abs(j) <= REACH:
            term = taps[j + REACH] * parts[k]
            acc = term if acc is None else acc + term
    return acc


def lat_rims(row, part, halos, height):
    low = lat_sum(halos.at[0], row, -REACH, REACH, part)
    return lat_sum(halos.at[1], row, height, REACH, low)


def fill_padded(padded, far, own, close):
    width = own.shape[1]
    low, high = sides(far[...], close[...], "lon")
    padded[:, 0:REACH, :] = low
    padded[:, REACH : REACH + width, :] = own[...]
    padded[:, REACH + width :, :] = high


def lon_conv(padded, taps, tile, start, width):
    middle = REACH + start
    acc = taps[tile, 0:1, :] * padded[tile, pl.ds(middle, width), :]
    for j in range(1, REACH + 1):
        both = padded[tile, pl.ds(middle + j, width), :] + padded[tile, pl.ds(middle - j, width), :]
        acc = acc + taps[tile, j : j + 1, :] * both
    return acc


def rounded(value):
    return value.astype(jnp.bfloat16).astype(jnp.float32)


def slabs_kernel(radiance, block_owner, channel_count, slabs, owners, counts, rows, tables, sems):
    recv_most = radiance.shape[0]
    moves = [
        pltpu.make_async_copy(radiance, slabs.at[pl.ds(0, recv_most)], sems.at[0]),
        pltpu.make_async_copy(block_owner, owners, sems.at[1]),
        pltpu.make_async_copy(channel_count, counts, sems.at[2]),
    ]
    for move in moves:
        move.start()
    rows[...] = jnp.full(rows.shape, -1.0, jnp.float32)
    moves[1].wait()
    moves[2].wait()
    rows[0:1, 0 : owners.shape[1]] = owners[...].astype(jnp.float32)
    rows[1:2, 0 : counts.shape[1]] = counts[...].astype(jnp.float32)
    tables[...] = rows[...].astype(jnp.bfloat16)
    last = pltpu.make_async_copy(tables, slabs.at[recv_most], sems.at[3])
    last.start()
    moves[0].wait()
    last.wait()


def prepare_kernel(
    lon_width,
    background,
    block_cells,
    block_owner,
    control,
    taps,
    turned,
    plan,
    own_part,
    widths,
    cells,
    owners,
    field,
    band,
    sems,
):
    moves = [
        pltpu.make_async_copy(lon_width, widths, sems.at[0]),
        pltpu.make_async_copy(block_cells, cells, sems.at[1]),
        pltpu.make_async_copy(block_owner, owners, sems.at[2]),
        pltpu.make_async_copy(background, field, sems.at[3]),
        pltpu.make_async_copy(control, band, sems.at[4]),
    ]
    for move in moves:
        move.start()
    tiles = turned.shape[0]
    height, levels, width = background.shape
    per_tile = height // tiles
    groups = width // BLOCK_COLS
    rim = REACH // BLOCK_COLS
    slot_count = cells.shape[1]

    lane_row = lax.broadcasted_iota(jnp.int32, (1, LANES), 1) // levels
    steps = lax.broadcasted_iota(jnp.int32, (taps.shape[1], LANES), 0)
    dist = steps.astype(jnp.float32)
    weight = jnp.where(steps == 0, 1.0, jnp.where(steps <= REACH, 2.0, 0.0))
    moves[0].wait()
    for tile in range(tiles):
        spread = jnp.zeros((1, LANES), jnp.int32)
        for sub in range(per_tile):
            spread = jnp.where(lane_row == sub, widths[tile * per_tile + sub], spread)
        spread = spread.astype(jnp.float32)
        raw = jnp.exp(-dist * dist / (2.0 * spread * spread))
        norm = jnp.sum(weight * raw * raw, axis=0, keepdims=True)
        taps[tile] = raw / jnp.sqrt(norm)

    moves[1].wait()
    moves[2].wait()
    rows = lax.broadcasted_iota(jnp.int32, (slot_count, slot_count), 0)
    lanes = lax.broadcasted_iota(jnp.int32, (slot_count, slot_count), 1)
    group = cells[...] % groups
    outer = ((group < rim) | (group >= groups - rim)) & (owners[...] >= 0)
    outer_here = jnp.where(outer, 1, 0)
    outer_count = jnp.sum(outer_here, axis=1, keepdims=True)
    earlier = jnp.sum(jnp.where(lanes < rows, outer_here, 0), axis=1, keepdims=True)
    here = jnp.sum(jnp.where(lanes == rows, outer_here, 0), axis=1, keepdims=True)
    cell = jnp.sum(jnp.where(lanes == rows, cells[...], 0), axis=1, keepdims=True)
    position = jnp.where(here == 1, earlier, outer_count + rows[:, 0:1] - earlier)
    at = lax.broadcasted_iota(jnp.int32, (slot_count, LANES), 1)
    hit = position == at
    slot = lax.broadcasted_iota(jnp.int32, (slot_count, LANES), 0)
    plan[...] = jnp.zeros_like(plan)
    plan[0:1, :] = jnp.sum(jnp.where(hit, cell, 0), axis=0, keepdims=True)
    plan[1:2, :] = jnp.sum(jnp.where(hit, slot, 0), axis=0, keepdims=True)
    plan[2:3, :] = jnp.broadcast_to(outer_count, (1, LANES))

    moves[3].wait()
    for tile in range(tiles):
        block = field[tile * per_tile : (tile + 1) * per_tile].reshape(per_tile * levels, width)
        turned[tile] = jnp.transpose(block)
    moves[4].wait()
    for row in range(height):
        own_part[row] = lat_sum(band, row, 0, height)


def swap_bits(count):
    return list(range(count.bit_length() - 2, 0, -1))


def routing(recv_most, slot_count, tables, table):
    count = tables.shape[0]
    half = count // 2
    here = lax.axis_index("lat")
    rows = lax.broadcasted_iota(jnp.int32, (slot_count, LANES), 0)
    lanes = lax.broadcasted_iota(jnp.int32, (slot_count, LANES), 1)
    diagonal = rows == lanes
    zero = jnp.zeros((slot_count, LANES), jnp.int32)

    bits = swap_bits(count)

    def device_of(k):
        apart = jnp.where(k < half, 0, 1)
        for place, bit in enumerate(bits):
            apart = apart + (((k >> place) & 1) << bit)
        return here ^ apart

    def line(k, row):
        return tables[k].astype(jnp.float32)[row : row + 1].astype(jnp.int32)

    owner = jnp.sum(jnp.where(diagonal, line(0, 0), 0), axis=1, keepdims=True)

    def rank(k, acc):
        device = device_of(k)
        before = (device < here) | ((device == here) & (lanes < rows))
        return acc + jnp.where((line(k, 0) == owner) & before, 1, 0)

    unroll = count <= 8
    arrival = jnp.sum(lax.fori_loop(0, count, rank, zero, unroll=unroll), axis=1, keepdims=True)

    def counted(k, acc):
        hit = (owner == device_of(k)) & (lanes == arrival)
        return acc + jnp.where(hit, line(k, 1), 0)

    kept = jnp.sum(lax.fori_loop(0, count, counted, zero, unroll=unroll), axis=1, keepdims=True)
    apart = owner ^ here
    entry = (apart & 1) * half
    for place, bit in enumerate(bits):
        entry = entry + (((apart >> bit) & 1) << place)
    target = jnp.where(owner >= 0, entry * (recv_most + 1) + arrival, 0)
    table[...] = jnp.zeros_like(table)
    for row, column in enumerate((target, kept)):
        table[row : row + 1, :] = jnp.sum(jnp.where(diagonal, column, 0), axis=0, keepdims=True)


def odd_index(axis):
    return lax.axis_index(axis) % 2 == 1


def sides(far, close, axis):
    odd = odd_index(axis)
    far, close = far.astype(jnp.float32), close.astype(jnp.float32)
    return jnp.where(odd, close, far), jnp.where(odd, far, close)


def split_sides(low, high, axis):
    odd = odd_index(axis)
    return jnp.where(odd, high, low), jnp.where(odd, low, high)


def lat_smooth_kernel(far, close, own_part, smoothed, to_far, to_close, halos):
    tiles = smoothed.shape[0]
    height, levels, width = own_part.shape
    per_tile = height // tiles
    halos[0], halos[1] = sides(far[...], close[...], "lat")
    for tile in range(tiles):
        rows = range(tile * per_tile, (tile + 1) * per_tile)
        rows = [lat_rims(row, own_part[row], halos, height) for row in rows]
        turned = jnp.transpose(jnp.concatenate(rows, axis=0))
        smoothed[tile] = turned
        to_far[tile], to_close[tile] = split_sides(turned[0:REACH], turned[width - REACH : width], "lon")


def block_place(plan, position, groups, per_tile, width):
    block = plan[0, position]
    row = block // groups
    start = (row // per_tile) * width + (block % groups) * BLOCK_COLS
    return pl.multiple_of(start, BLOCK_COLS), row % per_tile


def take_blocks(plan, profile, picked, first, count, per_tile, width):
    groups = width // BLOCK_COLS
    lane_row = lax.broadcasted_iota(jnp.int32, (BLOCK_COLS, LANES), 1) // (LANES // per_tile)
    for k in range(count):
        start, sub = block_place(plan, first + k, groups, per_tile, width)
        block = profile[pl.ds(start, BLOCK_COLS), :]
        picked[k * BLOCK_COLS : (k + 1) * BLOCK_COLS, :] = jnp.where(lane_row == sub, block, 0.0)


def land_blocks(plan, field, sens, first, count, per_tile, width):
    groups = width // BLOCK_COLS
    lane_row = lax.broadcasted_iota(jnp.int32, (BLOCK_COLS, LANES), 1) // (LANES // per_tile)
    for k in range(first, first + count):
        start, sub = block_place(plan, k, groups, per_tile, width)
        block = sens[k * BLOCK_COLS : (k + 1) * BLOCK_COLS, :]
        field[pl.ds(start, BLOCK_COLS), :] += jnp.where(lane_row == sub, block, 0.0)


def take_observed(plan, table, held, observed, first, count):
    channels = observed.shape[1]
    channel = lax.broadcasted_iota(jnp.int32, (BLOCK_COLS, LANES), 1)
    for k in range(count):
        slot = plan[1, first + k]
        slab = held[table[0, slot]].astype(jnp.float32)
        kept = table[1, slot]
        for h in range(channels // LANES):
            part = slab[h * BLOCK_COLS : (h + 1) * BLOCK_COLS]
            observed[k * BLOCK_COLS : (k + 1) * BLOCK_COLS, h * LANES : (h + 1) * LANES] = jnp.where(
                channel + h * LANES < kept, part, jnp.inf
            )


def dot(a, b):
    return jnp.dot(a, b, preferred_element_type=jnp.float32)


def dot_t(a, b):
    return lax.dot_general(a, b, (((1,), (1,)), ((), ())), preferred_element_type=jnp.float32)


def net_forward(picked, weights, states):
    wide_in, weight_two, weight_out, bias_one, bias_two, bias_out = weights
    act_one, act_two, emitted = states
    inputs = picked[...].astype(jnp.bfloat16)
    act_one[...] = jnp.tanh(dot(inputs, wide_in[...]) + bias_one[...]).astype(jnp.bfloat16)
    act_two[...] = jnp.tanh(dot(act_one[...], weight_two[...]) + bias_two[...]).astype(jnp.bfloat16)
    emitted[...] = dot(act_two[...], weight_out[...]) + bias_out[...]


def net_backward(observed, states, weights):
    wide_in, weight_two, weight_out = weights[:3]
    act_one, act_two, emitted = states
    seen = observed[...]
    misfit = jnp.where(seen < jnp.inf, emitted[...] - seen, 0.0).astype(jnp.bfloat16)
    two = act_two[...].astype(jnp.float32)
    grad_two = (dot_t(misfit, weight_out[...]) * (1.0 - two * two)).astype(jnp.bfloat16)
    one = act_one[...].astype(jnp.float32)
    grad_one = (dot_t(grad_two, weight_two[...]) * (1.0 - one * one)).astype(jnp.bfloat16)
    return rounded(dot_t(grad_one, wide_in[...]))


def inner_forward_kernel(
    outer_slots,
    plan,
    own,
    turned,
    taps,
    in_weight,
    in_bias,
    mid_weight,
    mid_bias,
    out_weight,
    out_bias,
    profile,
    act_one,
    act_two,
    emitted,
    wide_in,
    weight_two,
    weight_out,
    bias_one,
    bias_two,
    bias_out,
    rows,
    padded,
    picked,
    sems,
):
    tiles, width, _ = own.shape
    levels = in_weight.shape[0]
    per_tile = LANES // levels
    count = picked.shape[0] // BLOCK_COLS

    moves = [
        pltpu.make_async_copy(plan, rows, sems.at[0]),
        pltpu.make_async_copy(in_bias, bias_one, sems.at[1]),
        pltpu.make_async_copy(mid_weight, weight_two, sems.at[2]),
        pltpu.make_async_copy(mid_bias, bias_two, sems.at[3]),
        pltpu.make_async_copy(out_weight, weight_out, sems.at[4]),
        pltpu.make_async_copy(out_bias, bias_out, sems.at[5]),
    ] + [
        pltpu.make_async_copy(in_weight, wide_in.at[pl.ds(sub * levels, levels)], sems.at[6 + sub])
        for sub in range(per_tile)
    ]
    for move in moves:
        move.start()
    zeros = jnp.zeros((tiles, REACH, LANES), jnp.float32)
    padded[:, 0:REACH, :] = zeros
    padded[:, REACH : REACH + width, :] = own[...]
    padded[:, REACH + width :, :] = zeros
    for tile in range(tiles):
        total = turned[tile] + lon_conv(padded, taps, tile, 0, width)
        profile[tile * width : (tile + 1) * width, :] = rounded(total)
    for move in moves:
        move.wait()

    @pl.when(rows[2, 0] <= outer_slots)
    def _():
        take_blocks(rows, profile, picked, outer_slots, count, per_tile, width)
        weights = (wide_in, weight_two, weight_out, bias_one, bias_two, bias_out)
        net_forward(picked, weights, (act_one, act_two, emitted))


def outer_forward_kernel(
    per_tile,
    plan,
    far,
    close,
    own,
    turned,
    taps,
    inner_profile,
    *refs,
):
    weights, states, late_states, (rows, padded, profile, picked, late_picked, sem) = (
        refs[:6],
        refs[6:9],
        refs[9:12],
        refs[12:],
    )
    tiles, width, _ = own.shape
    outer_slots = picked.shape[0] // BLOCK_COLS
    late_slots = late_picked.shape[0] // BLOCK_COLS
    plan_in = pltpu.make_async_copy(plan, rows, sem)
    plan_in.start()
    fill_padded(padded, far, own, close)
    profile[...] = inner_profile[...]
    for tile in range(tiles):
        for start in (0, width - REACH):
            total = turned[tile, start : start + REACH, :] + lon_conv(padded, taps, tile, start, REACH)
            profile[tile * width + start : tile * width + start + REACH, :] = rounded(total)
    plan_in.wait()
    take_blocks(rows, profile, picked, 0, outer_slots, per_tile, width)
    net_forward(picked, weights, states)

    @pl.when(rows[2, 0] > outer_slots)
    def _():
        take_blocks(rows, profile, late_picked, outer_slots, late_slots, per_tile, width)
        net_forward(late_picked, weights, late_states)


def outer_backward_kernel(per_tile, parts, plan, *refs):
    slabs, refs = refs[:parts], refs[parts:]
    weights, states, late_states, refs = refs[:3], refs[3:6], refs[6:9], refs[9:]
    (held, table_rows, sens, to_far, to_close) = refs[:5]
    (rows, tables, table, observed, late_observed, field, sems) = refs[5:]
    tiles = to_far.shape[0]
    width = field.shape[0] // tiles
    owners = tables.shape[0]
    per_owner = held.shape[0] // owners
    outer_slots = observed.shape[0] // BLOCK_COLS
    late_slots = late_observed.shape[0] // BLOCK_COLS

    routes, bulk = [], []
    for part, ref in enumerate(slabs):
        sets = ref.shape[0] // per_owner
        for k in range(sets):
            entry = len(routes)
            source = ref.at[k * per_owner + per_owner - 1]
            routes.append(pltpu.make_async_copy(source, tables.at[entry], sems.at[entry]))
        start = len(routes) - sets
        bulk.append(
            pltpu.make_async_copy(
                ref, held.at[pl.ds(start * per_owner, ref.shape[0])], sems.at[owners + part]
            )
        )
    plan_in = pltpu.make_async_copy(plan, rows, sems.at[owners + parts])
    for move in routes + [plan_in] + bulk:
        move.start()
    field[...] = jnp.zeros_like(field)
    for move in routes:
        move.wait()
    routing(per_owner - 1, outer_slots + late_slots, tables, table_rows)
    table_in = pltpu.make_async_copy(table_rows, table, sems.at[owners + parts + 1])
    table_in.start()
    for move in bulk + [plan_in, table_in]:
        move.wait()

    take_observed(rows, table, held, observed, 0, outer_slots)
    sens[0 : outer_slots * BLOCK_COLS, :] = net_backward(observed, states, weights)
    land_blocks(rows, field, sens, 0, outer_slots, per_tile, width)

    @pl.when(rows[2, 0] > outer_slots)
    def _():
        take_observed(rows, table, held, late_observed, outer_slots, late_slots)
        sens[outer_slots * BLOCK_COLS :, :] = net_backward(late_observed, late_states, weights)
        land_blocks(rows, field, sens, outer_slots, late_slots, per_tile, width)

    for tile in range(tiles):
        low = field[tile * width : tile * width + REACH, :]
        high = field[(tile + 1) * width - REACH : (tile + 1) * width, :]
        low, high = split_sides(low, high, "lon")
        to_far[tile], to_close[tile] = low.astype(jnp.bfloat16), high.astype(jnp.bfloat16)


def inner_backward_kernel(per_tile, outer_slots, plan, held, table_rows, sens, *refs):
    weights, states, refs = refs[:3], refs[3:6], refs[6:]
    landing, rows, table, observed, inner, field, sems = refs
    tiles, width, _ = landing.shape
    late_slots = observed.shape[0] // BLOCK_COLS
    split = outer_slots * BLOCK_COLS
    moves = [
        pltpu.make_async_copy(plan, rows, sems.at[0]),
        pltpu.make_async_copy(table_rows, table, sems.at[1]),
    ]
    for move in moves:
        move.start()
    field[...] = jnp.zeros_like(field)
    inner[...] = sens[...]
    for move in moves:
        move.wait()

    @pl.when(rows[2, 0] <= outer_slots)
    def _():
        take_observed(rows, table, held, observed, outer_slots, late_slots)
        inner[split:, :] = net_backward(observed, states, weights)

    land_blocks(rows, field, inner, 0, outer_slots + late_slots, per_tile, width)
    for tile in range(tiles):
        landing[tile] = field[tile * width : (tile + 1) * width, :]


def lon_back_kernel(far, close, own, taps, back, halved, padded):
    tiles, width, _ = own.shape
    height, levels, _ = back.shape
    per_tile = height // tiles
    fill_padded(padded, far, own, close)
    for tile in range(tiles):
        rows = jnp.transpose(lon_conv(padded, taps, tile, 0, width))
        rows = rows.reshape(per_tile, levels, width)
        back[tile * per_tile : (tile + 1) * per_tile] = rows
        halved[tile * per_tile : (tile + 1) * per_tile] = rows.astype(jnp.bfloat16)


def own_back_kernel(back, control, own_part, held, sem):
    control_in = pltpu.make_async_copy(control, held, sem)
    control_in.start()
    control_in.wait()
    height = back.shape[0]
    for row in range(height):
        own_part[row] = lat_sum(back, row, 0, height, held[row])


def lat_back_kernel(far, close, own_part, gradient, halos):
    halos[0], halos[1] = sides(far[...], close[...], "lat")
    height = own_part.shape[0]
    for row in range(height):
        gradient[row] = lat_rims(row, own_part[row], halos, height)


def exchange(to_far, to_close, axis, periodic):
    count = lax.axis_size(axis)
    far = []
    for odd in range(1, count, 2):
        if odd + 1 < count or periodic:
            far += [(odd, (odd + 1) % count), ((odd + 1) % count, odd)]
    close = [(i, i ^ 1) for i in range(count)]
    return lax.ppermute(to_far, axis, far), lax.ppermute(to_close, axis, close)


def shards(
    control,
    background,
    lon_width,
    block_cells,
    block_owner,
    channel_count,
    radiance,
    in_weight,
    in_bias,
    mid_weight,
    mid_bias,
    out_weight,
    out_bias,
):
    height, levels, width = control.shape
    hidden = mid_weight.shape[0]
    channels, columns = radiance.shape
    slot_count = block_owner.shape[0]
    recv_most = channel_count.shape[0]
    per_tile = LANES // levels
    tiles = height // per_tile
    slab_rows = BLOCK_COLS * channels // LANES
    f32, bf16, i32 = jnp.float32, jnp.bfloat16, jnp.int32
    shape = jax.ShapeDtypeStruct
    field = height * levels * width
    conv_flops = 2 * 33 * field

    halves = channels // LANES
    radiance = radiance.T.reshape(recv_most, BLOCK_COLS, halves, LANES)
    radiance = jnp.swapaxes(radiance, 1, 2).reshape(recv_most, slab_rows, LANES)
    slabs = call(
        slabs_kernel,
        shape((recv_most + 1, slab_rows, LANES), bf16),
        [HBM] * 3,
        HBM,
        0,
        4 * channels * columns,
        scratch=(
            pltpu.VMEM((1, slot_count), i32),
            pltpu.VMEM((1, recv_most), i32),
            pltpu.VMEM((slab_rows, LANES), f32),
            pltpu.VMEM((slab_rows, LANES), bf16),
            pltpu.SemaphoreType.DMA((4,)),
        ),
        name="slabs",
    )(*pinned(radiance, block_owner.reshape(1, slot_count), channel_count.reshape(1, recv_most)))

    band = pltpu.VMEM((height, levels, width), f32)
    taps, turned, plan, own_part = call(
        prepare_kernel,
        (
            shape((tiles, 24, LANES), f32),
            shape((tiles, width, LANES), f32),
            shape((8, LANES), i32),
            shape(control.shape, f32),
        ),
        [HBM] * 5,
        (VMEM,) * 4,
        conv_flops // 2,
        12 * field,
        scratch=(
            pltpu.SMEM((height,), i32),
            pltpu.VMEM((1, slot_count), i32),
            pltpu.VMEM((1, slot_count), i32),
            band,
            band,
            pltpu.SemaphoreType.DMA((5,)),
        ),
        name="taps_background",
    )(
        *pinned(
            lon_width,
            background,
            block_cells.reshape(1, slot_count),
            block_owner.reshape(1, slot_count),
            control,
        )
    )

    far, close = exchange(control, control, "lat", False)
    lat_count = lax.axis_size("lat")
    near = [slabs]
    for step, bit in enumerate(swap_bits(lat_count)):
        if len(near) > 2:
            half = len(near) // 2
            near = [jnp.concatenate(near[:half], axis=0), jnp.concatenate(near[half:], axis=0)]
        if step == 1:
            near[1], far, close, taps = lax.optimization_barrier((near[1], far, close, taps))
        pairs = [(i, i ^ (1 << bit)) for i in range(lat_count)]
        near = near + [lax.ppermute(part, "lat", pairs) for part in near]
    near = [jnp.concatenate(near[:-1], axis=0), near[-1]]

    halos = pltpu.VMEM((2, REACH, levels, width), f32)
    smoothed, to_far, to_close = call(
        lat_smooth_kernel,
        (shape((tiles, width, LANES), f32),) + (shape((tiles, REACH, LANES), f32),) * 2,
        [VMEM] * 3,
        (VMEM,) * 3,
        conv_flops,
        16 * field,
        scratch=(halos,),
        name="lat_smooth",
    )(far, close, own_part)
    far, close = exchange(to_far, to_close, "lon", True)

    outer_slots = 3 * slot_count // 8
    late_slots = slot_count - outer_slots
    x_rows = slot_count * BLOCK_COLS
    outer_rows, late_rows = outer_slots * BLOCK_COLS, late_slots * BLOCK_COLS
    row_flops = 2 * hidden * (LANES + hidden + channels)
    weight_shapes = (
        shape((LANES, hidden), bf16),
        shape((hidden, hidden), bf16),
        shape((hidden, channels), bf16),
        shape((1, hidden), f32),
        shape((1, hidden), f32),
        shape((1, channels), f32),
    )

    def state_shapes(rows):
        return (shape((rows, hidden), bf16), shape((rows, hidden), bf16), shape((rows, channels), f32))

    plan_rows = pltpu.SMEM((8, LANES), i32)
    padded = pltpu.VMEM((tiles, width + 2 * REACH, LANES), f32)
    flat = pltpu.VMEM((tiles * width, LANES), f32)

    profile, *rest = call(
        functools.partial(inner_forward_kernel, outer_slots),
        (shape((tiles * width, LANES), f32),) + state_shapes(late_rows) + weight_shapes,
        [ANY] + [VMEM] * 3 + [HBM] * 6,
        (VMEM,) * 10,
        late_rows * row_flops,
        4 * 1024 * 1024,
        scratch=(
            plan_rows,
            padded,
            pltpu.VMEM((late_rows, LANES), f32),
            pltpu.SemaphoreType.DMA((6 + per_tile,)),
        ),
        name="inner_forward",
    )(
        plan,
        smoothed,
        turned,
        taps,
        *pinned(
            in_weight,
            in_bias.reshape(1, hidden),
            mid_weight,
            mid_bias.reshape(1, hidden),
            out_weight,
            out_bias.reshape(1, channels),
        ),
    )
    inner_states, weights = rest[:3], rest[3:]
    near, far, close, profile = lax.optimization_barrier((near, far, close, profile))
    across = [lax.ppermute(part, "lat", [(i, i ^ 1) for i in range(lat_count)]) for part in near]

    states = call(
        functools.partial(outer_forward_kernel, per_tile),
        state_shapes(outer_rows) + state_shapes(late_rows),
        [ANY] + [VMEM] * 12,
        (VMEM,) * 6,
        outer_rows * row_flops,
        4 * 1024 * 1024,
        scratch=(
            plan_rows,
            padded,
            flat,
            pltpu.VMEM((outer_rows, LANES), f32),
            pltpu.VMEM((late_rows, LANES), f32),
            pltpu.SemaphoreType.DMA,
        ),
        name="outer_forward",
    )(plan, far, close, smoothed, turned, taps, profile, *weights)

    slabs = [*near, *across]
    held_slabs, table, sens, to_far, to_close = call(
        functools.partial(outer_backward_kernel, per_tile, len(slabs)),
        (
            shape((lat_count * (recv_most + 1), slab_rows, LANES), bf16),
            shape((8, LANES), i32),
            shape((x_rows, LANES), f32),
            shape((tiles, REACH, LANES), bf16),
            shape((tiles, REACH, LANES), bf16),
        ),
        [ANY] + [ANY] * len(slabs) + [VMEM] * 9,
        (VMEM,) * 5,
        outer_rows * row_flops,
        4 * 1024 * 1024,
        scratch=(
            plan_rows,
            pltpu.VMEM((lat_count, slab_rows, LANES), bf16),
            pltpu.SMEM((8, LANES), i32),
            pltpu.VMEM((outer_rows, channels), f32),
            pltpu.VMEM((late_rows, channels), f32),
            flat,
            pltpu.SemaphoreType.DMA((lat_count + len(slabs) + 2,)),
        ),
        name="outer_backward",
    )(plan, *slabs, *weights[:3], *states)
    far, close = exchange(to_far, to_close, "lon", True)

    landing = call(
        functools.partial(inner_backward_kernel, per_tile, outer_slots),
        shape((tiles, width, LANES), f32),
        [ANY, VMEM, ANY] + [VMEM] * 7,
        VMEM,
        late_rows * row_flops,
        4 * 1024 * 1024,
        scratch=(
            plan_rows,
            pltpu.SMEM((8, LANES), i32),
            pltpu.VMEM((late_rows, channels), f32),
            pltpu.VMEM((x_rows, LANES), f32),
            flat,
            pltpu.SemaphoreType.DMA((2,)),
        ),
        name="inner_backward",
    )(plan, held_slabs, table, sens, *weights[:3], *inner_states)

    back, halved = call(
        lon_back_kernel,
        (shape((height, levels, width), f32), shape((height, levels, width), bf16)),
        [VMEM] * 4,
        (VMEM, VMEM),
        conv_flops,
        8 * field,
        scratch=(pltpu.VMEM((tiles, width + 2 * REACH, LANES), f32),),
        name="lon_back",
    )(far, close, landing, taps)
    far, close = exchange(halved, halved, "lat", False)
    own_part = call(
        own_back_kernel,
        shape((height, levels, width), f32),
        [VMEM, HBM],
        VMEM,
        conv_flops // 2,
        12 * field,
        scratch=(band, pltpu.SemaphoreType.DMA),
        name="lat_back_own",
    )(back, *pinned(control))

    return call(
        lat_back_kernel,
        shape((height, levels, width), f32),
        [VMEM] * 3,
        VMEM,
        conv_flops // 2,
        16 * field,
        scratch=(halos,),
        name="lat_back",
    )(far, close, own_part)


def solution(mesh):
    return jax.shard_map(
        shards,
        mesh=mesh,
        in_specs=(
            P("lat", None, "lon"),
            P("lat", None, "lon"),
            P("lat"),
            P("lat", "lon"),
            P("lat", "lon"),
            P("lat", "lon"),
            P("lat", "lon"),
            P(),
            P(),
            P(),
            P(),
            P(),
            P(),
        ),
        out_specs=P("lat", None, "lon"),
        check_vma=False,
    )
```

```python
import functools

import jax
import jax.numpy as jnp
import numpy as np
from jax import lax
from jax.experimental import pallas as pl
from jax.experimental.pallas import tpu as pltpu
from jax.sharding import PartitionSpec as P

REACH = 16
BLOCK_COLS = 8
LANES = 128
LAT_SIGMA = 8.0
WEIGHT_PIECES = 4
VMEM_BYTES = 40 * 1024 * 1024

VMEM = pl.BlockSpec(memory_space=pltpu.VMEM)
SMEM = pl.BlockSpec(memory_space=pltpu.SMEM)
HBM = pl.BlockSpec(memory_space=pltpu.HBM)
ANY = pl.BlockSpec(memory_space=pl.ANY)


def lat_taps():
    offsets = np.arange(-REACH, REACH + 1, dtype=np.float64)
    raw = np.exp(-offsets * offsets / (2.0 * LAT_SIGMA * LAT_SIGMA))
    return [float(v) for v in (raw / np.sqrt(np.sum(raw * raw))).astype(np.float32)]


def call(kernel, out_shape, in_specs, out_specs, flops, bytes_moved, scratch=(), name=None):
    return pl.pallas_call(
        kernel,
        out_shape=out_shape,
        in_specs=in_specs,
        out_specs=out_specs,
        scratch_shapes=list(scratch),
        compiler_params=pltpu.CompilerParams(vmem_limit_bytes=VMEM_BYTES),
        cost_estimate=pl.CostEstimate(flops=flops, bytes_accessed=bytes_moved, transcendentals=0),
        name=name,
    )


def pinned(*values):
    return [pltpu.with_memory_space_constraint(value, pltpu.HBM) for value in values]


def lat_sum(parts, row, first, height, start=None):
    taps = lat_taps()
    acc = start
    for k in range(height):
        j = first + k - row
        if abs(j) <= REACH:
            term = taps[j + REACH] * parts[k]
            acc = term if acc is None else acc + term
    return acc


def lat_rims(row, part, halos, height):
    low = lat_sum(halos.at[0], row, -REACH, REACH, part)
    return lat_sum(halos.at[1], row, height, REACH, low)


def fill_padded(padded, far, own, close):
    width = own.shape[1]
    low, high = sides(far[...], close[...], "lon")
    padded[:, 0:REACH, :] = low
    padded[:, REACH : REACH + width, :] = own[...]
    padded[:, REACH + width :, :] = high


def lon_conv(padded, taps, tile, start, width):
    middle = REACH + start
    acc = taps[tile, 0:1, :] * padded[tile, pl.ds(middle, width), :]
    for j in range(1, REACH + 1):
        both = padded[tile, pl.ds(middle + j, width), :] + padded[tile, pl.ds(middle - j, width), :]
        acc = acc + taps[tile, j : j + 1, :] * both
    return acc


def rounded(value):
    return value.astype(jnp.bfloat16).astype(jnp.float32)


def slabs_kernel(radiance, block_owner, channel_count, slabs, owners, counts, rows, tables, sems):
    recv_most = radiance.shape[0]
    moves = [
        pltpu.make_async_copy(radiance, slabs.at[pl.ds(0, recv_most)], sems.at[0]),
        pltpu.make_async_copy(block_owner, owners, sems.at[1]),
        pltpu.make_async_copy(channel_count, counts, sems.at[2]),
    ]
    for move in moves:
        move.start()
    rows[...] = jnp.full(rows.shape, -1.0, jnp.float32)
    moves[1].wait()
    moves[2].wait()
    rows[0:1, 0 : owners.shape[1]] = owners[...].astype(jnp.float32)
    rows[1:2, 0 : counts.shape[1]] = counts[...].astype(jnp.float32)
    tables[...] = rows[...].astype(jnp.bfloat16)
    last = pltpu.make_async_copy(tables, slabs.at[recv_most], sems.at[3])
    last.start()
    moves[0].wait()
    last.wait()


def prepare_kernel(
    lon_width,
    background,
    block_cells,
    block_owner,
    control,
    in_weight,
    in_bias,
    mid_weight,
    mid_bias,
    out_weight,
    out_bias,
    taps,
    turned,
    plan,
    own_part,
    wide_in,
    weight_two,
    weight_out,
    bias_one,
    bias_two,
    bias_out,
    widths,
    cells,
    owners,
    field,
    band,
    sems,
):
    moves = [
        pltpu.make_async_copy(lon_width, widths, sems.at[0]),
        pltpu.make_async_copy(block_cells, cells, sems.at[1]),
        pltpu.make_async_copy(block_owner, owners, sems.at[2]),
        pltpu.make_async_copy(background, field, sems.at[3]),
        pltpu.make_async_copy(control, band, sems.at[4]),
    ]
    tiles = turned.shape[0]
    height, levels, width = background.shape
    per_tile = height // tiles
    weights = [(in_bias, bias_one), (mid_bias, bias_two), (out_weight, weight_out), (out_bias, bias_out)]
    weights += [(in_weight, wide_in.at[pl.ds(sub * levels, levels)]) for sub in range(per_tile)]
    piece = mid_weight.shape[0] // WEIGHT_PIECES
    for k in range(WEIGHT_PIECES):
        rows = pl.ds(k * piece, piece)
        weights.append((mid_weight.at[rows], weight_two.at[rows]))
    loads = [
        pltpu.make_async_copy(source, target, sems.at[5 + k]) for k, (source, target) in enumerate(weights)
    ]
    for move in moves + loads:
        move.start()
    groups = width // BLOCK_COLS
    rim = REACH // BLOCK_COLS
    slot_count = cells.shape[1]

    lane_row = lax.broadcasted_iota(jnp.int32, (1, LANES), 1) // levels
    steps = lax.broadcasted_iota(jnp.int32, (taps.shape[1], LANES), 0)
    dist = steps.astype(jnp.float32)
    weight = jnp.where(steps == 0, 1.0, jnp.where(steps <= REACH, 2.0, 0.0))
    moves[0].wait()
    for tile in range(tiles):
        spread = jnp.zeros((1, LANES), jnp.int32)
        for sub in range(per_tile):
            spread = jnp.where(lane_row == sub, widths[tile * per_tile + sub], spread)
        spread = spread.astype(jnp.float32)
        raw = jnp.exp(-dist * dist / (2.0 * spread * spread))
        norm = jnp.sum(weight * raw * raw, axis=0, keepdims=True)
        taps[tile] = raw / jnp.sqrt(norm)

    moves[1].wait()
    moves[2].wait()
    rows = lax.broadcasted_iota(jnp.int32, (slot_count, slot_count), 0)
    lanes = lax.broadcasted_iota(jnp.int32, (slot_count, slot_count), 1)
    group = cells[...] % groups
    outer = ((group < rim) | (group >= groups - rim)) & (owners[...] >= 0)
    outer_here = jnp.where(outer, 1, 0)
    outer_count = jnp.sum(outer_here, axis=1, keepdims=True)
    earlier = jnp.sum(jnp.where(lanes < rows, outer_here, 0), axis=1, keepdims=True)
    here = jnp.sum(jnp.where(lanes == rows, outer_here, 0), axis=1, keepdims=True)
    cell = jnp.sum(jnp.where(lanes == rows, cells[...], 0), axis=1, keepdims=True)
    position = jnp.where(here == 1, earlier, outer_count + rows[:, 0:1] - earlier)
    at = lax.broadcasted_iota(jnp.int32, (slot_count, LANES), 1)
    hit = position == at
    slot = lax.broadcasted_iota(jnp.int32, (slot_count, LANES), 0)
    plan[...] = jnp.zeros_like(plan)
    plan[0:1, :] = jnp.sum(jnp.where(hit, cell, 0), axis=0, keepdims=True)
    plan[1:2, :] = jnp.sum(jnp.where(hit, slot, 0), axis=0, keepdims=True)
    plan[2:3, :] = jnp.broadcast_to(outer_count, (1, LANES))

    moves[3].wait()
    for tile in range(tiles):
        block = field[tile * per_tile : (tile + 1) * per_tile].reshape(per_tile * levels, width)
        turned[tile] = jnp.transpose(block)
    moves[4].wait()
    for row in range(height):
        own_part[row] = lat_sum(band, row, 0, height)
    for move in loads:
        move.wait()


def swap_bits(count):
    return list(range(count.bit_length() - 2, 0, -1))


def routing(recv_most, slot_count, slabs, table):
    per_owner = recv_most + 1
    spans, count = [], 0
    for ref in slabs:
        spans.append((ref, count))
        count += ref.shape[0] // per_owner
    half = count // 2
    here = lax.axis_index("lat")
    rows = lax.broadcasted_iota(jnp.int32, (slot_count, LANES), 0)
    lanes = lax.broadcasted_iota(jnp.int32, (slot_count, LANES), 1)
    diagonal = rows == lanes
    zero = jnp.zeros((slot_count, LANES), jnp.int32)

    bits = swap_bits(count)

    def device_of(k):
        apart = jnp.where(k < half, 0, 1)
        for place, bit in enumerate(bits):
            apart = apart + (((k >> place) & 1) << bit)
        return here ^ apart

    def over_sets(step):
        acc = zero
        for ref, first in spans:

            def add(k, acc, ref=ref, first=first):
                lines = ref[k * per_owner + recv_most].astype(jnp.float32)
                owners, counts = lines[0:1].astype(jnp.int32), lines[1:2].astype(jnp.int32)
                return acc + step(device_of(first + k), owners, counts)

            acc = lax.fori_loop(0, ref.shape[0] // per_owner, add, acc, unroll=count <= 8)
        return jnp.sum(acc, axis=1, keepdims=True)

    mine = slabs[0][recv_most].astype(jnp.float32)[0:1].astype(jnp.int32)
    owner = jnp.sum(jnp.where(diagonal, mine, 0), axis=1, keepdims=True)

    def rank(device, owners, counts):
        before = (device < here) | ((device == here) & (lanes < rows))
        return jnp.where((owners == owner) & before, 1, 0)

    arrival = over_sets(rank)

    def counted(device, owners, counts):
        return jnp.where((owner == device) & (lanes == arrival), counts, 0)

    kept = over_sets(counted)
    apart = owner ^ here
    entry = (apart & 1) * half
    for place, bit in enumerate(bits):
        entry = entry + (((apart >> bit) & 1) << place)
    target = jnp.where(owner >= 0, entry * per_owner + arrival, 0)
    table[...] = jnp.zeros_like(table)
    for row, column in enumerate((target, kept)):
        table[row : row + 1, :] = jnp.sum(jnp.where(diagonal, column, 0), axis=0, keepdims=True)


def odd_index(axis):
    return lax.axis_index(axis) % 2 == 1


def sides(far, close, axis):
    odd = odd_index(axis)
    far, close = far.astype(jnp.float32), close.astype(jnp.float32)
    return jnp.where(odd, close, far), jnp.where(odd, far, close)


def split_sides(low, high, axis):
    odd = odd_index(axis)
    return jnp.where(odd, high, low), jnp.where(odd, low, high)


def lat_smooth_kernel(far, close, own_part, smoothed, to_far, to_close, halos):
    tiles = smoothed.shape[0]
    height, levels, width = own_part.shape
    per_tile = height // tiles
    halos[0], halos[1] = sides(far[...], close[...], "lat")
    for tile in range(tiles):
        rows = range(tile * per_tile, (tile + 1) * per_tile)
        rows = [lat_rims(row, own_part[row], halos, height) for row in rows]
        turned = jnp.transpose(jnp.concatenate(rows, axis=0))
        smoothed[tile] = turned
        to_far[tile], to_close[tile] = split_sides(turned[0:REACH], turned[width - REACH : width], "lon")


def block_place(plan, position, groups, per_tile, width):
    block = plan[0, position]
    row = block // groups
    start = (row // per_tile) * width + (block % groups) * BLOCK_COLS
    return pl.multiple_of(start, BLOCK_COLS), row % per_tile


def take_blocks(plan, profile, picked, first, count, per_tile, width):
    groups = width // BLOCK_COLS
    lane_row = lax.broadcasted_iota(jnp.int32, (BLOCK_COLS, LANES), 1) // (LANES // per_tile)
    for k in range(count):
        start, sub = block_place(plan, first + k, groups, per_tile, width)
        block = profile[pl.ds(start, BLOCK_COLS), :]
        picked[k * BLOCK_COLS : (k + 1) * BLOCK_COLS, :] = jnp.where(lane_row == sub, block, 0.0)


def land_blocks(plan, field, sens, first, count, per_tile, width):
    groups = width // BLOCK_COLS
    lane_row = lax.broadcasted_iota(jnp.int32, (BLOCK_COLS, LANES), 1) // (LANES // per_tile)
    for k in range(first, first + count):
        start, sub = block_place(plan, k, groups, per_tile, width)
        block = sens[k * BLOCK_COLS : (k + 1) * BLOCK_COLS, :]
        field[pl.ds(start, BLOCK_COLS), :] += jnp.where(lane_row == sub, block, 0.0)


def take_observed(plan, table, slabs, observed, first, count):
    channels = observed.shape[1]
    channel = lax.broadcasted_iota(jnp.int32, (BLOCK_COLS, LANES), 1)
    for k in range(count):
        slot = plan[1, first + k]
        at, kept = table[0, slot], table[1, slot]
        start = 0
        for ref in slabs:
            size = ref.shape[0]

            @pl.when((at >= start) & (at < start + size))
            def _(ref=ref, start=start):
                slab = ref[at - start].astype(jnp.float32)
                for h in range(channels // LANES):
                    part = slab[h * BLOCK_COLS : (h + 1) * BLOCK_COLS]
                    part = jnp.where(channel + h * LANES < kept, part, jnp.inf)
                    observed[k * BLOCK_COLS : (k + 1) * BLOCK_COLS, h * LANES : (h + 1) * LANES] = part

            start += size


def dot(a, b):
    return jnp.dot(a, b, preferred_element_type=jnp.float32)


def dot_t(a, b):
    return lax.dot_general(a, b, (((1,), (1,)), ((), ())), preferred_element_type=jnp.float32)


def net_forward(picked, weights, states):
    wide_in, weight_two, weight_out, bias_one, bias_two, bias_out = weights
    act_one, act_two, emitted = states
    inputs = picked[...].astype(jnp.bfloat16)
    act_one[...] = jnp.tanh(dot(inputs, wide_in[...]) + bias_one[...]).astype(jnp.bfloat16)
    act_two[...] = jnp.tanh(dot(act_one[...], weight_two[...]) + bias_two[...]).astype(jnp.bfloat16)
    emitted[...] = dot(act_two[...], weight_out[...]) + bias_out[...]


def net_backward(observed, states, weights):
    wide_in, weight_two, weight_out = weights[:3]
    act_one, act_two, emitted = states
    seen = observed[...]
    misfit = jnp.where(seen < jnp.inf, emitted[...] - seen, 0.0).astype(jnp.bfloat16)
    two = act_two[...].astype(jnp.float32)
    grad_two = (dot_t(misfit, weight_out[...]) * (1.0 - two * two)).astype(jnp.bfloat16)
    one = act_one[...].astype(jnp.float32)
    grad_one = (dot_t(grad_two, weight_two[...]) * (1.0 - one * one)).astype(jnp.bfloat16)
    return rounded(dot_t(grad_one, wide_in[...]))


def inner_forward_kernel(per_tile, outer_slots, plan, own, turned, taps, *refs):
    weights, profile, states, (rows, padded, picked, sem) = refs[:6], refs[6], refs[7:10], refs[10:]
    tiles, width, _ = own.shape
    count = picked.shape[0] // BLOCK_COLS
    plan_in = pltpu.make_async_copy(plan, rows, sem)
    plan_in.start()
    zeros = jnp.zeros((tiles, REACH, LANES), jnp.float32)
    padded[:, 0:REACH, :] = zeros
    padded[:, REACH : REACH + width, :] = own[...]
    padded[:, REACH + width :, :] = zeros
    for tile in range(tiles):
        total = turned[tile] + lon_conv(padded, taps, tile, 0, width)
        profile[tile * width : (tile + 1) * width, :] = rounded(total)
    plan_in.wait()

    @pl.when(rows[2, 0] <= outer_slots)
    def _():
        take_blocks(rows, profile, picked, outer_slots, count, per_tile, width)
        net_forward(picked, weights, states)


def outer_forward_kernel(
    per_tile,
    plan,
    far,
    close,
    own,
    turned,
    taps,
    inner_profile,
    *refs,
):
    weights, states, late_states, (rows, padded, profile, picked, late_picked, sem) = (
        refs[:6],
        refs[6:9],
        refs[9:12],
        refs[12:],
    )
    tiles, width, _ = own.shape
    outer_slots = picked.shape[0] // BLOCK_COLS
    late_slots = late_picked.shape[0] // BLOCK_COLS
    plan_in = pltpu.make_async_copy(plan, rows, sem)
    plan_in.start()
    fill_padded(padded, far, own, close)
    profile[...] = inner_profile[...]
    for tile in range(tiles):
        for start in (0, width - REACH):
            total = turned[tile, start : start + REACH, :] + lon_conv(padded, taps, tile, start, REACH)
            profile[tile * width + start : tile * width + start + REACH, :] = rounded(total)
    plan_in.wait()
    take_blocks(rows, profile, picked, 0, outer_slots, per_tile, width)
    net_forward(picked, weights, states)

    @pl.when(rows[2, 0] > outer_slots)
    def _():
        take_blocks(rows, profile, late_picked, outer_slots, late_slots, per_tile, width)
        net_forward(late_picked, weights, late_states)


def outer_backward_kernel(per_tile, parts, recv_most, plan, *refs):
    slabs, refs = refs[:parts], refs[parts:]
    weights, states, late_states, refs = refs[:3], refs[3:6], refs[6:9], refs[9:]
    (table_rows, sens, to_far, to_close) = refs[:4]
    (rows, table, observed, late_observed, field, sems) = refs[4:]
    tiles = to_far.shape[0]
    width = field.shape[0] // tiles
    outer_slots = observed.shape[0] // BLOCK_COLS
    late_slots = late_observed.shape[0] // BLOCK_COLS

    plan_in = pltpu.make_async_copy(plan, rows, sems.at[0])
    plan_in.start()
    routing(recv_most, outer_slots + late_slots, slabs, table_rows)
    table_in = pltpu.make_async_copy(table_rows, table, sems.at[1])
    table_in.start()
    field[...] = jnp.zeros_like(field)
    plan_in.wait()
    table_in.wait()

    take_observed(rows, table, slabs, observed, 0, outer_slots)
    sens[0 : outer_slots * BLOCK_COLS, :] = net_backward(observed, states, weights)
    land_blocks(rows, field, sens, 0, outer_slots, per_tile, width)

    @pl.when(rows[2, 0] > outer_slots)
    def _():
        take_observed(rows, table, slabs, late_observed, outer_slots, late_slots)
        sens[outer_slots * BLOCK_COLS :, :] = net_backward(late_observed, late_states, weights)
        land_blocks(rows, field, sens, outer_slots, late_slots, per_tile, width)

    for tile in range(tiles):
        low = field[tile * width : tile * width + REACH, :]
        high = field[(tile + 1) * width - REACH : (tile + 1) * width, :]
        low, high = split_sides(low, high, "lon")
        to_far[tile], to_close[tile] = low.astype(jnp.bfloat16), high.astype(jnp.bfloat16)


def inner_backward_kernel(per_tile, parts, outer_slots, plan, table_rows, sens, *refs):
    slabs, refs = refs[:parts], refs[parts:]
    weights, states, refs = refs[:3], refs[3:6], refs[6:]
    landing, rows, table, observed, inner, field, sems = refs
    tiles, width, _ = landing.shape
    late_slots = observed.shape[0] // BLOCK_COLS
    split = outer_slots * BLOCK_COLS
    moves = [
        pltpu.make_async_copy(plan, rows, sems.at[0]),
        pltpu.make_async_copy(table_rows, table, sems.at[1]),
    ]
    for move in moves:
        move.start()
    field[...] = jnp.zeros_like(field)
    inner[...] = sens[...]
    for move in moves:
        move.wait()

    @pl.when(rows[2, 0] <= outer_slots)
    def _():
        take_observed(rows, table, slabs, observed, outer_slots, late_slots)
        inner[split:, :] = net_backward(observed, states, weights)

    land_blocks(rows, field, inner, 0, outer_slots + late_slots, per_tile, width)
    for tile in range(tiles):
        landing[tile] = field[tile * width : (tile + 1) * width, :]


def lon_back_kernel(far, close, own, taps, back, halved, padded):
    tiles, width, _ = own.shape
    height, levels, _ = back.shape
    per_tile = height // tiles
    fill_padded(padded, far, own, close)
    for tile in range(tiles):
        rows = jnp.transpose(lon_conv(padded, taps, tile, 0, width))
        rows = rows.reshape(per_tile, levels, width)
        back[tile * per_tile : (tile + 1) * per_tile] = rows
        halved[tile * per_tile : (tile + 1) * per_tile] = rows.astype(jnp.bfloat16)


def own_back_kernel(back, control, own_part, held, sem):
    control_in = pltpu.make_async_copy(control, held, sem)
    control_in.start()
    control_in.wait()
    height = back.shape[0]
    for row in range(height):
        own_part[row] = lat_sum(back, row, 0, height, held[row])


def lat_back_kernel(far, close, own_part, gradient, halos):
    halos[0], halos[1] = sides(far[...], close[...], "lat")
    height = own_part.shape[0]
    for row in range(height):
        gradient[row] = lat_rims(row, own_part[row], halos, height)


def exchange(to_far, to_close, axis, periodic):
    count = lax.axis_size(axis)
    far = []
    for odd in range(1, count, 2):
        if odd + 1 < count or periodic:
            far += [(odd, (odd + 1) % count), ((odd + 1) % count, odd)]
    close = [(i, i ^ 1) for i in range(count)]
    if to_far is not to_close:
        to_close, _ = lax.optimization_barrier((to_close, to_far))
    return lax.ppermute(to_far, axis, far), lax.ppermute(to_close, axis, close)


def shards(
    control,
    background,
    lon_width,
    block_cells,
    block_owner,
    channel_count,
    radiance,
    in_weight,
    in_bias,
    mid_weight,
    mid_bias,
    out_weight,
    out_bias,
):
    height, levels, width = control.shape
    hidden = mid_weight.shape[0]
    channels, columns = radiance.shape
    slot_count = block_owner.shape[0]
    recv_most = channel_count.shape[0]
    per_tile = LANES // levels
    tiles = height // per_tile
    slab_rows = BLOCK_COLS * channels // LANES
    f32, bf16, i32 = jnp.float32, jnp.bfloat16, jnp.int32
    shape = jax.ShapeDtypeStruct
    field = height * levels * width
    conv_flops = 2 * 33 * field

    halves = channels // LANES
    radiance = radiance.T.reshape(recv_most, BLOCK_COLS, halves, LANES)
    radiance = jnp.swapaxes(radiance, 1, 2).reshape(recv_most, slab_rows, LANES)
    slabs = call(
        slabs_kernel,
        shape((recv_most + 1, slab_rows, LANES), bf16),
        [HBM] * 3,
        HBM,
        0,
        4 * channels * columns,
        scratch=(
            pltpu.VMEM((1, slot_count), i32),
            pltpu.VMEM((1, recv_most), i32),
            pltpu.VMEM((slab_rows, LANES), f32),
            pltpu.VMEM((slab_rows, LANES), bf16),
            pltpu.SemaphoreType.DMA((4,)),
        ),
        name="slabs",
    )(*pinned(radiance, block_owner.reshape(1, slot_count), channel_count.reshape(1, recv_most)))

    band = pltpu.VMEM((height, levels, width), f32)
    taps, turned, plan, own_part, *weights = call(
        prepare_kernel,
        (
            shape((tiles, 24, LANES), f32),
            shape((tiles, width, LANES), f32),
            shape((8, LANES), i32),
            shape(control.shape, f32),
            shape((LANES, hidden), bf16),
            shape((hidden, hidden), bf16),
            shape((hidden, channels), bf16),
            shape((1, hidden), f32),
            shape((1, hidden), f32),
            shape((1, channels), f32),
        ),
        [HBM] * 11,
        (VMEM,) * 10,
        conv_flops // 2,
        12 * field + 6 * hidden * hidden,
        scratch=(
            pltpu.SMEM((height,), i32),
            pltpu.VMEM((1, slot_count), i32),
            pltpu.VMEM((1, slot_count), i32),
            band,
            band,
            pltpu.SemaphoreType.DMA((9 + per_tile + WEIGHT_PIECES,)),
        ),
        name="taps_background",
    )(
        *pinned(
            lon_width,
            background,
            block_cells.reshape(1, slot_count),
            block_owner.reshape(1, slot_count),
            control,
            in_weight,
            in_bias.reshape(1, hidden),
            mid_weight,
            mid_bias.reshape(1, hidden),
            out_weight,
            out_bias.reshape(1, channels),
        )
    )

    far, close = exchange(control, control, "lat", False)

    lat_count = lax.axis_size("lat")
    one, two, *others = swap_bits(lat_count)

    def swapped(part, bit, odd_bit):
        pairs = [(i, i ^ (1 << (odd_bit if i % 2 else bit))) for i in range(lat_count)]
        return lax.ppermute(part, "lat", pairs)

    first, second = swapped(slabs, one, one), swapped(slabs, two, two)

    halos = pltpu.VMEM((2, REACH, levels, width), f32)
    smoothed, to_far, to_close = call(
        lat_smooth_kernel,
        (shape((tiles, width, LANES), f32),) + (shape((tiles, REACH, LANES), f32),) * 2,
        [VMEM] * 3,
        (VMEM,) * 3,
        conv_flops,
        16 * field,
        scratch=(halos,),
        name="lat_smooth",
    )(far, close, own_part)
    far, close = exchange(to_far, to_close, "lon", True)
    first, second, *_ = lax.optimization_barrier((first, second, to_far, to_close))
    passed = jnp.where(odd_index("lat"), first, second)
    near = [slabs, first, second, swapped(passed, one, two)]
    for bit in others:
        near = [jnp.concatenate(near, axis=0)]
        near.append(swapped(near[0], bit, bit))
    near = [jnp.concatenate(near[:-1], axis=0), near[-1]]

    outer_slots = 3 * slot_count // 8
    late_slots = slot_count - outer_slots
    x_rows = slot_count * BLOCK_COLS
    outer_rows, late_rows = outer_slots * BLOCK_COLS, late_slots * BLOCK_COLS
    row_flops = 2 * hidden * (LANES + hidden + channels)
    def state_shapes(rows):
        return (shape((rows, hidden), bf16), shape((rows, hidden), bf16), shape((rows, channels), f32))

    plan_rows = pltpu.SMEM((8, LANES), i32)
    padded = pltpu.VMEM((tiles, width + 2 * REACH, LANES), f32)
    flat = pltpu.VMEM((tiles * width, LANES), f32)

    profile, *inner_states = call(
        functools.partial(inner_forward_kernel, per_tile, outer_slots),
        (shape((tiles * width, LANES), f32),) + state_shapes(late_rows),
        [ANY] + [VMEM] * 9,
        (VMEM,) * 4,
        late_rows * row_flops,
        4 * 1024 * 1024,
        scratch=(plan_rows, padded, pltpu.VMEM((late_rows, LANES), f32), pltpu.SemaphoreType.DMA),
        name="inner_forward",
    )(plan, smoothed, turned, taps, *weights)
    near, far, close, profile = lax.optimization_barrier((near, far, close, profile))
    across = [lax.ppermute(part, "lat", [(i, i ^ 1) for i in range(lat_count)]) for part in near]

    states = call(
        functools.partial(outer_forward_kernel, per_tile),
        state_shapes(outer_rows) + state_shapes(late_rows),
        [ANY] + [VMEM] * 12,
        (VMEM,) * 6,
        outer_rows * row_flops,
        4 * 1024 * 1024,
        scratch=(
            plan_rows,
            padded,
            flat,
            pltpu.VMEM((outer_rows, LANES), f32),
            pltpu.VMEM((late_rows, LANES), f32),
            pltpu.SemaphoreType.DMA,
        ),
        name="outer_forward",
    )(plan, far, close, smoothed, turned, taps, profile, *weights)

    slabs = [*near, *across]
    table, sens, to_far, to_close = call(
        functools.partial(outer_backward_kernel, per_tile, len(slabs), recv_most),
        (
            shape((8, LANES), i32),
            shape((x_rows, LANES), f32),
            shape((tiles, REACH, LANES), bf16),
            shape((tiles, REACH, LANES), bf16),
        ),
        [ANY] + [VMEM] * (len(slabs) + 9),
        (VMEM,) * 4,
        outer_rows * row_flops,
        4 * 1024 * 1024,
        scratch=(
            plan_rows,
            pltpu.SMEM((8, LANES), i32),
            pltpu.VMEM((outer_rows, channels), f32),
            pltpu.VMEM((late_rows, channels), f32),
            flat,
            pltpu.SemaphoreType.DMA((2,)),
        ),
        name="outer_backward",
    )(plan, *slabs, *weights[:3], *states)
    far, close = exchange(to_far, to_close, "lon", True)

    landing = call(
        functools.partial(inner_backward_kernel, per_tile, len(slabs), outer_slots),
        shape((tiles, width, LANES), f32),
        [ANY, ANY] + [VMEM] * (len(slabs) + 7),
        VMEM,
        late_rows * row_flops,
        4 * 1024 * 1024,
        scratch=(
            plan_rows,
            pltpu.SMEM((8, LANES), i32),
            pltpu.VMEM((late_rows, channels), f32),
            pltpu.VMEM((x_rows, LANES), f32),
            flat,
            pltpu.SemaphoreType.DMA((2,)),
        ),
        name="inner_backward",
    )(plan, table, sens, *slabs, *weights[:3], *inner_states)

    back, halved = call(
        lon_back_kernel,
        (shape((height, levels, width), f32), shape((height, levels, width), bf16)),
        [VMEM] * 4,
        (VMEM, VMEM),
        conv_flops,
        8 * field,
        scratch=(pltpu.VMEM((tiles, width + 2 * REACH, LANES), f32),),
        name="lon_back",
    )(far, close, landing, taps)
    far, close = exchange(halved, halved, "lat", False)
    own_part = call(
        own_back_kernel,
        shape((height, levels, width), f32),
        [VMEM, HBM],
        VMEM,
        conv_flops // 2,
        12 * field,
        scratch=(band, pltpu.SemaphoreType.DMA),
        name="lat_back_own",
    )(back, *pinned(control))
    far, own_part = lax.optimization_barrier((far, own_part))

    return call(
        lat_back_kernel,
        shape((height, levels, width), f32),
        [VMEM] * 3,
        VMEM,
        conv_flops // 2,
        16 * field,
        scratch=(halos,),
        name="lat_back",
    )(far, close, own_part)


def solution(mesh):
    return jax.shard_map(
        shards,
        mesh=mesh,
        in_specs=(
            P("lat", None, "lon"),
            P("lat", None, "lon"),
            P("lat"),
            P("lat", "lon"),
            P("lat", "lon"),
            P("lat", "lon"),
            P("lat", "lon"),
            P(),
            P(),
            P(),
            P(),
            P(),
            P(),
        ),
        out_specs=P("lat", None, "lon"),
        check_vma=False,
    )
```

```python
import functools

import jax
import jax.numpy as jnp
import numpy as np
from jax import lax
from jax.experimental import pallas as pl
from jax.experimental.pallas import tpu as pltpu
from jax.sharding import PartitionSpec as P

REACH = 16
BLOCK_COLS = 8
LANES = 128
LAT_SIGMA = 8.0
WEIGHT_PIECES = 4
VMEM_BYTES = 40 * 1024 * 1024

VMEM = pl.BlockSpec(memory_space=pltpu.VMEM)
SMEM = pl.BlockSpec(memory_space=pltpu.SMEM)
HBM = pl.BlockSpec(memory_space=pltpu.HBM)
ANY = pl.BlockSpec(memory_space=pl.ANY)


def lat_taps():
    offsets = np.arange(-REACH, REACH + 1, dtype=np.float64)
    raw = np.exp(-offsets * offsets / (2.0 * LAT_SIGMA * LAT_SIGMA))
    return [float(v) for v in (raw / np.sqrt(np.sum(raw * raw))).astype(np.float32)]


def call(kernel, out_shape, in_specs, out_specs, flops, bytes_moved, scratch=(), name=None):
    return pl.pallas_call(
        kernel,
        out_shape=out_shape,
        in_specs=in_specs,
        out_specs=out_specs,
        scratch_shapes=list(scratch),
        compiler_params=pltpu.CompilerParams(vmem_limit_bytes=VMEM_BYTES),
        cost_estimate=pl.CostEstimate(flops=flops, bytes_accessed=bytes_moved, transcendentals=0),
        name=name,
    )


def pinned(*values):
    return [pltpu.with_memory_space_constraint(value, pltpu.HBM) for value in values]


def lat_sum(parts, row, first, height, start=None):
    taps = lat_taps()
    acc = start
    for k in range(height):
        j = first + k - row
        if abs(j) <= REACH:
            term = taps[j + REACH] * parts[k]
            acc = term if acc is None else acc + term
    return acc


def lat_rims(row, part, halos, height):
    low = lat_sum(halos.at[0], row, -REACH, REACH, part)
    return lat_sum(halos.at[1], row, height, REACH, low)


def fill_padded(padded, far, own, close):
    width = own.shape[1]
    low, high = sides(far[...], close[...], "lon")
    padded[:, 0:REACH, :] = low
    padded[:, REACH : REACH + width, :] = own[...]
    padded[:, REACH + width :, :] = high


def lon_conv(padded, taps, tile, start, width):
    middle = REACH + start
    acc = taps[tile, 0:1, :] * padded[tile, pl.ds(middle, width), :]
    for j in range(1, REACH + 1):
        both = padded[tile, pl.ds(middle + j, width), :] + padded[tile, pl.ds(middle - j, width), :]
        acc = acc + taps[tile, j : j + 1, :] * both
    return acc


def rounded(value):
    return value.astype(jnp.bfloat16).astype(jnp.float32)


def halved_rows(rows, order):
    halves, carry = {}, None
    for row in order:
        value = rows[row] if carry is None else rows[row] + carry
        halves[row] = value.astype(jnp.bfloat16)
        carry = value - halves[row].astype(jnp.float32)
    return [halves[row] for row in sorted(halves)]


def halve_for_sides(rows, height, to_far, to_close):
    odd = odd_index("lat")
    upward = halved_rows(rows, range(height - 1, -1, -1))
    downward = halved_rows(rows, range(height))
    for row in range(height):
        to_far[row] = jnp.where(odd, upward[row], downward[row])
        to_close[row] = jnp.where(odd, downward[row], upward[row])


def first_kernel(
    radiance, block_owner, channel_count, control, slabs, to_far, to_close, owners, counts, rows, tables, held, sems
):
    recv_most = radiance.shape[0]
    moves = [
        pltpu.make_async_copy(radiance, slabs.at[pl.ds(0, recv_most)], sems.at[0]),
        pltpu.make_async_copy(block_owner, owners, sems.at[1]),
        pltpu.make_async_copy(channel_count, counts, sems.at[2]),
        pltpu.make_async_copy(control, held, sems.at[3]),
    ]
    for move in moves:
        move.start()
    rows[...] = jnp.full(rows.shape, -1.0, jnp.float32)
    moves[1].wait()
    moves[2].wait()
    rows[0:1, 0 : owners.shape[1]] = owners[...].astype(jnp.float32)
    rows[1:2, 0 : counts.shape[1]] = counts[...].astype(jnp.float32)
    tables[...] = rows[...].astype(jnp.bfloat16)
    last = pltpu.make_async_copy(tables, slabs.at[recv_most], sems.at[4])
    last.start()
    moves[3].wait()
    halve_for_sides(held, held.shape[0], to_far, to_close)
    moves[0].wait()
    last.wait()


def prepare_kernel(
    lon_width,
    background,
    block_cells,
    block_owner,
    control,
    taps,
    turned,
    plan,
    own_part,
    widths,
    cells,
    owners,
    field,
    band,
    sems,
):
    moves = [
        pltpu.make_async_copy(lon_width, widths, sems.at[0]),
        pltpu.make_async_copy(block_cells, cells, sems.at[1]),
        pltpu.make_async_copy(block_owner, owners, sems.at[2]),
        pltpu.make_async_copy(background, field, sems.at[3]),
        pltpu.make_async_copy(control, band, sems.at[4]),
    ]
    tiles = turned.shape[0]
    height, levels, width = background.shape
    per_tile = height // tiles
    for move in moves:
        move.start()
    groups = width // BLOCK_COLS
    rim = REACH // BLOCK_COLS
    slot_count = cells.shape[1]

    lane_row = lax.broadcasted_iota(jnp.int32, (1, LANES), 1) // levels
    steps = lax.broadcasted_iota(jnp.int32, (taps.shape[1], LANES), 0)
    dist = steps.astype(jnp.float32)
    weight = jnp.where(steps == 0, 1.0, jnp.where(steps <= REACH, 2.0, 0.0))
    moves[0].wait()
    for tile in range(tiles):
        spread = jnp.zeros((1, LANES), jnp.int32)
        for sub in range(per_tile):
            spread = jnp.where(lane_row == sub, widths[tile * per_tile + sub], spread)
        spread = spread.astype(jnp.float32)
        raw = jnp.exp(-dist * dist / (2.0 * spread * spread))
        norm = jnp.sum(weight * raw * raw, axis=0, keepdims=True)
        taps[tile] = raw / jnp.sqrt(norm)

    moves[1].wait()
    moves[2].wait()
    rows = lax.broadcasted_iota(jnp.int32, (slot_count, slot_count), 0)
    lanes = lax.broadcasted_iota(jnp.int32, (slot_count, slot_count), 1)
    group = cells[...] % groups
    outer = ((group < rim) | (group >= groups - rim)) & (owners[...] >= 0)
    outer_here = jnp.where(outer, 1, 0)
    outer_count = jnp.sum(outer_here, axis=1, keepdims=True)
    earlier = jnp.sum(jnp.where(lanes < rows, outer_here, 0), axis=1, keepdims=True)
    here = jnp.sum(jnp.where(lanes == rows, outer_here, 0), axis=1, keepdims=True)
    cell = jnp.sum(jnp.where(lanes == rows, cells[...], 0), axis=1, keepdims=True)
    position = jnp.where(here == 1, earlier, outer_count + rows[:, 0:1] - earlier)
    at = lax.broadcasted_iota(jnp.int32, (slot_count, LANES), 1)
    hit = position == at
    slot = lax.broadcasted_iota(jnp.int32, (slot_count, LANES), 0)
    plan[...] = jnp.zeros_like(plan)
    plan[0:1, :] = jnp.sum(jnp.where(hit, cell, 0), axis=0, keepdims=True)
    plan[1:2, :] = jnp.sum(jnp.where(hit, slot, 0), axis=0, keepdims=True)
    plan[2:3, :] = jnp.broadcast_to(outer_count, (1, LANES))

    moves[3].wait()
    for tile in range(tiles):
        block = field[tile * per_tile : (tile + 1) * per_tile].reshape(per_tile * levels, width)
        turned[tile] = jnp.transpose(block)
    moves[4].wait()
    for row in range(height):
        own_part[row] = lat_sum(band, row, 0, height)


def swap_bits(count):
    return list(range(count.bit_length() - 2, 0, -1))


def routing(recv_most, slot_count, slabs, table):
    per_owner = recv_most + 1
    spans, count = [], 0
    for ref in slabs:
        spans.append((ref, count))
        count += ref.shape[0] // per_owner
    half = count // 2
    here = lax.axis_index("lat")
    rows = lax.broadcasted_iota(jnp.int32, (slot_count, LANES), 0)
    lanes = lax.broadcasted_iota(jnp.int32, (slot_count, LANES), 1)
    diagonal = rows == lanes
    zero = jnp.zeros((slot_count, LANES), jnp.int32)

    bits = swap_bits(count)

    def device_of(k):
        apart = jnp.where(k < half, 0, 1)
        for place, bit in enumerate(bits):
            apart = apart + (((k >> place) & 1) << bit)
        return here ^ apart

    def over_sets(step):
        acc = zero
        for ref, first in spans:

            def add(k, acc, ref=ref, first=first):
                lines = ref[k * per_owner + recv_most].astype(jnp.float32)
                owners, counts = lines[0:1].astype(jnp.int32), lines[1:2].astype(jnp.int32)
                return acc + step(device_of(first + k), owners, counts)

            acc = lax.fori_loop(0, ref.shape[0] // per_owner, add, acc, unroll=count <= 8)
        return jnp.sum(acc, axis=1, keepdims=True)

    mine = slabs[0][recv_most].astype(jnp.float32)[0:1].astype(jnp.int32)
    owner = jnp.sum(jnp.where(diagonal, mine, 0), axis=1, keepdims=True)

    def rank(device, owners, counts):
        before = (device < here) | ((device == here) & (lanes < rows))
        return jnp.where((owners == owner) & before, 1, 0)

    arrival = over_sets(rank)

    def counted(device, owners, counts):
        return jnp.where((owner == device) & (lanes == arrival), counts, 0)

    kept = over_sets(counted)
    apart = owner ^ here
    entry = (apart & 1) * half
    for place, bit in enumerate(bits):
        entry = entry + (((apart >> bit) & 1) << place)
    target = jnp.where(owner >= 0, entry * per_owner + arrival, 0)
    table[...] = jnp.zeros_like(table)
    for row, column in enumerate((target, kept)):
        table[row : row + 1, :] = jnp.sum(jnp.where(diagonal, column, 0), axis=0, keepdims=True)


def odd_index(axis):
    return lax.axis_index(axis) % 2 == 1


def sides(far, close, axis):
    odd = odd_index(axis)
    far, close = far.astype(jnp.float32), close.astype(jnp.float32)
    return jnp.where(odd, close, far), jnp.where(odd, far, close)


def split_sides(low, high, axis):
    odd = odd_index(axis)
    return jnp.where(odd, high, low), jnp.where(odd, low, high)


def lat_smooth_kernel(far, close, own_part, smoothed, to_far, to_close, halos):
    tiles = smoothed.shape[0]
    height, levels, width = own_part.shape
    per_tile = height // tiles
    halos[0], halos[1] = sides(far[...], close[...], "lat")
    for tile in range(tiles):
        rows = range(tile * per_tile, (tile + 1) * per_tile)
        rows = [lat_rims(row, own_part[row], halos, height) for row in rows]
        turned = jnp.transpose(jnp.concatenate(rows, axis=0))
        smoothed[tile] = turned
        to_far[tile], to_close[tile] = split_sides(turned[0:REACH], turned[width - REACH : width], "lon")


def block_place(plan, position, groups, per_tile, width):
    block = plan[0, position]
    row = block // groups
    start = (row // per_tile) * width + (block % groups) * BLOCK_COLS
    return pl.multiple_of(start, BLOCK_COLS), row % per_tile


def take_blocks(plan, profile, picked, first, count, per_tile, width):
    groups = width // BLOCK_COLS
    lane_row = lax.broadcasted_iota(jnp.int32, (BLOCK_COLS, LANES), 1) // (LANES // per_tile)
    for k in range(count):
        start, sub = block_place(plan, first + k, groups, per_tile, width)
        block = profile[pl.ds(start, BLOCK_COLS), :]
        picked[k * BLOCK_COLS : (k + 1) * BLOCK_COLS, :] = jnp.where(lane_row == sub, block, 0.0)


def land_blocks(plan, field, sens, first, count, per_tile, width):
    groups = width // BLOCK_COLS
    lane_row = lax.broadcasted_iota(jnp.int32, (BLOCK_COLS, LANES), 1) // (LANES // per_tile)
    for k in range(first, first + count):
        start, sub = block_place(plan, k, groups, per_tile, width)
        block = sens[k * BLOCK_COLS : (k + 1) * BLOCK_COLS, :]
        field[pl.ds(start, BLOCK_COLS), :] += jnp.where(lane_row == sub, block, 0.0)


def take_observed(plan, table, slabs, observed, first, count):
    channels = observed.shape[1]
    channel = lax.broadcasted_iota(jnp.int32, (BLOCK_COLS, LANES), 1)
    for k in range(count):
        slot = plan[1, first + k]
        at, kept = table[0, slot], table[1, slot]
        slab, start = None, 0
        for ref in slabs:
            size = ref.shape[0]
            found = ref[jnp.clip(at - start, 0, size - 1)].astype(jnp.float32)
            slab = found if slab is None else jnp.where(at >= start, found, slab)
            start += size
        for h in range(channels // LANES):
            part = slab[h * BLOCK_COLS : (h + 1) * BLOCK_COLS]
            part = jnp.where(channel + h * LANES < kept, part, jnp.inf)
            observed[k * BLOCK_COLS : (k + 1) * BLOCK_COLS, h * LANES : (h + 1) * LANES] = part


def dot(a, b):
    return jnp.dot(a, b, preferred_element_type=jnp.float32)


def dot_t(a, b):
    return lax.dot_general(a, b, (((1,), (1,)), ((), ())), preferred_element_type=jnp.float32)


def net_first(picked, weights, act_one):
    inputs = picked[...].astype(jnp.bfloat16)
    act_one[...] = jnp.tanh(dot(inputs, weights[0][...]) + weights[3][...]).astype(jnp.bfloat16)


def net_rest(weights, states):
    _, weight_two, weight_out, _, bias_two, bias_out = weights
    act_one, act_two, emitted = states
    act_two[...] = jnp.tanh(dot(act_one[...], weight_two[...]) + bias_two[...]).astype(jnp.bfloat16)
    emitted[...] = dot(act_two[...], weight_out[...]) + bias_out[...]


def net_forward(picked, weights, states):
    net_first(picked, weights, states[0])
    net_rest(weights, states)


def net_backward(observed, states, weights):
    wide_in, weight_two, weight_out = weights[:3]
    act_one, act_two, emitted = states
    seen = observed[...]
    misfit = jnp.where(seen < jnp.inf, emitted[...] - seen, 0.0).astype(jnp.bfloat16)
    two = act_two[...].astype(jnp.float32)
    grad_two = (dot_t(misfit, weight_out[...]) * (1.0 - two * two)).astype(jnp.bfloat16)
    one = act_one[...].astype(jnp.float32)
    grad_one = (dot_t(grad_two, weight_two[...]) * (1.0 - one * one)).astype(jnp.bfloat16)
    return rounded(dot_t(grad_one, wide_in[...]))


def inner_forward_kernel(per_tile, outer_slots, plan, own, turned, taps, *refs):
    (in_weight, in_bias, mid_weight, mid_bias, out_weight, out_bias), refs = refs[:6], refs[6:]
    profile, states, weights, (rows, padded, picked, sems) = refs[0], refs[1:4], refs[4:10], refs[10:]
    wide_in, weight_two, weight_out, bias_one, bias_two, bias_out = weights
    tiles, width, _ = own.shape
    levels = in_weight.shape[0]
    count = picked.shape[0] // BLOCK_COLS
    piece = mid_weight.shape[0] // WEIGHT_PIECES
    pieces = [pl.ds(k * piece, piece) for k in range(WEIGHT_PIECES)]
    loads = [(plan, rows), (in_bias, bias_one)]
    loads += [(in_weight, wide_in.at[pl.ds(sub * levels, levels)]) for sub in range(per_tile)]
    early = len(loads)
    loads += [(mid_weight.at[part], weight_two.at[part]) for part in pieces] + [(mid_bias, bias_two)]
    loads += [(out_weight, weight_out), (out_bias, bias_out)]
    loads = [
        pltpu.make_async_copy(source, target, sems.at[k]) for k, (source, target) in enumerate(loads)
    ]
    for move in loads:
        move.start()
    zeros = jnp.zeros((tiles, REACH, LANES), jnp.float32)
    padded[:, 0:REACH, :] = zeros
    padded[:, REACH : REACH + width, :] = own[...]
    padded[:, REACH + width :, :] = zeros
    for tile in range(tiles):
        total = turned[tile] + lon_conv(padded, taps, tile, 0, width)
        profile[tile * width : (tile + 1) * width, :] = rounded(total)
    for move in loads[:early]:
        move.wait()
    take_blocks(rows, profile, picked, outer_slots, count, per_tile, width)
    act_one, act_two, emitted = states
    net_first(picked, weights, act_one)
    for move in loads[early:]:
        move.wait()

    @pl.when(rows[2, 0] <= outer_slots)
    def _():
        net_rest(weights, states)


def outer_forward_kernel(
    per_tile,
    plan,
    far,
    close,
    own,
    turned,
    taps,
    inner_profile,
    *refs,
):
    weights, states, late_states, (rows, padded, profile, picked, late_picked, sem) = (
        refs[:6],
        refs[6:9],
        refs[9:12],
        refs[12:],
    )
    tiles, width, _ = own.shape
    outer_slots = picked.shape[0] // BLOCK_COLS
    late_slots = late_picked.shape[0] // BLOCK_COLS
    plan_in = pltpu.make_async_copy(plan, rows, sem)
    plan_in.start()
    fill_padded(padded, far, own, close)
    profile[...] = inner_profile[...]
    for tile in range(tiles):
        for start in (0, width - REACH):
            total = turned[tile, start : start + REACH, :] + lon_conv(padded, taps, tile, start, REACH)
            profile[tile * width + start : tile * width + start + REACH, :] = rounded(total)
    plan_in.wait()
    take_blocks(rows, profile, picked, 0, outer_slots, per_tile, width)
    net_forward(picked, weights, states)

    @pl.when(rows[2, 0] > outer_slots)
    def _():
        take_blocks(rows, profile, late_picked, outer_slots, late_slots, per_tile, width)
        net_forward(late_picked, weights, late_states)


def outer_backward_kernel(per_tile, parts, recv_most, plan, *refs):
    slabs, refs = refs[:parts], refs[parts:]
    weights, states, late_states, refs = refs[:3], refs[3:6], refs[6:9], refs[9:]
    (table_rows, sens, to_far, to_close) = refs[:4]
    (rows, table, observed, late_observed, field, sems) = refs[4:]
    tiles = to_far.shape[0]
    width = field.shape[0] // tiles
    outer_slots = observed.shape[0] // BLOCK_COLS
    late_slots = late_observed.shape[0] // BLOCK_COLS

    plan_in = pltpu.make_async_copy(plan, rows, sems.at[0])
    plan_in.start()
    routing(recv_most, outer_slots + late_slots, slabs, table_rows)
    table_in = pltpu.make_async_copy(table_rows, table, sems.at[1])
    table_in.start()
    field[...] = jnp.zeros_like(field)
    plan_in.wait()
    table_in.wait()

    take_observed(rows, table, slabs, observed, 0, outer_slots)
    sens[0 : outer_slots * BLOCK_COLS, :] = net_backward(observed, states, weights)
    land_blocks(rows, field, sens, 0, outer_slots, per_tile, width)

    @pl.when(rows[2, 0] > outer_slots)
    def _():
        take_observed(rows, table, slabs, late_observed, outer_slots, late_slots)
        sens[outer_slots * BLOCK_COLS :, :] = net_backward(late_observed, late_states, weights)
        land_blocks(rows, field, sens, outer_slots, late_slots, per_tile, width)

    for tile in range(tiles):
        low = field[tile * width : tile * width + REACH, :]
        high = field[(tile + 1) * width - REACH : (tile + 1) * width, :]
        low, high = split_sides(low, high, "lon")
        to_far[tile], to_close[tile] = low.astype(jnp.bfloat16), high.astype(jnp.bfloat16)


def inner_backward_kernel(per_tile, parts, outer_slots, plan, table_rows, sens, *refs):
    slabs, refs = refs[:parts], refs[parts:]
    weights, states, refs = refs[:3], refs[3:6], refs[6:]
    landing, rows, table, observed, inner, field, sems = refs
    tiles, width, _ = landing.shape
    late_slots = observed.shape[0] // BLOCK_COLS
    split = outer_slots * BLOCK_COLS
    moves = [
        pltpu.make_async_copy(plan, rows, sems.at[0]),
        pltpu.make_async_copy(table_rows, table, sems.at[1]),
    ]
    for move in moves:
        move.start()
    field[...] = jnp.zeros_like(field)
    inner[...] = sens[...]
    for move in moves:
        move.wait()

    @pl.when(rows[2, 0] <= outer_slots)
    def _():
        take_observed(rows, table, slabs, observed, outer_slots, late_slots)
        inner[split:, :] = net_backward(observed, states, weights)

    land_blocks(rows, field, inner, 0, outer_slots + late_slots, per_tile, width)
    for tile in range(tiles):
        landing[tile] = field[tile * width : (tile + 1) * width, :]


def lon_back_kernel(far, close, own, taps, back, to_far, to_close, padded):
    tiles, width, _ = own.shape
    height, levels, _ = back.shape
    per_tile = height // tiles
    fill_padded(padded, far, own, close)
    for tile in range(tiles):
        rows = jnp.transpose(lon_conv(padded, taps, tile, 0, width))
        rows = rows.reshape(per_tile, levels, width)
        back[tile * per_tile : (tile + 1) * per_tile] = rows
    halve_for_sides(back, height, to_far, to_close)


def own_back_kernel(back, control, own_part, held, sem):
    control_in = pltpu.make_async_copy(control, held, sem)
    control_in.start()
    control_in.wait()
    height = back.shape[0]
    for row in range(height):
        own_part[row] = lat_sum(back, row, 0, height, held[row])


def lat_back_kernel(far, close, own_part, gradient, halos):
    halos[0], halos[1] = sides(far[...], close[...], "lat")
    height = own_part.shape[0]
    for row in range(height):
        gradient[row] = lat_rims(row, own_part[row], halos, height)


def exchange(to_far, to_close, axis, periodic):
    count = lax.axis_size(axis)
    far = []
    for odd in range(1, count, 2):
        if odd + 1 < count or periodic:
            far += [(odd, (odd + 1) % count), ((odd + 1) % count, odd)]
    close = [(i, i ^ 1) for i in range(count)]
    to_close, _ = lax.optimization_barrier((to_close, to_far))
    from_far, from_close = lax.ppermute(to_far, axis, far), lax.ppermute(to_close, axis, close)
    from_far = lax.optimization_barrier(from_far)
    from_close, _ = lax.optimization_barrier((from_close, from_far))
    return from_far, from_close, to_close


def shards(
    control,
    background,
    lon_width,
    block_cells,
    block_owner,
    channel_count,
    radiance,
    in_weight,
    in_bias,
    mid_weight,
    mid_bias,
    out_weight,
    out_bias,
):
    height, levels, width = control.shape
    hidden = mid_weight.shape[0]
    channels, columns = radiance.shape
    slot_count = block_owner.shape[0]
    recv_most = channel_count.shape[0]
    per_tile = LANES // levels
    tiles = height // per_tile
    slab_rows = BLOCK_COLS * channels // LANES
    f32, bf16, i32 = jnp.float32, jnp.bfloat16, jnp.int32
    shape = jax.ShapeDtypeStruct
    field = height * levels * width
    conv_flops = 2 * 33 * field

    halves = channels // LANES
    radiance = radiance.T.reshape(recv_most, BLOCK_COLS, halves, LANES)
    radiance = jnp.swapaxes(radiance, 1, 2).reshape(recv_most, slab_rows, LANES)
    half_field = shape(control.shape, bf16)
    slabs, to_far, to_close = call(
        first_kernel,
        (shape((recv_most + 1, slab_rows, LANES), bf16), half_field, half_field),
        [HBM] * 4,
        (HBM, VMEM, VMEM),
        0,
        16 * field,
        scratch=(
            pltpu.VMEM((1, slot_count), i32),
            pltpu.VMEM((1, recv_most), i32),
            pltpu.VMEM((slab_rows, LANES), f32),
            pltpu.VMEM((slab_rows, LANES), bf16),
            pltpu.VMEM(control.shape, f32),
            pltpu.SemaphoreType.DMA((5,)),
        ),
        name="slabs_halves",
    )(*pinned(radiance, block_owner.reshape(1, slot_count), channel_count.reshape(1, recv_most), control))
    far, close, sent = exchange(to_far, to_close, "lat", False)

    band = pltpu.VMEM((height, levels, width), f32)
    taps, turned, plan, own_part = call(
        prepare_kernel,
        (
            shape((tiles, 24, LANES), f32),
            shape((tiles, width, LANES), f32),
            shape((8, LANES), i32),
            shape(control.shape, f32),
        ),
        [HBM] * 5,
        (VMEM,) * 4,
        conv_flops // 2,
        12 * field,
        scratch=(
            pltpu.SMEM((height,), i32),
            pltpu.VMEM((1, slot_count), i32),
            pltpu.VMEM((1, slot_count), i32),
            band,
            band,
            pltpu.SemaphoreType.DMA((5,)),
        ),
        name="taps_background",
    )(
        *pinned(
            lon_width,
            background,
            block_cells.reshape(1, slot_count),
            block_owner.reshape(1, slot_count),
            control,
        )
    )

    lat_count = lax.axis_size("lat")
    one, two, *others = swap_bits(lat_count)

    def swapped(part, apart):
        return lax.ppermute(part, "lat", [(i, i ^ apart) for i in range(lat_count)])

    slabs, _ = lax.optimization_barrier((slabs, sent))
    near = [slabs] + [swapped(slabs, apart) for apart in (1 << one, 1 << two, (1 << one) + (1 << two))]

    halos = pltpu.VMEM((2, REACH, levels, width), f32)
    smoothed, to_far, to_close = call(
        lat_smooth_kernel,
        (shape((tiles, width, LANES), f32),) + (shape((tiles, REACH, LANES), f32),) * 2,
        [VMEM] * 3,
        (VMEM,) * 3,
        conv_flops,
        16 * field,
        scratch=(halos,),
        name="lat_smooth",
    )(far, close, own_part)
    far, close, sent = exchange(to_far, to_close, "lon", True)
    outer_slots = 3 * slot_count // 8
    late_slots = slot_count - outer_slots
    x_rows = slot_count * BLOCK_COLS
    outer_rows, late_rows = outer_slots * BLOCK_COLS, late_slots * BLOCK_COLS
    row_flops = 2 * hidden * (LANES + hidden + channels)
    def state_shapes(rows):
        return (shape((rows, hidden), bf16), shape((rows, hidden), bf16), shape((rows, channels), f32))

    plan_rows = pltpu.SMEM((8, LANES), i32)
    padded = pltpu.VMEM((tiles, width + 2 * REACH, LANES), f32)
    flat = pltpu.VMEM((tiles * width, LANES), f32)

    profile, *rest = call(
        functools.partial(inner_forward_kernel, per_tile, outer_slots),
        (shape((tiles * width, LANES), f32),)
        + state_shapes(late_rows)
        + (
            shape((LANES, hidden), bf16),
            shape((hidden, hidden), bf16),
            shape((hidden, channels), bf16),
            shape((1, hidden), f32),
            shape((1, hidden), f32),
            shape((1, channels), f32),
        ),
        [ANY] + [VMEM] * 3 + [HBM] * 6,
        (VMEM,) * 10,
        late_rows * row_flops,
        4 * 1024 * 1024,
        scratch=(
            plan_rows,
            padded,
            pltpu.VMEM((late_rows, LANES), f32),
            pltpu.SemaphoreType.DMA((5 + per_tile + WEIGHT_PIECES,)),
        ),
        name="inner_forward",
    )(
        plan,
        smoothed,
        turned,
        taps,
        *pinned(
            in_weight,
            in_bias.reshape(1, hidden),
            mid_weight,
            mid_bias.reshape(1, hidden),
            out_weight,
            out_bias.reshape(1, channels),
        ),
    )
    inner_states, weights = rest[:3], rest[3:]
    *near, far, close, profile = lax.optimization_barrier((*near, far, close, profile))
    for bit in others:
        near = [jnp.concatenate(near, axis=0)]
        near.append(swapped(near[0], 1 << bit))
    near = [jnp.concatenate(near[:-1], axis=0), near[-1]]
    across = [swapped(part, 1) for part in near]

    states = call(
        functools.partial(outer_forward_kernel, per_tile),
        state_shapes(outer_rows) + state_shapes(late_rows),
        [ANY] + [VMEM] * 12,
        (VMEM,) * 6,
        outer_rows * row_flops,
        4 * 1024 * 1024,
        scratch=(
            plan_rows,
            padded,
            flat,
            pltpu.VMEM((outer_rows, LANES), f32),
            pltpu.VMEM((late_rows, LANES), f32),
            pltpu.SemaphoreType.DMA,
        ),
        name="outer_forward",
    )(plan, far, close, smoothed, turned, taps, profile, *weights)

    slabs = [*near, *across]
    table, sens, to_far, to_close = call(
        functools.partial(outer_backward_kernel, per_tile, len(slabs), recv_most),
        (
            shape((8, LANES), i32),
            shape((x_rows, LANES), f32),
            shape((tiles, REACH, LANES), bf16),
            shape((tiles, REACH, LANES), bf16),
        ),
        [ANY] + [VMEM] * (len(slabs) + 9),
        (VMEM,) * 4,
        outer_rows * row_flops,
        4 * 1024 * 1024,
        scratch=(
            plan_rows,
            pltpu.SMEM((8, LANES), i32),
            pltpu.VMEM((outer_rows, channels), f32),
            pltpu.VMEM((late_rows, channels), f32),
            flat,
            pltpu.SemaphoreType.DMA((2,)),
        ),
        name="outer_backward",
    )(plan, *slabs, *weights[:3], *states)
    far, close, sent = exchange(to_far, to_close, "lon", True)

    landing = call(
        functools.partial(inner_backward_kernel, per_tile, len(slabs), outer_slots),
        shape((tiles, width, LANES), f32),
        [ANY, ANY] + [VMEM] * (len(slabs) + 7),
        VMEM,
        late_rows * row_flops,
        4 * 1024 * 1024,
        scratch=(
            plan_rows,
            pltpu.SMEM((8, LANES), i32),
            pltpu.VMEM((late_rows, channels), f32),
            pltpu.VMEM((x_rows, LANES), f32),
            flat,
            pltpu.SemaphoreType.DMA((2,)),
        ),
        name="inner_backward",
    )(plan, table, sens, *slabs, *weights[:3], *inner_states)

    back, to_far, to_close = call(
        lon_back_kernel,
        (shape((height, levels, width), f32), half_field, half_field),
        [VMEM] * 4,
        (VMEM,) * 3,
        conv_flops,
        8 * field,
        scratch=(pltpu.VMEM((tiles, width + 2 * REACH, LANES), f32),),
        name="lon_back",
    )(far, close, landing, taps)
    far, close, sent = exchange(to_far, to_close, "lat", False)
    own_part = call(
        own_back_kernel,
        shape((height, levels, width), f32),
        [VMEM, HBM],
        VMEM,
        conv_flops // 2,
        12 * field,
        scratch=(band, pltpu.SemaphoreType.DMA),
        name="lat_back_own",
    )(back, *pinned(control))

    return call(
        lat_back_kernel,
        shape((height, levels, width), f32),
        [VMEM] * 3,
        VMEM,
        conv_flops // 2,
        16 * field,
        scratch=(halos,),
        name="lat_back",
    )(far, close, own_part)


def solution(mesh):
    return jax.shard_map(
        shards,
        mesh=mesh,
        in_specs=(
            P("lat", None, "lon"),
            P("lat", None, "lon"),
            P("lat"),
            P("lat", "lon"),
            P("lat", "lon"),
            P("lat", "lon"),
            P("lat", "lon"),
            P(),
            P(),
            P(),
            P(),
            P(),
            P(),
        ),
        out_specs=P("lat", None, "lon"),
        check_vma=False,
    )
```

```python
import functools

import jax
import jax.numpy as jnp
import numpy as np
from jax import lax
from jax.experimental import pallas as pl
from jax.experimental.pallas import tpu as pltpu
from jax.sharding import PartitionSpec as P

REACH = 16
BLOCK_COLS = 8
LANES = 128
LAT_SIGMA = 8.0
WEIGHT_PIECES = 4
BAND_PIECES = 4
SWAP_COVER = 10
VMEM_BYTES = 40 * 1024 * 1024

VMEM = pl.BlockSpec(memory_space=pltpu.VMEM)
SMEM = pl.BlockSpec(memory_space=pltpu.SMEM)
HBM = pl.BlockSpec(memory_space=pltpu.HBM)
ANY = pl.BlockSpec(memory_space=pl.ANY)


def lat_taps():
    offsets = np.arange(-REACH, REACH + 1, dtype=np.float64)
    raw = np.exp(-offsets * offsets / (2.0 * LAT_SIGMA * LAT_SIGMA))
    return [float(v) for v in (raw / np.sqrt(np.sum(raw * raw))).astype(np.float32)]


def call(kernel, out_shape, in_specs, out_specs, flops, bytes_moved, scratch=(), name=None):
    return pl.pallas_call(
        kernel,
        out_shape=out_shape,
        in_specs=in_specs,
        out_specs=out_specs,
        scratch_shapes=list(scratch),
        compiler_params=pltpu.CompilerParams(vmem_limit_bytes=VMEM_BYTES),
        cost_estimate=pl.CostEstimate(flops=flops, bytes_accessed=bytes_moved, transcendentals=0),
        name=name,
    )


def pinned(*values):
    return [pltpu.with_memory_space_constraint(value, pltpu.HBM) for value in values]


def lat_sum(parts, row, first, height, start=None):
    taps = lat_taps()
    acc = start
    for k in range(height):
        j = first + k - row
        if abs(j) <= REACH:
            term = taps[j + REACH] * parts[k]
            acc = term if acc is None else acc + term
    return acc


def lat_rims(row, part, halos, height):
    low = lat_sum(halos.at[0], row, -REACH, REACH, part)
    return lat_sum(halos.at[1], row, height, REACH, low)


def fill_padded(padded, far, own, close):
    width = own.shape[1]
    low, high = sides(far[...], close[...], "lon")
    padded[:, 0:REACH, :] = low
    padded[:, REACH : REACH + width, :] = own[...]
    padded[:, REACH + width :, :] = high


def lon_conv(padded, taps, tile, start, width):
    middle = REACH + start
    acc = taps[tile, 0:1, :] * padded[tile, pl.ds(middle, width), :]
    for j in range(1, REACH + 1):
        both = padded[tile, pl.ds(middle + j, width), :] + padded[tile, pl.ds(middle - j, width), :]
        acc = acc + taps[tile, j : j + 1, :] * both
    return acc


def rounded(value):
    return value.astype(jnp.bfloat16).astype(jnp.float32)


def halved_rows(rows, order):
    halves, carry = {}, None
    for row in order:
        value = rows[row] if carry is None else rows[row] + carry
        halves[row] = value.astype(jnp.bfloat16)
        carry = value - halves[row].astype(jnp.float32)
    return [halves[row] for row in sorted(halves)]


def halve_for_sides(rows, height, to_far, to_close):
    odd = odd_index("lat")
    upward = halved_rows(rows, range(height - 1, -1, -1))
    downward = halved_rows(rows, range(height))
    for row in range(height):
        to_far[row] = jnp.where(odd, upward[row], downward[row])
        to_close[row] = jnp.where(odd, downward[row], upward[row])


def first_kernel(
    radiance, block_owner, channel_count, control, slabs, to_far, to_close, owners, counts, rows, tables, held, sems
):
    recv_most = radiance.shape[0]
    moves = [
        pltpu.make_async_copy(radiance, slabs.at[pl.ds(0, recv_most)], sems.at[0]),
        pltpu.make_async_copy(block_owner, owners, sems.at[1]),
        pltpu.make_async_copy(channel_count, counts, sems.at[2]),
    ]
    piece = control.shape[0] // BAND_PIECES
    for k in range(BAND_PIECES):
        part = pl.ds(k * piece, piece)
        moves.append(pltpu.make_async_copy(control.at[part], held.at[part], sems.at[4 + k]))
    for move in moves[3:] + moves[:3]:
        move.start()
    rows[...] = jnp.full(rows.shape, -1.0, jnp.float32)
    moves[1].wait()
    moves[2].wait()
    rows[0:1, 0 : owners.shape[1]] = owners[...].astype(jnp.float32)
    rows[1:2, 0 : counts.shape[1]] = counts[...].astype(jnp.float32)
    tables[...] = rows[...].astype(jnp.bfloat16)
    last = pltpu.make_async_copy(tables, slabs.at[recv_most], sems.at[3])
    last.start()
    for move in moves[3:]:
        move.wait()
    halve_for_sides(held, held.shape[0], to_far, to_close)
    moves[0].wait()
    last.wait()


def prepare_kernel(
    lon_width,
    background,
    block_cells,
    block_owner,
    control,
    taps,
    turned,
    plan,
    own_part,
    widths,
    cells,
    owners,
    field,
    band,
    sems,
):
    moves = [
        pltpu.make_async_copy(lon_width, widths, sems.at[0]),
        pltpu.make_async_copy(block_cells, cells, sems.at[1]),
        pltpu.make_async_copy(block_owner, owners, sems.at[2]),
        pltpu.make_async_copy(background, field, sems.at[3]),
        pltpu.make_async_copy(control, band, sems.at[4]),
    ]
    tiles = turned.shape[0]
    height, levels, width = background.shape
    per_tile = height // tiles
    for move in moves:
        move.start()
    groups = width // BLOCK_COLS
    rim = REACH // BLOCK_COLS
    slot_count = cells.shape[1]

    lane_row = lax.broadcasted_iota(jnp.int32, (1, LANES), 1) // levels
    steps = lax.broadcasted_iota(jnp.int32, (taps.shape[1], LANES), 0)
    dist = steps.astype(jnp.float32)
    weight = jnp.where(steps == 0, 1.0, jnp.where(steps <= REACH, 2.0, 0.0))
    moves[0].wait()
    for tile in range(tiles):
        spread = jnp.zeros((1, LANES), jnp.int32)
        for sub in range(per_tile):
            spread = jnp.where(lane_row == sub, widths[tile * per_tile + sub], spread)
        spread = spread.astype(jnp.float32)
        raw = jnp.exp(-dist * dist / (2.0 * spread * spread))
        norm = jnp.sum(weight * raw * raw, axis=0, keepdims=True)
        taps[tile] = raw / jnp.sqrt(norm)

    moves[1].wait()
    moves[2].wait()
    rows = lax.broadcasted_iota(jnp.int32, (slot_count, slot_count), 0)
    lanes = lax.broadcasted_iota(jnp.int32, (slot_count, slot_count), 1)
    group = cells[...] % groups
    outer = ((group < rim) | (group >= groups - rim)) & (owners[...] >= 0)
    outer_here = jnp.where(outer, 1, 0)
    outer_count = jnp.sum(outer_here, axis=1, keepdims=True)
    earlier = jnp.sum(jnp.where(lanes < rows, outer_here, 0), axis=1, keepdims=True)
    here = jnp.sum(jnp.where(lanes == rows, outer_here, 0), axis=1, keepdims=True)
    cell = jnp.sum(jnp.where(lanes == rows, cells[...], 0), axis=1, keepdims=True)
    position = jnp.where(here == 1, earlier, outer_count + rows[:, 0:1] - earlier)
    at = lax.broadcasted_iota(jnp.int32, (slot_count, LANES), 1)
    hit = position == at
    slot = lax.broadcasted_iota(jnp.int32, (slot_count, LANES), 0)
    plan[...] = jnp.zeros_like(plan)
    plan[0:1, :] = jnp.sum(jnp.where(hit, cell, 0), axis=0, keepdims=True)
    plan[1:2, :] = jnp.sum(jnp.where(hit, slot, 0), axis=0, keepdims=True)
    plan[2:3, :] = jnp.broadcast_to(outer_count, (1, LANES))

    moves[3].wait()
    for tile in range(tiles):
        block = field[tile * per_tile : (tile + 1) * per_tile].reshape(per_tile * levels, width)
        turned[tile] = jnp.transpose(block)
    moves[4].wait()
    for row in range(height):
        own_part[row] = lat_sum(band, row, 0, height)


def swap_bits(count):
    return list(range(count.bit_length() - 2, 0, -1))


def routing(recv_most, slot_count, slabs, table):
    per_owner = recv_most + 1
    spans, count = [], 0
    for ref in slabs:
        spans.append((ref, count))
        count += ref.shape[0] // per_owner
    half = count // 2
    here = lax.axis_index("lat")
    rows = lax.broadcasted_iota(jnp.int32, (slot_count, LANES), 0)
    lanes = lax.broadcasted_iota(jnp.int32, (slot_count, LANES), 1)
    diagonal = rows == lanes
    zero = jnp.zeros((slot_count, LANES), jnp.int32)

    bits = swap_bits(count)

    def device_of(k):
        apart = jnp.where(k < half, 0, 1)
        for place, bit in enumerate(bits):
            apart = apart + (((k >> place) & 1) << bit)
        return here ^ apart

    def over_sets(step):
        acc = zero
        for ref, first in spans:

            def add(k, acc, ref=ref, first=first):
                lines = ref[k * per_owner + recv_most].astype(jnp.float32)
                owners, counts = lines[0:1].astype(jnp.int32), lines[1:2].astype(jnp.int32)
                return acc + step(device_of(first + k), owners, counts)

            acc = lax.fori_loop(0, ref.shape[0] // per_owner, add, acc, unroll=count <= 8)
        return jnp.sum(acc, axis=1, keepdims=True)

    mine = slabs[0][recv_most].astype(jnp.float32)[0:1].astype(jnp.int32)
    owner = jnp.sum(jnp.where(diagonal, mine, 0), axis=1, keepdims=True)

    def rank(device, owners, counts):
        before = (device < here) | ((device == here) & (lanes < rows))
        return jnp.where((owners == owner) & before, 1, 0)

    arrival = over_sets(rank)

    def counted(device, owners, counts):
        return jnp.where((owner == device) & (lanes == arrival), counts, 0)

    kept = over_sets(counted)
    apart = owner ^ here
    entry = (apart & 1) * half
    for place, bit in enumerate(bits):
        entry = entry + (((apart >> bit) & 1) << place)
    target = jnp.where(owner >= 0, entry * per_owner + arrival, 0)
    table[...] = jnp.zeros_like(table)
    for row, column in enumerate((target, kept)):
        table[row : row + 1, :] = jnp.sum(jnp.where(diagonal, column, 0), axis=0, keepdims=True)


def odd_index(axis):
    return lax.axis_index(axis) % 2 == 1


def sides(far, close, axis):
    odd = odd_index(axis)
    far, close = far.astype(jnp.float32), close.astype(jnp.float32)
    return jnp.where(odd, close, far), jnp.where(odd, far, close)


def split_sides(low, high, axis):
    odd = odd_index(axis)
    return jnp.where(odd, high, low), jnp.where(odd, low, high)


def lat_smooth_kernel(far, close, own_part, smoothed, to_far, to_close, halos):
    tiles = smoothed.shape[0]
    height, levels, width = own_part.shape
    per_tile = height // tiles
    halos[0], halos[1] = sides(far[...], close[...], "lat")
    for tile in range(tiles):
        rows = range(tile * per_tile, (tile + 1) * per_tile)
        rows = [lat_rims(row, own_part[row], halos, height) for row in rows]
        turned = jnp.transpose(jnp.concatenate(rows, axis=0))
        smoothed[tile] = turned
        to_far[tile], to_close[tile] = split_sides(turned[0:REACH], turned[width - REACH : width], "lon")


def block_place(plan, position, groups, per_tile, width):
    block = plan[0, position]
    row = block // groups
    start = (row // per_tile) * width + (block % groups) * BLOCK_COLS
    return pl.multiple_of(start, BLOCK_COLS), row % per_tile


def take_blocks(plan, profile, picked, first, count, per_tile, width):
    groups = width // BLOCK_COLS
    lane_row = lax.broadcasted_iota(jnp.int32, (BLOCK_COLS, LANES), 1) // (LANES // per_tile)
    for k in range(count):
        start, sub = block_place(plan, first + k, groups, per_tile, width)
        block = profile[pl.ds(start, BLOCK_COLS), :]
        picked[k * BLOCK_COLS : (k + 1) * BLOCK_COLS, :] = jnp.where(lane_row == sub, block, 0.0)


def land_blocks(plan, field, sens, first, count, per_tile, width):
    groups = width // BLOCK_COLS
    lane_row = lax.broadcasted_iota(jnp.int32, (BLOCK_COLS, LANES), 1) // (LANES // per_tile)
    for k in range(first, first + count):
        start, sub = block_place(plan, k, groups, per_tile, width)
        block = sens[k * BLOCK_COLS : (k + 1) * BLOCK_COLS, :]
        field[pl.ds(start, BLOCK_COLS), :] += jnp.where(lane_row == sub, block, 0.0)


def take_observed(plan, table, slabs, observed, first, count):
    channels = observed.shape[1]
    channel = lax.broadcasted_iota(jnp.int32, (BLOCK_COLS, LANES), 1)
    for k in range(count):
        slot = plan[1, first + k]
        at, kept = table[0, slot], table[1, slot]
        slab, start = None, 0
        for ref in slabs:
            size = ref.shape[0]
            found = ref[jnp.clip(at - start, 0, size - 1)].astype(jnp.float32)
            slab = found if slab is None else jnp.where(at >= start, found, slab)
            start += size
        for h in range(channels // LANES):
            part = slab[h * BLOCK_COLS : (h + 1) * BLOCK_COLS]
            part = jnp.where(channel + h * LANES < kept, part, jnp.inf)
            observed[k * BLOCK_COLS : (k + 1) * BLOCK_COLS, h * LANES : (h + 1) * LANES] = part


def dot(a, b):
    return jnp.dot(a, b, preferred_element_type=jnp.float32)


def dot_t(a, b):
    return lax.dot_general(a, b, (((1,), (1,)), ((), ())), preferred_element_type=jnp.float32)


def net_first(picked, weights, act_one):
    inputs = picked[...].astype(jnp.bfloat16)
    act_one[...] = jnp.tanh(dot(inputs, weights[0][...]) + weights[3][...]).astype(jnp.bfloat16)


def net_rest(weights, states):
    _, weight_two, weight_out, _, bias_two, bias_out = weights
    act_one, act_two, emitted = states
    act_two[...] = jnp.tanh(dot(act_one[...], weight_two[...]) + bias_two[...]).astype(jnp.bfloat16)
    emitted[...] = dot(act_two[...], weight_out[...]) + bias_out[...]


def net_forward(picked, weights, states):
    net_first(picked, weights, states[0])
    net_rest(weights, states)


def slopes(states, slope_one, slope_two):
    for act, slope in zip(states, (slope_one, slope_two)):
        value = act[...].astype(jnp.float32)
        slope[...] = 1.0 - value * value


def net_backward(observed, emitted, slope_one, slope_two, weights):
    wide_in, weight_two, weight_out = weights[:3]
    seen = observed[...]
    misfit = jnp.where(seen < jnp.inf, emitted[...] - seen, 0.0).astype(jnp.bfloat16)
    grad_two = (dot_t(misfit, weight_out[...]) * slope_two[...]).astype(jnp.bfloat16)
    grad_one = (dot_t(grad_two, weight_two[...]) * slope_one[...]).astype(jnp.bfloat16)
    return rounded(dot_t(grad_one, wide_in[...]))


def inner_forward_kernel(per_tile, outer_slots, plan, own, turned, taps, *refs):
    (in_weight, in_bias, mid_weight, mid_bias, out_weight, out_bias), refs = refs[:6], refs[6:]
    profile, states, weights, (rows, padded, picked, sems) = refs[0], refs[1:4], refs[4:10], refs[10:]
    wide_in, weight_two, weight_out, bias_one, bias_two, bias_out = weights
    tiles, width, _ = own.shape
    levels = in_weight.shape[0]
    count = picked.shape[0] // BLOCK_COLS
    piece = mid_weight.shape[0] // WEIGHT_PIECES
    pieces = [pl.ds(k * piece, piece) for k in range(WEIGHT_PIECES)]
    loads = [(plan, rows), (in_bias, bias_one)]
    loads += [(in_weight, wide_in.at[pl.ds(sub * levels, levels)]) for sub in range(per_tile)]
    early = len(loads)
    loads += [(mid_weight.at[part], weight_two.at[part]) for part in pieces] + [(mid_bias, bias_two)]
    loads += [(out_weight, weight_out), (out_bias, bias_out)]
    loads = [
        pltpu.make_async_copy(source, target, sems.at[k]) for k, (source, target) in enumerate(loads)
    ]
    for move in loads:
        move.start()
    zeros = jnp.zeros((tiles, REACH, LANES), jnp.float32)
    padded[:, 0:REACH, :] = zeros
    padded[:, REACH : REACH + width, :] = own[...]
    padded[:, REACH + width :, :] = zeros
    for tile in range(tiles):
        total = turned[tile] + lon_conv(padded, taps, tile, 0, width)
        profile[tile * width : (tile + 1) * width, :] = rounded(total)
    for move in loads[:early]:
        move.wait()
    take_blocks(rows, profile, picked, outer_slots, count, per_tile, width)
    act_one, act_two, emitted = states
    net_first(picked, weights, act_one)
    for move in loads[early:]:
        move.wait()

    @pl.when(rows[2, 0] <= outer_slots)
    def _():
        net_rest(weights, states)


def outer_forward_kernel(
    per_tile,
    plan,
    far,
    close,
    own,
    turned,
    taps,
    inner_profile,
    *refs,
):
    weights, states, late_states, (rows, padded, profile, picked, late_picked, sem) = (
        refs[:6],
        refs[6:9],
        refs[9:12],
        refs[12:],
    )
    tiles, width, _ = own.shape
    outer_slots = picked.shape[0] // BLOCK_COLS
    late_slots = late_picked.shape[0] // BLOCK_COLS
    plan_in = pltpu.make_async_copy(plan, rows, sem)
    plan_in.start()
    fill_padded(padded, far, own, close)
    profile[...] = inner_profile[...]
    for tile in range(tiles):
        for start in (0, width - REACH):
            total = turned[tile, start : start + REACH, :] + lon_conv(padded, taps, tile, start, REACH)
            profile[tile * width + start : tile * width + start + REACH, :] = rounded(total)
    plan_in.wait()
    take_blocks(rows, profile, picked, 0, outer_slots, per_tile, width)
    net_forward(picked, weights, states)

    @pl.when(rows[2, 0] > outer_slots)
    def _():
        take_blocks(rows, profile, late_picked, outer_slots, late_slots, per_tile, width)
        net_forward(late_picked, weights, late_states)


def outer_backward_kernel(per_tile, parts, recv_most, plan, *refs):
    slabs, refs = refs[:parts], refs[parts:]
    weights, states, late_states, refs = refs[:3], refs[3:6], refs[6:9], refs[9:]
    (table_rows, sens, to_far, to_close) = refs[:4]
    (rows, table, observed, late_observed, field, *slope, sems) = refs[4:]
    tiles = to_far.shape[0]
    width = field.shape[0] // tiles
    outer_slots = observed.shape[0] // BLOCK_COLS
    late_slots = late_observed.shape[0] // BLOCK_COLS

    plan_in = pltpu.make_async_copy(plan, rows, sems.at[0])
    plan_in.start()
    routing(recv_most, outer_slots + late_slots, slabs, table_rows)
    table_in = pltpu.make_async_copy(table_rows, table, sems.at[1])
    table_in.start()
    field[...] = jnp.zeros_like(field)
    slopes(states, *slope[:2])
    plan_in.wait()
    table_in.wait()

    take_observed(rows, table, slabs, observed, 0, outer_slots)
    sens[0 : outer_slots * BLOCK_COLS, :] = net_backward(observed, states[2], *slope[:2], weights)
    land_blocks(rows, field, sens, 0, outer_slots, per_tile, width)

    @pl.when(rows[2, 0] > outer_slots)
    def _():
        take_observed(rows, table, slabs, late_observed, outer_slots, late_slots)
        slopes(late_states, *slope[2:])
        sens[outer_slots * BLOCK_COLS :, :] = net_backward(
            late_observed, late_states[2], *slope[2:], weights
        )
        land_blocks(rows, field, sens, outer_slots, late_slots, per_tile, width)

    for tile in range(tiles):
        low = field[tile * width : tile * width + REACH, :]
        high = field[(tile + 1) * width - REACH : (tile + 1) * width, :]
        low, high = split_sides(low, high, "lon")
        to_far[tile], to_close[tile] = low.astype(jnp.bfloat16), high.astype(jnp.bfloat16)


def inner_backward_kernel(per_tile, parts, outer_slots, plan, table_rows, sens, *refs):
    slabs, refs = refs[:parts], refs[parts:]
    weights, states, refs = refs[:3], refs[3:6], refs[6:]
    landing, rows, table, observed, inner, field, *slope, sems = refs
    tiles, width, _ = landing.shape
    late_slots = observed.shape[0] // BLOCK_COLS
    split = outer_slots * BLOCK_COLS
    moves = [
        pltpu.make_async_copy(plan, rows, sems.at[0]),
        pltpu.make_async_copy(table_rows, table, sems.at[1]),
    ]
    for move in moves:
        move.start()
    field[...] = jnp.zeros_like(field)
    inner[...] = sens[...]
    slopes(states, *slope)
    for move in moves:
        move.wait()

    @pl.when(rows[2, 0] <= outer_slots)
    def _():
        take_observed(rows, table, slabs, observed, outer_slots, late_slots)
        inner[split:, :] = net_backward(observed, states[2], *slope, weights)

    land_blocks(rows, field, inner, 0, outer_slots + late_slots, per_tile, width)
    for tile in range(tiles):
        landing[tile] = field[tile * width : (tile + 1) * width, :]


def lon_back_kernel(far, close, own, taps, back, to_far, to_close, padded):
    tiles, width, _ = own.shape
    height, levels, _ = back.shape
    per_tile = height // tiles
    fill_padded(padded, far, own, close)
    for tile in range(tiles):
        rows = jnp.transpose(lon_conv(padded, taps, tile, 0, width))
        rows = rows.reshape(per_tile, levels, width)
        back[tile * per_tile : (tile + 1) * per_tile] = rows
    halve_for_sides(back, height, to_far, to_close)


def own_back_kernel(back, control, own_part, held, sem):
    control_in = pltpu.make_async_copy(control, held, sem)
    control_in.start()
    control_in.wait()
    height = back.shape[0]
    for row in range(height):
        own_part[row] = lat_sum(back, row, 0, height, held[row])


def lat_back_kernel(far, close, own_part, gradient, halos, done, sems):
    halos[0], halos[1] = sides(far[...], close[...], "lat")
    height = own_part.shape[0]
    piece = height // BAND_PIECES
    moves = []
    for k in range(BAND_PIECES):
        part = pl.ds(k * piece, piece)
        for row in range(k * piece, (k + 1) * piece):
            done[row] = lat_rims(row, own_part[row], halos, height)
        moves.append(pltpu.make_async_copy(done.at[part], gradient.at[part], sems.at[k]))
        moves[-1].start()
    for move in moves:
        move.wait()


def exchange(to_far, to_close, axis, periodic):
    count = lax.axis_size(axis)
    far = []
    for odd in range(1, count, 2):
        if odd + 1 < count or periodic:
            far += [(odd, (odd + 1) % count), ((odd + 1) % count, odd)]
    close = [(i, i ^ 1) for i in range(count)]
    to_close, _ = lax.optimization_barrier((to_close, to_far))
    from_far, from_close = lax.ppermute(to_far, axis, far), lax.ppermute(to_close, axis, close)
    from_far = lax.optimization_barrier(from_far)
    from_close, _ = lax.optimization_barrier((from_close, from_far))
    return from_far, from_close, to_close


def shards(
    control,
    background,
    lon_width,
    block_cells,
    block_owner,
    channel_count,
    radiance,
    in_weight,
    in_bias,
    mid_weight,
    mid_bias,
    out_weight,
    out_bias,
):
    height, levels, width = control.shape
    hidden = mid_weight.shape[0]
    channels, columns = radiance.shape
    slot_count = block_owner.shape[0]
    recv_most = channel_count.shape[0]
    per_tile = LANES // levels
    tiles = height // per_tile
    slab_rows = BLOCK_COLS * channels // LANES
    f32, bf16, i32 = jnp.float32, jnp.bfloat16, jnp.int32
    shape = jax.ShapeDtypeStruct
    field = height * levels * width
    conv_flops = 2 * 33 * field

    halves = channels // LANES
    radiance = radiance.T.reshape(recv_most, BLOCK_COLS, halves, LANES)
    radiance = jnp.swapaxes(radiance, 1, 2).reshape(recv_most, slab_rows, LANES)
    half_field = shape(control.shape, bf16)
    slabs, to_far, to_close = call(
        first_kernel,
        (shape((recv_most + 1, slab_rows, LANES), bf16), half_field, half_field),
        [HBM] * 4,
        (HBM, VMEM, VMEM),
        0,
        16 * field,
        scratch=(
            pltpu.VMEM((1, slot_count), i32),
            pltpu.VMEM((1, recv_most), i32),
            pltpu.VMEM((slab_rows, LANES), f32),
            pltpu.VMEM((slab_rows, LANES), bf16),
            pltpu.VMEM(control.shape, f32),
            pltpu.SemaphoreType.DMA((4 + BAND_PIECES,)),
        ),
        name="slabs_halves",
    )(*pinned(radiance, block_owner.reshape(1, slot_count), channel_count.reshape(1, recv_most), control))
    far, close, sent = exchange(to_far, to_close, "lat", False)

    band = pltpu.VMEM((height, levels, width), f32)
    taps, turned, plan, own_part = call(
        prepare_kernel,
        (
            shape((tiles, 24, LANES), f32),
            shape((tiles, width, LANES), f32),
            shape((8, LANES), i32),
            shape(control.shape, f32),
        ),
        [HBM] * 5,
        (VMEM,) * 4,
        conv_flops // 2,
        12 * field,
        scratch=(
            pltpu.SMEM((height,), i32),
            pltpu.VMEM((1, slot_count), i32),
            pltpu.VMEM((1, slot_count), i32),
            band,
            band,
            pltpu.SemaphoreType.DMA((5,)),
        ),
        name="taps_background",
    )(
        *pinned(
            lon_width,
            background,
            block_cells.reshape(1, slot_count),
            block_owner.reshape(1, slot_count),
            control,
        )
    )

    lat_count = lax.axis_size("lat")
    one, two, *others = swap_bits(lat_count)

    def swapped(part, apart):
        return lax.ppermute(part, "lat", [(i, i ^ apart) for i in range(lat_count)])

    slabs, _ = lax.optimization_barrier((slabs, sent))
    near = [slabs] + [swapped(slabs, apart) for apart in (1 << one, 1 << two, (1 << one) + (1 << two))]

    halos = pltpu.VMEM((2, REACH, levels, width), f32)
    smoothed, to_far, to_close = call(
        lat_smooth_kernel,
        (shape((tiles, width, LANES), f32),) + (shape((tiles, REACH, LANES), f32),) * 2,
        [VMEM] * 3,
        (VMEM,) * 3,
        conv_flops,
        16 * field,
        scratch=(halos,),
        name="lat_smooth",
    )(far, close, own_part)
    far, close, sent = exchange(to_far, to_close, "lon", True)
    outer_slots = 3 * slot_count // 8
    late_slots = slot_count - outer_slots
    x_rows = slot_count * BLOCK_COLS
    outer_rows, late_rows = outer_slots * BLOCK_COLS, late_slots * BLOCK_COLS
    row_flops = 2 * hidden * (LANES + hidden + channels)
    def state_shapes(rows):
        return (shape((rows, hidden), bf16), shape((rows, hidden), bf16), shape((rows, channels), f32))

    plan_rows = pltpu.SMEM((8, LANES), i32)
    padded = pltpu.VMEM((tiles, width + 2 * REACH, LANES), f32)
    flat = pltpu.VMEM((tiles * width, LANES), f32)

    profile, *rest = call(
        functools.partial(inner_forward_kernel, per_tile, outer_slots),
        (shape((tiles * width, LANES), f32),)
        + state_shapes(late_rows)
        + (
            shape((LANES, hidden), bf16),
            shape((hidden, hidden), bf16),
            shape((hidden, channels), bf16),
            shape((1, hidden), f32),
            shape((1, hidden), f32),
            shape((1, channels), f32),
        ),
        [ANY] + [VMEM] * 3 + [HBM] * 6,
        (VMEM,) * 10,
        late_rows * row_flops,
        4 * 1024 * 1024,
        scratch=(
            plan_rows,
            padded,
            pltpu.VMEM((late_rows, LANES), f32),
            pltpu.SemaphoreType.DMA((5 + per_tile + WEIGHT_PIECES,)),
        ),
        name="inner_forward",
    )(
        plan,
        smoothed,
        turned,
        taps,
        *pinned(
            in_weight,
            in_bias.reshape(1, hidden),
            mid_weight,
            mid_bias.reshape(1, hidden),
            out_weight,
            out_bias.reshape(1, channels),
        ),
    )
    inner_states, weights = rest[:3], rest[3:]
    *near, _ = lax.optimization_barrier((*near, profile))
    for bit in others:
        near = [jnp.concatenate(near, axis=0)]
        near.append(swapped(near[0], 1 << bit))
    near = [jnp.concatenate(near[:-1], axis=0), near[-1]]
    across = [swapped(part, 1) for part in near]

    states = call(
        functools.partial(outer_forward_kernel, per_tile),
        state_shapes(outer_rows) + state_shapes(late_rows),
        [ANY] + [VMEM] * 12,
        (VMEM,) * 6,
        SWAP_COVER * outer_rows * row_flops,
        SWAP_COVER * 4 * 1024 * 1024,
        scratch=(
            plan_rows,
            padded,
            flat,
            pltpu.VMEM((outer_rows, LANES), f32),
            pltpu.VMEM((late_rows, LANES), f32),
            pltpu.SemaphoreType.DMA,
        ),
        name="outer_forward",
    )(plan, far, close, smoothed, turned, taps, profile, *weights)

    slabs = [*near, *across]
    table, sens, to_far, to_close = call(
        functools.partial(outer_backward_kernel, per_tile, len(slabs), recv_most),
        (
            shape((8, LANES), i32),
            shape((x_rows, LANES), f32),
            shape((tiles, REACH, LANES), bf16),
            shape((tiles, REACH, LANES), bf16),
        ),
        [ANY] + [VMEM] * (len(slabs) + 9),
        (VMEM,) * 4,
        outer_rows * row_flops,
        4 * 1024 * 1024,
        scratch=(
            plan_rows,
            pltpu.SMEM((8, LANES), i32),
            pltpu.VMEM((outer_rows, channels), f32),
            pltpu.VMEM((late_rows, channels), f32),
            flat,
            pltpu.VMEM((outer_rows, hidden), f32),
            pltpu.VMEM((outer_rows, hidden), f32),
            pltpu.VMEM((late_rows, hidden), f32),
            pltpu.VMEM((late_rows, hidden), f32),
            pltpu.SemaphoreType.DMA((2,)),
        ),
        name="outer_backward",
    )(plan, *slabs, *weights[:3], *states)
    far, close, sent = exchange(to_far, to_close, "lon", True)

    landing = call(
        functools.partial(inner_backward_kernel, per_tile, len(slabs), outer_slots),
        shape((tiles, width, LANES), f32),
        [ANY, ANY] + [VMEM] * (len(slabs) + 7),
        VMEM,
        late_rows * row_flops,
        4 * 1024 * 1024,
        scratch=(
            plan_rows,
            pltpu.SMEM((8, LANES), i32),
            pltpu.VMEM((late_rows, channels), f32),
            pltpu.VMEM((x_rows, LANES), f32),
            flat,
            pltpu.VMEM((late_rows, hidden), f32),
            pltpu.VMEM((late_rows, hidden), f32),
            pltpu.SemaphoreType.DMA((2,)),
        ),
        name="inner_backward",
    )(plan, table, sens, *slabs, *weights[:3], *inner_states)

    back, to_far, to_close = call(
        lon_back_kernel,
        (shape((height, levels, width), f32), half_field, half_field),
        [VMEM] * 4,
        (VMEM,) * 3,
        conv_flops,
        8 * field,
        scratch=(pltpu.VMEM((tiles, width + 2 * REACH, LANES), f32),),
        name="lon_back",
    )(far, close, landing, taps)
    far, close, sent = exchange(to_far, to_close, "lat", False)
    own_part = call(
        own_back_kernel,
        shape((height, levels, width), f32),
        [VMEM, HBM],
        VMEM,
        conv_flops // 2,
        12 * field,
        scratch=(band, pltpu.SemaphoreType.DMA),
        name="lat_back_own",
    )(back, *pinned(control))

    return call(
        lat_back_kernel,
        shape((height, levels, width), f32),
        [VMEM] * 3,
        HBM,
        conv_flops // 2,
        16 * field,
        scratch=(halos, band, pltpu.SemaphoreType.DMA((BAND_PIECES,))),
        name="lat_back",
    )(far, close, own_part)


def solution(mesh):
    return jax.shard_map(
        shards,
        mesh=mesh,
        in_specs=(
            P("lat", None, "lon"),
            P("lat", None, "lon"),
            P("lat"),
            P("lat", "lon"),
            P("lat", "lon"),
            P("lat", "lon"),
            P("lat", "lon"),
            P(),
            P(),
            P(),
            P(),
            P(),
            P(),
        ),
        out_specs=P("lat", None, "lon"),
        check_vma=False,
    )
```

```python
import functools

import jax
import jax.numpy as jnp
import numpy as np
from jax import lax
from jax.experimental import pallas as pl
from jax.experimental.pallas import tpu as pltpu
from jax.sharding import PartitionSpec as P

REACH = 16
BLOCK_COLS = 8
LANES = 128
LAT_SIGMA = 8.0
WEIGHT_PIECES = 4
BAND_PIECES = 4
SWAP_COVER = 10
VMEM_BYTES = 40 * 1024 * 1024

VMEM = pl.BlockSpec(memory_space=pltpu.VMEM)
SMEM = pl.BlockSpec(memory_space=pltpu.SMEM)
HBM = pl.BlockSpec(memory_space=pltpu.HBM)
ANY = pl.BlockSpec(memory_space=pl.ANY)


def lat_taps():
    offsets = np.arange(-REACH, REACH + 1, dtype=np.float64)
    raw = np.exp(-offsets * offsets / (2.0 * LAT_SIGMA * LAT_SIGMA))
    return [float(v) for v in (raw / np.sqrt(np.sum(raw * raw))).astype(np.float32)]


def call(kernel, out_shape, in_specs, out_specs, flops, bytes_moved, scratch=(), name=None):
    return pl.pallas_call(
        kernel,
        out_shape=out_shape,
        in_specs=in_specs,
        out_specs=out_specs,
        scratch_shapes=list(scratch),
        compiler_params=pltpu.CompilerParams(vmem_limit_bytes=VMEM_BYTES),
        cost_estimate=pl.CostEstimate(flops=flops, bytes_accessed=bytes_moved, transcendentals=0),
        name=name,
    )


def pinned(*values):
    return [pltpu.with_memory_space_constraint(value, pltpu.HBM) for value in values]


def lat_sum(parts, row, first, height, start=None):
    taps = lat_taps()
    acc = start
    for k in range(height):
        j = first + k - row
        if abs(j) <= REACH:
            term = taps[j + REACH] * parts[k]
            acc = term if acc is None else acc + term
    return acc


def lat_rims(row, part, halos, height):
    low = lat_sum(halos.at[0], row, -REACH, REACH, part)
    return lat_sum(halos.at[1], row, height, REACH, low)


def fill_padded(padded, far, own, close):
    width = own.shape[1]
    low, high = sides(far[...], close[...], "lon")
    padded[:, 0:REACH, :] = low
    padded[:, REACH : REACH + width, :] = own[...]
    padded[:, REACH + width :, :] = high


def lon_conv(padded, taps, tile, start, width):
    middle = REACH + start
    acc = taps[tile, 0:1, :] * padded[tile, pl.ds(middle, width), :]
    for j in range(1, REACH + 1):
        both = padded[tile, pl.ds(middle + j, width), :] + padded[tile, pl.ds(middle - j, width), :]
        acc = acc + taps[tile, j : j + 1, :] * both
    return acc


def rounded(value):
    return value.astype(jnp.bfloat16).astype(jnp.float32)


def halved_rows(rows, order):
    halves, carry = {}, None
    for row in order:
        value = rows[row] if carry is None else rows[row] + carry
        halves[row] = value.astype(jnp.bfloat16)
        carry = value - halves[row].astype(jnp.float32)
    return [halves[row] for row in sorted(halves)]


def halve_for_sides(rows, height, to_far, to_close):
    odd = odd_index("lat")
    upward = halved_rows(rows, range(height - 1, -1, -1))
    downward = halved_rows(rows, range(height))
    for row in range(height):
        to_far[row] = jnp.where(odd, upward[row], downward[row])
        to_close[row] = jnp.where(odd, downward[row], upward[row])


def first_kernel(
    radiance,
    block_owner,
    channel_count,
    control,
    background,
    slabs,
    to_far,
    to_close,
    held,
    field,
    owners,
    counts,
    rows,
    tables,
    sems,
):
    recv_most = radiance.shape[0]
    moves = [
        pltpu.make_async_copy(radiance, slabs.at[pl.ds(0, recv_most)], sems.at[0]),
        pltpu.make_async_copy(block_owner, owners, sems.at[1]),
        pltpu.make_async_copy(channel_count, counts, sems.at[2]),
    ]
    piece = control.shape[0] // BAND_PIECES
    for k in range(BAND_PIECES):
        part = pl.ds(k * piece, piece)
        moves.append(pltpu.make_async_copy(control.at[part], held.at[part], sems.at[5 + k]))
    field_in = pltpu.make_async_copy(background, field, sems.at[4])
    for move in moves[3:] + moves[:3] + [field_in]:
        move.start()
    rows[...] = jnp.full(rows.shape, -1.0, jnp.float32)
    moves[1].wait()
    moves[2].wait()
    rows[0:1, 0 : owners.shape[1]] = owners[...].astype(jnp.float32)
    rows[1:2, 0 : counts.shape[1]] = counts[...].astype(jnp.float32)
    tables[...] = rows[...].astype(jnp.bfloat16)
    last = pltpu.make_async_copy(tables, slabs.at[recv_most], sems.at[3])
    last.start()
    for move in moves[3:]:
        move.wait()
    halve_for_sides(held, held.shape[0], to_far, to_close)
    moves[0].wait()
    field_in.wait()
    last.wait()


def prepare_kernel(
    lon_width,
    block_cells,
    block_owner,
    field,
    band,
    taps,
    turned,
    plan,
    own_part,
    widths,
    cells,
    owners,
    sems,
):
    moves = [
        pltpu.make_async_copy(lon_width, widths, sems.at[0]),
        pltpu.make_async_copy(block_cells, cells, sems.at[1]),
        pltpu.make_async_copy(block_owner, owners, sems.at[2]),
    ]
    tiles = turned.shape[0]
    height, levels, width = field.shape
    per_tile = height // tiles
    for move in moves:
        move.start()
    groups = width // BLOCK_COLS
    rim = REACH // BLOCK_COLS
    slot_count = cells.shape[1]

    for row in range(height):
        own_part[row] = lat_sum(band, row, 0, height)
    for tile in range(tiles):
        block = field[tile * per_tile : (tile + 1) * per_tile].reshape(per_tile * levels, width)
        turned[tile] = jnp.transpose(block)

    lane_row = lax.broadcasted_iota(jnp.int32, (1, LANES), 1) // levels
    steps = lax.broadcasted_iota(jnp.int32, (taps.shape[1], LANES), 0)
    dist = steps.astype(jnp.float32)
    weight = jnp.where(steps == 0, 1.0, jnp.where(steps <= REACH, 2.0, 0.0))
    moves[0].wait()
    for tile in range(tiles):
        spread = jnp.zeros((1, LANES), jnp.int32)
        for sub in range(per_tile):
            spread = jnp.where(lane_row == sub, widths[tile * per_tile + sub], spread)
        spread = spread.astype(jnp.float32)
        raw = jnp.exp(-dist * dist / (2.0 * spread * spread))
        norm = jnp.sum(weight * raw * raw, axis=0, keepdims=True)
        taps[tile] = raw / jnp.sqrt(norm)

    moves[1].wait()
    moves[2].wait()
    rows = lax.broadcasted_iota(jnp.int32, (slot_count, slot_count), 0)
    lanes = lax.broadcasted_iota(jnp.int32, (slot_count, slot_count), 1)
    group = cells[...] % groups
    outer = ((group < rim) | (group >= groups - rim)) & (owners[...] >= 0)
    outer_here = jnp.where(outer, 1, 0)
    outer_count = jnp.sum(outer_here, axis=1, keepdims=True)
    earlier = jnp.sum(jnp.where(lanes < rows, outer_here, 0), axis=1, keepdims=True)
    here = jnp.sum(jnp.where(lanes == rows, outer_here, 0), axis=1, keepdims=True)
    cell = jnp.sum(jnp.where(lanes == rows, cells[...], 0), axis=1, keepdims=True)
    position = jnp.where(here == 1, earlier, outer_count + rows[:, 0:1] - earlier)
    at = lax.broadcasted_iota(jnp.int32, (slot_count, LANES), 1)
    hit = position == at
    slot = lax.broadcasted_iota(jnp.int32, (slot_count, LANES), 0)
    plan[...] = jnp.zeros_like(plan)
    plan[0:1, :] = jnp.sum(jnp.where(hit, cell, 0), axis=0, keepdims=True)
    plan[1:2, :] = jnp.sum(jnp.where(hit, slot, 0), axis=0, keepdims=True)
    plan[2:3, :] = jnp.broadcast_to(outer_count, (1, LANES))


def swap_bits(count):
    return list(range(count.bit_length() - 2, 0, -1))


def routing(recv_most, slot_count, slabs, table):
    per_owner = recv_most + 1
    spans, count = [], 0
    for ref in slabs:
        spans.append((ref, count))
        count += ref.shape[0] // per_owner
    half = count // 2
    here = lax.axis_index("lat")
    rows = lax.broadcasted_iota(jnp.int32, (slot_count, LANES), 0)
    lanes = lax.broadcasted_iota(jnp.int32, (slot_count, LANES), 1)
    diagonal = rows == lanes
    zero = jnp.zeros((slot_count, LANES), jnp.int32)

    bits = swap_bits(count)

    def device_of(k):
        apart = jnp.where(k < half, 0, 1)
        for place, bit in enumerate(bits):
            apart = apart + (((k >> place) & 1) << bit)
        return here ^ apart

    def over_sets(step):
        acc = zero
        for ref, first in spans:

            def add(k, acc, ref=ref, first=first):
                lines = ref[k * per_owner + recv_most].astype(jnp.float32)
                owners, counts = lines[0:1].astype(jnp.int32), lines[1:2].astype(jnp.int32)
                return acc + step(device_of(first + k), owners, counts)

            acc = lax.fori_loop(0, ref.shape[0] // per_owner, add, acc, unroll=count <= 8)
        return jnp.sum(acc, axis=1, keepdims=True)

    mine = slabs[0][recv_most].astype(jnp.float32)[0:1].astype(jnp.int32)
    owner = jnp.sum(jnp.where(diagonal, mine, 0), axis=1, keepdims=True)

    def rank(device, owners, counts):
        before = (device < here) | ((device == here) & (lanes < rows))
        return jnp.where((owners == owner) & before, 1, 0)

    arrival = over_sets(rank)

    def counted(device, owners, counts):
        return jnp.where((owner == device) & (lanes == arrival), counts, 0)

    kept = over_sets(counted)
    apart = owner ^ here
    entry = (apart & 1) * half
    for place, bit in enumerate(bits):
        entry = entry + (((apart >> bit) & 1) << place)
    target = jnp.where(owner >= 0, entry * per_owner + arrival, 0)
    table[...] = jnp.zeros_like(table)
    for row, column in enumerate((target, kept)):
        table[row : row + 1, :] = jnp.sum(jnp.where(diagonal, column, 0), axis=0, keepdims=True)


def odd_index(axis):
    return lax.axis_index(axis) % 2 == 1


def sides(far, close, axis):
    odd = odd_index(axis)
    far, close = far.astype(jnp.float32), close.astype(jnp.float32)
    return jnp.where(odd, close, far), jnp.where(odd, far, close)


def split_sides(low, high, axis):
    odd = odd_index(axis)
    return jnp.where(odd, high, low), jnp.where(odd, low, high)


def lat_smooth_kernel(far, close, own_part, smoothed, to_far, to_close, halos):
    tiles = smoothed.shape[0]
    height, levels, width = own_part.shape
    per_tile = height // tiles
    halos[0], halos[1] = sides(far[...], close[...], "lat")
    for tile in range(tiles):
        rows = range(tile * per_tile, (tile + 1) * per_tile)
        rows = [lat_rims(row, own_part[row], halos, height) for row in rows]
        turned = jnp.transpose(jnp.concatenate(rows, axis=0))
        smoothed[tile] = turned
        to_far[tile], to_close[tile] = split_sides(turned[0:REACH], turned[width - REACH : width], "lon")


def block_place(plan, position, groups, per_tile, width):
    block = plan[0, position]
    row = block // groups
    start = (row // per_tile) * width + (block % groups) * BLOCK_COLS
    return pl.multiple_of(start, BLOCK_COLS), row % per_tile


def take_blocks(plan, profile, picked, first, count, per_tile, width):
    groups = width // BLOCK_COLS
    lane_row = lax.broadcasted_iota(jnp.int32, (BLOCK_COLS, LANES), 1) // (LANES // per_tile)
    for k in range(count):
        start, sub = block_place(plan, first + k, groups, per_tile, width)
        block = profile[pl.ds(start, BLOCK_COLS), :]
        picked[k * BLOCK_COLS : (k + 1) * BLOCK_COLS, :] = jnp.where(lane_row == sub, block, 0.0)


def land_blocks(plan, field, sens, first, count, per_tile, width):
    groups = width // BLOCK_COLS
    lane_row = lax.broadcasted_iota(jnp.int32, (BLOCK_COLS, LANES), 1) // (LANES // per_tile)
    for k in range(first, first + count):
        start, sub = block_place(plan, k, groups, per_tile, width)
        block = sens[k * BLOCK_COLS : (k + 1) * BLOCK_COLS, :]
        field[pl.ds(start, BLOCK_COLS), :] += jnp.where(lane_row == sub, block, 0.0)


def take_observed(plan, table, slabs, observed, first, count):
    channels = observed.shape[1]
    channel = lax.broadcasted_iota(jnp.int32, (BLOCK_COLS, LANES), 1)
    for k in range(count):
        slot = plan[1, first + k]
        at, kept = table[0, slot], table[1, slot]
        slab, start = None, 0
        for ref in slabs:
            size = ref.shape[0]
            found = ref[jnp.clip(at - start, 0, size - 1)].astype(jnp.float32)
            slab = found if slab is None else jnp.where(at >= start, found, slab)
            start += size
        for h in range(channels // LANES):
            part = slab[h * BLOCK_COLS : (h + 1) * BLOCK_COLS]
            part = jnp.where(channel + h * LANES < kept, part, jnp.inf)
            observed[k * BLOCK_COLS : (k + 1) * BLOCK_COLS, h * LANES : (h + 1) * LANES] = part


def dot(a, b):
    return jnp.dot(a, b, preferred_element_type=jnp.float32)


def dot_t(a, b):
    return lax.dot_general(a, b, (((1,), (1,)), ((), ())), preferred_element_type=jnp.float32)


def net_first(picked, weights, act_one):
    inputs = picked[...].astype(jnp.bfloat16)
    act_one[...] = jnp.tanh(dot(inputs, weights[0][...]) + weights[3][...]).astype(jnp.bfloat16)


def net_rest(weights, states):
    _, weight_two, weight_out, _, bias_two, bias_out = weights
    act_one, act_two, emitted = states
    act_two[...] = jnp.tanh(dot(act_one[...], weight_two[...]) + bias_two[...]).astype(jnp.bfloat16)
    emitted[...] = dot(act_two[...], weight_out[...]) + bias_out[...]


def net_forward(picked, weights, states):
    net_first(picked, weights, states[0])
    net_rest(weights, states)


def net_backward(observed, states, weights):
    wide_in, weight_two, weight_out = weights[:3]
    act_one, act_two, emitted = states
    seen = observed[...]
    misfit = jnp.where(seen < jnp.inf, emitted[...] - seen, 0.0).astype(jnp.bfloat16)
    two = act_two[...].astype(jnp.float32)
    grad_two = (dot_t(misfit, weight_out[...]) * (1.0 - two * two)).astype(jnp.bfloat16)
    one = act_one[...].astype(jnp.float32)
    grad_one = (dot_t(grad_two, weight_two[...]) * (1.0 - one * one)).astype(jnp.bfloat16)
    return rounded(dot_t(grad_one, wide_in[...]))


def inner_forward_kernel(per_tile, outer_slots, plan, own, turned, taps, *refs):
    (in_weight, in_bias, mid_weight, mid_bias, out_weight, out_bias), refs = refs[:6], refs[6:]
    profile, states, weights, (rows, padded, picked, sems) = refs[0], refs[1:4], refs[4:10], refs[10:]
    wide_in, weight_two, weight_out, bias_one, bias_two, bias_out = weights
    tiles, width, _ = own.shape
    levels = in_weight.shape[0]
    count = picked.shape[0] // BLOCK_COLS
    piece = mid_weight.shape[0] // WEIGHT_PIECES
    pieces = [pl.ds(k * piece, piece) for k in range(WEIGHT_PIECES)]
    loads = [(plan, rows), (in_bias, bias_one)]
    loads += [(in_weight, wide_in.at[pl.ds(sub * levels, levels)]) for sub in range(per_tile)]
    early = len(loads)
    loads += [(mid_weight.at[part], weight_two.at[part]) for part in pieces] + [(mid_bias, bias_two)]
    loads += [(out_weight, weight_out), (out_bias, bias_out)]
    loads = [
        pltpu.make_async_copy(source, target, sems.at[k]) for k, (source, target) in enumerate(loads)
    ]
    for move in loads:
        move.start()
    zeros = jnp.zeros((tiles, REACH, LANES), jnp.float32)
    padded[:, 0:REACH, :] = zeros
    padded[:, REACH : REACH + width, :] = own[...]
    padded[:, REACH + width :, :] = zeros
    for tile in range(tiles):
        total = turned[tile] + lon_conv(padded, taps, tile, 0, width)
        profile[tile * width : (tile + 1) * width, :] = rounded(total)
    for move in loads[:early]:
        move.wait()
    take_blocks(rows, profile, picked, outer_slots, count, per_tile, width)
    act_one, act_two, emitted = states
    net_first(picked, weights, act_one)
    for move in loads[early:]:
        move.wait()

    @pl.when(rows[2, 0] <= outer_slots)
    def _():
        net_rest(weights, states)


def outer_forward_kernel(
    per_tile,
    plan,
    far,
    close,
    own,
    turned,
    taps,
    inner_profile,
    *refs,
):
    weights, states, late_states, (rows, padded, profile, picked, late_picked, sem) = (
        refs[:6],
        refs[6:9],
        refs[9:12],
        refs[12:],
    )
    tiles, width, _ = own.shape
    outer_slots = picked.shape[0] // BLOCK_COLS
    late_slots = late_picked.shape[0] // BLOCK_COLS
    plan_in = pltpu.make_async_copy(plan, rows, sem)
    plan_in.start()
    fill_padded(padded, far, own, close)
    profile[...] = inner_profile[...]
    for tile in range(tiles):
        for start in (0, width - REACH):
            total = turned[tile, start : start + REACH, :] + lon_conv(padded, taps, tile, start, REACH)
            profile[tile * width + start : tile * width + start + REACH, :] = rounded(total)
    plan_in.wait()
    take_blocks(rows, profile, picked, 0, outer_slots, per_tile, width)
    net_forward(picked, weights, states)

    @pl.when(rows[2, 0] > outer_slots)
    def _():
        take_blocks(rows, profile, late_picked, outer_slots, late_slots, per_tile, width)
        net_forward(late_picked, weights, late_states)


def outer_backward_kernel(per_tile, parts, recv_most, plan, *refs):
    slabs, refs = refs[:parts], refs[parts:]
    weights, states, late_states, refs = refs[:3], refs[3:6], refs[6:9], refs[9:]
    (table_rows, sens, to_far, to_close) = refs[:4]
    (rows, table, observed, late_observed, field, sems) = refs[4:]
    tiles = to_far.shape[0]
    width = field.shape[0] // tiles
    outer_slots = observed.shape[0] // BLOCK_COLS
    late_slots = late_observed.shape[0] // BLOCK_COLS

    plan_in = pltpu.make_async_copy(plan, rows, sems.at[0])
    plan_in.start()
    routing(recv_most, outer_slots + late_slots, slabs, table_rows)
    table_in = pltpu.make_async_copy(table_rows, table, sems.at[1])
    table_in.start()
    field[...] = jnp.zeros_like(field)
    plan_in.wait()
    table_in.wait()

    take_observed(rows, table, slabs, observed, 0, outer_slots)
    sens[0 : outer_slots * BLOCK_COLS, :] = net_backward(observed, states, weights)
    land_blocks(rows, field, sens, 0, outer_slots, per_tile, width)

    @pl.when(rows[2, 0] > outer_slots)
    def _():
        take_observed(rows, table, slabs, late_observed, outer_slots, late_slots)
        sens[outer_slots * BLOCK_COLS :, :] = net_backward(late_observed, late_states, weights)
        land_blocks(rows, field, sens, outer_slots, late_slots, per_tile, width)

    for tile in range(tiles):
        low = field[tile * width : tile * width + REACH, :]
        high = field[(tile + 1) * width - REACH : (tile + 1) * width, :]
        low, high = split_sides(low, high, "lon")
        to_far[tile], to_close[tile] = low.astype(jnp.bfloat16), high.astype(jnp.bfloat16)


def inner_backward_kernel(per_tile, parts, outer_slots, plan, table_rows, sens, *refs):
    slabs, refs = refs[:parts], refs[parts:]
    weights, states, refs = refs[:3], refs[3:6], refs[6:]
    landing, rows, table, observed, inner, field, sems = refs
    tiles, width, _ = landing.shape
    late_slots = observed.shape[0] // BLOCK_COLS
    split = outer_slots * BLOCK_COLS
    moves = [
        pltpu.make_async_copy(plan, rows, sems.at[0]),
        pltpu.make_async_copy(table_rows, table, sems.at[1]),
    ]
    for move in moves:
        move.start()
    field[...] = jnp.zeros_like(field)
    inner[...] = sens[...]
    for move in moves:
        move.wait()

    @pl.when(rows[2, 0] <= outer_slots)
    def _():
        take_observed(rows, table, slabs, observed, outer_slots, late_slots)
        inner[split:, :] = net_backward(observed, states, weights)

    land_blocks(rows, field, inner, 0, outer_slots + late_slots, per_tile, width)
    for tile in range(tiles):
        landing[tile] = field[tile * width : (tile + 1) * width, :]


def lon_back_kernel(far, close, own, taps, back, to_far, to_close, padded):
    tiles, width, _ = own.shape
    height, levels, _ = back.shape
    per_tile = height // tiles
    fill_padded(padded, far, own, close)
    for tile in range(tiles):
        rows = jnp.transpose(lon_conv(padded, taps, tile, 0, width))
        rows = rows.reshape(per_tile, levels, width)
        back[tile * per_tile : (tile + 1) * per_tile] = rows
    halve_for_sides(back, height, to_far, to_close)


def own_back_kernel(back, control, own_part):
    height = back.shape[0]
    for row in range(height):
        own_part[row] = lat_sum(back, row, 0, height, control[row])


def lat_back_kernel(far, close, own_part, gradient, halos, done, sems):
    halos[0], halos[1] = sides(far[...], close[...], "lat")
    height = own_part.shape[0]
    piece = height // BAND_PIECES
    moves = []
    for k in range(BAND_PIECES):
        part = pl.ds(k * piece, piece)
        for row in range(k * piece, (k + 1) * piece):
            done[row] = lat_rims(row, own_part[row], halos, height)
        moves.append(pltpu.make_async_copy(done.at[part], gradient.at[part], sems.at[k]))
        moves[-1].start()
    for move in moves:
        move.wait()


def exchange(to_far, to_close, axis, periodic):
    count = lax.axis_size(axis)
    far = []
    for odd in range(1, count, 2):
        if odd + 1 < count or periodic:
            far += [(odd, (odd + 1) % count), ((odd + 1) % count, odd)]
    close = [(i, i ^ 1) for i in range(count)]
    to_close, _ = lax.optimization_barrier((to_close, to_far))
    from_far, from_close = lax.ppermute(to_far, axis, far), lax.ppermute(to_close, axis, close)
    from_far = lax.optimization_barrier(from_far)
    from_close, _ = lax.optimization_barrier((from_close, from_far))
    return from_far, from_close, to_close


def shards(
    control,
    background,
    lon_width,
    block_cells,
    block_owner,
    channel_count,
    radiance,
    in_weight,
    in_bias,
    mid_weight,
    mid_bias,
    out_weight,
    out_bias,
):
    height, levels, width = control.shape
    hidden = mid_weight.shape[0]
    channels, columns = radiance.shape
    slot_count = block_owner.shape[0]
    recv_most = channel_count.shape[0]
    per_tile = LANES // levels
    tiles = height // per_tile
    slab_rows = BLOCK_COLS * channels // LANES
    f32, bf16, i32 = jnp.float32, jnp.bfloat16, jnp.int32
    shape = jax.ShapeDtypeStruct
    field = height * levels * width
    conv_flops = 2 * 33 * field

    halves = channels // LANES
    radiance = radiance.T.reshape(recv_most, BLOCK_COLS, halves, LANES)
    radiance = jnp.swapaxes(radiance, 1, 2).reshape(recv_most, slab_rows, LANES)
    half_field = shape(control.shape, bf16)
    slabs, to_far, to_close, held, ground = call(
        first_kernel,
        (
            shape((recv_most + 1, slab_rows, LANES), bf16),
            half_field,
            half_field,
            shape(control.shape, f32),
            shape(control.shape, f32),
        ),
        [HBM] * 5,
        (HBM,) + (VMEM,) * 4,
        0,
        24 * field,
        scratch=(
            pltpu.VMEM((1, slot_count), i32),
            pltpu.VMEM((1, recv_most), i32),
            pltpu.VMEM((slab_rows, LANES), f32),
            pltpu.VMEM((slab_rows, LANES), bf16),
            pltpu.SemaphoreType.DMA((5 + BAND_PIECES,)),
        ),
        name="slabs_halves",
    )(
        *pinned(
            radiance,
            block_owner.reshape(1, slot_count),
            channel_count.reshape(1, recv_most),
            control,
            background,
        )
    )
    far, close, sent = exchange(to_far, to_close, "lat", False)

    band = pltpu.VMEM((height, levels, width), f32)
    taps, turned, plan, own_part = call(
        prepare_kernel,
        (
            shape((tiles, 24, LANES), f32),
            shape((tiles, width, LANES), f32),
            shape((8, LANES), i32),
            shape(control.shape, f32),
        ),
        [HBM] * 3 + [VMEM] * 2,
        (VMEM,) * 4,
        conv_flops // 2,
        12 * field,
        scratch=(
            pltpu.SMEM((height,), i32),
            pltpu.VMEM((1, slot_count), i32),
            pltpu.VMEM((1, slot_count), i32),
            pltpu.SemaphoreType.DMA((3,)),
        ),
        name="taps_background",
    )(
        *pinned(lon_width, block_cells.reshape(1, slot_count), block_owner.reshape(1, slot_count)),
        ground,
        held,
    )

    lat_count = lax.axis_size("lat")
    one, two, *others = swap_bits(lat_count)

    def swapped(part, apart):
        return lax.ppermute(part, "lat", [(i, i ^ apart) for i in range(lat_count)])

    slabs, _ = lax.optimization_barrier((slabs, sent))
    near = [slabs] + [swapped(slabs, apart) for apart in (1 << one, 1 << two, (1 << one) + (1 << two))]

    halos = pltpu.VMEM((2, REACH, levels, width), f32)
    smoothed, to_far, to_close = call(
        lat_smooth_kernel,
        (shape((tiles, width, LANES), f32),) + (shape((tiles, REACH, LANES), f32),) * 2,
        [VMEM] * 3,
        (VMEM,) * 3,
        conv_flops,
        16 * field,
        scratch=(halos,),
        name="lat_smooth",
    )(far, close, own_part)
    far, close, sent = exchange(to_far, to_close, "lon", True)
    outer_slots = 3 * slot_count // 8
    late_slots = slot_count - outer_slots
    x_rows = slot_count * BLOCK_COLS
    outer_rows, late_rows = outer_slots * BLOCK_COLS, late_slots * BLOCK_COLS
    row_flops = 2 * hidden * (LANES + hidden + channels)
    def state_shapes(rows):
        return (shape((rows, hidden), bf16), shape((rows, hidden), bf16), shape((rows, channels), f32))

    plan_rows = pltpu.SMEM((8, LANES), i32)
    padded = pltpu.VMEM((tiles, width + 2 * REACH, LANES), f32)
    flat = pltpu.VMEM((tiles * width, LANES), f32)

    profile, *rest = call(
        functools.partial(inner_forward_kernel, per_tile, outer_slots),
        (shape((tiles * width, LANES), f32),)
        + state_shapes(late_rows)
        + (
            shape((LANES, hidden), bf16),
            shape((hidden, hidden), bf16),
            shape((hidden, channels), bf16),
            shape((1, hidden), f32),
            shape((1, hidden), f32),
            shape((1, channels), f32),
        ),
        [ANY] + [VMEM] * 3 + [HBM] * 6,
        (VMEM,) * 10,
        late_rows * row_flops,
        4 * 1024 * 1024,
        scratch=(
            plan_rows,
            padded,
            pltpu.VMEM((late_rows, LANES), f32),
            pltpu.SemaphoreType.DMA((5 + per_tile + WEIGHT_PIECES,)),
        ),
        name="inner_forward",
    )(
        plan,
        smoothed,
        turned,
        taps,
        *pinned(
            in_weight,
            in_bias.reshape(1, hidden),
            mid_weight,
            mid_bias.reshape(1, hidden),
            out_weight,
            out_bias.reshape(1, channels),
        ),
    )
    inner_states, weights = rest[:3], rest[3:]
    *near, _ = lax.optimization_barrier((*near, profile))
    for bit in others:
        near = [jnp.concatenate(near, axis=0)]
        near.append(swapped(near[0], 1 << bit))
    near = [jnp.concatenate(near[:-1], axis=0), near[-1]]
    across = [swapped(part, 1) for part in near]

    states = call(
        functools.partial(outer_forward_kernel, per_tile),
        state_shapes(outer_rows) + state_shapes(late_rows),
        [ANY] + [VMEM] * 12,
        (VMEM,) * 6,
        SWAP_COVER * outer_rows * row_flops,
        SWAP_COVER * 4 * 1024 * 1024,
        scratch=(
            plan_rows,
            padded,
            flat,
            pltpu.VMEM((outer_rows, LANES), f32),
            pltpu.VMEM((late_rows, LANES), f32),
            pltpu.SemaphoreType.DMA,
        ),
        name="outer_forward",
    )(plan, far, close, smoothed, turned, taps, profile, *weights)

    slabs = [*near, *across]
    table, sens, to_far, to_close = call(
        functools.partial(outer_backward_kernel, per_tile, len(slabs), recv_most),
        (
            shape((8, LANES), i32),
            shape((x_rows, LANES), f32),
            shape((tiles, REACH, LANES), bf16),
            shape((tiles, REACH, LANES), bf16),
        ),
        [ANY] + [VMEM] * (len(slabs) + 9),
        (VMEM,) * 4,
        outer_rows * row_flops,
        4 * 1024 * 1024,
        scratch=(
            plan_rows,
            pltpu.SMEM((8, LANES), i32),
            pltpu.VMEM((outer_rows, channels), f32),
            pltpu.VMEM((late_rows, channels), f32),
            flat,
            pltpu.SemaphoreType.DMA((2,)),
        ),
        name="outer_backward",
    )(plan, *slabs, *weights[:3], *states)
    far, close, sent = exchange(to_far, to_close, "lon", True)

    landing = call(
        functools.partial(inner_backward_kernel, per_tile, len(slabs), outer_slots),
        shape((tiles, width, LANES), f32),
        [ANY, ANY] + [VMEM] * (len(slabs) + 7),
        VMEM,
        late_rows * row_flops,
        4 * 1024 * 1024,
        scratch=(
            plan_rows,
            pltpu.SMEM((8, LANES), i32),
            pltpu.VMEM((late_rows, channels), f32),
            pltpu.VMEM((x_rows, LANES), f32),
            flat,
            pltpu.SemaphoreType.DMA((2,)),
        ),
        name="inner_backward",
    )(plan, table, sens, *slabs, *weights[:3], *inner_states)

    back, to_far, to_close = call(
        lon_back_kernel,
        (shape((height, levels, width), f32), half_field, half_field),
        [VMEM] * 4,
        (VMEM,) * 3,
        conv_flops,
        8 * field,
        scratch=(pltpu.VMEM((tiles, width + 2 * REACH, LANES), f32),),
        name="lon_back",
    )(far, close, landing, taps)
    back, _ = lax.optimization_barrier((back, to_far))
    own_part = call(
        own_back_kernel,
        shape((height, levels, width), f32),
        [VMEM, VMEM],
        VMEM,
        conv_flops // 2,
        12 * field,
        name="lat_back_own",
    )(back, held)
    to_close, _ = lax.optimization_barrier((to_close, own_part))
    far, close, _ = exchange(to_far, to_close, "lat", False)

    return call(
        lat_back_kernel,
        shape((height, levels, width), f32),
        [VMEM] * 3,
        HBM,
        conv_flops // 2,
        16 * field,
        scratch=(halos, band, pltpu.SemaphoreType.DMA((BAND_PIECES,))),
        name="lat_back",
    )(far, close, own_part)


def solution(mesh):
    return jax.shard_map(
        shards,
        mesh=mesh,
        in_specs=(
            P("lat", None, "lon"),
            P("lat", None, "lon"),
            P("lat"),
            P("lat", "lon"),
            P("lat", "lon"),
            P("lat", "lon"),
            P("lat", "lon"),
            P(),
            P(),
            P(),
            P(),
            P(),
            P(),
        ),
        out_specs=P("lat", None, "lon"),
        check_vma=False,
    )
```

```python
import functools

import jax
import jax.numpy as jnp
import numpy as np
from jax import lax
from jax.experimental import pallas as pl
from jax.experimental.pallas import tpu as pltpu
from jax.sharding import PartitionSpec as P

REACH = 16
BLOCK_COLS = 8
LANES = 128
LAT_SIGMA = 8.0
WEIGHT_PIECES = 8
BAND_PIECES = 4
LAT_COVER = 64
LON_COVER = 10
SWAP_COVER = 10
VMEM_BYTES = 40 * 1024 * 1024

VMEM = pl.BlockSpec(memory_space=pltpu.VMEM)
SMEM = pl.BlockSpec(memory_space=pltpu.SMEM)
HBM = pl.BlockSpec(memory_space=pltpu.HBM)
ANY = pl.BlockSpec(memory_space=pl.ANY)


def lat_taps():
    offsets = np.arange(-REACH, REACH + 1, dtype=np.float64)
    raw = np.exp(-offsets * offsets / (2.0 * LAT_SIGMA * LAT_SIGMA))
    return [float(v) for v in (raw / np.sqrt(np.sum(raw * raw))).astype(np.float32)]


def call(kernel, out_shape, in_specs, out_specs, flops, bytes_moved, scratch=(), name=None):
    return pl.pallas_call(
        kernel,
        out_shape=out_shape,
        in_specs=in_specs,
        out_specs=out_specs,
        scratch_shapes=list(scratch),
        compiler_params=pltpu.CompilerParams(vmem_limit_bytes=VMEM_BYTES),
        cost_estimate=pl.CostEstimate(flops=flops, bytes_accessed=bytes_moved, transcendentals=0),
        name=name,
    )


def pinned(*values):
    return [pltpu.with_memory_space_constraint(value, pltpu.HBM) for value in values]


def lat_sum(parts, row, first, height, start=None):
    taps = lat_taps()
    acc = start
    for k in range(height):
        j = first + k - row
        if abs(j) <= REACH:
            term = taps[j + REACH] * parts[k]
            acc = term if acc is None else acc + term
    return acc


def lat_rims(row, part, halos, height):
    low = lat_sum(halos.at[0], row, -REACH, REACH, part)
    return lat_sum(halos.at[1], row, height, REACH, low)


def fill_padded(padded, far, own, close):
    width = own.shape[1]
    low, high = sides(far[...], close[...], "lon")
    padded[:, 0:REACH, :] = low
    padded[:, REACH : REACH + width, :] = own[...]
    padded[:, REACH + width :, :] = high


def lon_conv(padded, taps, tile, start, width):
    middle = REACH + start
    acc = taps[tile, 0:1, :] * padded[tile, pl.ds(middle, width), :]
    for j in range(1, REACH + 1):
        both = padded[tile, pl.ds(middle + j, width), :] + padded[tile, pl.ds(middle - j, width), :]
        acc = acc + taps[tile, j : j + 1, :] * both
    return acc


def rounded(value):
    return value.astype(jnp.bfloat16).astype(jnp.float32)


def halved_rows(rows, order):
    halves, carry = {}, None
    for row in order:
        value = rows[row] if carry is None else rows[row] + carry
        halves[row] = value.astype(jnp.bfloat16)
        carry = value - halves[row].astype(jnp.float32)
    return [halves[row] for row in sorted(halves)]


def halve_for_sides(rows, height, to_far, to_close):
    odd = odd_index("lat")
    upward = halved_rows(rows, range(height - 1, -1, -1))
    downward = halved_rows(rows, range(height))
    for row in range(height):
        to_far[row] = jnp.where(odd, upward[row], downward[row])
        to_close[row] = jnp.where(odd, downward[row], upward[row])


def first_kernel(
    radiance,
    block_owner,
    channel_count,
    control,
    background,
    slabs,
    to_far,
    to_close,
    held,
    field,
    owners,
    counts,
    rows,
    tables,
    sems,
):
    recv_most = radiance.shape[0]
    moves = [
        pltpu.make_async_copy(radiance, slabs.at[pl.ds(0, recv_most)], sems.at[0]),
        pltpu.make_async_copy(block_owner, owners, sems.at[1]),
        pltpu.make_async_copy(channel_count, counts, sems.at[2]),
    ]
    piece = control.shape[0] // BAND_PIECES
    for k in range(BAND_PIECES):
        part = pl.ds(k * piece, piece)
        moves.append(pltpu.make_async_copy(control.at[part], held.at[part], sems.at[5 + k]))
    field_in = pltpu.make_async_copy(background, field, sems.at[4])
    for move in moves[3:] + moves[:3] + [field_in]:
        move.start()
    rows[...] = jnp.full(rows.shape, -1.0, jnp.float32)
    moves[1].wait()
    moves[2].wait()
    rows[0:1, 0 : owners.shape[1]] = owners[...].astype(jnp.float32)
    rows[1:2, 0 : counts.shape[1]] = counts[...].astype(jnp.float32)
    tables[...] = rows[...].astype(jnp.bfloat16)
    last = pltpu.make_async_copy(tables, slabs.at[recv_most], sems.at[3])
    last.start()
    for move in moves[3:]:
        move.wait()
    halve_for_sides(held, held.shape[0], to_far, to_close)
    moves[0].wait()
    field_in.wait()
    last.wait()


def prepare_kernel(
    lon_width,
    block_cells,
    block_owner,
    field,
    band,
    in_weight,
    in_bias,
    mid_weight,
    mid_bias,
    out_weight,
    out_bias,
    taps,
    turned,
    plan,
    own_part,
    wide_in,
    weight_two,
    weight_out,
    bias_one,
    bias_two,
    bias_out,
    widths,
    cells,
    owners,
    sems,
):
    moves = [
        pltpu.make_async_copy(lon_width, widths, sems.at[0]),
        pltpu.make_async_copy(block_cells, cells, sems.at[1]),
        pltpu.make_async_copy(block_owner, owners, sems.at[2]),
    ]
    tiles = turned.shape[0]
    height, levels, width = field.shape
    per_tile = height // tiles
    piece = mid_weight.shape[0] // WEIGHT_PIECES
    pieces = [pl.ds(k * piece, piece) for k in range(WEIGHT_PIECES)]
    loads = [(in_bias, bias_one), (mid_bias, bias_two), (out_bias, bias_out), (out_weight, weight_out)]
    loads += [(in_weight, wide_in.at[pl.ds(sub * levels, levels)]) for sub in range(per_tile)]
    loads += [(mid_weight.at[part], weight_two.at[part]) for part in pieces]
    loads = [
        pltpu.make_async_copy(source, target, sems.at[3 + k]) for k, (source, target) in enumerate(loads)
    ]
    for move in moves + loads:
        move.start()
    groups = width // BLOCK_COLS
    rim = REACH // BLOCK_COLS
    slot_count = cells.shape[1]

    for row in range(height):
        own_part[row] = lat_sum(band, row, 0, height)
    for tile in range(tiles):
        block = field[tile * per_tile : (tile + 1) * per_tile].reshape(per_tile * levels, width)
        turned[tile] = jnp.transpose(block)

    lane_row = lax.broadcasted_iota(jnp.int32, (1, LANES), 1) // levels
    steps = lax.broadcasted_iota(jnp.int32, (taps.shape[1], LANES), 0)
    dist = steps.astype(jnp.float32)
    weight = jnp.where(steps == 0, 1.0, jnp.where(steps <= REACH, 2.0, 0.0))
    moves[0].wait()
    for tile in range(tiles):
        spread = jnp.zeros((1, LANES), jnp.int32)
        for sub in range(per_tile):
            spread = jnp.where(lane_row == sub, widths[tile * per_tile + sub], spread)
        spread = spread.astype(jnp.float32)
        raw = jnp.exp(-dist * dist / (2.0 * spread * spread))
        norm = jnp.sum(weight * raw * raw, axis=0, keepdims=True)
        taps[tile] = raw / jnp.sqrt(norm)

    moves[1].wait()
    moves[2].wait()
    rows = lax.broadcasted_iota(jnp.int32, (slot_count, slot_count), 0)
    lanes = lax.broadcasted_iota(jnp.int32, (slot_count, slot_count), 1)
    group = cells[...] % groups
    outer = ((group < rim) | (group >= groups - rim)) & (owners[...] >= 0)
    outer_here = jnp.where(outer, 1, 0)
    outer_count = jnp.sum(outer_here, axis=1, keepdims=True)
    earlier = jnp.sum(jnp.where(lanes < rows, outer_here, 0), axis=1, keepdims=True)
    here = jnp.sum(jnp.where(lanes == rows, outer_here, 0), axis=1, keepdims=True)
    cell = jnp.sum(jnp.where(lanes == rows, cells[...], 0), axis=1, keepdims=True)
    position = jnp.where(here == 1, earlier, outer_count + rows[:, 0:1] - earlier)
    at = lax.broadcasted_iota(jnp.int32, (slot_count, LANES), 1)
    hit = position == at
    slot = lax.broadcasted_iota(jnp.int32, (slot_count, LANES), 0)
    plan[...] = jnp.zeros_like(plan)
    plan[0:1, :] = jnp.sum(jnp.where(hit, cell, 0), axis=0, keepdims=True)
    plan[1:2, :] = jnp.sum(jnp.where(hit, slot, 0), axis=0, keepdims=True)
    plan[2:3, :] = jnp.broadcast_to(outer_count, (1, LANES))
    for move in loads:
        move.wait()


def swap_bits(count):
    return list(range(count.bit_length() - 2, 0, -1))


def routing(recv_most, slot_count, slabs, table):
    per_owner = recv_most + 1
    spans, count = [], 0
    for ref in slabs:
        spans.append((ref, count))
        count += ref.shape[0] // per_owner
    half = count // 2
    here = lax.axis_index("lat")
    rows = lax.broadcasted_iota(jnp.int32, (slot_count, LANES), 0)
    lanes = lax.broadcasted_iota(jnp.int32, (slot_count, LANES), 1)
    diagonal = rows == lanes
    zero = jnp.zeros((slot_count, LANES), jnp.int32)

    bits = swap_bits(count)

    def device_of(k):
        apart = jnp.where(k < half, 0, 1)
        for place, bit in enumerate(bits):
            apart = apart + (((k >> place) & 1) << bit)
        return here ^ apart

    def over_sets(step):
        acc = zero
        for ref, first in spans:

            def add(k, acc, ref=ref, first=first):
                lines = ref[k * per_owner + recv_most].astype(jnp.float32)
                owners, counts = lines[0:1].astype(jnp.int32), lines[1:2].astype(jnp.int32)
                return acc + step(device_of(first + k), owners, counts)

            acc = lax.fori_loop(0, ref.shape[0] // per_owner, add, acc, unroll=count <= 8)
        return jnp.sum(acc, axis=1, keepdims=True)

    mine = slabs[0][recv_most].astype(jnp.float32)[0:1].astype(jnp.int32)
    owner = jnp.sum(jnp.where(diagonal, mine, 0), axis=1, keepdims=True)

    def rank(device, owners, counts):
        before = (device < here) | ((device == here) & (lanes < rows))
        return jnp.where((owners == owner) & before, 1, 0)

    arrival = over_sets(rank)

    def counted(device, owners, counts):
        return jnp.where((owner == device) & (lanes == arrival), counts, 0)

    kept = over_sets(counted)
    apart = owner ^ here
    entry = (apart & 1) * half
    for place, bit in enumerate(bits):
        entry = entry + (((apart >> bit) & 1) << place)
    target = jnp.where(owner >= 0, entry * per_owner + arrival, 0)
    table[...] = jnp.zeros_like(table)
    for row, column in enumerate((target, kept)):
        table[row : row + 1, :] = jnp.sum(jnp.where(diagonal, column, 0), axis=0, keepdims=True)


def odd_index(axis):
    return lax.axis_index(axis) % 2 == 1


def sides(far, close, axis):
    odd = odd_index(axis)
    far, close = far.astype(jnp.float32), close.astype(jnp.float32)
    return jnp.where(odd, close, far), jnp.where(odd, far, close)


def split_sides(low, high, axis):
    odd = odd_index(axis)
    return jnp.where(odd, high, low), jnp.where(odd, low, high)


def lat_smooth_kernel(far, close, own_part, smoothed, to_far, to_close, halos):
    tiles = smoothed.shape[0]
    height, levels, width = own_part.shape
    per_tile = height // tiles
    halos[0], halos[1] = sides(far[...], close[...], "lat")
    for tile in range(tiles):
        rows = range(tile * per_tile, (tile + 1) * per_tile)
        rows = [lat_rims(row, own_part[row], halos, height) for row in rows]
        turned = jnp.transpose(jnp.concatenate(rows, axis=0))
        smoothed[tile] = turned
        to_far[tile], to_close[tile] = split_sides(turned[0:REACH], turned[width - REACH : width], "lon")


def block_place(plan, position, groups, per_tile, width):
    block = plan[0, position]
    row = block // groups
    start = (row // per_tile) * width + (block % groups) * BLOCK_COLS
    return pl.multiple_of(start, BLOCK_COLS), row % per_tile


def take_blocks(plan, profile, picked, first, count, per_tile, width):
    groups = width // BLOCK_COLS
    lane_row = lax.broadcasted_iota(jnp.int32, (BLOCK_COLS, LANES), 1) // (LANES // per_tile)
    for k in range(count):
        start, sub = block_place(plan, first + k, groups, per_tile, width)
        block = profile[pl.ds(start, BLOCK_COLS), :]
        picked[k * BLOCK_COLS : (k + 1) * BLOCK_COLS, :] = jnp.where(lane_row == sub, block, 0.0)


def land_blocks(plan, field, sens, first, count, per_tile, width):
    groups = width // BLOCK_COLS
    lane_row = lax.broadcasted_iota(jnp.int32, (BLOCK_COLS, LANES), 1) // (LANES // per_tile)
    for k in range(first, first + count):
        start, sub = block_place(plan, k, groups, per_tile, width)
        block = sens[k * BLOCK_COLS : (k + 1) * BLOCK_COLS, :]
        field[pl.ds(start, BLOCK_COLS), :] += jnp.where(lane_row == sub, block, 0.0)


def take_observed(plan, table, slabs, observed, first, count):
    channels = observed.shape[1]
    channel = lax.broadcasted_iota(jnp.int32, (BLOCK_COLS, LANES), 1)
    for k in range(count):
        slot = plan[1, first + k]
        at, kept = table[0, slot], table[1, slot]
        slab, start = None, 0
        for ref in slabs:
            size = ref.shape[0]
            found = ref[jnp.clip(at - start, 0, size - 1)].astype(jnp.float32)
            slab = found if slab is None else jnp.where(at >= start, found, slab)
            start += size
        for h in range(channels // LANES):
            part = slab[h * BLOCK_COLS : (h + 1) * BLOCK_COLS]
            part = jnp.where(channel + h * LANES < kept, part, jnp.inf)
            observed[k * BLOCK_COLS : (k + 1) * BLOCK_COLS, h * LANES : (h + 1) * LANES] = part


def dot(a, b):
    return jnp.dot(a, b, preferred_element_type=jnp.float32)


def dot_t(a, b):
    return lax.dot_general(a, b, (((1,), (1,)), ((), ())), preferred_element_type=jnp.float32)


def net_first(picked, weights, act_one):
    inputs = picked[...].astype(jnp.bfloat16)
    act_one[...] = jnp.tanh(dot(inputs, weights[0][...]) + weights[3][...]).astype(jnp.bfloat16)


def net_rest(weights, states):
    _, weight_two, weight_out, _, bias_two, bias_out = weights
    act_one, act_two, emitted = states
    act_two[...] = jnp.tanh(dot(act_one[...], weight_two[...]) + bias_two[...]).astype(jnp.bfloat16)
    emitted[...] = dot(act_two[...], weight_out[...]) + bias_out[...]


def net_forward(picked, weights, states):
    net_first(picked, weights, states[0])
    net_rest(weights, states)


def net_backward(observed, states, weights):
    wide_in, weight_two, weight_out = weights[:3]
    act_one, act_two, emitted = states
    seen = observed[...]
    misfit = jnp.where(seen < jnp.inf, emitted[...] - seen, 0.0).astype(jnp.bfloat16)
    two = act_two[...].astype(jnp.float32)
    grad_two = (dot_t(misfit, weight_out[...]) * (1.0 - two * two)).astype(jnp.bfloat16)
    one = act_one[...].astype(jnp.float32)
    grad_one = (dot_t(grad_two, weight_two[...]) * (1.0 - one * one)).astype(jnp.bfloat16)
    return rounded(dot_t(grad_one, wide_in[...]))


def inner_forward_kernel(per_tile, outer_slots, plan, own, turned, taps, *refs):
    weights, profile, states, (rows, padded, picked, sem) = refs[:6], refs[6], refs[7:10], refs[10:]
    tiles, width, _ = own.shape
    count = picked.shape[0] // BLOCK_COLS
    plan_in = pltpu.make_async_copy(plan, rows, sem)
    plan_in.start()
    zeros = jnp.zeros((tiles, REACH, LANES), jnp.float32)
    padded[:, 0:REACH, :] = zeros
    padded[:, REACH : REACH + width, :] = own[...]
    padded[:, REACH + width :, :] = zeros
    for tile in range(tiles):
        total = turned[tile] + lon_conv(padded, taps, tile, 0, width)
        profile[tile * width : (tile + 1) * width, :] = rounded(total)
    plan_in.wait()

    @pl.when(rows[2, 0] <= outer_slots)
    def _():
        take_blocks(rows, profile, picked, outer_slots, count, per_tile, width)
        net_forward(picked, weights, states)


def outer_forward_kernel(
    per_tile,
    plan,
    far,
    close,
    own,
    turned,
    taps,
    inner_profile,
    *refs,
):
    weights, states, late_states, (rows, padded, profile, picked, late_picked, sem) = (
        refs[:6],
        refs[6:9],
        refs[9:12],
        refs[12:],
    )
    tiles, width, _ = own.shape
    outer_slots = picked.shape[0] // BLOCK_COLS
    late_slots = late_picked.shape[0] // BLOCK_COLS
    plan_in = pltpu.make_async_copy(plan, rows, sem)
    plan_in.start()
    fill_padded(padded, far, own, close)
    profile[...] = inner_profile[...]
    for tile in range(tiles):
        for start in (0, width - REACH):
            total = turned[tile, start : start + REACH, :] + lon_conv(padded, taps, tile, start, REACH)
            profile[tile * width + start : tile * width + start + REACH, :] = rounded(total)
    plan_in.wait()
    take_blocks(rows, profile, picked, 0, outer_slots, per_tile, width)
    net_forward(picked, weights, states)

    @pl.when(rows[2, 0] > outer_slots)
    def _():
        take_blocks(rows, profile, late_picked, outer_slots, late_slots, per_tile, width)
        net_forward(late_picked, weights, late_states)


def outer_backward_kernel(per_tile, parts, recv_most, plan, *refs):
    slabs, refs = refs[:parts], refs[parts:]
    weights, states, late_states, refs = refs[:3], refs[3:6], refs[6:9], refs[9:]
    (table_rows, sens, to_far, to_close) = refs[:4]
    (rows, table, observed, late_observed, field, sems) = refs[4:]
    tiles = to_far.shape[0]
    width = field.shape[0] // tiles
    outer_slots = observed.shape[0] // BLOCK_COLS
    late_slots = late_observed.shape[0] // BLOCK_COLS

    plan_in = pltpu.make_async_copy(plan, rows, sems.at[0])
    plan_in.start()
    routing(recv_most, outer_slots + late_slots, slabs, table_rows)
    table_in = pltpu.make_async_copy(table_rows, table, sems.at[1])
    table_in.start()
    field[...] = jnp.zeros_like(field)
    plan_in.wait()
    table_in.wait()

    take_observed(rows, table, slabs, observed, 0, outer_slots)
    sens[0 : outer_slots * BLOCK_COLS, :] = net_backward(observed, states, weights)
    land_blocks(rows, field, sens, 0, outer_slots, per_tile, width)

    @pl.when(rows[2, 0] > outer_slots)
    def _():
        take_observed(rows, table, slabs, late_observed, outer_slots, late_slots)
        sens[outer_slots * BLOCK_COLS :, :] = net_backward(late_observed, late_states, weights)
        land_blocks(rows, field, sens, outer_slots, late_slots, per_tile, width)

    for tile in range(tiles):
        low = field[tile * width : tile * width + REACH, :]
        high = field[(tile + 1) * width - REACH : (tile + 1) * width, :]
        low, high = split_sides(low, high, "lon")
        to_far[tile], to_close[tile] = low.astype(jnp.bfloat16), high.astype(jnp.bfloat16)


def inner_backward_kernel(per_tile, parts, outer_slots, plan, table_rows, sens, *refs):
    slabs, refs = refs[:parts], refs[parts:]
    weights, states, refs = refs[:3], refs[3:6], refs[6:]
    landing, rows, table, observed, inner, field, sems = refs
    tiles, width, _ = landing.shape
    late_slots = observed.shape[0] // BLOCK_COLS
    split = outer_slots * BLOCK_COLS
    moves = [
        pltpu.make_async_copy(plan, rows, sems.at[0]),
        pltpu.make_async_copy(table_rows, table, sems.at[1]),
    ]
    for move in moves:
        move.start()
    field[...] = jnp.zeros_like(field)
    inner[...] = sens[...]
    for move in moves:
        move.wait()

    @pl.when(rows[2, 0] <= outer_slots)
    def _():
        take_observed(rows, table, slabs, observed, outer_slots, late_slots)
        inner[split:, :] = net_backward(observed, states, weights)

    land_blocks(rows, field, inner, 0, outer_slots + late_slots, per_tile, width)
    for tile in range(tiles):
        landing[tile] = field[tile * width : (tile + 1) * width, :]


def lon_back_kernel(far, close, own, taps, back, to_far, to_close, padded):
    tiles, width, _ = own.shape
    height, levels, _ = back.shape
    per_tile = height // tiles
    fill_padded(padded, far, own, close)
    for tile in range(tiles):
        rows = jnp.transpose(lon_conv(padded, taps, tile, 0, width))
        rows = rows.reshape(per_tile, levels, width)
        back[tile * per_tile : (tile + 1) * per_tile] = rows
    halve_for_sides(back, height, to_far, to_close)


def own_back_kernel(back, control, own_part):
    height = back.shape[0]
    for row in range(height):
        own_part[row] = lat_sum(back, row, 0, height, control[row])


def lat_back_kernel(far, close, own_part, gradient, halos, done, sems):
    halos[0], halos[1] = sides(far[...], close[...], "lat")
    height = own_part.shape[0]
    piece = height // BAND_PIECES
    moves = []
    for k in range(BAND_PIECES):
        part = pl.ds(k * piece, piece)
        for row in range(k * piece, (k + 1) * piece):
            done[row] = lat_rims(row, own_part[row], halos, height)
        moves.append(pltpu.make_async_copy(done.at[part], gradient.at[part], sems.at[k]))
        moves[-1].start()
    for move in moves:
        move.wait()


def exchange(to_far, to_close, axis, periodic):
    count = lax.axis_size(axis)
    far = []
    for odd in range(1, count, 2):
        if odd + 1 < count or periodic:
            far += [(odd, (odd + 1) % count), ((odd + 1) % count, odd)]
    close = [(i, i ^ 1) for i in range(count)]
    to_close, _ = lax.optimization_barrier((to_close, to_far))
    from_far, from_close = lax.ppermute(to_far, axis, far), lax.ppermute(to_close, axis, close)
    from_far = lax.optimization_barrier(from_far)
    from_close, _ = lax.optimization_barrier((from_close, from_far))
    return from_far, from_close, to_close


def shards(
    control,
    background,
    lon_width,
    block_cells,
    block_owner,
    channel_count,
    radiance,
    in_weight,
    in_bias,
    mid_weight,
    mid_bias,
    out_weight,
    out_bias,
):
    height, levels, width = control.shape
    hidden = mid_weight.shape[0]
    channels, columns = radiance.shape
    slot_count = block_owner.shape[0]
    recv_most = channel_count.shape[0]
    per_tile = LANES // levels
    tiles = height // per_tile
    slab_rows = BLOCK_COLS * channels // LANES
    f32, bf16, i32 = jnp.float32, jnp.bfloat16, jnp.int32
    shape = jax.ShapeDtypeStruct
    field = height * levels * width
    conv_flops = 2 * 33 * field

    halves = channels // LANES
    radiance = radiance.T.reshape(recv_most, BLOCK_COLS, halves, LANES)
    radiance = jnp.swapaxes(radiance, 1, 2).reshape(recv_most, slab_rows, LANES)
    half_field = shape(control.shape, bf16)
    slabs, to_far, to_close, held, ground = call(
        first_kernel,
        (
            shape((recv_most + 1, slab_rows, LANES), bf16),
            half_field,
            half_field,
            shape(control.shape, f32),
            shape(control.shape, f32),
        ),
        [HBM] * 5,
        (HBM,) + (VMEM,) * 4,
        0,
        24 * field,
        scratch=(
            pltpu.VMEM((1, slot_count), i32),
            pltpu.VMEM((1, recv_most), i32),
            pltpu.VMEM((slab_rows, LANES), f32),
            pltpu.VMEM((slab_rows, LANES), bf16),
            pltpu.SemaphoreType.DMA((5 + BAND_PIECES,)),
        ),
        name="slabs_halves",
    )(
        *pinned(
            radiance,
            block_owner.reshape(1, slot_count),
            channel_count.reshape(1, recv_most),
            control,
            background,
        )
    )
    far, close, sent = exchange(to_far, to_close, "lat", False)

    band = pltpu.VMEM((height, levels, width), f32)
    taps, turned, plan, own_part, *weights = call(
        prepare_kernel,
        (
            shape((tiles, 24, LANES), f32),
            shape((tiles, width, LANES), f32),
            shape((8, LANES), i32),
            shape(control.shape, f32),
            shape((LANES, hidden), bf16),
            shape((hidden, hidden), bf16),
            shape((hidden, channels), bf16),
            shape((1, hidden), f32),
            shape((1, hidden), f32),
            shape((1, channels), f32),
        ),
        [HBM] * 3 + [VMEM] * 2 + [HBM] * 6,
        (VMEM,) * 10,
        conv_flops // 2,
        12 * field,
        scratch=(
            pltpu.SMEM((height,), i32),
            pltpu.VMEM((1, slot_count), i32),
            pltpu.VMEM((1, slot_count), i32),
            pltpu.SemaphoreType.DMA((7 + per_tile + WEIGHT_PIECES,)),
        ),
        name="taps_background",
    )(
        *pinned(lon_width, block_cells.reshape(1, slot_count), block_owner.reshape(1, slot_count)),
        ground,
        held,
        *pinned(
            in_weight,
            in_bias.reshape(1, hidden),
            mid_weight,
            mid_bias.reshape(1, hidden),
            out_weight,
            out_bias.reshape(1, channels),
        ),
    )

    lat_count = lax.axis_size("lat")
    one, two, *others = swap_bits(lat_count)

    def swapped(part, apart, odd_apart=None):
        pairs = [(i, i ^ (odd_apart if odd_apart and i % 2 else apart)) for i in range(lat_count)]
        return lax.ppermute(part, "lat", pairs)

    slabs, _ = lax.optimization_barrier((slabs, sent))
    first, second = swapped(slabs, 1 << one), swapped(slabs, 1 << two)

    halos = pltpu.VMEM((2, REACH, levels, width), f32)
    smoothed, to_far, to_close = call(
        lat_smooth_kernel,
        (shape((tiles, width, LANES), f32),) + (shape((tiles, REACH, LANES), f32),) * 2,
        [VMEM] * 3,
        (VMEM,) * 3,
        LAT_COVER * conv_flops,
        LAT_COVER * 16 * field,
        scratch=(halos,),
        name="lat_smooth",
    )(far, close, own_part)
    far, close, _ = exchange(to_far, to_close, "lon", True)
    first, second, *_ = lax.optimization_barrier((first, second, to_far, to_close))
    passed = jnp.where(odd_index("lat"), first, second)
    near = [slabs, first, second, swapped(passed, 1 << one, 1 << two)]

    outer_slots = 3 * slot_count // 8
    late_slots = slot_count - outer_slots
    x_rows = slot_count * BLOCK_COLS
    outer_rows, late_rows = outer_slots * BLOCK_COLS, late_slots * BLOCK_COLS
    row_flops = 2 * hidden * (LANES + hidden + channels)
    def state_shapes(rows):
        return (shape((rows, hidden), bf16), shape((rows, hidden), bf16), shape((rows, channels), f32))

    plan_rows = pltpu.SMEM((8, LANES), i32)
    padded = pltpu.VMEM((tiles, width + 2 * REACH, LANES), f32)
    flat = pltpu.VMEM((tiles * width, LANES), f32)

    profile, *inner_states = call(
        functools.partial(inner_forward_kernel, per_tile, outer_slots),
        (shape((tiles * width, LANES), f32),) + state_shapes(late_rows),
        [ANY] + [VMEM] * 9,
        (VMEM,) * 4,
        LON_COVER * late_rows * row_flops,
        LON_COVER * 4 * 1024 * 1024,
        scratch=(plan_rows, padded, pltpu.VMEM((late_rows, LANES), f32), pltpu.SemaphoreType.DMA),
        name="inner_forward",
    )(plan, smoothed, turned, taps, *weights)
    *near, _ = lax.optimization_barrier((*near, profile))
    for bit in others:
        near = [jnp.concatenate(near, axis=0)]
        near.append(swapped(near[0], 1 << bit))
    near = [jnp.concatenate(near[:-1], axis=0), near[-1]]
    across = [swapped(part, 1) for part in near]

    states = call(
        functools.partial(outer_forward_kernel, per_tile),
        state_shapes(outer_rows) + state_shapes(late_rows),
        [ANY] + [VMEM] * 12,
        (VMEM,) * 6,
        SWAP_COVER * outer_rows * row_flops,
        SWAP_COVER * 4 * 1024 * 1024,
        scratch=(
            plan_rows,
            padded,
            flat,
            pltpu.VMEM((outer_rows, LANES), f32),
            pltpu.VMEM((late_rows, LANES), f32),
            pltpu.SemaphoreType.DMA,
        ),
        name="outer_forward",
    )(plan, far, close, smoothed, turned, taps, profile, *weights)

    slabs = [*near, *across]
    table, sens, to_far, to_close = call(
        functools.partial(outer_backward_kernel, per_tile, len(slabs), recv_most),
        (
            shape((8, LANES), i32),
            shape((x_rows, LANES), f32),
            shape((tiles, REACH, LANES), bf16),
            shape((tiles, REACH, LANES), bf16),
        ),
        [ANY] + [VMEM] * (len(slabs) + 9),
        (VMEM,) * 4,
        outer_rows * row_flops,
        4 * 1024 * 1024,
        scratch=(
            plan_rows,
            pltpu.SMEM((8, LANES), i32),
            pltpu.VMEM((outer_rows, channels), f32),
            pltpu.VMEM((late_rows, channels), f32),
            flat,
            pltpu.SemaphoreType.DMA((2,)),
        ),
        name="outer_backward",
    )(plan, *slabs, *weights[:3], *states)
    far, close, sent = exchange(to_far, to_close, "lon", True)

    landing = call(
        functools.partial(inner_backward_kernel, per_tile, len(slabs), outer_slots),
        shape((tiles, width, LANES), f32),
        [ANY, ANY] + [VMEM] * (len(slabs) + 7),
        VMEM,
        late_rows * row_flops,
        4 * 1024 * 1024,
        scratch=(
            plan_rows,
            pltpu.SMEM((8, LANES), i32),
            pltpu.VMEM((late_rows, channels), f32),
            pltpu.VMEM((x_rows, LANES), f32),
            flat,
            pltpu.SemaphoreType.DMA((2,)),
        ),
        name="inner_backward",
    )(plan, table, sens, *slabs, *weights[:3], *inner_states)

    back, to_far, to_close = call(
        lon_back_kernel,
        (shape((height, levels, width), f32), half_field, half_field),
        [VMEM] * 4,
        (VMEM,) * 3,
        conv_flops,
        8 * field,
        scratch=(pltpu.VMEM((tiles, width + 2 * REACH, LANES), f32),),
        name="lon_back",
    )(far, close, landing, taps)
    far, close, _ = exchange(to_far, to_close, "lat", False)
    own_part = call(
        own_back_kernel,
        shape((height, levels, width), f32),
        [VMEM, VMEM],
        VMEM,
        conv_flops // 2,
        12 * field,
        name="lat_back_own",
    )(back, held)
    return call(
        lat_back_kernel,
        shape((height, levels, width), f32),
        [VMEM] * 3,
        HBM,
        conv_flops // 2,
        16 * field,
        scratch=(halos, band, pltpu.SemaphoreType.DMA((BAND_PIECES,))),
        name="lat_back",
    )(far, close, own_part)


def solution(mesh):
    return jax.shard_map(
        shards,
        mesh=mesh,
        in_specs=(
            P("lat", None, "lon"),
            P("lat", None, "lon"),
            P("lat"),
            P("lat", "lon"),
            P("lat", "lon"),
            P("lat", "lon"),
            P("lat", "lon"),
            P(),
            P(),
            P(),
            P(),
            P(),
            P(),
        ),
        out_specs=P("lat", None, "lon"),
        check_vma=False,
    )
```

```python
import functools

import jax
import jax.numpy as jnp
import numpy as np
from jax import lax
from jax.experimental import pallas as pl
from jax.experimental.pallas import tpu as pltpu
from jax.sharding import PartitionSpec as P

REACH = 16
BLOCK_COLS = 8
LANES = 128
LAT_SIGMA = 8.0
WEIGHT_PIECES = 8
BAND_PIECES = 4
FEW_SLOTS = 8
LAT_COVER = 64
LON_COVER = 10
SWAP_COVER = 10
VMEM_BYTES = 40 * 1024 * 1024

VMEM = pl.BlockSpec(memory_space=pltpu.VMEM)
SMEM = pl.BlockSpec(memory_space=pltpu.SMEM)
HBM = pl.BlockSpec(memory_space=pltpu.HBM)
ANY = pl.BlockSpec(memory_space=pl.ANY)


def lat_taps():
    offsets = np.arange(-REACH, REACH + 1, dtype=np.float64)
    raw = np.exp(-offsets * offsets / (2.0 * LAT_SIGMA * LAT_SIGMA))
    return [float(v) for v in (raw / np.sqrt(np.sum(raw * raw))).astype(np.float32)]


def call(kernel, out_shape, in_specs, out_specs, flops, bytes_moved, scratch=(), name=None):
    return pl.pallas_call(
        kernel,
        out_shape=out_shape,
        in_specs=in_specs,
        out_specs=out_specs,
        scratch_shapes=list(scratch),
        compiler_params=pltpu.CompilerParams(vmem_limit_bytes=VMEM_BYTES),
        cost_estimate=pl.CostEstimate(flops=flops, bytes_accessed=bytes_moved, transcendentals=0),
        name=name,
    )


def pinned(*values):
    return [pltpu.with_memory_space_constraint(value, pltpu.HBM) for value in values]


def lat_sum(parts, row, first, height, start=None):
    taps = lat_taps()
    acc = start
    for k in range(height):
        j = first + k - row
        if abs(j) <= REACH:
            term = taps[j + REACH] * parts[k]
            acc = term if acc is None else acc + term
    return acc


def lat_rims(row, part, halos, height):
    low = lat_sum(halos.at[0], row, -REACH, REACH, part)
    return lat_sum(halos.at[1], row, height, REACH, low)


def fill_padded(padded, far, own, close):
    width = own.shape[1]
    low, high = sides(far[...], close[...], "lon")
    padded[:, 0:REACH, :] = low
    padded[:, REACH : REACH + width, :] = own[...]
    padded[:, REACH + width :, :] = high


def lon_conv(padded, taps, tile, start, width):
    middle = REACH + start
    acc = taps[tile, 0:1, :] * padded[tile, pl.ds(middle, width), :]
    for j in range(1, REACH + 1):
        both = padded[tile, pl.ds(middle + j, width), :] + padded[tile, pl.ds(middle - j, width), :]
        acc = acc + taps[tile, j : j + 1, :] * both
    return acc


def rounded(value):
    return value.astype(jnp.bfloat16).astype(jnp.float32)


def halved_rows(rows, order):
    halves, carry = {}, None
    for row in order:
        value = rows[row] if carry is None else rows[row] + carry
        halves[row] = value.astype(jnp.bfloat16)
        carry = value - halves[row].astype(jnp.float32)
    return [halves[row] for row in sorted(halves)]


def halve_for_sides(rows, height, to_far, to_close):
    odd = odd_index("lat")
    upward = halved_rows(rows, range(height - 1, -1, -1))
    downward = halved_rows(rows, range(height))
    for row in range(height):
        to_far[row] = jnp.where(odd, upward[row], downward[row])
        to_close[row] = jnp.where(odd, downward[row], upward[row])


def first_kernel(
    radiance,
    block_owner,
    channel_count,
    control,
    background,
    slabs,
    to_far,
    to_close,
    held,
    field,
    owners,
    counts,
    rows,
    tables,
    sems,
):
    recv_most = radiance.shape[0]
    moves = [
        pltpu.make_async_copy(radiance, slabs.at[pl.ds(0, recv_most)], sems.at[0]),
        pltpu.make_async_copy(block_owner, owners, sems.at[1]),
        pltpu.make_async_copy(channel_count, counts, sems.at[2]),
    ]
    piece = control.shape[0] // BAND_PIECES
    for k in range(BAND_PIECES):
        part = pl.ds(k * piece, piece)
        moves.append(pltpu.make_async_copy(control.at[part], held.at[part], sems.at[5 + k]))
    field_in = pltpu.make_async_copy(background, field, sems.at[4])
    for move in moves[3:] + moves[:3] + [field_in]:
        move.start()
    rows[...] = jnp.full(rows.shape, -1.0, jnp.float32)
    moves[1].wait()
    moves[2].wait()
    rows[0:1, 0 : owners.shape[1]] = owners[...].astype(jnp.float32)
    rows[1:2, 0 : counts.shape[1]] = counts[...].astype(jnp.float32)
    tables[...] = rows[...].astype(jnp.bfloat16)
    last = pltpu.make_async_copy(tables, slabs.at[recv_most], sems.at[3])
    last.start()
    for move in moves[3:]:
        move.wait()
    halve_for_sides(held, held.shape[0], to_far, to_close)
    moves[0].wait()
    field_in.wait()
    last.wait()


def prepare_kernel(
    lon_width,
    block_cells,
    block_owner,
    field,
    band,
    in_weight,
    in_bias,
    mid_weight,
    mid_bias,
    out_weight,
    out_bias,
    taps,
    turned,
    plan,
    own_part,
    wide_in,
    weight_two,
    weight_out,
    bias_one,
    bias_two,
    bias_out,
    widths,
    cells,
    owners,
    sems,
):
    moves = [
        pltpu.make_async_copy(lon_width, widths, sems.at[0]),
        pltpu.make_async_copy(block_cells, cells, sems.at[1]),
        pltpu.make_async_copy(block_owner, owners, sems.at[2]),
    ]
    tiles = turned.shape[0]
    height, levels, width = field.shape
    per_tile = height // tiles
    piece = mid_weight.shape[0] // WEIGHT_PIECES
    pieces = [pl.ds(k * piece, piece) for k in range(WEIGHT_PIECES)]
    loads = [(in_bias, bias_one), (mid_bias, bias_two), (out_bias, bias_out), (out_weight, weight_out)]
    loads += [(in_weight, wide_in.at[pl.ds(sub * levels, levels)]) for sub in range(per_tile)]
    loads += [(mid_weight.at[part], weight_two.at[part]) for part in pieces]
    loads = [
        pltpu.make_async_copy(source, target, sems.at[3 + k]) for k, (source, target) in enumerate(loads)
    ]
    for move in moves + loads:
        move.start()
    groups = width // BLOCK_COLS
    rim = REACH // BLOCK_COLS
    slot_count = cells.shape[1]

    for row in range(height):
        own_part[row] = lat_sum(band, row, 0, height)
    for tile in range(tiles):
        block = field[tile * per_tile : (tile + 1) * per_tile].reshape(per_tile * levels, width)
        turned[tile] = jnp.transpose(block)

    lane_row = lax.broadcasted_iota(jnp.int32, (1, LANES), 1) // levels
    steps = lax.broadcasted_iota(jnp.int32, (taps.shape[1], LANES), 0)
    dist = steps.astype(jnp.float32)
    weight = jnp.where(steps == 0, 1.0, jnp.where(steps <= REACH, 2.0, 0.0))
    moves[0].wait()
    for tile in range(tiles):
        spread = jnp.zeros((1, LANES), jnp.int32)
        for sub in range(per_tile):
            spread = jnp.where(lane_row == sub, widths[tile * per_tile + sub], spread)
        spread = spread.astype(jnp.float32)
        raw = jnp.exp(-dist * dist / (2.0 * spread * spread))
        norm = jnp.sum(weight * raw * raw, axis=0, keepdims=True)
        taps[tile] = raw / jnp.sqrt(norm)

    moves[1].wait()
    moves[2].wait()
    rows = lax.broadcasted_iota(jnp.int32, (slot_count, slot_count), 0)
    lanes = lax.broadcasted_iota(jnp.int32, (slot_count, slot_count), 1)
    group = cells[...] % groups
    outer = ((group < rim) | (group >= groups - rim)) & (owners[...] >= 0)
    outer_here = jnp.where(outer, 1, 0)
    outer_count = jnp.sum(outer_here, axis=1, keepdims=True)
    earlier = jnp.sum(jnp.where(lanes < rows, outer_here, 0), axis=1, keepdims=True)
    here = jnp.sum(jnp.where(lanes == rows, outer_here, 0), axis=1, keepdims=True)
    cell = jnp.sum(jnp.where(lanes == rows, cells[...], 0), axis=1, keepdims=True)
    position = jnp.where(here == 1, earlier, outer_count + rows[:, 0:1] - earlier)
    at = lax.broadcasted_iota(jnp.int32, (slot_count, LANES), 1)
    hit = position == at
    slot = lax.broadcasted_iota(jnp.int32, (slot_count, LANES), 0)
    plan[...] = jnp.zeros_like(plan)
    plan[0:1, :] = jnp.sum(jnp.where(hit, cell, 0), axis=0, keepdims=True)
    plan[1:2, :] = jnp.sum(jnp.where(hit, slot, 0), axis=0, keepdims=True)
    plan[2:3, :] = jnp.broadcast_to(outer_count, (1, LANES))
    live_count = jnp.sum(jnp.where(owners[...] >= 0, 1, 0), axis=1, keepdims=True)
    plan[3:4, :] = jnp.broadcast_to(live_count, (1, LANES))
    for move in loads:
        move.wait()


def swap_bits(count):
    return list(range(count.bit_length() - 2, 0, -1))


def routing(recv_most, slot_count, slabs, table):
    per_owner = recv_most + 1
    spans, count = [], 0
    for ref in slabs:
        spans.append((ref, count))
        count += ref.shape[0] // per_owner
    half = count // 2
    here = lax.axis_index("lat")
    rows = lax.broadcasted_iota(jnp.int32, (slot_count, LANES), 0)
    lanes = lax.broadcasted_iota(jnp.int32, (slot_count, LANES), 1)
    diagonal = rows == lanes
    zero = jnp.zeros((slot_count, LANES), jnp.int32)

    bits = swap_bits(count)

    def device_of(k):
        apart = jnp.where(k < half, 0, 1)
        for place, bit in enumerate(bits):
            apart = apart + (((k >> place) & 1) << bit)
        return here ^ apart

    def over_sets(step):
        acc = zero
        for ref, first in spans:

            def add(k, acc, ref=ref, first=first):
                lines = ref[k * per_owner + recv_most].astype(jnp.float32)
                owners, counts = lines[0:1].astype(jnp.int32), lines[1:2].astype(jnp.int32)
                return acc + step(device_of(first + k), owners, counts)

            acc = lax.fori_loop(0, ref.shape[0] // per_owner, add, acc, unroll=count <= 8)
        return jnp.sum(acc, axis=1, keepdims=True)

    mine = slabs[0][recv_most].astype(jnp.float32)[0:1].astype(jnp.int32)
    owner = jnp.sum(jnp.where(diagonal, mine, 0), axis=1, keepdims=True)

    def rank(device, owners, counts):
        before = (device < here) | ((device == here) & (lanes < rows))
        return jnp.where((owners == owner) & before, 1, 0)

    arrival = over_sets(rank)

    def counted(device, owners, counts):
        return jnp.where((owner == device) & (lanes == arrival), counts, 0)

    kept = over_sets(counted)
    apart = owner ^ here
    entry = (apart & 1) * half
    for place, bit in enumerate(bits):
        entry = entry + (((apart >> bit) & 1) << place)
    target = jnp.where(owner >= 0, entry * per_owner + arrival, 0)
    table[...] = jnp.zeros_like(table)
    for row, column in enumerate((target, kept)):
        table[row : row + 1, :] = jnp.sum(jnp.where(diagonal, column, 0), axis=0, keepdims=True)


def odd_index(axis):
    return lax.axis_index(axis) % 2 == 1


def sides(far, close, axis):
    odd = odd_index(axis)
    far, close = far.astype(jnp.float32), close.astype(jnp.float32)
    return jnp.where(odd, close, far), jnp.where(odd, far, close)


def split_sides(low, high, axis):
    odd = odd_index(axis)
    return jnp.where(odd, high, low), jnp.where(odd, low, high)


def lat_smooth_kernel(far, close, own_part, smoothed, to_far, to_close, halos):
    tiles = smoothed.shape[0]
    height, levels, width = own_part.shape
    per_tile = height // tiles
    halos[0], halos[1] = sides(far[...], close[...], "lat")
    for tile in range(tiles):
        rows = range(tile * per_tile, (tile + 1) * per_tile)
        rows = [lat_rims(row, own_part[row], halos, height) for row in rows]
        turned = jnp.transpose(jnp.concatenate(rows, axis=0))
        smoothed[tile] = turned
        to_far[tile], to_close[tile] = split_sides(turned[0:REACH], turned[width - REACH : width], "lon")


def block_place(plan, position, groups, per_tile, width):
    block = plan[0, position]
    row = block // groups
    start = (row // per_tile) * width + (block % groups) * BLOCK_COLS
    return pl.multiple_of(start, BLOCK_COLS), row % per_tile


def take_blocks(plan, profile, picked, first, count, per_tile, width):
    groups = width // BLOCK_COLS
    lane_row = lax.broadcasted_iota(jnp.int32, (BLOCK_COLS, LANES), 1) // (LANES // per_tile)
    for k in range(count):
        start, sub = block_place(plan, first + k, groups, per_tile, width)
        block = profile[pl.ds(start, BLOCK_COLS), :]
        picked[k * BLOCK_COLS : (k + 1) * BLOCK_COLS, :] = jnp.where(lane_row == sub, block, 0.0)


def land_blocks(plan, field, sens, first, count, per_tile, width):
    groups = width // BLOCK_COLS
    lane_row = lax.broadcasted_iota(jnp.int32, (BLOCK_COLS, LANES), 1) // (LANES // per_tile)
    for k in range(first, first + count):
        start, sub = block_place(plan, k, groups, per_tile, width)
        block = sens[k * BLOCK_COLS : (k + 1) * BLOCK_COLS, :]
        field[pl.ds(start, BLOCK_COLS), :] += jnp.where(lane_row == sub, block, 0.0)


def take_observed(plan, table, slabs, observed, first, count):
    channels = observed.shape[1]
    channel = lax.broadcasted_iota(jnp.int32, (BLOCK_COLS, LANES), 1)
    for k in range(count):
        slot = plan[1, first + k]
        at, kept = table[0, slot], table[1, slot]
        slab, start = None, 0
        for ref in slabs:
            size = ref.shape[0]
            found = ref[jnp.clip(at - start, 0, size - 1)].astype(jnp.float32)
            slab = found if slab is None else jnp.where(at >= start, found, slab)
            start += size
        for h in range(channels // LANES):
            part = slab[h * BLOCK_COLS : (h + 1) * BLOCK_COLS]
            part = jnp.where(channel + h * LANES < kept, part, jnp.inf)
            observed[k * BLOCK_COLS : (k + 1) * BLOCK_COLS, h * LANES : (h + 1) * LANES] = part


def dot(a, b):
    return jnp.dot(a, b, preferred_element_type=jnp.float32)


def dot_t(a, b):
    return lax.dot_general(a, b, (((1,), (1,)), ((), ())), preferred_element_type=jnp.float32)


def net_first(picked, weights, act_one):
    inputs = picked[...].astype(jnp.bfloat16)
    act_one[...] = jnp.tanh(dot(inputs, weights[0][...]) + weights[3][...]).astype(jnp.bfloat16)


def net_rest(weights, states):
    _, weight_two, weight_out, _, bias_two, bias_out = weights
    act_one, act_two, emitted = states
    act_two[...] = jnp.tanh(dot(act_one[...], weight_two[...]) + bias_two[...]).astype(jnp.bfloat16)
    emitted[...] = dot(act_two[...], weight_out[...]) + bias_out[...]


def net_forward(picked, weights, states):
    net_first(picked, weights, states[0])
    net_rest(weights, states)


def net_backward(observed, states, weights):
    wide_in, weight_two, weight_out = weights[:3]
    act_one, act_two, emitted = states
    seen = observed[...]
    misfit = jnp.where(seen < jnp.inf, emitted[...] - seen, 0.0).astype(jnp.bfloat16)
    two = act_two[...].astype(jnp.float32)
    grad_two = (dot_t(misfit, weight_out[...]) * (1.0 - two * two)).astype(jnp.bfloat16)
    one = act_one[...].astype(jnp.float32)
    grad_one = (dot_t(grad_two, weight_two[...]) * (1.0 - one * one)).astype(jnp.bfloat16)
    return rounded(dot_t(grad_one, wide_in[...]))


def few_of(ref):
    return ref.at[pl.ds(0, FEW_SLOTS * BLOCK_COLS)]


def inner_forward_kernel(per_tile, outer_slots, plan, own, turned, taps, *refs):
    weights, profile, states, (rows, padded, picked, sem) = refs[:6], refs[6], refs[7:10], refs[10:]
    tiles, width, _ = own.shape
    count = picked.shape[0] // BLOCK_COLS
    plan_in = pltpu.make_async_copy(plan, rows, sem)
    plan_in.start()
    zeros = jnp.zeros((tiles, REACH, LANES), jnp.float32)
    padded[:, 0:REACH, :] = zeros
    padded[:, REACH : REACH + width, :] = own[...]
    padded[:, REACH + width :, :] = zeros
    for tile in range(tiles):
        total = turned[tile] + lon_conv(padded, taps, tile, 0, width)
        profile[tile * width : (tile + 1) * width, :] = rounded(total)
    plan_in.wait()

    in_time, many = rows[2, 0] <= outer_slots, rows[3, 0] > outer_slots + FEW_SLOTS

    @pl.when(in_time & many)
    def _():
        take_blocks(rows, profile, picked, outer_slots, count, per_tile, width)
        net_forward(picked, weights, states)

    @pl.when(in_time & ~many)
    def _():
        take_blocks(rows, profile, picked, outer_slots, FEW_SLOTS, per_tile, width)
        net_forward(few_of(picked), weights, [few_of(state) for state in states])


def outer_forward_kernel(
    per_tile,
    plan,
    far,
    close,
    own,
    turned,
    taps,
    inner_profile,
    *refs,
):
    weights, states, late_states, (rows, padded, profile, picked, late_picked, sem) = (
        refs[:6],
        refs[6:9],
        refs[9:12],
        refs[12:],
    )
    tiles, width, _ = own.shape
    outer_slots = picked.shape[0] // BLOCK_COLS
    late_slots = late_picked.shape[0] // BLOCK_COLS
    plan_in = pltpu.make_async_copy(plan, rows, sem)
    plan_in.start()
    fill_padded(padded, far, own, close)
    profile[...] = inner_profile[...]
    for tile in range(tiles):
        for start in (0, width - REACH):
            total = turned[tile, start : start + REACH, :] + lon_conv(padded, taps, tile, start, REACH)
            profile[tile * width + start : tile * width + start + REACH, :] = rounded(total)
    plan_in.wait()
    take_blocks(rows, profile, picked, 0, outer_slots, per_tile, width)
    net_forward(picked, weights, states)

    @pl.when(rows[2, 0] > outer_slots)
    def _():
        take_blocks(rows, profile, late_picked, outer_slots, late_slots, per_tile, width)
        net_forward(late_picked, weights, late_states)


def outer_backward_kernel(per_tile, parts, recv_most, plan, *refs):
    slabs, refs = refs[:parts], refs[parts:]
    weights, states, late_states, refs = refs[:3], refs[3:6], refs[6:9], refs[9:]
    (table_rows, sens, to_far, to_close) = refs[:4]
    (rows, table, observed, late_observed, field, sems) = refs[4:]
    tiles = to_far.shape[0]
    width = field.shape[0] // tiles
    outer_slots = observed.shape[0] // BLOCK_COLS
    late_slots = late_observed.shape[0] // BLOCK_COLS

    plan_in = pltpu.make_async_copy(plan, rows, sems.at[0])
    plan_in.start()
    routing(recv_most, outer_slots + late_slots, slabs, table_rows)
    table_in = pltpu.make_async_copy(table_rows, table, sems.at[1])
    table_in.start()
    field[...] = jnp.zeros_like(field)
    plan_in.wait()
    table_in.wait()

    take_observed(rows, table, slabs, observed, 0, outer_slots)
    sens[0 : outer_slots * BLOCK_COLS, :] = net_backward(observed, states, weights)
    land_blocks(rows, field, sens, 0, outer_slots, per_tile, width)

    @pl.when(rows[2, 0] > outer_slots)
    def _():
        take_observed(rows, table, slabs, late_observed, outer_slots, late_slots)
        sens[outer_slots * BLOCK_COLS :, :] = net_backward(late_observed, late_states, weights)
        land_blocks(rows, field, sens, outer_slots, late_slots, per_tile, width)

    for tile in range(tiles):
        low = field[tile * width : tile * width + REACH, :]
        high = field[(tile + 1) * width - REACH : (tile + 1) * width, :]
        low, high = split_sides(low, high, "lon")
        to_far[tile], to_close[tile] = low.astype(jnp.bfloat16), high.astype(jnp.bfloat16)


def inner_backward_kernel(per_tile, parts, outer_slots, plan, table_rows, sens, *refs):
    slabs, refs = refs[:parts], refs[parts:]
    weights, states, refs = refs[:3], refs[3:6], refs[6:]
    landing, rows, table, observed, inner, field, sems = refs
    tiles, width, _ = landing.shape
    late_slots = observed.shape[0] // BLOCK_COLS
    split = outer_slots * BLOCK_COLS
    moves = [
        pltpu.make_async_copy(plan, rows, sems.at[0]),
        pltpu.make_async_copy(table_rows, table, sems.at[1]),
    ]
    for move in moves:
        move.start()
    field[...] = jnp.zeros_like(field)
    inner[...] = sens[...]
    for move in moves:
        move.wait()

    in_time, many = rows[2, 0] <= outer_slots, rows[3, 0] > outer_slots + FEW_SLOTS
    first = outer_slots + FEW_SLOTS

    @pl.when(in_time & many)
    def _():
        take_observed(rows, table, slabs, observed, outer_slots, late_slots)
        inner[split:, :] = net_backward(observed, states, weights)

    @pl.when(in_time & ~many)
    def _():
        take_observed(rows, table, slabs, observed, outer_slots, FEW_SLOTS)
        inner[split : split + FEW_SLOTS * BLOCK_COLS, :] = net_backward(
            few_of(observed), [few_of(state) for state in states], weights
        )

    land_blocks(rows, field, inner, 0, first, per_tile, width)

    @pl.when(many)
    def _():
        land_blocks(rows, field, inner, first, outer_slots + late_slots - first, per_tile, width)

    for tile in range(tiles):
        landing[tile] = field[tile * width : (tile + 1) * width, :]


def lon_back_kernel(far, close, own, taps, back, to_far, to_close, padded):
    tiles, width, _ = own.shape
    height, levels, _ = back.shape
    per_tile = height // tiles
    fill_padded(padded, far, own, close)
    for tile in range(tiles):
        rows = jnp.transpose(lon_conv(padded, taps, tile, 0, width))
        rows = rows.reshape(per_tile, levels, width)
        back[tile * per_tile : (tile + 1) * per_tile] = rows
    halve_for_sides(back, height, to_far, to_close)


def own_back_kernel(back, control, own_part):
    height = back.shape[0]
    for row in range(height):
        own_part[row] = lat_sum(back, row, 0, height, control[row])


def lat_back_kernel(far, close, own_part, gradient, halos, done, sems):
    halos[0], halos[1] = sides(far[...], close[...], "lat")
    height = own_part.shape[0]
    piece = height // BAND_PIECES
    moves = []
    for k in range(BAND_PIECES):
        part = pl.ds(k * piece, piece)
        for row in range(k * piece, (k + 1) * piece):
            done[row] = lat_rims(row, own_part[row], halos, height)
        moves.append(pltpu.make_async_copy(done.at[part], gradient.at[part], sems.at[k]))
        moves[-1].start()
    for move in moves:
        move.wait()


def exchange(to_far, to_close, axis, periodic):
    count = lax.axis_size(axis)
    far = []
    for odd in range(1, count, 2):
        if odd + 1 < count or periodic:
            far += [(odd, (odd + 1) % count), ((odd + 1) % count, odd)]
    close = [(i, i ^ 1) for i in range(count)]
    to_close, _ = lax.optimization_barrier((to_close, to_far))
    from_far, from_close = lax.ppermute(to_far, axis, far), lax.ppermute(to_close, axis, close)
    from_far = lax.optimization_barrier(from_far)
    from_close, _ = lax.optimization_barrier((from_close, from_far))
    return from_far, from_close, to_close


def shards(
    control,
    background,
    lon_width,
    block_cells,
    block_owner,
    channel_count,
    radiance,
    in_weight,
    in_bias,
    mid_weight,
    mid_bias,
    out_weight,
    out_bias,
):
    height, levels, width = control.shape
    hidden = mid_weight.shape[0]
    channels, columns = radiance.shape
    slot_count = block_owner.shape[0]
    recv_most = channel_count.shape[0]
    per_tile = LANES // levels
    tiles = height // per_tile
    slab_rows = BLOCK_COLS * channels // LANES
    f32, bf16, i32 = jnp.float32, jnp.bfloat16, jnp.int32
    shape = jax.ShapeDtypeStruct
    field = height * levels * width
    conv_flops = 2 * 33 * field

    halves = channels // LANES
    radiance = radiance.T.reshape(recv_most, BLOCK_COLS, halves, LANES)
    radiance = jnp.swapaxes(radiance, 1, 2).reshape(recv_most, slab_rows, LANES)
    half_field = shape(control.shape, bf16)
    slabs, to_far, to_close, held, ground = call(
        first_kernel,
        (
            shape((recv_most + 1, slab_rows, LANES), bf16),
            half_field,
            half_field,
            shape(control.shape, f32),
            shape(control.shape, f32),
        ),
        [HBM] * 5,
        (HBM,) + (VMEM,) * 4,
        0,
        24 * field,
        scratch=(
            pltpu.VMEM((1, slot_count), i32),
            pltpu.VMEM((1, recv_most), i32),
            pltpu.VMEM((slab_rows, LANES), f32),
            pltpu.VMEM((slab_rows, LANES), bf16),
            pltpu.SemaphoreType.DMA((5 + BAND_PIECES,)),
        ),
        name="slabs_halves",
    )(
        *pinned(
            radiance,
            block_owner.reshape(1, slot_count),
            channel_count.reshape(1, recv_most),
            control,
            background,
        )
    )
    far, close, sent = exchange(to_far, to_close, "lat", False)

    band = pltpu.VMEM((height, levels, width), f32)
    taps, turned, plan, own_part, *weights = call(
        prepare_kernel,
        (
            shape((tiles, 24, LANES), f32),
            shape((tiles, width, LANES), f32),
            shape((8, LANES), i32),
            shape(control.shape, f32),
            shape((LANES, hidden), bf16),
            shape((hidden, hidden), bf16),
            shape((hidden, channels), bf16),
            shape((1, hidden), f32),
            shape((1, hidden), f32),
            shape((1, channels), f32),
        ),
        [HBM] * 3 + [VMEM] * 2 + [HBM] * 6,
        (VMEM,) * 10,
        conv_flops // 2,
        12 * field,
        scratch=(
            pltpu.SMEM((height,), i32),
            pltpu.VMEM((1, slot_count), i32),
            pltpu.VMEM((1, slot_count), i32),
            pltpu.SemaphoreType.DMA((7 + per_tile + WEIGHT_PIECES,)),
        ),
        name="taps_background",
    )(
        *pinned(lon_width, block_cells.reshape(1, slot_count), block_owner.reshape(1, slot_count)),
        ground,
        held,
        *pinned(
            in_weight,
            in_bias.reshape(1, hidden),
            mid_weight,
            mid_bias.reshape(1, hidden),
            out_weight,
            out_bias.reshape(1, channels),
        ),
    )

    lat_count = lax.axis_size("lat")
    one, two, *others = swap_bits(lat_count)

    def swapped(part, apart):
        return lax.ppermute(part, "lat", [(i, i ^ apart) for i in range(lat_count)])

    later, _ = lax.optimization_barrier((slabs, sent))
    near = [slabs, swapped(later, 1 << one), swapped(later, 1 << two), swapped(slabs, (1 << one) + (1 << two))]

    halos = pltpu.VMEM((2, REACH, levels, width), f32)
    smoothed, to_far, to_close = call(
        lat_smooth_kernel,
        (shape((tiles, width, LANES), f32),) + (shape((tiles, REACH, LANES), f32),) * 2,
        [VMEM] * 3,
        (VMEM,) * 3,
        LAT_COVER * conv_flops,
        LAT_COVER * 16 * field,
        scratch=(halos,),
        name="lat_smooth",
    )(far, close, own_part)
    far, close, _ = exchange(to_far, to_close, "lon", True)

    outer_slots = 3 * slot_count // 8
    late_slots = slot_count - outer_slots
    x_rows = slot_count * BLOCK_COLS
    outer_rows, late_rows = outer_slots * BLOCK_COLS, late_slots * BLOCK_COLS
    row_flops = 2 * hidden * (LANES + hidden + channels)
    def state_shapes(rows):
        return (shape((rows, hidden), bf16), shape((rows, hidden), bf16), shape((rows, channels), f32))

    plan_rows = pltpu.SMEM((8, LANES), i32)
    padded = pltpu.VMEM((tiles, width + 2 * REACH, LANES), f32)
    flat = pltpu.VMEM((tiles * width, LANES), f32)

    profile, *inner_states = call(
        functools.partial(inner_forward_kernel, per_tile, outer_slots),
        (shape((tiles * width, LANES), f32),) + state_shapes(late_rows),
        [ANY] + [VMEM] * 9,
        (VMEM,) * 4,
        LON_COVER * late_rows * row_flops,
        LON_COVER * 4 * 1024 * 1024,
        scratch=(plan_rows, padded, pltpu.VMEM((late_rows, LANES), f32), pltpu.SemaphoreType.DMA),
        name="inner_forward",
    )(plan, smoothed, turned, taps, *weights)
    *near, _ = lax.optimization_barrier((*near, profile))
    for bit in others:
        near = [jnp.concatenate(near, axis=0)]
        near.append(swapped(near[0], 1 << bit))
    near = [jnp.concatenate(near[:-1], axis=0), near[-1]]
    across = [swapped(part, 1) for part in near]

    states = call(
        functools.partial(outer_forward_kernel, per_tile),
        state_shapes(outer_rows) + state_shapes(late_rows),
        [ANY] + [VMEM] * 12,
        (VMEM,) * 6,
        SWAP_COVER * outer_rows * row_flops,
        SWAP_COVER * 4 * 1024 * 1024,
        scratch=(
            plan_rows,
            padded,
            flat,
            pltpu.VMEM((outer_rows, LANES), f32),
            pltpu.VMEM((late_rows, LANES), f32),
            pltpu.SemaphoreType.DMA,
        ),
        name="outer_forward",
    )(plan, far, close, smoothed, turned, taps, profile, *weights)

    slabs = [*near, *across]
    table, sens, to_far, to_close = call(
        functools.partial(outer_backward_kernel, per_tile, len(slabs), recv_most),
        (
            shape((8, LANES), i32),
            shape((x_rows, LANES), f32),
            shape((tiles, REACH, LANES), bf16),
            shape((tiles, REACH, LANES), bf16),
        ),
        [ANY] + [VMEM] * (len(slabs) + 9),
        (VMEM,) * 4,
        outer_rows * row_flops,
        4 * 1024 * 1024,
        scratch=(
            plan_rows,
            pltpu.SMEM((8, LANES), i32),
            pltpu.VMEM((outer_rows, channels), f32),
            pltpu.VMEM((late_rows, channels), f32),
            flat,
            pltpu.SemaphoreType.DMA((2,)),
        ),
        name="outer_backward",
    )(plan, *slabs, *weights[:3], *states)
    far, close, sent = exchange(to_far, to_close, "lon", True)

    landing = call(
        functools.partial(inner_backward_kernel, per_tile, len(slabs), outer_slots),
        shape((tiles, width, LANES), f32),
        [ANY, ANY] + [VMEM] * (len(slabs) + 7),
        VMEM,
        late_rows * row_flops,
        4 * 1024 * 1024,
        scratch=(
            plan_rows,
            pltpu.SMEM((8, LANES), i32),
            pltpu.VMEM((late_rows, channels), f32),
            pltpu.VMEM((x_rows, LANES), f32),
            flat,
            pltpu.SemaphoreType.DMA((2,)),
        ),
        name="inner_backward",
    )(plan, table, sens, *slabs, *weights[:3], *inner_states)

    back, to_far, to_close = call(
        lon_back_kernel,
        (shape((height, levels, width), f32), half_field, half_field),
        [VMEM] * 4,
        (VMEM,) * 3,
        conv_flops,
        8 * field,
        scratch=(pltpu.VMEM((tiles, width + 2 * REACH, LANES), f32),),
        name="lon_back",
    )(far, close, landing, taps)
    far, close, _ = exchange(to_far, to_close, "lat", False)
    own_part = call(
        own_back_kernel,
        shape((height, levels, width), f32),
        [VMEM, VMEM],
        VMEM,
        conv_flops // 2,
        12 * field,
        name="lat_back_own",
    )(back, held)
    return call(
        lat_back_kernel,
        shape((height, levels, width), f32),
        [VMEM] * 3,
        HBM,
        conv_flops // 2,
        16 * field,
        scratch=(halos, band, pltpu.SemaphoreType.DMA((BAND_PIECES,))),
        name="lat_back",
    )(far, close, own_part)


def solution(mesh):
    return jax.shard_map(
        shards,
        mesh=mesh,
        in_specs=(
            P("lat", None, "lon"),
            P("lat", None, "lon"),
            P("lat"),
            P("lat", "lon"),
            P("lat", "lon"),
            P("lat", "lon"),
            P("lat", "lon"),
            P(),
            P(),
            P(),
            P(),
            P(),
            P(),
        ),
        out_specs=P("lat", None, "lon"),
        check_vma=False,
    )
```

```python
import functools

import jax
import jax.numpy as jnp
import numpy as np
from jax import lax
from jax.experimental import pallas as pl
from jax.experimental.pallas import tpu as pltpu
from jax.sharding import PartitionSpec as P

REACH = 16
BLOCK_COLS = 8
LANES = 128
LAT_SIGMA = 8.0
WEIGHT_PIECES = 4
BAND_PIECES = 4
FEW_SLOTS = 8
LAT_COVER = 64
LON_COVER = 10
SWAP_COVER = 10
VMEM_BYTES = 40 * 1024 * 1024

VMEM = pl.BlockSpec(memory_space=pltpu.VMEM)
SMEM = pl.BlockSpec(memory_space=pltpu.SMEM)
HBM = pl.BlockSpec(memory_space=pltpu.HBM)
ANY = pl.BlockSpec(memory_space=pl.ANY)


def lat_taps():
    offsets = np.arange(-REACH, REACH + 1, dtype=np.float64)
    raw = np.exp(-offsets * offsets / (2.0 * LAT_SIGMA * LAT_SIGMA))
    return [float(v) for v in (raw / np.sqrt(np.sum(raw * raw))).astype(np.float32)]


def call(kernel, out_shape, in_specs, out_specs, flops, bytes_moved, scratch=(), name=None):
    return pl.pallas_call(
        kernel,
        out_shape=out_shape,
        in_specs=in_specs,
        out_specs=out_specs,
        scratch_shapes=list(scratch),
        compiler_params=pltpu.CompilerParams(vmem_limit_bytes=VMEM_BYTES),
        cost_estimate=pl.CostEstimate(flops=flops, bytes_accessed=bytes_moved, transcendentals=0),
        name=name,
    )


def pinned(*values):
    return [pltpu.with_memory_space_constraint(value, pltpu.HBM) for value in values]


def lat_sum(parts, row, first, height, start=None):
    taps = lat_taps()
    acc = start
    for k in range(height):
        j = first + k - row
        if abs(j) <= REACH:
            term = taps[j + REACH] * parts[k]
            acc = term if acc is None else acc + term
    return acc


def lat_rims(row, part, halos, height):
    low = lat_sum(halos.at[0], row, -REACH, REACH, part)
    return lat_sum(halos.at[1], row, height, REACH, low)


def fill_padded(padded, far, own, close):
    width = own.shape[1]
    low, high = sides(far[...], close[...], "lon")
    padded[:, 0:REACH, :] = low
    padded[:, REACH : REACH + width, :] = own[...]
    padded[:, REACH + width :, :] = high


def lon_conv(padded, taps, tile, start, width):
    middle = REACH + start
    acc = taps[tile, 0:1, :] * padded[tile, pl.ds(middle, width), :]
    for j in range(1, REACH + 1):
        both = padded[tile, pl.ds(middle + j, width), :] + padded[tile, pl.ds(middle - j, width), :]
        acc = acc + taps[tile, j : j + 1, :] * both
    return acc


def rounded(value):
    return value.astype(jnp.bfloat16).astype(jnp.float32)


def halved_rows(rows, order):
    halves, carry = {}, None
    for row in order:
        value = rows[row] if carry is None else rows[row] + carry
        halves[row] = value.astype(jnp.bfloat16)
        carry = value - halves[row].astype(jnp.float32)
    return [halves[row] for row in sorted(halves)]


def halve_for_sides(rows, height, to_far, to_close):
    odd = odd_index("lat")
    upward = halved_rows(rows, range(height - 1, -1, -1))
    downward = halved_rows(rows, range(height))
    for row in range(height):
        to_far[row] = jnp.where(odd, upward[row], downward[row])
        to_close[row] = jnp.where(odd, downward[row], upward[row])


def first_kernel(
    radiance,
    block_owner,
    channel_count,
    control,
    background,
    slabs,
    to_far,
    to_close,
    held,
    field,
    owners,
    counts,
    rows,
    tables,
    sems,
):
    recv_most = radiance.shape[0]
    moves = [
        pltpu.make_async_copy(radiance, slabs.at[pl.ds(0, recv_most)], sems.at[0]),
        pltpu.make_async_copy(block_owner, owners, sems.at[1]),
        pltpu.make_async_copy(channel_count, counts, sems.at[2]),
    ]
    piece = control.shape[0] // BAND_PIECES
    for k in range(BAND_PIECES):
        part = pl.ds(k * piece, piece)
        moves.append(pltpu.make_async_copy(control.at[part], held.at[part], sems.at[5 + k]))
    field_in = pltpu.make_async_copy(background, field, sems.at[4])
    for move in moves[3:] + moves[:3] + [field_in]:
        move.start()
    rows[...] = jnp.full(rows.shape, -1.0, jnp.float32)
    moves[1].wait()
    moves[2].wait()
    rows[0:1, 0 : owners.shape[1]] = owners[...].astype(jnp.float32)
    rows[1:2, 0 : counts.shape[1]] = counts[...].astype(jnp.float32)
    tables[...] = rows[...].astype(jnp.bfloat16)
    last = pltpu.make_async_copy(tables, slabs.at[recv_most], sems.at[3])
    last.start()
    for move in moves[3:]:
        move.wait()
    halve_for_sides(held, held.shape[0], to_far, to_close)
    moves[0].wait()
    field_in.wait()
    last.wait()


def prepare_kernel(
    lon_width,
    block_cells,
    block_owner,
    field,
    band,
    taps,
    turned,
    plan,
    own_part,
    widths,
    cells,
    owners,
    sems,
):
    moves = [
        pltpu.make_async_copy(lon_width, widths, sems.at[0]),
        pltpu.make_async_copy(block_cells, cells, sems.at[1]),
        pltpu.make_async_copy(block_owner, owners, sems.at[2]),
    ]
    tiles = turned.shape[0]
    height, levels, width = field.shape
    per_tile = height // tiles
    for move in moves:
        move.start()
    groups = width // BLOCK_COLS
    rim = REACH // BLOCK_COLS
    slot_count = cells.shape[1]

    for row in range(height):
        own_part[row] = lat_sum(band, row, 0, height)
    for tile in range(tiles):
        block = field[tile * per_tile : (tile + 1) * per_tile].reshape(per_tile * levels, width)
        turned[tile] = jnp.transpose(block)

    lane_row = lax.broadcasted_iota(jnp.int32, (1, LANES), 1) // levels
    steps = lax.broadcasted_iota(jnp.int32, (taps.shape[1], LANES), 0)
    dist = steps.astype(jnp.float32)
    weight = jnp.where(steps == 0, 1.0, jnp.where(steps <= REACH, 2.0, 0.0))
    moves[0].wait()
    for tile in range(tiles):
        spread = jnp.zeros((1, LANES), jnp.int32)
        for sub in range(per_tile):
            spread = jnp.where(lane_row == sub, widths[tile * per_tile + sub], spread)
        spread = spread.astype(jnp.float32)
        raw = jnp.exp(-dist * dist / (2.0 * spread * spread))
        norm = jnp.sum(weight * raw * raw, axis=0, keepdims=True)
        taps[tile] = raw / jnp.sqrt(norm)

    moves[1].wait()
    moves[2].wait()
    rows = lax.broadcasted_iota(jnp.int32, (slot_count, slot_count), 0)
    lanes = lax.broadcasted_iota(jnp.int32, (slot_count, slot_count), 1)
    group = cells[...] % groups
    outer = ((group < rim) | (group >= groups - rim)) & (owners[...] >= 0)
    outer_here = jnp.where(outer, 1, 0)
    outer_count = jnp.sum(outer_here, axis=1, keepdims=True)
    earlier = jnp.sum(jnp.where(lanes < rows, outer_here, 0), axis=1, keepdims=True)
    here = jnp.sum(jnp.where(lanes == rows, outer_here, 0), axis=1, keepdims=True)
    cell = jnp.sum(jnp.where(lanes == rows, cells[...], 0), axis=1, keepdims=True)
    position = jnp.where(here == 1, earlier, outer_count + rows[:, 0:1] - earlier)
    at = lax.broadcasted_iota(jnp.int32, (slot_count, LANES), 1)
    hit = position == at
    slot = lax.broadcasted_iota(jnp.int32, (slot_count, LANES), 0)
    plan[...] = jnp.zeros_like(plan)
    plan[0:1, :] = jnp.sum(jnp.where(hit, cell, 0), axis=0, keepdims=True)
    plan[1:2, :] = jnp.sum(jnp.where(hit, slot, 0), axis=0, keepdims=True)
    plan[2:3, :] = jnp.broadcast_to(outer_count, (1, LANES))
    live_count = jnp.sum(jnp.where(owners[...] >= 0, 1, 0), axis=1, keepdims=True)
    plan[3:4, :] = jnp.broadcast_to(live_count, (1, LANES))


def swap_bits(count):
    return list(range(count.bit_length() - 2, 0, -1))


def routing(recv_most, slot_count, slabs, table):
    per_owner = recv_most + 1
    spans, count = [], 0
    for ref in slabs:
        spans.append((ref, count))
        count += ref.shape[0] // per_owner
    half = count // 2
    here = lax.axis_index("lat")
    rows = lax.broadcasted_iota(jnp.int32, (slot_count, LANES), 0)
    lanes = lax.broadcasted_iota(jnp.int32, (slot_count, LANES), 1)
    diagonal = rows == lanes
    zero = jnp.zeros((slot_count, LANES), jnp.int32)

    bits = swap_bits(count)

    def device_of(k):
        apart = jnp.where(k < half, 0, 1)
        for place, bit in enumerate(bits):
            apart = apart + (((k >> place) & 1) << bit)
        return here ^ apart

    def over_sets(step):
        acc = zero
        for ref, first in spans:

            def add(k, acc, ref=ref, first=first):
                lines = ref[k * per_owner + recv_most].astype(jnp.float32)
                owners, counts = lines[0:1].astype(jnp.int32), lines[1:2].astype(jnp.int32)
                return acc + step(device_of(first + k), owners, counts)

            acc = lax.fori_loop(0, ref.shape[0] // per_owner, add, acc, unroll=count <= 8)
        return jnp.sum(acc, axis=1, keepdims=True)

    mine = slabs[0][recv_most].astype(jnp.float32)[0:1].astype(jnp.int32)
    owner = jnp.sum(jnp.where(diagonal, mine, 0), axis=1, keepdims=True)

    def rank(device, owners, counts):
        before = (device < here) | ((device == here) & (lanes < rows))
        return jnp.where((owners == owner) & before, 1, 0)

    arrival = over_sets(rank)

    def counted(device, owners, counts):
        return jnp.where((owner == device) & (lanes == arrival), counts, 0)

    kept = over_sets(counted)
    apart = owner ^ here
    entry = (apart & 1) * half
    for place, bit in enumerate(bits):
        entry = entry + (((apart >> bit) & 1) << place)
    target = jnp.where(owner >= 0, entry * per_owner + arrival, 0)
    table[...] = jnp.zeros_like(table)
    for row, column in enumerate((target, kept)):
        table[row : row + 1, :] = jnp.sum(jnp.where(diagonal, column, 0), axis=0, keepdims=True)


def odd_index(axis):
    return lax.axis_index(axis) % 2 == 1


def sides(far, close, axis):
    odd = odd_index(axis)
    far, close = far.astype(jnp.float32), close.astype(jnp.float32)
    return jnp.where(odd, close, far), jnp.where(odd, far, close)


def split_sides(low, high, axis):
    odd = odd_index(axis)
    return jnp.where(odd, high, low), jnp.where(odd, low, high)


def lat_smooth_kernel(far, close, own_part, smoothed, to_far, to_close, halos):
    tiles = smoothed.shape[0]
    height, levels, width = own_part.shape
    per_tile = height // tiles
    halos[0], halos[1] = sides(far[...], close[...], "lat")
    for tile in range(tiles):
        rows = range(tile * per_tile, (tile + 1) * per_tile)
        rows = [lat_rims(row, own_part[row], halos, height) for row in rows]
        turned = jnp.transpose(jnp.concatenate(rows, axis=0))
        smoothed[tile] = turned
        to_far[tile], to_close[tile] = split_sides(turned[0:REACH], turned[width - REACH : width], "lon")


def block_place(plan, position, groups, per_tile, width):
    block = plan[0, position]
    row = block // groups
    start = (row // per_tile) * width + (block % groups) * BLOCK_COLS
    return pl.multiple_of(start, BLOCK_COLS), row % per_tile


def take_blocks(plan, profile, picked, first, count, per_tile, width):
    groups = width // BLOCK_COLS
    lane_row = lax.broadcasted_iota(jnp.int32, (BLOCK_COLS, LANES), 1) // (LANES // per_tile)
    for k in range(count):
        start, sub = block_place(plan, first + k, groups, per_tile, width)
        block = profile[pl.ds(start, BLOCK_COLS), :]
        picked[k * BLOCK_COLS : (k + 1) * BLOCK_COLS, :] = jnp.where(lane_row == sub, block, 0.0)


def land_blocks(plan, field, sens, first, count, per_tile, width):
    groups = width // BLOCK_COLS
    lane_row = lax.broadcasted_iota(jnp.int32, (BLOCK_COLS, LANES), 1) // (LANES // per_tile)
    for k in range(first, first + count):
        start, sub = block_place(plan, k, groups, per_tile, width)
        block = sens[k * BLOCK_COLS : (k + 1) * BLOCK_COLS, :]
        field[pl.ds(start, BLOCK_COLS), :] += jnp.where(lane_row == sub, block, 0.0)


def take_observed(plan, table, slabs, observed, first, count):
    channels = observed.shape[1]
    channel = lax.broadcasted_iota(jnp.int32, (BLOCK_COLS, LANES), 1)
    for k in range(count):
        slot = plan[1, first + k]
        at, kept = table[0, slot], table[1, slot]
        slab, start = None, 0
        for ref in slabs:
            size = ref.shape[0]
            found = ref[jnp.clip(at - start, 0, size - 1)].astype(jnp.float32)
            slab = found if slab is None else jnp.where(at >= start, found, slab)
            start += size
        for h in range(channels // LANES):
            part = slab[h * BLOCK_COLS : (h + 1) * BLOCK_COLS]
            part = jnp.where(channel + h * LANES < kept, part, jnp.inf)
            observed[k * BLOCK_COLS : (k + 1) * BLOCK_COLS, h * LANES : (h + 1) * LANES] = part


def dot(a, b):
    return jnp.dot(a, b, preferred_element_type=jnp.float32)


def dot_t(a, b):
    return lax.dot_general(a, b, (((1,), (1,)), ((), ())), preferred_element_type=jnp.float32)


def net_first(picked, weights, act_one):
    inputs = picked[...].astype(jnp.bfloat16)
    act_one[...] = jnp.tanh(dot(inputs, weights[0][...]) + weights[3][...]).astype(jnp.bfloat16)


def net_rest(weights, states):
    _, weight_two, weight_out, _, bias_two, bias_out = weights
    act_one, act_two, emitted = states
    act_two[...] = jnp.tanh(dot(act_one[...], weight_two[...]) + bias_two[...]).astype(jnp.bfloat16)
    emitted[...] = dot(act_two[...], weight_out[...]) + bias_out[...]


def net_forward(picked, weights, states):
    net_first(picked, weights, states[0])
    net_rest(weights, states)


def net_backward(observed, states, weights):
    wide_in, weight_two, weight_out = weights[:3]
    act_one, act_two, emitted = states
    seen = observed[...]
    misfit = jnp.where(seen < jnp.inf, emitted[...] - seen, 0.0).astype(jnp.bfloat16)
    two = act_two[...].astype(jnp.float32)
    grad_two = (dot_t(misfit, weight_out[...]) * (1.0 - two * two)).astype(jnp.bfloat16)
    one = act_one[...].astype(jnp.float32)
    grad_one = (dot_t(grad_two, weight_two[...]) * (1.0 - one * one)).astype(jnp.bfloat16)
    return rounded(dot_t(grad_one, wide_in[...]))


def few_of(ref):
    return ref.at[pl.ds(0, FEW_SLOTS * BLOCK_COLS)]


def inner_forward_kernel(per_tile, outer_slots, plan, own, turned, taps, *refs):
    (in_weight, in_bias, mid_weight, mid_bias, out_weight, out_bias), refs = refs[:6], refs[6:]
    profile, states, weights, (rows, padded, picked, sems) = refs[0], refs[1:4], refs[4:10], refs[10:]
    wide_in, weight_two, weight_out, bias_one, bias_two, bias_out = weights
    tiles, width, _ = own.shape
    levels = in_weight.shape[0]
    count = picked.shape[0] // BLOCK_COLS
    piece = mid_weight.shape[0] // WEIGHT_PIECES
    pieces = [pl.ds(k * piece, piece) for k in range(WEIGHT_PIECES)]
    loads = [(plan, rows), (in_bias, bias_one)]
    loads += [(in_weight, wide_in.at[pl.ds(sub * levels, levels)]) for sub in range(per_tile)]
    early = len(loads)
    loads += [(mid_weight.at[part], weight_two.at[part]) for part in pieces] + [(mid_bias, bias_two)]
    loads += [(out_weight, weight_out), (out_bias, bias_out)]
    loads = [
        pltpu.make_async_copy(source, target, sems.at[k]) for k, (source, target) in enumerate(loads)
    ]
    for move in loads:
        move.start()
    zeros = jnp.zeros((tiles, REACH, LANES), jnp.float32)
    padded[:, 0:REACH, :] = zeros
    padded[:, REACH : REACH + width, :] = own[...]
    padded[:, REACH + width :, :] = zeros
    for tile in range(tiles):
        total = turned[tile] + lon_conv(padded, taps, tile, 0, width)
        profile[tile * width : (tile + 1) * width, :] = rounded(total)
    for move in loads[:early]:
        move.wait()
    in_time, many = rows[2, 0] <= outer_slots, rows[3, 0] > outer_slots + FEW_SLOTS

    @pl.when(in_time & many)
    def _():
        take_blocks(rows, profile, picked, outer_slots, count, per_tile, width)
        net_first(picked, weights, states[0])

    @pl.when(in_time & ~many)
    def _():
        take_blocks(rows, profile, picked, outer_slots, FEW_SLOTS, per_tile, width)
        net_first(few_of(picked), weights, few_of(states[0]))

    for move in loads[early:]:
        move.wait()

    @pl.when(in_time & many)
    def _():
        net_rest(weights, states)

    @pl.when(in_time & ~many)
    def _():
        net_rest(weights, [few_of(state) for state in states])


def outer_forward_kernel(
    per_tile,
    plan,
    far,
    close,
    own,
    turned,
    taps,
    inner_profile,
    *refs,
):
    weights, states, late_states, (rows, padded, profile, picked, late_picked, sem) = (
        refs[:6],
        refs[6:9],
        refs[9:12],
        refs[12:],
    )
    tiles, width, _ = own.shape
    outer_slots = picked.shape[0] // BLOCK_COLS
    late_slots = late_picked.shape[0] // BLOCK_COLS
    plan_in = pltpu.make_async_copy(plan, rows, sem)
    plan_in.start()
    fill_padded(padded, far, own, close)
    profile[...] = inner_profile[...]
    for tile in range(tiles):
        for start in (0, width - REACH):
            total = turned[tile, start : start + REACH, :] + lon_conv(padded, taps, tile, start, REACH)
            profile[tile * width + start : tile * width + start + REACH, :] = rounded(total)
    plan_in.wait()
    take_blocks(rows, profile, picked, 0, outer_slots, per_tile, width)
    net_forward(picked, weights, states)

    @pl.when(rows[2, 0] > outer_slots)
    def _():
        take_blocks(rows, profile, late_picked, outer_slots, late_slots, per_tile, width)
        net_forward(late_picked, weights, late_states)


def outer_backward_kernel(per_tile, parts, recv_most, plan, *refs):
    slabs, refs = refs[:parts], refs[parts:]
    weights, states, late_states, refs = refs[:3], refs[3:6], refs[6:9], refs[9:]
    (table_rows, sens, to_far, to_close) = refs[:4]
    (rows, table, observed, late_observed, field, sems) = refs[4:]
    tiles = to_far.shape[0]
    width = field.shape[0] // tiles
    outer_slots = observed.shape[0] // BLOCK_COLS
    late_slots = late_observed.shape[0] // BLOCK_COLS

    plan_in = pltpu.make_async_copy(plan, rows, sems.at[0])
    plan_in.start()
    routing(recv_most, outer_slots + late_slots, slabs, table_rows)
    table_in = pltpu.make_async_copy(table_rows, table, sems.at[1])
    table_in.start()
    field[...] = jnp.zeros_like(field)
    plan_in.wait()
    table_in.wait()

    take_observed(rows, table, slabs, observed, 0, outer_slots)
    sens[0 : outer_slots * BLOCK_COLS, :] = net_backward(observed, states, weights)
    land_blocks(rows, field, sens, 0, outer_slots, per_tile, width)

    @pl.when(rows[2, 0] > outer_slots)
    def _():
        take_observed(rows, table, slabs, late_observed, outer_slots, late_slots)
        sens[outer_slots * BLOCK_COLS :, :] = net_backward(late_observed, late_states, weights)
        land_blocks(rows, field, sens, outer_slots, late_slots, per_tile, width)

    for tile in range(tiles):
        low = field[tile * width : tile * width + REACH, :]
        high = field[(tile + 1) * width - REACH : (tile + 1) * width, :]
        low, high = split_sides(low, high, "lon")
        to_far[tile], to_close[tile] = low.astype(jnp.bfloat16), high.astype(jnp.bfloat16)


def inner_backward_kernel(per_tile, parts, outer_slots, plan, table_rows, sens, *refs):
    slabs, refs = refs[:parts], refs[parts:]
    weights, states, refs = refs[:3], refs[3:6], refs[6:]
    landing, rows, table, observed, inner, field, sems = refs
    tiles, width, _ = landing.shape
    late_slots = observed.shape[0] // BLOCK_COLS
    split = outer_slots * BLOCK_COLS
    moves = [
        pltpu.make_async_copy(plan, rows, sems.at[0]),
        pltpu.make_async_copy(table_rows, table, sems.at[1]),
    ]
    for move in moves:
        move.start()
    field[...] = jnp.zeros_like(field)
    inner[...] = sens[...]
    for move in moves:
        move.wait()

    in_time, many = rows[2, 0] <= outer_slots, rows[3, 0] > outer_slots + FEW_SLOTS
    first = outer_slots + FEW_SLOTS

    @pl.when(in_time & many)
    def _():
        take_observed(rows, table, slabs, observed, outer_slots, late_slots)
        inner[split:, :] = net_backward(observed, states, weights)

    @pl.when(in_time & ~many)
    def _():
        take_observed(rows, table, slabs, observed, outer_slots, FEW_SLOTS)
        inner[split : split + FEW_SLOTS * BLOCK_COLS, :] = net_backward(
            few_of(observed), [few_of(state) for state in states], weights
        )

    land_blocks(rows, field, inner, 0, first, per_tile, width)

    @pl.when(many)
    def _():
        land_blocks(rows, field, inner, first, outer_slots + late_slots - first, per_tile, width)

    for tile in range(tiles):
        landing[tile] = field[tile * width : (tile + 1) * width, :]


def lon_back_kernel(far, close, own, taps, back, to_far, to_close, padded):
    tiles, width, _ = own.shape
    height, levels, _ = back.shape
    per_tile = height // tiles
    fill_padded(padded, far, own, close)
    for tile in range(tiles):
        rows = jnp.transpose(lon_conv(padded, taps, tile, 0, width))
        rows = rows.reshape(per_tile, levels, width)
        back[tile * per_tile : (tile + 1) * per_tile] = rows
    halve_for_sides(back, height, to_far, to_close)


def own_back_kernel(back, control, own_part):
    height = back.shape[0]
    for row in range(height):
        own_part[row] = lat_sum(back, row, 0, height, control[row])


def lat_back_kernel(far, close, own_part, gradient, halos, done, sems):
    halos[0], halos[1] = sides(far[...], close[...], "lat")
    height = own_part.shape[0]
    piece = height // BAND_PIECES
    moves = []
    for k in range(BAND_PIECES):
        part = pl.ds(k * piece, piece)
        for row in range(k * piece, (k + 1) * piece):
            done[row] = lat_rims(row, own_part[row], halos, height)
        moves.append(pltpu.make_async_copy(done.at[part], gradient.at[part], sems.at[k]))
        moves[-1].start()
    for move in moves:
        move.wait()


def exchange(to_far, to_close, axis, periodic):
    count = lax.axis_size(axis)
    far = []
    for odd in range(1, count, 2):
        if odd + 1 < count or periodic:
            far += [(odd, (odd + 1) % count), ((odd + 1) % count, odd)]
    close = [(i, i ^ 1) for i in range(count)]
    to_close, _ = lax.optimization_barrier((to_close, to_far))
    from_far, from_close = lax.ppermute(to_far, axis, far), lax.ppermute(to_close, axis, close)
    from_far = lax.optimization_barrier(from_far)
    from_close, _ = lax.optimization_barrier((from_close, from_far))
    return from_far, from_close, to_close


def shards(
    control,
    background,
    lon_width,
    block_cells,
    block_owner,
    channel_count,
    radiance,
    in_weight,
    in_bias,
    mid_weight,
    mid_bias,
    out_weight,
    out_bias,
):
    height, levels, width = control.shape
    hidden = mid_weight.shape[0]
    channels, columns = radiance.shape
    slot_count = block_owner.shape[0]
    recv_most = channel_count.shape[0]
    per_tile = LANES // levels
    tiles = height // per_tile
    slab_rows = BLOCK_COLS * channels // LANES
    f32, bf16, i32 = jnp.float32, jnp.bfloat16, jnp.int32
    shape = jax.ShapeDtypeStruct
    field = height * levels * width
    conv_flops = 2 * 33 * field

    halves = channels // LANES
    radiance = radiance.T.reshape(recv_most, BLOCK_COLS, halves, LANES)
    radiance = jnp.swapaxes(radiance, 1, 2).reshape(recv_most, slab_rows, LANES)
    half_field = shape(control.shape, bf16)
    slabs, to_far, to_close, held, ground = call(
        first_kernel,
        (
            shape((recv_most + 1, slab_rows, LANES), bf16),
            half_field,
            half_field,
            shape(control.shape, f32),
            shape(control.shape, f32),
        ),
        [HBM] * 5,
        (HBM,) + (VMEM,) * 4,
        0,
        24 * field,
        scratch=(
            pltpu.VMEM((1, slot_count), i32),
            pltpu.VMEM((1, recv_most), i32),
            pltpu.VMEM((slab_rows, LANES), f32),
            pltpu.VMEM((slab_rows, LANES), bf16),
            pltpu.SemaphoreType.DMA((5 + BAND_PIECES,)),
        ),
        name="slabs_halves",
    )(
        *pinned(
            radiance,
            block_owner.reshape(1, slot_count),
            channel_count.reshape(1, recv_most),
            control,
            background,
        )
    )
    far, close, sent = exchange(to_far, to_close, "lat", False)

    band = pltpu.VMEM((height, levels, width), f32)
    taps, turned, plan, own_part = call(
        prepare_kernel,
        (
            shape((tiles, 24, LANES), f32),
            shape((tiles, width, LANES), f32),
            shape((8, LANES), i32),
            shape(control.shape, f32),
        ),
        [HBM] * 3 + [VMEM] * 2,
        (VMEM,) * 4,
        conv_flops // 2,
        12 * field,
        scratch=(
            pltpu.SMEM((height,), i32),
            pltpu.VMEM((1, slot_count), i32),
            pltpu.VMEM((1, slot_count), i32),
            pltpu.SemaphoreType.DMA((3,)),
        ),
        name="taps_background",
    )(
        *pinned(lon_width, block_cells.reshape(1, slot_count), block_owner.reshape(1, slot_count)),
        ground,
        held,
    )

    lat_count = lax.axis_size("lat")
    one, two, *others = swap_bits(lat_count)

    def swapped(part, apart):
        return lax.ppermute(part, "lat", [(i, i ^ apart) for i in range(lat_count)])

    later, _ = lax.optimization_barrier((slabs, sent))
    near = [slabs, swapped(later, 1 << one), swapped(later, 1 << two), swapped(slabs, (1 << one) + (1 << two))]

    halos = pltpu.VMEM((2, REACH, levels, width), f32)
    smoothed, to_far, to_close = call(
        lat_smooth_kernel,
        (shape((tiles, width, LANES), f32),) + (shape((tiles, REACH, LANES), f32),) * 2,
        [VMEM] * 3,
        (VMEM,) * 3,
        LAT_COVER * conv_flops,
        LAT_COVER * 16 * field,
        scratch=(halos,),
        name="lat_smooth",
    )(far, close, own_part)
    far, close, _ = exchange(to_far, to_close, "lon", True)

    outer_slots = 3 * slot_count // 8
    late_slots = slot_count - outer_slots
    x_rows = slot_count * BLOCK_COLS
    outer_rows, late_rows = outer_slots * BLOCK_COLS, late_slots * BLOCK_COLS
    row_flops = 2 * hidden * (LANES + hidden + channels)
    def state_shapes(rows):
        return (shape((rows, hidden), bf16), shape((rows, hidden), bf16), shape((rows, channels), f32))

    plan_rows = pltpu.SMEM((8, LANES), i32)
    padded = pltpu.VMEM((tiles, width + 2 * REACH, LANES), f32)
    flat = pltpu.VMEM((tiles * width, LANES), f32)

    profile, *rest = call(
        functools.partial(inner_forward_kernel, per_tile, outer_slots),
        (shape((tiles * width, LANES), f32),)
        + state_shapes(late_rows)
        + (
            shape((LANES, hidden), bf16),
            shape((hidden, hidden), bf16),
            shape((hidden, channels), bf16),
            shape((1, hidden), f32),
            shape((1, hidden), f32),
            shape((1, channels), f32),
        ),
        [ANY] + [VMEM] * 3 + [HBM] * 6,
        (VMEM,) * 10,
        LON_COVER * late_rows * row_flops,
        LON_COVER * 4 * 1024 * 1024,
        scratch=(
            plan_rows,
            padded,
            pltpu.VMEM((late_rows, LANES), f32),
            pltpu.SemaphoreType.DMA((5 + per_tile + WEIGHT_PIECES,)),
        ),
        name="inner_forward",
    )(
        plan,
        smoothed,
        turned,
        taps,
        *pinned(
            in_weight,
            in_bias.reshape(1, hidden),
            mid_weight,
            mid_bias.reshape(1, hidden),
            out_weight,
            out_bias.reshape(1, channels),
        ),
    )
    inner_states, weights = rest[:3], rest[3:]
    *near, _ = lax.optimization_barrier((*near, profile))
    for bit in others:
        near = [jnp.concatenate(near, axis=0)]
        near.append(swapped(near[0], 1 << bit))
    near = [jnp.concatenate(near[:-1], axis=0), near[-1]]
    across = [swapped(part, 1) for part in near]

    states = call(
        functools.partial(outer_forward_kernel, per_tile),
        state_shapes(outer_rows) + state_shapes(late_rows),
        [ANY] + [VMEM] * 12,
        (VMEM,) * 6,
        SWAP_COVER * outer_rows * row_flops,
        SWAP_COVER * 4 * 1024 * 1024,
        scratch=(
            plan_rows,
            padded,
            flat,
            pltpu.VMEM((outer_rows, LANES), f32),
            pltpu.VMEM((late_rows, LANES), f32),
            pltpu.SemaphoreType.DMA,
        ),
        name="outer_forward",
    )(plan, far, close, smoothed, turned, taps, profile, *weights)

    slabs = [*near, *across]
    table, sens, to_far, to_close = call(
        functools.partial(outer_backward_kernel, per_tile, len(slabs), recv_most),
        (
            shape((8, LANES), i32),
            shape((x_rows, LANES), f32),
            shape((tiles, REACH, LANES), bf16),
            shape((tiles, REACH, LANES), bf16),
        ),
        [ANY] + [VMEM] * (len(slabs) + 9),
        (VMEM,) * 4,
        outer_rows * row_flops,
        4 * 1024 * 1024,
        scratch=(
            plan_rows,
            pltpu.SMEM((8, LANES), i32),
            pltpu.VMEM((outer_rows, channels), f32),
            pltpu.VMEM((late_rows, channels), f32),
            flat,
            pltpu.SemaphoreType.DMA((2,)),
        ),
        name="outer_backward",
    )(plan, *slabs, *weights[:3], *states)
    far, close, sent = exchange(to_far, to_close, "lon", True)

    landing = call(
        functools.partial(inner_backward_kernel, per_tile, len(slabs), outer_slots),
        shape((tiles, width, LANES), f32),
        [ANY, ANY] + [VMEM] * (len(slabs) + 7),
        VMEM,
        late_rows * row_flops,
        4 * 1024 * 1024,
        scratch=(
            plan_rows,
            pltpu.SMEM((8, LANES), i32),
            pltpu.VMEM((late_rows, channels), f32),
            pltpu.VMEM((x_rows, LANES), f32),
            flat,
            pltpu.SemaphoreType.DMA((2,)),
        ),
        name="inner_backward",
    )(plan, table, sens, *slabs, *weights[:3], *inner_states)

    back, to_far, to_close = call(
        lon_back_kernel,
        (shape((height, levels, width), f32), half_field, half_field),
        [VMEM] * 4,
        (VMEM,) * 3,
        conv_flops,
        8 * field,
        scratch=(pltpu.VMEM((tiles, width + 2 * REACH, LANES), f32),),
        name="lon_back",
    )(far, close, landing, taps)
    far, close, _ = exchange(to_far, to_close, "lat", False)
    own_part = call(
        own_back_kernel,
        shape((height, levels, width), f32),
        [VMEM, VMEM],
        VMEM,
        conv_flops // 2,
        12 * field,
        name="lat_back_own",
    )(back, held)
    return call(
        lat_back_kernel,
        shape((height, levels, width), f32),
        [VMEM] * 3,
        HBM,
        conv_flops // 2,
        16 * field,
        scratch=(halos, band, pltpu.SemaphoreType.DMA((BAND_PIECES,))),
        name="lat_back",
    )(far, close, own_part)


def solution(mesh):
    return jax.shard_map(
        shards,
        mesh=mesh,
        in_specs=(
            P("lat", None, "lon"),
            P("lat", None, "lon"),
            P("lat"),
            P("lat", "lon"),
            P("lat", "lon"),
            P("lat", "lon"),
            P("lat", "lon"),
            P(),
            P(),
            P(),
            P(),
            P(),
            P(),
        ),
        out_specs=P("lat", None, "lon"),
        check_vma=False,
    )
```

```python
import functools

import jax
import jax.numpy as jnp
import numpy as np
from jax import lax
from jax.experimental import pallas as pl
from jax.experimental.pallas import tpu as pltpu
from jax.sharding import PartitionSpec as P

REACH = 16
BLOCK_COLS = 8
LANES = 128
LAT_SIGMA = 8.0
WEIGHT_PIECES = 4
BAND_PIECES = 4
FEW_SLOTS = 8
LAT_COVER = 64
LON_COVER = 10
SWAP_COVER = 10
VMEM_BYTES = 40 * 1024 * 1024

VMEM = pl.BlockSpec(memory_space=pltpu.VMEM)
SMEM = pl.BlockSpec(memory_space=pltpu.SMEM)
HBM = pl.BlockSpec(memory_space=pltpu.HBM)
ANY = pl.BlockSpec(memory_space=pl.ANY)


def lat_taps():
    offsets = np.arange(-REACH, REACH + 1, dtype=np.float64)
    raw = np.exp(-offsets * offsets / (2.0 * LAT_SIGMA * LAT_SIGMA))
    return [float(v) for v in (raw / np.sqrt(np.sum(raw * raw))).astype(np.float32)]


def call(kernel, out_shape, in_specs, out_specs, flops, bytes_moved, scratch=(), name=None):
    return pl.pallas_call(
        kernel,
        out_shape=out_shape,
        in_specs=in_specs,
        out_specs=out_specs,
        scratch_shapes=list(scratch),
        compiler_params=pltpu.CompilerParams(vmem_limit_bytes=VMEM_BYTES),
        cost_estimate=pl.CostEstimate(flops=flops, bytes_accessed=bytes_moved, transcendentals=0),
        name=name,
    )


def pinned(*values):
    return [pltpu.with_memory_space_constraint(value, pltpu.HBM) for value in values]


def lat_sum(parts, row, first, height, start=None):
    taps = lat_taps()
    acc = start
    for k in range(height):
        j = first + k - row
        if abs(j) <= REACH:
            term = taps[j + REACH] * parts[k]
            acc = term if acc is None else acc + term
    return acc


def lat_rims(row, part, halos, height):
    low = lat_sum(halos.at[0], row, -REACH, REACH, part)
    return lat_sum(halos.at[1], row, height, REACH, low)


def fill_padded(padded, far, own, close):
    width = own.shape[1]
    low, high = sides(far[...], close[...], "lon")
    padded[:, 0:REACH, :] = low
    padded[:, REACH : REACH + width, :] = own[...]
    padded[:, REACH + width :, :] = high


def lon_conv(padded, taps, tile, start, width):
    middle = REACH + start
    acc = taps[tile, 0:1, :] * padded[tile, pl.ds(middle, width), :]
    for j in range(1, REACH + 1):
        both = padded[tile, pl.ds(middle + j, width), :] + padded[tile, pl.ds(middle - j, width), :]
        acc = acc + taps[tile, j : j + 1, :] * both
    return acc


def rounded(value):
    return value.astype(jnp.bfloat16).astype(jnp.float32)


def halved_rows(rows, order):
    halves, carry = {}, None
    for row in order:
        value = rows[row] if carry is None else rows[row] + carry
        halves[row] = value.astype(jnp.bfloat16)
        carry = value - halves[row].astype(jnp.float32)
    return [halves[row] for row in sorted(halves)]


def halve_for_sides(rows, height, to_far, to_close):
    odd = odd_index("lat")
    upward = halved_rows(rows, range(height - 1, -1, -1))
    downward = halved_rows(rows, range(height))
    for row in range(height):
        to_far[row] = jnp.where(odd, upward[row], downward[row])
        to_close[row] = jnp.where(odd, downward[row], upward[row])


def first_kernel(
    radiance,
    block_owner,
    channel_count,
    control,
    slabs,
    to_far,
    to_close,
    held,
    owners,
    counts,
    rows,
    tables,
    sems,
):
    recv_most = radiance.shape[0]
    moves = [
        pltpu.make_async_copy(radiance, slabs.at[pl.ds(0, recv_most)], sems.at[0]),
        pltpu.make_async_copy(block_owner, owners, sems.at[1]),
        pltpu.make_async_copy(channel_count, counts, sems.at[2]),
    ]
    piece = control.shape[0] // BAND_PIECES
    for k in range(BAND_PIECES):
        part = pl.ds(k * piece, piece)
        moves.append(pltpu.make_async_copy(control.at[part], held.at[part], sems.at[4 + k]))
    for move in moves[3:] + moves[:3]:
        move.start()
    rows[...] = jnp.full(rows.shape, -1.0, jnp.float32)
    moves[1].wait()
    moves[2].wait()
    rows[0:1, 0 : owners.shape[1]] = owners[...].astype(jnp.float32)
    rows[1:2, 0 : counts.shape[1]] = counts[...].astype(jnp.float32)
    tables[...] = rows[...].astype(jnp.bfloat16)
    last = pltpu.make_async_copy(tables, slabs.at[recv_most], sems.at[3])
    last.start()
    for move in moves[3:]:
        move.wait()
    halve_for_sides(held, held.shape[0], to_far, to_close)
    moves[0].wait()
    last.wait()


def prepare_kernel(
    lon_width,
    block_cells,
    block_owner,
    background,
    band,
    taps,
    turned,
    plan,
    own_part,
    widths,
    cells,
    owners,
    field,
    sems,
):
    moves = [
        pltpu.make_async_copy(lon_width, widths, sems.at[0]),
        pltpu.make_async_copy(block_cells, cells, sems.at[1]),
        pltpu.make_async_copy(block_owner, owners, sems.at[2]),
    ]
    piece = background.shape[0] // BAND_PIECES
    for k in range(BAND_PIECES):
        part = pl.ds(k * piece, piece)
        moves.append(pltpu.make_async_copy(background.at[part], field.at[part], sems.at[3 + k]))
    tiles = turned.shape[0]
    height, levels, width = field.shape
    per_tile = height // tiles
    for move in moves:
        move.start()
    groups = width // BLOCK_COLS
    rim = REACH // BLOCK_COLS
    slot_count = cells.shape[1]

    for row in range(height):
        own_part[row] = lat_sum(band, row, 0, height)

    lane_row = lax.broadcasted_iota(jnp.int32, (1, LANES), 1) // levels
    steps = lax.broadcasted_iota(jnp.int32, (taps.shape[1], LANES), 0)
    dist = steps.astype(jnp.float32)
    weight = jnp.where(steps == 0, 1.0, jnp.where(steps <= REACH, 2.0, 0.0))
    moves[0].wait()
    for tile in range(tiles):
        spread = jnp.zeros((1, LANES), jnp.int32)
        for sub in range(per_tile):
            spread = jnp.where(lane_row == sub, widths[tile * per_tile + sub], spread)
        spread = spread.astype(jnp.float32)
        raw = jnp.exp(-dist * dist / (2.0 * spread * spread))
        norm = jnp.sum(weight * raw * raw, axis=0, keepdims=True)
        taps[tile] = raw / jnp.sqrt(norm)

    moves[1].wait()
    moves[2].wait()
    rows = lax.broadcasted_iota(jnp.int32, (slot_count, slot_count), 0)
    lanes = lax.broadcasted_iota(jnp.int32, (slot_count, slot_count), 1)
    group = cells[...] % groups
    outer = ((group < rim) | (group >= groups - rim)) & (owners[...] >= 0)
    outer_here = jnp.where(outer, 1, 0)
    outer_count = jnp.sum(outer_here, axis=1, keepdims=True)
    earlier = jnp.sum(jnp.where(lanes < rows, outer_here, 0), axis=1, keepdims=True)
    here = jnp.sum(jnp.where(lanes == rows, outer_here, 0), axis=1, keepdims=True)
    cell = jnp.sum(jnp.where(lanes == rows, cells[...], 0), axis=1, keepdims=True)
    position = jnp.where(here == 1, earlier, outer_count + rows[:, 0:1] - earlier)
    at = lax.broadcasted_iota(jnp.int32, (slot_count, LANES), 1)
    hit = position == at
    slot = lax.broadcasted_iota(jnp.int32, (slot_count, LANES), 0)
    plan[...] = jnp.zeros_like(plan)
    plan[0:1, :] = jnp.sum(jnp.where(hit, cell, 0), axis=0, keepdims=True)
    plan[1:2, :] = jnp.sum(jnp.where(hit, slot, 0), axis=0, keepdims=True)
    plan[2:3, :] = jnp.broadcast_to(outer_count, (1, LANES))
    live_count = jnp.sum(jnp.where(owners[...] >= 0, 1, 0), axis=1, keepdims=True)
    plan[3:4, :] = jnp.broadcast_to(live_count, (1, LANES))
    for move in moves[3:]:
        move.wait()
    for tile in range(tiles):
        block = field[tile * per_tile : (tile + 1) * per_tile].reshape(per_tile * levels, width)
        turned[tile] = jnp.transpose(block)


def swap_bits(count):
    return list(range(count.bit_length() - 2, 0, -1))


def routing(recv_most, slot_count, slabs, table):
    per_owner = recv_most + 1
    spans, count = [], 0
    for ref in slabs:
        spans.append((ref, count))
        count += ref.shape[0] // per_owner
    half = count // 2
    here = lax.axis_index("lat")
    rows = lax.broadcasted_iota(jnp.int32, (slot_count, LANES), 0)
    lanes = lax.broadcasted_iota(jnp.int32, (slot_count, LANES), 1)
    diagonal = rows == lanes
    zero = jnp.zeros((slot_count, LANES), jnp.int32)

    bits = swap_bits(count)

    def device_of(k):
        apart = jnp.where(k < half, 0, 1)
        for place, bit in enumerate(bits):
            apart = apart + (((k >> place) & 1) << bit)
        return here ^ apart

    def over_sets(step):
        acc = zero
        for ref, first in spans:

            def add(k, acc, ref=ref, first=first):
                lines = ref[k * per_owner + recv_most].astype(jnp.float32)
                owners, counts = lines[0:1].astype(jnp.int32), lines[1:2].astype(jnp.int32)
                return acc + step(device_of(first + k), owners, counts)

            acc = lax.fori_loop(0, ref.shape[0] // per_owner, add, acc, unroll=count <= 8)
        return jnp.sum(acc, axis=1, keepdims=True)

    mine = slabs[0][recv_most].astype(jnp.float32)[0:1].astype(jnp.int32)
    owner = jnp.sum(jnp.where(diagonal, mine, 0), axis=1, keepdims=True)

    def rank(device, owners, counts):
        before = (device < here) | ((device == here) & (lanes < rows))
        return jnp.where((owners == owner) & before, 1, 0)

    arrival = over_sets(rank)

    def counted(device, owners, counts):
        return jnp.where((owner == device) & (lanes == arrival), counts, 0)

    kept = over_sets(counted)
    apart = owner ^ here
    entry = (apart & 1) * half
    for place, bit in enumerate(bits):
        entry = entry + (((apart >> bit) & 1) << place)
    target = jnp.where(owner >= 0, entry * per_owner + arrival, 0)
    table[...] = jnp.zeros_like(table)
    for row, column in enumerate((target, kept)):
        table[row : row + 1, :] = jnp.sum(jnp.where(diagonal, column, 0), axis=0, keepdims=True)


def odd_index(axis):
    return lax.axis_index(axis) % 2 == 1


def sides(far, close, axis):
    odd = odd_index(axis)
    far, close = far.astype(jnp.float32), close.astype(jnp.float32)
    return jnp.where(odd, close, far), jnp.where(odd, far, close)


def split_sides(low, high, axis):
    odd = odd_index(axis)
    return jnp.where(odd, high, low), jnp.where(odd, low, high)


def lat_smooth_kernel(far, close, own_part, smoothed, to_far, to_close, halos):
    tiles = smoothed.shape[0]
    height, levels, width = own_part.shape
    per_tile = height // tiles
    halos[0], halos[1] = sides(far[...], close[...], "lat")
    for tile in range(tiles):
        rows = range(tile * per_tile, (tile + 1) * per_tile)
        rows = [lat_rims(row, own_part[row], halos, height) for row in rows]
        turned = jnp.transpose(jnp.concatenate(rows, axis=0))
        smoothed[tile] = turned
        to_far[tile], to_close[tile] = split_sides(turned[0:REACH], turned[width - REACH : width], "lon")


def block_place(plan, position, groups, per_tile, width):
    block = plan[0, position]
    row = block // groups
    start = (row // per_tile) * width + (block % groups) * BLOCK_COLS
    return pl.multiple_of(start, BLOCK_COLS), row % per_tile


def take_blocks(plan, profile, picked, first, count, per_tile, width):
    groups = width // BLOCK_COLS
    lane_row = lax.broadcasted_iota(jnp.int32, (BLOCK_COLS, LANES), 1) // (LANES // per_tile)
    for k in range(count):
        start, sub = block_place(plan, first + k, groups, per_tile, width)
        block = profile[pl.ds(start, BLOCK_COLS), :]
        picked[k * BLOCK_COLS : (k + 1) * BLOCK_COLS, :] = jnp.where(lane_row == sub, block, 0.0)


def land_blocks(plan, field, sens, first, count, per_tile, width):
    groups = width // BLOCK_COLS
    lane_row = lax.broadcasted_iota(jnp.int32, (BLOCK_COLS, LANES), 1) // (LANES // per_tile)
    for k in range(first, first + count):
        start, sub = block_place(plan, k, groups, per_tile, width)
        block = sens[k * BLOCK_COLS : (k + 1) * BLOCK_COLS, :]
        field[pl.ds(start, BLOCK_COLS), :] += jnp.where(lane_row == sub, block, 0.0)


def take_observed(plan, table, slabs, observed, first, count):
    channels = observed.shape[1]
    channel = lax.broadcasted_iota(jnp.int32, (BLOCK_COLS, LANES), 1)
    for k in range(count):
        slot = plan[1, first + k]
        at, kept = table[0, slot], table[1, slot]
        slab, start = None, 0
        for ref in slabs:
            size = ref.shape[0]
            found = ref[jnp.clip(at - start, 0, size - 1)].astype(jnp.float32)
            slab = found if slab is None else jnp.where(at >= start, found, slab)
            start += size
        for h in range(channels // LANES):
            part = slab[h * BLOCK_COLS : (h + 1) * BLOCK_COLS]
            part = jnp.where(channel + h * LANES < kept, part, jnp.inf)
            observed[k * BLOCK_COLS : (k + 1) * BLOCK_COLS, h * LANES : (h + 1) * LANES] = part


def dot(a, b):
    return jnp.dot(a, b, preferred_element_type=jnp.float32)


def dot_t(a, b):
    return lax.dot_general(a, b, (((1,), (1,)), ((), ())), preferred_element_type=jnp.float32)


def net_first(picked, weights, act_one):
    inputs = picked[...].astype(jnp.bfloat16)
    act_one[...] = jnp.tanh(dot(inputs, weights[0][...]) + weights[3][...]).astype(jnp.bfloat16)


def net_rest(weights, states):
    _, weight_two, weight_out, _, bias_two, bias_out = weights
    act_one, act_two, emitted = states
    act_two[...] = jnp.tanh(dot(act_one[...], weight_two[...]) + bias_two[...]).astype(jnp.bfloat16)
    emitted[...] = dot(act_two[...], weight_out[...]) + bias_out[...]


def net_forward(picked, weights, states):
    net_first(picked, weights, states[0])
    net_rest(weights, states)


def net_backward(observed, states, weights):
    wide_in, weight_two, weight_out = weights[:3]
    act_one, act_two, emitted = states
    seen = observed[...]
    misfit = jnp.where(seen < jnp.inf, emitted[...] - seen, 0.0).astype(jnp.bfloat16)
    two = act_two[...].astype(jnp.float32)
    grad_two = (dot_t(misfit, weight_out[...]) * (1.0 - two * two)).astype(jnp.bfloat16)
    one = act_one[...].astype(jnp.float32)
    grad_one = (dot_t(grad_two, weight_two[...]) * (1.0 - one * one)).astype(jnp.bfloat16)
    return rounded(dot_t(grad_one, wide_in[...]))


def few_of(ref):
    return ref.at[pl.ds(0, FEW_SLOTS * BLOCK_COLS)]


def inner_forward_kernel(per_tile, outer_slots, plan, own, turned, taps, *refs):
    (in_weight, in_bias, mid_weight, mid_bias, out_weight, out_bias), refs = refs[:6], refs[6:]
    profile, states, weights, (rows, padded, picked, sems) = refs[0], refs[1:4], refs[4:10], refs[10:]
    wide_in, weight_two, weight_out, bias_one, bias_two, bias_out = weights
    tiles, width, _ = own.shape
    levels = in_weight.shape[0]
    count = picked.shape[0] // BLOCK_COLS
    piece = mid_weight.shape[0] // WEIGHT_PIECES
    pieces = [pl.ds(k * piece, piece) for k in range(WEIGHT_PIECES)]
    loads = [(plan, rows), (in_bias, bias_one)]
    loads += [(in_weight, wide_in.at[pl.ds(sub * levels, levels)]) for sub in range(per_tile)]
    early = len(loads)
    loads += [(mid_weight.at[part], weight_two.at[part]) for part in pieces] + [(mid_bias, bias_two)]
    loads += [(out_weight, weight_out), (out_bias, bias_out)]
    loads = [
        pltpu.make_async_copy(source, target, sems.at[k]) for k, (source, target) in enumerate(loads)
    ]
    for move in loads:
        move.start()
    zeros = jnp.zeros((tiles, REACH, LANES), jnp.float32)
    padded[:, 0:REACH, :] = zeros
    padded[:, REACH : REACH + width, :] = own[...]
    padded[:, REACH + width :, :] = zeros
    for tile in range(tiles):
        total = turned[tile] + lon_conv(padded, taps, tile, 0, width)
        profile[tile * width : (tile + 1) * width, :] = rounded(total)
    for move in loads[:early]:
        move.wait()
    in_time, many = rows[2, 0] <= outer_slots, rows[3, 0] > outer_slots + FEW_SLOTS

    @pl.when(in_time & many)
    def _():
        take_blocks(rows, profile, picked, outer_slots, count, per_tile, width)
        net_first(picked, weights, states[0])

    @pl.when(in_time & ~many)
    def _():
        take_blocks(rows, profile, picked, outer_slots, FEW_SLOTS, per_tile, width)
        net_first(few_of(picked), weights, few_of(states[0]))

    for move in loads[early:]:
        move.wait()

    @pl.when(in_time & many)
    def _():
        net_rest(weights, states)

    @pl.when(in_time & ~many)
    def _():
        net_rest(weights, [few_of(state) for state in states])


def outer_forward_kernel(
    per_tile,
    plan,
    far,
    close,
    own,
    turned,
    taps,
    inner_profile,
    *refs,
):
    weights, states, late_states, (rows, padded, profile, picked, late_picked, sem) = (
        refs[:6],
        refs[6:9],
        refs[9:12],
        refs[12:],
    )
    tiles, width, _ = own.shape
    outer_slots = picked.shape[0] // BLOCK_COLS
    late_slots = late_picked.shape[0] // BLOCK_COLS
    plan_in = pltpu.make_async_copy(plan, rows, sem)
    plan_in.start()
    fill_padded(padded, far, own, close)
    profile[...] = inner_profile[...]
    for tile in range(tiles):
        for start in (0, width - REACH):
            total = turned[tile, start : start + REACH, :] + lon_conv(padded, taps, tile, start, REACH)
            profile[tile * width + start : tile * width + start + REACH, :] = rounded(total)
    plan_in.wait()
    take_blocks(rows, profile, picked, 0, outer_slots, per_tile, width)
    net_forward(picked, weights, states)

    @pl.when(rows[2, 0] > outer_slots)
    def _():
        take_blocks(rows, profile, late_picked, outer_slots, late_slots, per_tile, width)
        net_forward(late_picked, weights, late_states)


def outer_backward_kernel(per_tile, parts, recv_most, plan, *refs):
    slabs, refs = refs[:parts], refs[parts:]
    weights, states, late_states, refs = refs[:3], refs[3:6], refs[6:9], refs[9:]
    (table_rows, sens, to_far, to_close) = refs[:4]
    (rows, table, observed, late_observed, field, sems) = refs[4:]
    tiles = to_far.shape[0]
    width = field.shape[0] // tiles
    outer_slots = observed.shape[0] // BLOCK_COLS
    late_slots = late_observed.shape[0] // BLOCK_COLS

    plan_in = pltpu.make_async_copy(plan, rows, sems.at[0])
    plan_in.start()
    routing(recv_most, outer_slots + late_slots, slabs, table_rows)
    table_in = pltpu.make_async_copy(table_rows, table, sems.at[1])
    table_in.start()
    field[...] = jnp.zeros_like(field)
    plan_in.wait()
    table_in.wait()

    take_observed(rows, table, slabs, observed, 0, outer_slots)
    sens[0 : outer_slots * BLOCK_COLS, :] = net_backward(observed, states, weights)
    land_blocks(rows, field, sens, 0, outer_slots, per_tile, width)

    @pl.when(rows[2, 0] > outer_slots)
    def _():
        take_observed(rows, table, slabs, late_observed, outer_slots, late_slots)
        sens[outer_slots * BLOCK_COLS :, :] = net_backward(late_observed, late_states, weights)
        land_blocks(rows, field, sens, outer_slots, late_slots, per_tile, width)

    for tile in range(tiles):
        low = field[tile * width : tile * width + REACH, :]
        high = field[(tile + 1) * width - REACH : (tile + 1) * width, :]
        low, high = split_sides(low, high, "lon")
        to_far[tile], to_close[tile] = low.astype(jnp.bfloat16), high.astype(jnp.bfloat16)


def inner_backward_kernel(per_tile, parts, outer_slots, plan, table_rows, sens, *refs):
    slabs, refs = refs[:parts], refs[parts:]
    weights, states, refs = refs[:3], refs[3:6], refs[6:]
    landing, rows, table, observed, inner, field, sems = refs
    tiles, width, _ = landing.shape
    late_slots = observed.shape[0] // BLOCK_COLS
    split = outer_slots * BLOCK_COLS
    moves = [
        pltpu.make_async_copy(plan, rows, sems.at[0]),
        pltpu.make_async_copy(table_rows, table, sems.at[1]),
    ]
    for move in moves:
        move.start()
    field[...] = jnp.zeros_like(field)
    inner[...] = sens[...]
    for move in moves:
        move.wait()

    in_time, many = rows[2, 0] <= outer_slots, rows[3, 0] > outer_slots + FEW_SLOTS
    first = outer_slots + FEW_SLOTS

    @pl.when(in_time & many)
    def _():
        take_observed(rows, table, slabs, observed, outer_slots, late_slots)
        inner[split:, :] = net_backward(observed, states, weights)

    @pl.when(in_time & ~many)
    def _():
        take_observed(rows, table, slabs, observed, outer_slots, FEW_SLOTS)
        inner[split : split + FEW_SLOTS * BLOCK_COLS, :] = net_backward(
            few_of(observed), [few_of(state) for state in states], weights
        )

    land_blocks(rows, field, inner, 0, first, per_tile, width)

    @pl.when(many)
    def _():
        land_blocks(rows, field, inner, first, outer_slots + late_slots - first, per_tile, width)

    for tile in range(tiles):
        landing[tile] = field[tile * width : (tile + 1) * width, :]


def lon_back_kernel(far, close, own, taps, back, halved, padded):
    tiles, width, _ = own.shape
    height, levels, _ = back.shape
    per_tile = height // tiles
    fill_padded(padded, far, own, close)
    for tile in range(tiles):
        rows = jnp.transpose(lon_conv(padded, taps, tile, 0, width))
        rows = rows.reshape(per_tile, levels, width)
        back[tile * per_tile : (tile + 1) * per_tile] = rows
        halved[tile * per_tile : (tile + 1) * per_tile] = rows.astype(jnp.bfloat16)


def own_back_kernel(back, control, own_part):
    height = back.shape[0]
    for row in range(height):
        own_part[row] = lat_sum(back, row, 0, height, control[row])


def lat_back_kernel(far, close, own_part, gradient, halos, done, sems):
    halos[0], halos[1] = sides(far[...], close[...], "lat")
    height = own_part.shape[0]
    piece = height // BAND_PIECES
    moves = []
    for k in range(BAND_PIECES):
        part = pl.ds(k * piece, piece)
        for row in range(k * piece, (k + 1) * piece):
            done[row] = lat_rims(row, own_part[row], halos, height)
        moves.append(pltpu.make_async_copy(done.at[part], gradient.at[part], sems.at[k]))
        moves[-1].start()
    for move in moves:
        move.wait()


def exchange(to_far, to_close, axis, periodic):
    count = lax.axis_size(axis)
    far = []
    for odd in range(1, count, 2):
        if odd + 1 < count or periodic:
            far += [(odd, (odd + 1) % count), ((odd + 1) % count, odd)]
    close = [(i, i ^ 1) for i in range(count)]
    to_close, _ = lax.optimization_barrier((to_close, to_far))
    from_far, from_close = lax.ppermute(to_far, axis, far), lax.ppermute(to_close, axis, close)
    from_far = lax.optimization_barrier(from_far)
    from_close, _ = lax.optimization_barrier((from_close, from_far))
    return from_far, from_close, to_close


def shards(
    control,
    background,
    lon_width,
    block_cells,
    block_owner,
    channel_count,
    radiance,
    in_weight,
    in_bias,
    mid_weight,
    mid_bias,
    out_weight,
    out_bias,
):
    height, levels, width = control.shape
    hidden = mid_weight.shape[0]
    channels, columns = radiance.shape
    slot_count = block_owner.shape[0]
    recv_most = channel_count.shape[0]
    per_tile = LANES // levels
    tiles = height // per_tile
    slab_rows = BLOCK_COLS * channels // LANES
    f32, bf16, i32 = jnp.float32, jnp.bfloat16, jnp.int32
    shape = jax.ShapeDtypeStruct
    field = height * levels * width
    conv_flops = 2 * 33 * field

    halves = channels // LANES
    radiance = radiance.T.reshape(recv_most, BLOCK_COLS, halves, LANES)
    radiance = jnp.swapaxes(radiance, 1, 2).reshape(recv_most, slab_rows, LANES)
    half_field = shape(control.shape, bf16)
    slabs, to_far, to_close, held = call(
        first_kernel,
        (
            shape((recv_most + 1, slab_rows, LANES), bf16),
            half_field,
            half_field,
            shape(control.shape, f32),
        ),
        [HBM] * 4,
        (HBM,) + (VMEM,) * 3,
        0,
        20 * field,
        scratch=(
            pltpu.VMEM((1, slot_count), i32),
            pltpu.VMEM((1, recv_most), i32),
            pltpu.VMEM((slab_rows, LANES), f32),
            pltpu.VMEM((slab_rows, LANES), bf16),
            pltpu.SemaphoreType.DMA((4 + BAND_PIECES,)),
        ),
        name="slabs_halves",
    )(
        *pinned(
            radiance,
            block_owner.reshape(1, slot_count),
            channel_count.reshape(1, recv_most),
            control,
        )
    )
    far, close, sent = exchange(to_far, to_close, "lat", False)

    band = pltpu.VMEM((height, levels, width), f32)
    taps, turned, plan, own_part = call(
        prepare_kernel,
        (
            shape((tiles, 24, LANES), f32),
            shape((tiles, width, LANES), f32),
            shape((8, LANES), i32),
            shape(control.shape, f32),
        ),
        [HBM] * 4 + [VMEM],
        (VMEM,) * 4,
        conv_flops // 2,
        12 * field,
        scratch=(
            pltpu.SMEM((height,), i32),
            pltpu.VMEM((1, slot_count), i32),
            pltpu.VMEM((1, slot_count), i32),
            band,
            pltpu.SemaphoreType.DMA((3 + BAND_PIECES,)),
        ),
        name="taps_background",
    )(
        *pinned(
            lon_width, block_cells.reshape(1, slot_count), block_owner.reshape(1, slot_count), background
        ),
        held,
    )

    lat_count = lax.axis_size("lat")
    one, two, *others = swap_bits(lat_count)

    def swapped(part, apart):
        return lax.ppermute(part, "lat", [(i, i ^ apart) for i in range(lat_count)])

    later, _ = lax.optimization_barrier((slabs, sent))
    near = [slabs, swapped(later, 1 << one), swapped(later, 1 << two), swapped(slabs, (1 << one) + (1 << two))]

    halos = pltpu.VMEM((2, REACH, levels, width), f32)
    smoothed, to_far, to_close = call(
        lat_smooth_kernel,
        (shape((tiles, width, LANES), f32),) + (shape((tiles, REACH, LANES), f32),) * 2,
        [VMEM] * 3,
        (VMEM,) * 3,
        LAT_COVER * conv_flops,
        LAT_COVER * 16 * field,
        scratch=(halos,),
        name="lat_smooth",
    )(far, close, own_part)
    far, close, _ = exchange(to_far, to_close, "lon", True)

    outer_slots = 3 * slot_count // 8
    late_slots = slot_count - outer_slots
    x_rows = slot_count * BLOCK_COLS
    outer_rows, late_rows = outer_slots * BLOCK_COLS, late_slots * BLOCK_COLS
    row_flops = 2 * hidden * (LANES + hidden + channels)
    def state_shapes(rows):
        return (shape((rows, hidden), bf16), shape((rows, hidden), bf16), shape((rows, channels), f32))

    plan_rows = pltpu.SMEM((8, LANES), i32)
    padded = pltpu.VMEM((tiles, width + 2 * REACH, LANES), f32)
    flat = pltpu.VMEM((tiles * width, LANES), f32)

    profile, *rest = call(
        functools.partial(inner_forward_kernel, per_tile, outer_slots),
        (shape((tiles * width, LANES), f32),)
        + state_shapes(late_rows)
        + (
            shape((LANES, hidden), bf16),
            shape((hidden, hidden), bf16),
            shape((hidden, channels), bf16),
            shape((1, hidden), f32),
            shape((1, hidden), f32),
            shape((1, channels), f32),
        ),
        [ANY] + [VMEM] * 3 + [HBM] * 6,
        (VMEM,) * 10,
        LON_COVER * late_rows * row_flops,
        LON_COVER * 4 * 1024 * 1024,
        scratch=(
            plan_rows,
            padded,
            pltpu.VMEM((late_rows, LANES), f32),
            pltpu.SemaphoreType.DMA((5 + per_tile + WEIGHT_PIECES,)),
        ),
        name="inner_forward",
    )(
        plan,
        smoothed,
        turned,
        taps,
        *pinned(
            in_weight,
            in_bias.reshape(1, hidden),
            mid_weight,
            mid_bias.reshape(1, hidden),
            out_weight,
            out_bias.reshape(1, channels),
        ),
    )
    inner_states, weights = rest[:3], rest[3:]
    *near, _ = lax.optimization_barrier((*near, profile))
    for bit in others:
        near = [jnp.concatenate(near, axis=0)]
        near.append(swapped(near[0], 1 << bit))
    near = [jnp.concatenate(near[:-1], axis=0), near[-1]]
    across = [swapped(part, 1) for part in near]

    states = call(
        functools.partial(outer_forward_kernel, per_tile),
        state_shapes(outer_rows) + state_shapes(late_rows),
        [ANY] + [VMEM] * 12,
        (VMEM,) * 6,
        SWAP_COVER * outer_rows * row_flops,
        SWAP_COVER * 4 * 1024 * 1024,
        scratch=(
            plan_rows,
            padded,
            flat,
            pltpu.VMEM((outer_rows, LANES), f32),
            pltpu.VMEM((late_rows, LANES), f32),
            pltpu.SemaphoreType.DMA,
        ),
        name="outer_forward",
    )(plan, far, close, smoothed, turned, taps, profile, *weights)

    slabs = [*near, *across]
    table, sens, to_far, to_close = call(
        functools.partial(outer_backward_kernel, per_tile, len(slabs), recv_most),
        (
            shape((8, LANES), i32),
            shape((x_rows, LANES), f32),
            shape((tiles, REACH, LANES), bf16),
            shape((tiles, REACH, LANES), bf16),
        ),
        [ANY] + [VMEM] * (len(slabs) + 9),
        (VMEM,) * 4,
        outer_rows * row_flops,
        4 * 1024 * 1024,
        scratch=(
            plan_rows,
            pltpu.SMEM((8, LANES), i32),
            pltpu.VMEM((outer_rows, channels), f32),
            pltpu.VMEM((late_rows, channels), f32),
            flat,
            pltpu.SemaphoreType.DMA((2,)),
        ),
        name="outer_backward",
    )(plan, *slabs, *weights[:3], *states)
    far, close, sent = exchange(to_far, to_close, "lon", True)

    landing = call(
        functools.partial(inner_backward_kernel, per_tile, len(slabs), outer_slots),
        shape((tiles, width, LANES), f32),
        [ANY, ANY] + [VMEM] * (len(slabs) + 7),
        VMEM,
        late_rows * row_flops,
        4 * 1024 * 1024,
        scratch=(
            plan_rows,
            pltpu.SMEM((8, LANES), i32),
            pltpu.VMEM((late_rows, channels), f32),
            pltpu.VMEM((x_rows, LANES), f32),
            flat,
            pltpu.SemaphoreType.DMA((2,)),
        ),
        name="inner_backward",
    )(plan, table, sens, *slabs, *weights[:3], *inner_states)

    back, halved = call(
        lon_back_kernel,
        (shape((height, levels, width), f32), half_field),
        [VMEM] * 4,
        (VMEM,) * 2,
        conv_flops,
        8 * field,
        scratch=(pltpu.VMEM((tiles, width + 2 * REACH, LANES), f32),),
        name="lon_back",
    )(far, close, landing, taps)
    far, close, _ = exchange(halved, halved, "lat", False)
    own_part = call(
        own_back_kernel,
        shape((height, levels, width), f32),
        [VMEM, VMEM],
        VMEM,
        conv_flops // 2,
        12 * field,
        name="lat_back_own",
    )(back, held)
    return call(
        lat_back_kernel,
        shape((height, levels, width), f32),
        [VMEM] * 3,
        HBM,
        conv_flops // 2,
        16 * field,
        scratch=(halos, band, pltpu.SemaphoreType.DMA((BAND_PIECES,))),
        name="lat_back",
    )(far, close, own_part)


def solution(mesh):
    return jax.shard_map(
        shards,
        mesh=mesh,
        in_specs=(
            P("lat", None, "lon"),
            P("lat", None, "lon"),
            P("lat"),
            P("lat", "lon"),
            P("lat", "lon"),
            P("lat", "lon"),
            P("lat", "lon"),
            P(),
            P(),
            P(),
            P(),
            P(),
            P(),
        ),
        out_specs=P("lat", None, "lon"),
        check_vma=False,
    )
```

```python
import functools

import jax
import jax.numpy as jnp
import numpy as np
from jax import lax
from jax.experimental import pallas as pl
from jax.experimental.pallas import tpu as pltpu
from jax.sharding import PartitionSpec as P

REACH = 16
BLOCK_COLS = 8
LANES = 128
LAT_SIGMA = 8.0
WEIGHT_PIECES = 4
BAND_PIECES = 4
FEW_SLOTS = 8
LAT_COVER = 64
LON_COVER = 10
SWAP_COVER = 10
VMEM_BYTES = 40 * 1024 * 1024

VMEM = pl.BlockSpec(memory_space=pltpu.VMEM)
SMEM = pl.BlockSpec(memory_space=pltpu.SMEM)
HBM = pl.BlockSpec(memory_space=pltpu.HBM)
ANY = pl.BlockSpec(memory_space=pl.ANY)


def lat_taps():
    offsets = np.arange(-REACH, REACH + 1, dtype=np.float64)
    raw = np.exp(-offsets * offsets / (2.0 * LAT_SIGMA * LAT_SIGMA))
    return [float(v) for v in (raw / np.sqrt(np.sum(raw * raw))).astype(np.float32)]


def call(kernel, out_shape, in_specs, out_specs, flops, bytes_moved, scratch=(), name=None):
    return pl.pallas_call(
        kernel,
        out_shape=out_shape,
        in_specs=in_specs,
        out_specs=out_specs,
        scratch_shapes=list(scratch),
        compiler_params=pltpu.CompilerParams(vmem_limit_bytes=VMEM_BYTES),
        cost_estimate=pl.CostEstimate(flops=flops, bytes_accessed=bytes_moved, transcendentals=0),
        name=name,
    )


def pinned(*values):
    return [pltpu.with_memory_space_constraint(value, pltpu.HBM) for value in values]


def lat_sum(parts, row, first, height, start=None):
    taps = lat_taps()
    acc = start
    for k in range(height):
        j = first + k - row
        if abs(j) <= REACH:
            term = taps[j + REACH] * parts[k]
            acc = term if acc is None else acc + term
    return acc


def lat_rims(row, part, halos, height):
    low = lat_sum(halos.at[0], row, -REACH, REACH, part)
    return lat_sum(halos.at[1], row, height, REACH, low)


def fill_padded(padded, far, own, close):
    width = own.shape[1]
    low, high = sides(far[...], close[...], "lon")
    padded[:, 0:REACH, :] = low
    padded[:, REACH : REACH + width, :] = own[...]
    padded[:, REACH + width :, :] = high


def lon_conv(padded, taps, tile, start, width):
    middle = REACH + start
    acc = taps[tile, 0:1, :] * padded[tile, pl.ds(middle, width), :]
    for j in range(1, REACH + 1):
        both = padded[tile, pl.ds(middle + j, width), :] + padded[tile, pl.ds(middle - j, width), :]
        acc = acc + taps[tile, j : j + 1, :] * both
    return acc


def rounded(value):
    return value.astype(jnp.bfloat16).astype(jnp.float32)


def halved_rows(rows, order):
    halves, carry = {}, None
    for row in order:
        value = rows[row] if carry is None else rows[row] + carry
        halves[row] = value.astype(jnp.bfloat16)
        carry = value - halves[row].astype(jnp.float32)
    return [halves[row] for row in sorted(halves)]


def halve_for_sides(rows, height, to_far, to_close):
    odd = odd_index("lat")
    upward = halved_rows(rows, range(height - 1, -1, -1))
    downward = halved_rows(rows, range(height))
    for row in range(height):
        to_far[row] = jnp.where(odd, upward[row], downward[row])
        to_close[row] = jnp.where(odd, downward[row], upward[row])


def first_kernel(
    radiance,
    block_owner,
    channel_count,
    control,
    slabs,
    to_far,
    to_close,
    held,
    owners,
    counts,
    rows,
    tables,
    sems,
):
    recv_most = radiance.shape[0]
    moves = [
        pltpu.make_async_copy(radiance, slabs.at[pl.ds(0, recv_most)], sems.at[0]),
        pltpu.make_async_copy(block_owner, owners, sems.at[1]),
        pltpu.make_async_copy(channel_count, counts, sems.at[2]),
    ]
    piece = control.shape[0] // BAND_PIECES
    for k in range(BAND_PIECES):
        part = pl.ds(k * piece, piece)
        moves.append(pltpu.make_async_copy(control.at[part], held.at[part], sems.at[4 + k]))
    for move in moves[3:] + moves[:3]:
        move.start()
    rows[...] = jnp.full(rows.shape, -1.0, jnp.float32)
    moves[1].wait()
    moves[2].wait()
    rows[0:1, 0 : owners.shape[1]] = owners[...].astype(jnp.float32)
    rows[1:2, 0 : counts.shape[1]] = counts[...].astype(jnp.float32)
    tables[...] = rows[...].astype(jnp.bfloat16)
    last = pltpu.make_async_copy(tables, slabs.at[recv_most], sems.at[3])
    last.start()
    for move in moves[3:]:
        move.wait()
    halve_for_sides(held, held.shape[0], to_far, to_close)
    moves[0].wait()
    last.wait()


def prepare_kernel(
    lon_width,
    block_cells,
    block_owner,
    background,
    band,
    taps,
    turned,
    plan,
    own_part,
    widths,
    cells,
    owners,
    field,
    sems,
):
    moves = [
        pltpu.make_async_copy(lon_width, widths, sems.at[0]),
        pltpu.make_async_copy(block_cells, cells, sems.at[1]),
        pltpu.make_async_copy(block_owner, owners, sems.at[2]),
    ]
    piece = background.shape[0] // BAND_PIECES
    for k in range(BAND_PIECES):
        part = pl.ds(k * piece, piece)
        moves.append(pltpu.make_async_copy(background.at[part], field.at[part], sems.at[3 + k]))
    tiles = turned.shape[0]
    height, levels, width = field.shape
    per_tile = height // tiles
    for move in moves:
        move.start()
    groups = width // BLOCK_COLS
    rim = REACH // BLOCK_COLS
    slot_count = cells.shape[1]

    for row in range(height):
        own_part[row] = lat_sum(band, row, 0, height)

    lane_row = lax.broadcasted_iota(jnp.int32, (1, LANES), 1) // levels
    steps = lax.broadcasted_iota(jnp.int32, (taps.shape[1], LANES), 0)
    dist = steps.astype(jnp.float32)
    weight = jnp.where(steps == 0, 1.0, jnp.where(steps <= REACH, 2.0, 0.0))
    moves[0].wait()
    for tile in range(tiles):
        spread = jnp.zeros((1, LANES), jnp.int32)
        for sub in range(per_tile):
            spread = jnp.where(lane_row == sub, widths[tile * per_tile + sub], spread)
        spread = spread.astype(jnp.float32)
        raw = jnp.exp(-dist * dist / (2.0 * spread * spread))
        norm = jnp.sum(weight * raw * raw, axis=0, keepdims=True)
        taps[tile] = raw / jnp.sqrt(norm)

    moves[1].wait()
    moves[2].wait()
    rows = lax.broadcasted_iota(jnp.int32, (slot_count, slot_count), 0)
    lanes = lax.broadcasted_iota(jnp.int32, (slot_count, slot_count), 1)
    group = cells[...] % groups
    outer = ((group < rim) | (group >= groups - rim)) & (owners[...] >= 0)
    outer_here = jnp.where(outer, 1, 0)
    outer_count = jnp.sum(outer_here, axis=1, keepdims=True)
    earlier = jnp.sum(jnp.where(lanes < rows, outer_here, 0), axis=1, keepdims=True)
    here = jnp.sum(jnp.where(lanes == rows, outer_here, 0), axis=1, keepdims=True)
    cell = jnp.sum(jnp.where(lanes == rows, cells[...], 0), axis=1, keepdims=True)
    position = jnp.where(here == 1, earlier, outer_count + rows[:, 0:1] - earlier)
    at = lax.broadcasted_iota(jnp.int32, (slot_count, LANES), 1)
    hit = position == at
    slot = lax.broadcasted_iota(jnp.int32, (slot_count, LANES), 0)
    plan[...] = jnp.zeros_like(plan)
    plan[0:1, :] = jnp.sum(jnp.where(hit, cell, 0), axis=0, keepdims=True)
    plan[1:2, :] = jnp.sum(jnp.where(hit, slot, 0), axis=0, keepdims=True)
    plan[2:3, :] = jnp.broadcast_to(outer_count, (1, LANES))
    live_count = jnp.sum(jnp.where(owners[...] >= 0, 1, 0), axis=1, keepdims=True)
    plan[3:4, :] = jnp.broadcast_to(live_count, (1, LANES))
    for move in moves[3:]:
        move.wait()
    for tile in range(tiles):
        block = field[tile * per_tile : (tile + 1) * per_tile].reshape(per_tile * levels, width)
        turned[tile] = jnp.transpose(block)


def swap_bits(count):
    return list(range(count.bit_length() - 2, 0, -1))


def routing(recv_most, slot_count, slabs, table):
    per_owner = recv_most + 1
    spans, count = [], 0
    for ref in slabs:
        spans.append((ref, count))
        count += ref.shape[0] // per_owner
    half = count // 2
    here = lax.axis_index("lat")
    rows = lax.broadcasted_iota(jnp.int32, (slot_count, LANES), 0)
    lanes = lax.broadcasted_iota(jnp.int32, (slot_count, LANES), 1)
    diagonal = rows == lanes
    zero = jnp.zeros((slot_count, LANES), jnp.int32)

    bits = swap_bits(count)

    def device_of(k):
        apart = jnp.where(k < half, 0, 1)
        for place, bit in enumerate(bits):
            apart = apart + (((k >> place) & 1) << bit)
        return here ^ apart

    def over_sets(step):
        acc = zero
        for ref, first in spans:

            def add(k, acc, ref=ref, first=first):
                lines = ref[k * per_owner + recv_most].astype(jnp.float32)
                owners, counts = lines[0:1].astype(jnp.int32), lines[1:2].astype(jnp.int32)
                return acc + step(device_of(first + k), owners, counts)

            acc = lax.fori_loop(0, ref.shape[0] // per_owner, add, acc, unroll=count <= 8)
        return jnp.sum(acc, axis=1, keepdims=True)

    mine = slabs[0][recv_most].astype(jnp.float32)[0:1].astype(jnp.int32)
    owner = jnp.sum(jnp.where(diagonal, mine, 0), axis=1, keepdims=True)

    def rank(device, owners, counts):
        before = (device < here) | ((device == here) & (lanes < rows))
        return jnp.where((owners == owner) & before, 1, 0)

    arrival = over_sets(rank)

    def counted(device, owners, counts):
        return jnp.where((owner == device) & (lanes == arrival), counts, 0)

    kept = over_sets(counted)
    apart = owner ^ here
    entry = (apart & 1) * half
    for place, bit in enumerate(bits):
        entry = entry + (((apart >> bit) & 1) << place)
    target = jnp.where(owner >= 0, entry * per_owner + arrival, 0)
    table[...] = jnp.zeros_like(table)
    for row, column in enumerate((target, kept)):
        table[row : row + 1, :] = jnp.sum(jnp.where(diagonal, column, 0), axis=0, keepdims=True)


def odd_index(axis):
    return lax.axis_index(axis) % 2 == 1


def sides(far, close, axis):
    odd = odd_index(axis)
    far, close = far.astype(jnp.float32), close.astype(jnp.float32)
    return jnp.where(odd, close, far), jnp.where(odd, far, close)


def split_sides(low, high, axis):
    odd = odd_index(axis)
    return jnp.where(odd, high, low), jnp.where(odd, low, high)


def lat_smooth_kernel(far, close, own_part, smoothed, to_far, to_close, halos):
    tiles = smoothed.shape[0]
    height, levels, width = own_part.shape
    per_tile = height // tiles
    halos[0], halos[1] = sides(far[...], close[...], "lat")
    for tile in range(tiles):
        rows = range(tile * per_tile, (tile + 1) * per_tile)
        rows = [lat_rims(row, own_part[row], halos, height) for row in rows]
        turned = jnp.transpose(jnp.concatenate(rows, axis=0))
        smoothed[tile] = turned
        to_far[tile], to_close[tile] = split_sides(turned[0:REACH], turned[width - REACH : width], "lon")


def block_place(plan, position, groups, per_tile, width):
    block = plan[0, position]
    row = block // groups
    start = (row // per_tile) * width + (block % groups) * BLOCK_COLS
    return pl.multiple_of(start, BLOCK_COLS), row % per_tile


def take_blocks(plan, profile, picked, first, count, per_tile, width):
    groups = width // BLOCK_COLS
    lane_row = lax.broadcasted_iota(jnp.int32, (BLOCK_COLS, LANES), 1) // (LANES // per_tile)
    for k in range(count):
        start, sub = block_place(plan, first + k, groups, per_tile, width)
        block = profile[pl.ds(start, BLOCK_COLS), :]
        picked[k * BLOCK_COLS : (k + 1) * BLOCK_COLS, :] = jnp.where(lane_row == sub, block, 0.0)


def land_blocks(plan, field, sens, first, count, per_tile, width):
    groups = width // BLOCK_COLS
    lane_row = lax.broadcasted_iota(jnp.int32, (BLOCK_COLS, LANES), 1) // (LANES // per_tile)
    for k in range(first, first + count):
        start, sub = block_place(plan, k, groups, per_tile, width)
        block = sens[k * BLOCK_COLS : (k + 1) * BLOCK_COLS, :]
        field[pl.ds(start, BLOCK_COLS), :] += jnp.where(lane_row == sub, block, 0.0)


def take_observed(plan, table, slabs, observed, first, count):
    channels = observed.shape[1]
    channel = lax.broadcasted_iota(jnp.int32, (BLOCK_COLS, LANES), 1)
    for k in range(count):
        slot = plan[1, first + k]
        at, kept = table[0, slot], table[1, slot]
        slab, start = None, 0
        for ref in slabs:
            size = ref.shape[0]
            found = ref[jnp.clip(at - start, 0, size - 1)].astype(jnp.float32)
            slab = found if slab is None else jnp.where(at >= start, found, slab)
            start += size
        for h in range(channels // LANES):
            part = slab[h * BLOCK_COLS : (h + 1) * BLOCK_COLS]
            part = jnp.where(channel + h * LANES < kept, part, jnp.inf)
            observed[k * BLOCK_COLS : (k + 1) * BLOCK_COLS, h * LANES : (h + 1) * LANES] = part


def dot(a, b):
    return jnp.dot(a, b, preferred_element_type=jnp.float32)


def dot_t(a, b):
    return lax.dot_general(a, b, (((1,), (1,)), ((), ())), preferred_element_type=jnp.float32)


def net_first(picked, weights, act_one):
    inputs = picked[...].astype(jnp.bfloat16)
    act_one[...] = jnp.tanh(dot(inputs, weights[0][...]) + weights[3][...]).astype(jnp.bfloat16)


def net_rest(weights, states):
    _, weight_two, weight_out, _, bias_two, bias_out = weights
    act_one, act_two, emitted = states
    act_two[...] = jnp.tanh(dot(act_one[...], weight_two[...]) + bias_two[...]).astype(jnp.bfloat16)
    emitted[...] = dot(act_two[...], weight_out[...]) + bias_out[...]


def net_forward(picked, weights, states):
    net_first(picked, weights, states[0])
    net_rest(weights, states)


def net_backward(observed, states, weights):
    wide_in, weight_two, weight_out = weights[:3]
    act_one, act_two, emitted = states
    seen = observed[...]
    misfit = jnp.where(seen < jnp.inf, emitted[...] - seen, 0.0).astype(jnp.bfloat16)
    two = act_two[...].astype(jnp.float32)
    grad_two = (dot_t(misfit, weight_out[...]) * (1.0 - two * two)).astype(jnp.bfloat16)
    one = act_one[...].astype(jnp.float32)
    grad_one = (dot_t(grad_two, weight_two[...]) * (1.0 - one * one)).astype(jnp.bfloat16)
    return rounded(dot_t(grad_one, wide_in[...]))


def few_of(ref):
    return ref.at[pl.ds(0, FEW_SLOTS * BLOCK_COLS)]


def inner_forward_kernel(per_tile, outer_slots, plan, own, turned, taps, *refs):
    (in_weight, in_bias, mid_weight, mid_bias, out_weight, out_bias), refs = refs[:6], refs[6:]
    profile, states, weights, (rows, padded, picked, sems) = refs[0], refs[1:4], refs[4:10], refs[10:]
    wide_in, weight_two, weight_out, bias_one, bias_two, bias_out = weights
    tiles, width, _ = own.shape
    levels = in_weight.shape[0]
    count = picked.shape[0] // BLOCK_COLS
    piece = mid_weight.shape[0] // WEIGHT_PIECES
    pieces = [pl.ds(k * piece, piece) for k in range(WEIGHT_PIECES)]
    loads = [(plan, rows), (in_bias, bias_one)]
    loads += [(in_weight, wide_in.at[pl.ds(sub * levels, levels)]) for sub in range(per_tile)]
    early = len(loads)
    loads += [(mid_weight.at[part], weight_two.at[part]) for part in pieces] + [(mid_bias, bias_two)]
    loads += [(out_weight, weight_out), (out_bias, bias_out)]
    loads = [
        pltpu.make_async_copy(source, target, sems.at[k]) for k, (source, target) in enumerate(loads)
    ]
    for move in loads:
        move.start()
    zeros = jnp.zeros((tiles, REACH, LANES), jnp.float32)
    padded[:, 0:REACH, :] = zeros
    padded[:, REACH : REACH + width, :] = own[...]
    padded[:, REACH + width :, :] = zeros
    for tile in range(tiles):
        total = turned[tile] + lon_conv(padded, taps, tile, 0, width)
        profile[tile * width : (tile + 1) * width, :] = rounded(total)
    for move in loads[:early]:
        move.wait()
    in_time, many = rows[2, 0] <= outer_slots, rows[3, 0] > outer_slots + FEW_SLOTS

    @pl.when(in_time & many)
    def _():
        take_blocks(rows, profile, picked, outer_slots, count, per_tile, width)
        net_first(picked, weights, states[0])

    @pl.when(in_time & ~many)
    def _():
        take_blocks(rows, profile, picked, outer_slots, FEW_SLOTS, per_tile, width)
        net_first(few_of(picked), weights, few_of(states[0]))

    for move in loads[early:]:
        move.wait()

    @pl.when(in_time & many)
    def _():
        net_rest(weights, states)

    @pl.when(in_time & ~many)
    def _():
        net_rest(weights, [few_of(state) for state in states])


def outer_forward_kernel(
    per_tile,
    plan,
    far,
    close,
    own,
    turned,
    taps,
    inner_profile,
    *refs,
):
    weights, states, late_states, (rows, padded, profile, picked, late_picked, sem) = (
        refs[:6],
        refs[6:9],
        refs[9:12],
        refs[12:],
    )
    tiles, width, _ = own.shape
    outer_slots = picked.shape[0] // BLOCK_COLS
    late_slots = late_picked.shape[0] // BLOCK_COLS
    plan_in = pltpu.make_async_copy(plan, rows, sem)
    plan_in.start()
    fill_padded(padded, far, own, close)
    profile[...] = inner_profile[...]
    for tile in range(tiles):
        for start in (0, width - REACH):
            total = turned[tile, start : start + REACH, :] + lon_conv(padded, taps, tile, start, REACH)
            profile[tile * width + start : tile * width + start + REACH, :] = rounded(total)
    plan_in.wait()
    take_blocks(rows, profile, picked, 0, outer_slots, per_tile, width)
    net_forward(picked, weights, states)

    @pl.when(rows[2, 0] > outer_slots)
    def _():
        take_blocks(rows, profile, late_picked, outer_slots, late_slots, per_tile, width)
        net_forward(late_picked, weights, late_states)


def outer_backward_kernel(per_tile, parts, recv_most, plan, *refs):
    slabs, refs = refs[:parts], refs[parts:]
    weights, states, late_states, refs = refs[:3], refs[3:6], refs[6:9], refs[9:]
    (table_rows, sens, to_far, to_close) = refs[:4]
    (rows, table, observed, late_observed, field, sems) = refs[4:]
    tiles = to_far.shape[0]
    width = field.shape[0] // tiles
    outer_slots = observed.shape[0] // BLOCK_COLS
    late_slots = late_observed.shape[0] // BLOCK_COLS

    plan_in = pltpu.make_async_copy(plan, rows, sems.at[0])
    plan_in.start()
    routing(recv_most, outer_slots + late_slots, slabs, table_rows)
    table_in = pltpu.make_async_copy(table_rows, table, sems.at[1])
    table_in.start()
    field[...] = jnp.zeros_like(field)
    plan_in.wait()
    table_in.wait()

    take_observed(rows, table, slabs, observed, 0, outer_slots)
    sens[0 : outer_slots * BLOCK_COLS, :] = net_backward(observed, states, weights)
    land_blocks(rows, field, sens, 0, outer_slots, per_tile, width)

    @pl.when(rows[2, 0] > outer_slots)
    def _():
        take_observed(rows, table, slabs, late_observed, outer_slots, late_slots)
        sens[outer_slots * BLOCK_COLS :, :] = net_backward(late_observed, late_states, weights)
        land_blocks(rows, field, sens, outer_slots, late_slots, per_tile, width)

    for tile in range(tiles):
        low = field[tile * width : tile * width + REACH, :]
        high = field[(tile + 1) * width - REACH : (tile + 1) * width, :]
        low, high = split_sides(low, high, "lon")
        to_far[tile], to_close[tile] = low.astype(jnp.bfloat16), high.astype(jnp.bfloat16)


def inner_backward_kernel(per_tile, parts, outer_slots, plan, table_rows, sens, *refs):
    slabs, refs = refs[:parts], refs[parts:]
    weights, states, refs = refs[:3], refs[3:6], refs[6:]
    landing, rows, table, observed, inner, field, sems = refs
    tiles, width, _ = landing.shape
    late_slots = observed.shape[0] // BLOCK_COLS
    split = outer_slots * BLOCK_COLS
    moves = [
        pltpu.make_async_copy(plan, rows, sems.at[0]),
        pltpu.make_async_copy(table_rows, table, sems.at[1]),
    ]
    for move in moves:
        move.start()
    field[...] = jnp.zeros_like(field)
    inner[...] = sens[...]
    for move in moves:
        move.wait()

    in_time, many = rows[2, 0] <= outer_slots, rows[3, 0] > outer_slots + FEW_SLOTS
    first = outer_slots + FEW_SLOTS

    @pl.when(in_time & many)
    def _():
        take_observed(rows, table, slabs, observed, outer_slots, late_slots)
        inner[split:, :] = net_backward(observed, states, weights)

    @pl.when(in_time & ~many)
    def _():
        take_observed(rows, table, slabs, observed, outer_slots, FEW_SLOTS)
        inner[split : split + FEW_SLOTS * BLOCK_COLS, :] = net_backward(
            few_of(observed), [few_of(state) for state in states], weights
        )

    land_blocks(rows, field, inner, 0, first, per_tile, width)

    @pl.when(many)
    def _():
        land_blocks(rows, field, inner, first, outer_slots + late_slots - first, per_tile, width)

    for tile in range(tiles):
        landing[tile] = field[tile * width : (tile + 1) * width, :]


def lon_back_kernel(far, close, own, taps, back, halved, padded):
    tiles, width, _ = own.shape
    height, levels, _ = back.shape
    per_tile = height // tiles
    fill_padded(padded, far, own, close)
    for tile in range(tiles):
        rows = jnp.transpose(lon_conv(padded, taps, tile, 0, width))
        rows = rows.reshape(per_tile, levels, width)
        back[tile * per_tile : (tile + 1) * per_tile] = rows
        halved[tile * per_tile : (tile + 1) * per_tile] = rows.astype(jnp.bfloat16)


def own_back_kernel(back, control, own_part):
    height = back.shape[0]
    for row in range(height):
        own_part[row] = lat_sum(back, row, 0, height, control[row])


def lat_back_kernel(far, close, own_part, gradient, halos, done, sems):
    halos[0], halos[1] = sides(far[...], close[...], "lat")
    height = own_part.shape[0]
    piece = height // BAND_PIECES
    moves = []
    for k in range(BAND_PIECES):
        part = pl.ds(k * piece, piece)
        for row in range(k * piece, (k + 1) * piece):
            done[row] = lat_rims(row, own_part[row], halos, height)
        moves.append(pltpu.make_async_copy(done.at[part], gradient.at[part], sems.at[k]))
        moves[-1].start()
    for move in moves:
        move.wait()


def exchange(to_far, to_close, axis, periodic):
    count = lax.axis_size(axis)
    far = []
    for odd in range(1, count, 2):
        if odd + 1 < count or periodic:
            far += [(odd, (odd + 1) % count), ((odd + 1) % count, odd)]
    close = [(i, i ^ 1) for i in range(count)]
    to_close, _ = lax.optimization_barrier((to_close, to_far))
    from_far, from_close = lax.ppermute(to_far, axis, far), lax.ppermute(to_close, axis, close)
    from_far = lax.optimization_barrier(from_far)
    from_close, _ = lax.optimization_barrier((from_close, from_far))
    return from_far, from_close, to_close


def shards(
    control,
    background,
    lon_width,
    block_cells,
    block_owner,
    channel_count,
    radiance,
    in_weight,
    in_bias,
    mid_weight,
    mid_bias,
    out_weight,
    out_bias,
):
    height, levels, width = control.shape
    hidden = mid_weight.shape[0]
    channels, columns = radiance.shape
    slot_count = block_owner.shape[0]
    recv_most = channel_count.shape[0]
    per_tile = LANES // levels
    tiles = height // per_tile
    slab_rows = BLOCK_COLS * channels // LANES
    f32, bf16, i32 = jnp.float32, jnp.bfloat16, jnp.int32
    shape = jax.ShapeDtypeStruct
    field = height * levels * width
    conv_flops = 2 * 33 * field

    halves = channels // LANES
    radiance = radiance.T.reshape(recv_most, BLOCK_COLS, halves, LANES)
    radiance = jnp.swapaxes(radiance, 1, 2).reshape(recv_most, slab_rows, LANES)
    half_field = shape(control.shape, bf16)
    slabs, to_far, to_close, held = call(
        first_kernel,
        (
            shape((recv_most + 1, slab_rows, LANES), bf16),
            half_field,
            half_field,
            shape(control.shape, f32),
        ),
        [HBM] * 4,
        (HBM,) + (VMEM,) * 3,
        0,
        20 * field,
        scratch=(
            pltpu.VMEM((1, slot_count), i32),
            pltpu.VMEM((1, recv_most), i32),
            pltpu.VMEM((slab_rows, LANES), f32),
            pltpu.VMEM((slab_rows, LANES), bf16),
            pltpu.SemaphoreType.DMA((4 + BAND_PIECES,)),
        ),
        name="slabs_halves",
    )(
        *pinned(
            radiance,
            block_owner.reshape(1, slot_count),
            channel_count.reshape(1, recv_most),
            control,
        )
    )
    far, close, sent = exchange(to_far, to_close, "lat", False)

    band = pltpu.VMEM((height, levels, width), f32)
    taps, turned, plan, own_part = call(
        prepare_kernel,
        (
            shape((tiles, 24, LANES), f32),
            shape((tiles, width, LANES), f32),
            shape((8, LANES), i32),
            shape(control.shape, f32),
        ),
        [HBM] * 4 + [VMEM],
        (VMEM,) * 4,
        conv_flops // 2,
        12 * field,
        scratch=(
            pltpu.SMEM((height,), i32),
            pltpu.VMEM((1, slot_count), i32),
            pltpu.VMEM((1, slot_count), i32),
            band,
            pltpu.SemaphoreType.DMA((3 + BAND_PIECES,)),
        ),
        name="taps_background",
    )(
        *pinned(
            lon_width, block_cells.reshape(1, slot_count), block_owner.reshape(1, slot_count), background
        ),
        held,
    )

    lat_count = lax.axis_size("lat")
    one, two, *others = swap_bits(lat_count)

    def swapped(part, apart):
        return lax.ppermute(part, "lat", [(i, i ^ apart) for i in range(lat_count)])

    later, _ = lax.optimization_barrier((slabs, sent))
    near = [slabs, swapped(later, 1 << one), swapped(later, 1 << two), swapped(slabs, (1 << one) + (1 << two))]

    halos = pltpu.VMEM((2, REACH, levels, width), f32)
    smoothed, to_far, to_close = call(
        lat_smooth_kernel,
        (shape((tiles, width, LANES), f32),) + (shape((tiles, REACH, LANES), f32),) * 2,
        [VMEM] * 3,
        (VMEM,) * 3,
        LAT_COVER * conv_flops,
        LAT_COVER * 16 * field,
        scratch=(halos,),
        name="lat_smooth",
    )(far, close, own_part)
    far, close, _ = exchange(to_far, to_close, "lon", True)

    outer_slots = 3 * slot_count // 8
    late_slots = slot_count - outer_slots
    x_rows = slot_count * BLOCK_COLS
    outer_rows, late_rows = outer_slots * BLOCK_COLS, late_slots * BLOCK_COLS
    row_flops = 2 * hidden * (LANES + hidden + channels)
    def state_shapes(rows):
        return (shape((rows, hidden), bf16), shape((rows, hidden), bf16), shape((rows, channels), f32))

    plan_rows = pltpu.SMEM((8, LANES), i32)
    padded = pltpu.VMEM((tiles, width + 2 * REACH, LANES), f32)
    flat = pltpu.VMEM((tiles * width, LANES), f32)

    profile, *rest = call(
        functools.partial(inner_forward_kernel, per_tile, outer_slots),
        (shape((tiles * width, LANES), f32),)
        + state_shapes(late_rows)
        + (
            shape((LANES, hidden), bf16),
            shape((hidden, hidden), bf16),
            shape((hidden, channels), bf16),
            shape((1, hidden), f32),
            shape((1, hidden), f32),
            shape((1, channels), f32),
        ),
        [ANY] + [VMEM] * 3 + [HBM] * 6,
        (VMEM,) * 10,
        LON_COVER * late_rows * row_flops,
        LON_COVER * 4 * 1024 * 1024,
        scratch=(
            plan_rows,
            padded,
            pltpu.VMEM((late_rows, LANES), f32),
            pltpu.SemaphoreType.DMA((5 + per_tile + WEIGHT_PIECES,)),
        ),
        name="inner_forward",
    )(
        plan,
        smoothed,
        turned,
        taps,
        *pinned(
            in_weight,
            in_bias.reshape(1, hidden),
            mid_weight,
            mid_bias.reshape(1, hidden),
            out_weight,
            out_bias.reshape(1, channels),
        ),
    )
    inner_states, weights = rest[:3], rest[3:]
    *near, far, close, profile = lax.optimization_barrier((*near, far, close, profile))
    for bit in others:
        near = [jnp.concatenate(near, axis=0)]
        near.append(swapped(near[0], 1 << bit))
    near = [jnp.concatenate(near[:-1], axis=0), near[-1]]
    across = [swapped(part, 1) for part in near]

    states = call(
        functools.partial(outer_forward_kernel, per_tile),
        state_shapes(outer_rows) + state_shapes(late_rows),
        [ANY] + [VMEM] * 12,
        (VMEM,) * 6,
        SWAP_COVER * outer_rows * row_flops,
        SWAP_COVER * 4 * 1024 * 1024,
        scratch=(
            plan_rows,
            padded,
            flat,
            pltpu.VMEM((outer_rows, LANES), f32),
            pltpu.VMEM((late_rows, LANES), f32),
            pltpu.SemaphoreType.DMA,
        ),
        name="outer_forward",
    )(plan, far, close, smoothed, turned, taps, profile, *weights)

    slabs = [*near, *across]
    table, sens, to_far, to_close = call(
        functools.partial(outer_backward_kernel, per_tile, len(slabs), recv_most),
        (
            shape((8, LANES), i32),
            shape((x_rows, LANES), f32),
            shape((tiles, REACH, LANES), bf16),
            shape((tiles, REACH, LANES), bf16),
        ),
        [ANY] + [VMEM] * (len(slabs) + 9),
        (VMEM,) * 4,
        outer_rows * row_flops,
        4 * 1024 * 1024,
        scratch=(
            plan_rows,
            pltpu.SMEM((8, LANES), i32),
            pltpu.VMEM((outer_rows, channels), f32),
            pltpu.VMEM((late_rows, channels), f32),
            flat,
            pltpu.SemaphoreType.DMA((2,)),
        ),
        name="outer_backward",
    )(plan, *slabs, *weights[:3], *states)
    far, close, sent = exchange(to_far, to_close, "lon", True)

    landing = call(
        functools.partial(inner_backward_kernel, per_tile, len(slabs), outer_slots),
        shape((tiles, width, LANES), f32),
        [ANY, ANY] + [VMEM] * (len(slabs) + 7),
        VMEM,
        late_rows * row_flops,
        4 * 1024 * 1024,
        scratch=(
            plan_rows,
            pltpu.SMEM((8, LANES), i32),
            pltpu.VMEM((late_rows, channels), f32),
            pltpu.VMEM((x_rows, LANES), f32),
            flat,
            pltpu.SemaphoreType.DMA((2,)),
        ),
        name="inner_backward",
    )(plan, table, sens, *slabs, *weights[:3], *inner_states)

    back, halved = call(
        lon_back_kernel,
        (shape((height, levels, width), f32), half_field),
        [VMEM] * 4,
        (VMEM,) * 2,
        conv_flops,
        8 * field,
        scratch=(pltpu.VMEM((tiles, width + 2 * REACH, LANES), f32),),
        name="lon_back",
    )(far, close, landing, taps)
    far, close, _ = exchange(halved, halved, "lat", False)
    own_part = call(
        own_back_kernel,
        shape((height, levels, width), f32),
        [VMEM, VMEM],
        VMEM,
        conv_flops // 2,
        12 * field,
        name="lat_back_own",
    )(back, held)
    return call(
        lat_back_kernel,
        shape((height, levels, width), f32),
        [VMEM] * 3,
        HBM,
        conv_flops // 2,
        16 * field,
        scratch=(halos, band, pltpu.SemaphoreType.DMA((BAND_PIECES,))),
        name="lat_back",
    )(far, close, own_part)


def solution(mesh):
    return jax.shard_map(
        shards,
        mesh=mesh,
        in_specs=(
            P("lat", None, "lon"),
            P("lat", None, "lon"),
            P("lat"),
            P("lat", "lon"),
            P("lat", "lon"),
            P("lat", "lon"),
            P("lat", "lon"),
            P(),
            P(),
            P(),
            P(),
            P(),
            P(),
        ),
        out_specs=P("lat", None, "lon"),
        check_vma=False,
    )
```

```python
import functools

import jax
import jax.numpy as jnp
import numpy as np
from jax import lax
from jax.experimental import pallas as pl
from jax.experimental.pallas import tpu as pltpu
from jax.sharding import PartitionSpec as P

REACH = 16
BLOCK_COLS = 8
LANES = 128
LAT_SIGMA = 8.0
WEIGHT_PIECES = 4
BAND_PIECES = 4
FEW_SLOTS = 8
LAT_COVER = 64
LON_COVER = 10
SWAP_COVER = 10
VMEM_BYTES = 40 * 1024 * 1024

VMEM = pl.BlockSpec(memory_space=pltpu.VMEM)
SMEM = pl.BlockSpec(memory_space=pltpu.SMEM)
HBM = pl.BlockSpec(memory_space=pltpu.HBM)
ANY = pl.BlockSpec(memory_space=pl.ANY)


def lat_taps():
    offsets = np.arange(-REACH, REACH + 1, dtype=np.float64)
    raw = np.exp(-offsets * offsets / (2.0 * LAT_SIGMA * LAT_SIGMA))
    return [float(v) for v in (raw / np.sqrt(np.sum(raw * raw))).astype(np.float32)]


def call(kernel, out_shape, in_specs, out_specs, flops, bytes_moved, scratch=(), name=None):
    return pl.pallas_call(
        kernel,
        out_shape=out_shape,
        in_specs=in_specs,
        out_specs=out_specs,
        scratch_shapes=list(scratch),
        compiler_params=pltpu.CompilerParams(vmem_limit_bytes=VMEM_BYTES),
        cost_estimate=pl.CostEstimate(flops=flops, bytes_accessed=bytes_moved, transcendentals=0),
        name=name,
    )


def pinned(*values):
    return [pltpu.with_memory_space_constraint(value, pltpu.HBM) for value in values]


def lat_sum(parts, row, first, height, start=None):
    taps = lat_taps()
    acc = start
    for k in range(height):
        j = first + k - row
        if abs(j) <= REACH:
            term = taps[j + REACH] * parts[k]
            acc = term if acc is None else acc + term
    return acc


def lat_rims(row, part, halos, height):
    low = lat_sum(halos.at[0], row, -REACH, REACH, part)
    return lat_sum(halos.at[1], row, height, REACH, low)


def fill_padded(padded, far, own, close):
    width = own.shape[1]
    low, high = sides(far[...], close[...], "lon")
    padded[:, 0:REACH, :] = low
    padded[:, REACH : REACH + width, :] = own[...]
    padded[:, REACH + width :, :] = high


def lon_conv(padded, taps, tile, start, width):
    middle = REACH + start
    acc = taps[tile, 0:1, :] * padded[tile, pl.ds(middle, width), :]
    for j in range(1, REACH + 1):
        both = padded[tile, pl.ds(middle + j, width), :] + padded[tile, pl.ds(middle - j, width), :]
        acc = acc + taps[tile, j : j + 1, :] * both
    return acc


def rounded(value):
    return value.astype(jnp.bfloat16).astype(jnp.float32)


def halved_rows(rows, order):
    halves, carry = {}, None
    for row in order:
        value = rows[row] if carry is None else rows[row] + carry
        halves[row] = value.astype(jnp.bfloat16)
        carry = value - halves[row].astype(jnp.float32)
    return [halves[row] for row in sorted(halves)]


def halve_for_sides(rows, height, to_far, to_close):
    odd = odd_index("lat")
    upward = halved_rows(rows, range(height - 1, -1, -1))
    downward = halved_rows(rows, range(height))
    for row in range(height):
        to_far[row] = jnp.where(odd, upward[row], downward[row])
        to_close[row] = jnp.where(odd, downward[row], upward[row])


def first_kernel(
    radiance,
    block_owner,
    channel_count,
    control,
    slabs,
    to_far,
    to_close,
    held,
    owners,
    counts,
    rows,
    tables,
    sems,
):
    recv_most = radiance.shape[0]
    moves = [
        pltpu.make_async_copy(radiance, slabs.at[pl.ds(0, recv_most)], sems.at[0]),
        pltpu.make_async_copy(block_owner, owners, sems.at[1]),
        pltpu.make_async_copy(channel_count, counts, sems.at[2]),
    ]
    piece = control.shape[0] // BAND_PIECES
    for k in range(BAND_PIECES):
        part = pl.ds(k * piece, piece)
        moves.append(pltpu.make_async_copy(control.at[part], held.at[part], sems.at[4 + k]))
    for move in moves[3:] + moves[:3]:
        move.start()
    rows[...] = jnp.full(rows.shape, -1.0, jnp.float32)
    moves[1].wait()
    moves[2].wait()
    rows[0:1, 0 : owners.shape[1]] = owners[...].astype(jnp.float32)
    rows[1:2, 0 : counts.shape[1]] = counts[...].astype(jnp.float32)
    tables[...] = rows[...].astype(jnp.bfloat16)
    last = pltpu.make_async_copy(tables, slabs.at[recv_most], sems.at[3])
    last.start()
    for move in moves[3:]:
        move.wait()
    halve_for_sides(held, held.shape[0], to_far, to_close)
    moves[0].wait()
    last.wait()


def prepare_kernel(
    lon_width,
    block_cells,
    block_owner,
    background,
    band,
    taps,
    turned,
    plan,
    own_part,
    widths,
    cells,
    owners,
    field,
    sems,
):
    moves = [
        pltpu.make_async_copy(lon_width, widths, sems.at[0]),
        pltpu.make_async_copy(block_cells, cells, sems.at[1]),
        pltpu.make_async_copy(block_owner, owners, sems.at[2]),
    ]
    piece = background.shape[0] // BAND_PIECES
    for k in range(BAND_PIECES):
        part = pl.ds(k * piece, piece)
        moves.append(pltpu.make_async_copy(background.at[part], field.at[part], sems.at[3 + k]))
    tiles = turned.shape[0]
    height, levels, width = field.shape
    per_tile = height // tiles
    for move in moves:
        move.start()
    groups = width // BLOCK_COLS
    rim = REACH // BLOCK_COLS
    slot_count = cells.shape[1]

    for row in range(height):
        own_part[row] = lat_sum(band, row, 0, height)

    lane_row = lax.broadcasted_iota(jnp.int32, (1, LANES), 1) // levels
    steps = lax.broadcasted_iota(jnp.int32, (taps.shape[1], LANES), 0)
    dist = steps.astype(jnp.float32)
    weight = jnp.where(steps == 0, 1.0, jnp.where(steps <= REACH, 2.0, 0.0))
    moves[0].wait()
    for tile in range(tiles):
        spread = jnp.zeros((1, LANES), jnp.int32)
        for sub in range(per_tile):
            spread = jnp.where(lane_row == sub, widths[tile * per_tile + sub], spread)
        spread = spread.astype(jnp.float32)
        raw = jnp.exp(-dist * dist / (2.0 * spread * spread))
        norm = jnp.sum(weight * raw * raw, axis=0, keepdims=True)
        taps[tile] = raw / jnp.sqrt(norm)

    moves[1].wait()
    moves[2].wait()
    rows = lax.broadcasted_iota(jnp.int32, (slot_count, slot_count), 0)
    lanes = lax.broadcasted_iota(jnp.int32, (slot_count, slot_count), 1)
    group = cells[...] % groups
    outer = ((group < rim) | (group >= groups - rim)) & (owners[...] >= 0)
    outer_here = jnp.where(outer, 1, 0)
    outer_count = jnp.sum(outer_here, axis=1, keepdims=True)
    earlier = jnp.sum(jnp.where(lanes < rows, outer_here, 0), axis=1, keepdims=True)
    here = jnp.sum(jnp.where(lanes == rows, outer_here, 0), axis=1, keepdims=True)
    cell = jnp.sum(jnp.where(lanes == rows, cells[...], 0), axis=1, keepdims=True)
    position = jnp.where(here == 1, earlier, outer_count + rows[:, 0:1] - earlier)
    at = lax.broadcasted_iota(jnp.int32, (slot_count, LANES), 1)
    hit = position == at
    slot = lax.broadcasted_iota(jnp.int32, (slot_count, LANES), 0)
    plan[...] = jnp.zeros_like(plan)
    plan[0:1, :] = jnp.sum(jnp.where(hit, cell, 0), axis=0, keepdims=True)
    plan[1:2, :] = jnp.sum(jnp.where(hit, slot, 0), axis=0, keepdims=True)
    plan[2:3, :] = jnp.broadcast_to(outer_count, (1, LANES))
    live_count = jnp.sum(jnp.where(owners[...] >= 0, 1, 0), axis=1, keepdims=True)
    plan[3:4, :] = jnp.broadcast_to(live_count, (1, LANES))
    for move in moves[3:]:
        move.wait()
    for tile in range(tiles):
        block = field[tile * per_tile : (tile + 1) * per_tile].reshape(per_tile * levels, width)
        turned[tile] = jnp.transpose(block)


def swap_bits(count):
    return list(range(count.bit_length() - 2, 0, -1))


def routing(recv_most, slot_count, slabs, table):
    per_owner = recv_most + 1
    spans, count = [], 0
    for ref in slabs:
        spans.append((ref, count))
        count += ref.shape[0] // per_owner
    half = count // 2
    here = lax.axis_index("lat")
    rows = lax.broadcasted_iota(jnp.int32, (slot_count, LANES), 0)
    lanes = lax.broadcasted_iota(jnp.int32, (slot_count, LANES), 1)
    diagonal = rows == lanes
    zero = jnp.zeros((slot_count, LANES), jnp.int32)

    bits = swap_bits(count)

    def device_of(k):
        apart = jnp.where(k < half, 0, 1)
        for place, bit in enumerate(bits):
            apart = apart + (((k >> place) & 1) << bit)
        return here ^ apart

    def over_sets(step):
        acc = zero
        for ref, first in spans:

            def add(k, acc, ref=ref, first=first):
                lines = ref[k * per_owner + recv_most].astype(jnp.float32)
                owners, counts = lines[0:1].astype(jnp.int32), lines[1:2].astype(jnp.int32)
                return acc + step(device_of(first + k), owners, counts)

            acc = lax.fori_loop(0, ref.shape[0] // per_owner, add, acc, unroll=count <= 8)
        return jnp.sum(acc, axis=1, keepdims=True)

    mine = slabs[0][recv_most].astype(jnp.float32)[0:1].astype(jnp.int32)
    owner = jnp.sum(jnp.where(diagonal, mine, 0), axis=1, keepdims=True)

    def rank(device, owners, counts):
        before = (device < here) | ((device == here) & (lanes < rows))
        return jnp.where((owners == owner) & before, 1, 0)

    arrival = over_sets(rank)

    def counted(device, owners, counts):
        return jnp.where((owner == device) & (lanes == arrival), counts, 0)

    kept = over_sets(counted)
    apart = owner ^ here
    entry = (apart & 1) * half
    for place, bit in enumerate(bits):
        entry = entry + (((apart >> bit) & 1) << place)
    target = jnp.where(owner >= 0, entry * per_owner + arrival, 0)
    table[...] = jnp.zeros_like(table)
    for row, column in enumerate((target, kept)):
        table[row : row + 1, :] = jnp.sum(jnp.where(diagonal, column, 0), axis=0, keepdims=True)


def odd_index(axis):
    return lax.axis_index(axis) % 2 == 1


def sides(far, close, axis):
    odd = odd_index(axis)
    far, close = far.astype(jnp.float32), close.astype(jnp.float32)
    return jnp.where(odd, close, far), jnp.where(odd, far, close)


def split_sides(low, high, axis):
    odd = odd_index(axis)
    return jnp.where(odd, high, low), jnp.where(odd, low, high)


def lat_smooth_kernel(far, close, own_part, smoothed, to_far, to_close, halos):
    tiles = smoothed.shape[0]
    height, levels, width = own_part.shape
    per_tile = height // tiles
    halos[0], halos[1] = sides(far[...], close[...], "lat")
    for tile in range(tiles):
        rows = range(tile * per_tile, (tile + 1) * per_tile)
        rows = [lat_rims(row, own_part[row], halos, height) for row in rows]
        turned = jnp.transpose(jnp.concatenate(rows, axis=0))
        smoothed[tile] = turned
        to_far[tile], to_close[tile] = split_sides(turned[0:REACH], turned[width - REACH : width], "lon")


def block_place(plan, position, groups, per_tile, width):
    block = plan[0, position]
    row = block // groups
    start = (row // per_tile) * width + (block % groups) * BLOCK_COLS
    return pl.multiple_of(start, BLOCK_COLS), row % per_tile


def take_blocks(plan, profile, picked, first, count, per_tile, width):
    groups = width // BLOCK_COLS
    lane_row = lax.broadcasted_iota(jnp.int32, (BLOCK_COLS, LANES), 1) // (LANES // per_tile)
    for k in range(count):
        start, sub = block_place(plan, first + k, groups, per_tile, width)
        block = profile[pl.ds(start, BLOCK_COLS), :]
        picked[k * BLOCK_COLS : (k + 1) * BLOCK_COLS, :] = jnp.where(lane_row == sub, block, 0.0)


def land_blocks(plan, field, sens, first, count, per_tile, width):
    groups = width // BLOCK_COLS
    lane_row = lax.broadcasted_iota(jnp.int32, (BLOCK_COLS, LANES), 1) // (LANES // per_tile)
    for k in range(first, first + count):
        start, sub = block_place(plan, k, groups, per_tile, width)
        block = sens[k * BLOCK_COLS : (k + 1) * BLOCK_COLS, :]
        field[pl.ds(start, BLOCK_COLS), :] += jnp.where(lane_row == sub, block, 0.0)


def take_observed(plan, table, slabs, observed, first, count):
    channels = observed.shape[1]
    channel = lax.broadcasted_iota(jnp.int32, (BLOCK_COLS, LANES), 1)
    for k in range(count):
        slot = plan[1, first + k]
        at, kept = table[0, slot], table[1, slot]
        slab, start = None, 0
        for ref in slabs:
            size = ref.shape[0]
            found = ref[jnp.clip(at - start, 0, size - 1)].astype(jnp.float32)
            slab = found if slab is None else jnp.where(at >= start, found, slab)
            start += size
        for h in range(channels // LANES):
            part = slab[h * BLOCK_COLS : (h + 1) * BLOCK_COLS]
            part = jnp.where(channel + h * LANES < kept, part, jnp.inf)
            observed[k * BLOCK_COLS : (k + 1) * BLOCK_COLS, h * LANES : (h + 1) * LANES] = part


def dot(a, b):
    return jnp.dot(a, b, preferred_element_type=jnp.float32)


def dot_t(a, b):
    return lax.dot_general(a, b, (((1,), (1,)), ((), ())), preferred_element_type=jnp.float32)


def net_first(picked, weights, act_one):
    inputs = picked[...].astype(jnp.bfloat16)
    act_one[...] = jnp.tanh(dot(inputs, weights[0][...]) + weights[3][...]).astype(jnp.bfloat16)


def net_rest(weights, states):
    _, weight_two, weight_out, _, bias_two, bias_out = weights
    act_one, act_two, emitted = states
    act_two[...] = jnp.tanh(dot(act_one[...], weight_two[...]) + bias_two[...]).astype(jnp.bfloat16)
    emitted[...] = dot(act_two[...], weight_out[...]) + bias_out[...]


def net_forward(picked, weights, states):
    net_first(picked, weights, states[0])
    net_rest(weights, states)


def net_backward(observed, states, weights):
    wide_in, weight_two, weight_out = weights[:3]
    act_one, act_two, emitted = states
    seen = observed[...]
    misfit = jnp.where(seen < jnp.inf, emitted[...] - seen, 0.0).astype(jnp.bfloat16)
    two = act_two[...].astype(jnp.float32)
    grad_two = (dot_t(misfit, weight_out[...]) * (1.0 - two * two)).astype(jnp.bfloat16)
    one = act_one[...].astype(jnp.float32)
    grad_one = (dot_t(grad_two, weight_two[...]) * (1.0 - one * one)).astype(jnp.bfloat16)
    return rounded(dot_t(grad_one, wide_in[...]))


def few_of(ref):
    return ref.at[pl.ds(0, FEW_SLOTS * BLOCK_COLS)]


def inner_forward_kernel(per_tile, outer_slots, plan, own, turned, taps, *refs):
    (in_weight, in_bias, mid_weight, mid_bias, out_weight, out_bias), refs = refs[:6], refs[6:]
    profile, states, weights, (rows, padded, picked, sems) = refs[0], refs[1:4], refs[4:10], refs[10:]
    wide_in, weight_two, weight_out, bias_one, bias_two, bias_out = weights
    tiles, width, _ = own.shape
    levels = in_weight.shape[0]
    count = picked.shape[0] // BLOCK_COLS
    piece = mid_weight.shape[0] // WEIGHT_PIECES
    pieces = [pl.ds(k * piece, piece) for k in range(WEIGHT_PIECES)]
    loads = [(plan, rows), (in_bias, bias_one)]
    loads += [(in_weight, wide_in.at[pl.ds(sub * levels, levels)]) for sub in range(per_tile)]
    early = len(loads)
    loads += [(mid_weight.at[part], weight_two.at[part]) for part in pieces] + [(mid_bias, bias_two)]
    loads += [(out_weight, weight_out), (out_bias, bias_out)]
    loads = [
        pltpu.make_async_copy(source, target, sems.at[k]) for k, (source, target) in enumerate(loads)
    ]
    for move in loads:
        move.start()
    zeros = jnp.zeros((tiles, REACH, LANES), jnp.float32)
    padded[:, 0:REACH, :] = zeros
    padded[:, REACH : REACH + width, :] = own[...]
    padded[:, REACH + width :, :] = zeros
    for tile in range(tiles):
        total = turned[tile] + lon_conv(padded, taps, tile, 0, width)
        profile[tile * width : (tile + 1) * width, :] = rounded(total)
    for move in loads[:early]:
        move.wait()
    in_time, many = rows[2, 0] <= outer_slots, rows[3, 0] > outer_slots + FEW_SLOTS

    @pl.when(in_time & many)
    def _():
        take_blocks(rows, profile, picked, outer_slots, count, per_tile, width)
        net_first(picked, weights, states[0])

    @pl.when(in_time & ~many)
    def _():
        take_blocks(rows, profile, picked, outer_slots, FEW_SLOTS, per_tile, width)
        net_first(few_of(picked), weights, few_of(states[0]))

    for move in loads[early:]:
        move.wait()

    @pl.when(in_time & many)
    def _():
        net_rest(weights, states)

    @pl.when(in_time & ~many)
    def _():
        net_rest(weights, [few_of(state) for state in states])


def outer_forward_kernel(
    per_tile,
    plan,
    far,
    close,
    own,
    turned,
    taps,
    inner_profile,
    *refs,
):
    weights, states, late_states, (rows, padded, profile, picked, late_picked, sem) = (
        refs[:6],
        refs[6:9],
        refs[9:12],
        refs[12:],
    )
    tiles, width, _ = own.shape
    outer_slots = picked.shape[0] // BLOCK_COLS
    late_slots = late_picked.shape[0] // BLOCK_COLS
    plan_in = pltpu.make_async_copy(plan, rows, sem)
    plan_in.start()
    fill_padded(padded, far, own, close)
    profile[...] = inner_profile[...]
    for tile in range(tiles):
        for start in (0, width - REACH):
            total = turned[tile, start : start + REACH, :] + lon_conv(padded, taps, tile, start, REACH)
            profile[tile * width + start : tile * width + start + REACH, :] = rounded(total)
    plan_in.wait()
    take_blocks(rows, profile, picked, 0, outer_slots, per_tile, width)
    net_forward(picked, weights, states)

    @pl.when(rows[2, 0] > outer_slots)
    def _():
        take_blocks(rows, profile, late_picked, outer_slots, late_slots, per_tile, width)
        net_forward(late_picked, weights, late_states)


def outer_backward_kernel(per_tile, parts, recv_most, plan, *refs):
    slabs, refs = refs[:parts], refs[parts:]
    weights, states, late_states, refs = refs[:3], refs[3:6], refs[6:9], refs[9:]
    (table_rows, sens, to_far, to_close) = refs[:4]
    (rows, table, observed, late_observed, field, sems) = refs[4:]
    tiles = to_far.shape[0]
    width = field.shape[0] // tiles
    outer_slots = observed.shape[0] // BLOCK_COLS
    late_slots = late_observed.shape[0] // BLOCK_COLS

    plan_in = pltpu.make_async_copy(plan, rows, sems.at[0])
    plan_in.start()
    routing(recv_most, outer_slots + late_slots, slabs, table_rows)
    table_in = pltpu.make_async_copy(table_rows, table, sems.at[1])
    table_in.start()
    field[...] = jnp.zeros_like(field)
    plan_in.wait()
    table_in.wait()

    take_observed(rows, table, slabs, observed, 0, outer_slots)
    sens[0 : outer_slots * BLOCK_COLS, :] = net_backward(observed, states, weights)
    land_blocks(rows, field, sens, 0, outer_slots, per_tile, width)

    @pl.when(rows[2, 0] > outer_slots)
    def _():
        take_observed(rows, table, slabs, late_observed, outer_slots, late_slots)
        sens[outer_slots * BLOCK_COLS :, :] = net_backward(late_observed, late_states, weights)
        land_blocks(rows, field, sens, outer_slots, late_slots, per_tile, width)

    for tile in range(tiles):
        low = field[tile * width : tile * width + REACH, :]
        high = field[(tile + 1) * width - REACH : (tile + 1) * width, :]
        low, high = split_sides(low, high, "lon")
        to_far[tile], to_close[tile] = low.astype(jnp.bfloat16), high.astype(jnp.bfloat16)


def inner_backward_kernel(per_tile, parts, outer_slots, plan, table_rows, sens, *refs):
    slabs, refs = refs[:parts], refs[parts:]
    weights, states, refs = refs[:3], refs[3:6], refs[6:]
    landing, rows, table, observed, inner, field, sems = refs
    tiles, width, _ = landing.shape
    late_slots = observed.shape[0] // BLOCK_COLS
    split = outer_slots * BLOCK_COLS
    moves = [
        pltpu.make_async_copy(plan, rows, sems.at[0]),
        pltpu.make_async_copy(table_rows, table, sems.at[1]),
    ]
    for move in moves:
        move.start()
    field[...] = jnp.zeros_like(field)
    inner[...] = sens[...]
    for move in moves:
        move.wait()

    in_time, many = rows[2, 0] <= outer_slots, rows[3, 0] > outer_slots + FEW_SLOTS
    first = outer_slots + FEW_SLOTS

    @pl.when(in_time & many)
    def _():
        take_observed(rows, table, slabs, observed, outer_slots, late_slots)
        inner[split:, :] = net_backward(observed, states, weights)

    @pl.when(in_time & ~many)
    def _():
        take_observed(rows, table, slabs, observed, outer_slots, FEW_SLOTS)
        inner[split : split + FEW_SLOTS * BLOCK_COLS, :] = net_backward(
            few_of(observed), [few_of(state) for state in states], weights
        )

    land_blocks(rows, field, inner, 0, first, per_tile, width)

    @pl.when(many)
    def _():
        land_blocks(rows, field, inner, first, outer_slots + late_slots - first, per_tile, width)

    for tile in range(tiles):
        landing[tile] = field[tile * width : (tile + 1) * width, :]


def lon_back_kernel(far, close, own, taps, back, halved, padded):
    tiles, width, _ = own.shape
    height, levels, _ = back.shape
    per_tile = height // tiles
    fill_padded(padded, far, own, close)
    for tile in range(tiles):
        rows = jnp.transpose(lon_conv(padded, taps, tile, 0, width))
        rows = rows.reshape(per_tile, levels, width)
        back[tile * per_tile : (tile + 1) * per_tile] = rows
        halved[tile * per_tile : (tile + 1) * per_tile] = rows.astype(jnp.bfloat16)


def own_back_kernel(back, control, own_part):
    height = back.shape[0]
    for row in range(height):
        own_part[row] = lat_sum(back, row, 0, height, control[row])


def lat_back_kernel(far, close, own_part, gradient, halos, done, sems):
    halos[0], halos[1] = sides(far[...], close[...], "lat")
    height = own_part.shape[0]
    piece = height // BAND_PIECES
    moves = []
    for k in range(BAND_PIECES):
        part = pl.ds(k * piece, piece)
        for row in range(k * piece, (k + 1) * piece):
            done[row] = lat_rims(row, own_part[row], halos, height)
        moves.append(pltpu.make_async_copy(done.at[part], gradient.at[part], sems.at[k]))
        moves[-1].start()
    for move in moves:
        move.wait()


def exchange(to_far, to_close, axis, periodic):
    count = lax.axis_size(axis)
    far = []
    for odd in range(1, count, 2):
        if odd + 1 < count or periodic:
            far += [(odd, (odd + 1) % count), ((odd + 1) % count, odd)]
    close = [(i, i ^ 1) for i in range(count)]
    to_close, _ = lax.optimization_barrier((to_close, to_far))
    from_far, from_close = lax.ppermute(to_far, axis, far), lax.ppermute(to_close, axis, close)
    from_far = lax.optimization_barrier(from_far)
    from_close, _ = lax.optimization_barrier((from_close, from_far))
    return from_far, from_close, to_close


def shards(
    control,
    background,
    lon_width,
    block_cells,
    block_owner,
    channel_count,
    radiance,
    in_weight,
    in_bias,
    mid_weight,
    mid_bias,
    out_weight,
    out_bias,
):
    height, levels, width = control.shape
    hidden = mid_weight.shape[0]
    channels, columns = radiance.shape
    slot_count = block_owner.shape[0]
    recv_most = channel_count.shape[0]
    per_tile = LANES // levels
    tiles = height // per_tile
    slab_rows = BLOCK_COLS * channels // LANES
    f32, bf16, i32 = jnp.float32, jnp.bfloat16, jnp.int32
    shape = jax.ShapeDtypeStruct
    field = height * levels * width
    conv_flops = 2 * 33 * field

    halves = channels // LANES
    radiance = radiance.T.reshape(recv_most, BLOCK_COLS, halves, LANES)
    radiance = jnp.swapaxes(radiance, 1, 2).reshape(recv_most, slab_rows, LANES)
    half_field = shape(control.shape, bf16)
    slabs, to_far, to_close, held = call(
        first_kernel,
        (
            shape((recv_most + 1, slab_rows, LANES), bf16),
            half_field,
            half_field,
            shape(control.shape, f32),
        ),
        [HBM] * 4,
        (HBM,) + (VMEM,) * 3,
        0,
        20 * field,
        scratch=(
            pltpu.VMEM((1, slot_count), i32),
            pltpu.VMEM((1, recv_most), i32),
            pltpu.VMEM((slab_rows, LANES), f32),
            pltpu.VMEM((slab_rows, LANES), bf16),
            pltpu.SemaphoreType.DMA((4 + BAND_PIECES,)),
        ),
        name="slabs_halves",
    )(
        *pinned(
            radiance,
            block_owner.reshape(1, slot_count),
            channel_count.reshape(1, recv_most),
            control,
        )
    )
    lat_count = lax.axis_size("lat")
    one, two, *others = swap_bits(lat_count)

    def swapped(part, apart):
        return lax.ppermute(part, "lat", [(i, i ^ apart) for i in range(lat_count)])

    second = swapped(slabs, 1 << two)
    far, close, sent = exchange(to_far, to_close, "lat", False)
    second, far, close = lax.optimization_barrier((second, far, close))
    later, _ = lax.optimization_barrier((slabs, sent))
    near = [slabs, swapped(later, 1 << one), second, swapped(later, (1 << one) + (1 << two))]


    band = pltpu.VMEM((height, levels, width), f32)
    taps, turned, plan, own_part = call(
        prepare_kernel,
        (
            shape((tiles, 24, LANES), f32),
            shape((tiles, width, LANES), f32),
            shape((8, LANES), i32),
            shape(control.shape, f32),
        ),
        [HBM] * 4 + [VMEM],
        (VMEM,) * 4,
        conv_flops // 2,
        12 * field,
        scratch=(
            pltpu.SMEM((height,), i32),
            pltpu.VMEM((1, slot_count), i32),
            pltpu.VMEM((1, slot_count), i32),
            band,
            pltpu.SemaphoreType.DMA((3 + BAND_PIECES,)),
        ),
        name="taps_background",
    )(
        *pinned(
            lon_width, block_cells.reshape(1, slot_count), block_owner.reshape(1, slot_count), background
        ),
        held,
    )

    halos = pltpu.VMEM((2, REACH, levels, width), f32)
    smoothed, to_far, to_close = call(
        lat_smooth_kernel,
        (shape((tiles, width, LANES), f32),) + (shape((tiles, REACH, LANES), f32),) * 2,
        [VMEM] * 3,
        (VMEM,) * 3,
        LAT_COVER * conv_flops,
        LAT_COVER * 16 * field,
        scratch=(halos,),
        name="lat_smooth",
    )(far, close, own_part)
    far, close, _ = exchange(to_far, to_close, "lon", True)

    outer_slots = 3 * slot_count // 8
    late_slots = slot_count - outer_slots
    x_rows = slot_count * BLOCK_COLS
    outer_rows, late_rows = outer_slots * BLOCK_COLS, late_slots * BLOCK_COLS
    row_flops = 2 * hidden * (LANES + hidden + channels)
    def state_shapes(rows):
        return (shape((rows, hidden), bf16), shape((rows, hidden), bf16), shape((rows, channels), f32))

    plan_rows = pltpu.SMEM((8, LANES), i32)
    padded = pltpu.VMEM((tiles, width + 2 * REACH, LANES), f32)
    flat = pltpu.VMEM((tiles * width, LANES), f32)

    profile, *rest = call(
        functools.partial(inner_forward_kernel, per_tile, outer_slots),
        (shape((tiles * width, LANES), f32),)
        + state_shapes(late_rows)
        + (
            shape((LANES, hidden), bf16),
            shape((hidden, hidden), bf16),
            shape((hidden, channels), bf16),
            shape((1, hidden), f32),
            shape((1, hidden), f32),
            shape((1, channels), f32),
        ),
        [ANY] + [VMEM] * 3 + [HBM] * 6,
        (VMEM,) * 10,
        LON_COVER * late_rows * row_flops,
        LON_COVER * 4 * 1024 * 1024,
        scratch=(
            plan_rows,
            padded,
            pltpu.VMEM((late_rows, LANES), f32),
            pltpu.SemaphoreType.DMA((5 + per_tile + WEIGHT_PIECES,)),
        ),
        name="inner_forward",
    )(
        plan,
        smoothed,
        turned,
        taps,
        *pinned(
            in_weight,
            in_bias.reshape(1, hidden),
            mid_weight,
            mid_bias.reshape(1, hidden),
            out_weight,
            out_bias.reshape(1, channels),
        ),
    )
    inner_states, weights = rest[:3], rest[3:]
    *near, _ = lax.optimization_barrier((*near, profile))
    for bit in others:
        near = [jnp.concatenate(near, axis=0)]
        near.append(swapped(near[0], 1 << bit))
    near = [jnp.concatenate(near[:-1], axis=0), near[-1]]
    across = [swapped(part, 1) for part in near]

    states = call(
        functools.partial(outer_forward_kernel, per_tile),
        state_shapes(outer_rows) + state_shapes(late_rows),
        [ANY] + [VMEM] * 12,
        (VMEM,) * 6,
        SWAP_COVER * outer_rows * row_flops,
        SWAP_COVER * 4 * 1024 * 1024,
        scratch=(
            plan_rows,
            padded,
            flat,
            pltpu.VMEM((outer_rows, LANES), f32),
            pltpu.VMEM((late_rows, LANES), f32),
            pltpu.SemaphoreType.DMA,
        ),
        name="outer_forward",
    )(plan, far, close, smoothed, turned, taps, profile, *weights)

    slabs = [*near, *across]
    table, sens, to_far, to_close = call(
        functools.partial(outer_backward_kernel, per_tile, len(slabs), recv_most),
        (
            shape((8, LANES), i32),
            shape((x_rows, LANES), f32),
            shape((tiles, REACH, LANES), bf16),
            shape((tiles, REACH, LANES), bf16),
        ),
        [ANY] + [VMEM] * (len(slabs) + 9),
        (VMEM,) * 4,
        outer_rows * row_flops,
        4 * 1024 * 1024,
        scratch=(
            plan_rows,
            pltpu.SMEM((8, LANES), i32),
            pltpu.VMEM((outer_rows, channels), f32),
            pltpu.VMEM((late_rows, channels), f32),
            flat,
            pltpu.SemaphoreType.DMA((2,)),
        ),
        name="outer_backward",
    )(plan, *slabs, *weights[:3], *states)
    far, close, sent = exchange(to_far, to_close, "lon", True)

    landing = call(
        functools.partial(inner_backward_kernel, per_tile, len(slabs), outer_slots),
        shape((tiles, width, LANES), f32),
        [ANY, ANY] + [VMEM] * (len(slabs) + 7),
        VMEM,
        late_rows * row_flops,
        4 * 1024 * 1024,
        scratch=(
            plan_rows,
            pltpu.SMEM((8, LANES), i32),
            pltpu.VMEM((late_rows, channels), f32),
            pltpu.VMEM((x_rows, LANES), f32),
            flat,
            pltpu.SemaphoreType.DMA((2,)),
        ),
        name="inner_backward",
    )(plan, table, sens, *slabs, *weights[:3], *inner_states)

    back, halved = call(
        lon_back_kernel,
        (shape((height, levels, width), f32), half_field),
        [VMEM] * 4,
        (VMEM,) * 2,
        conv_flops,
        8 * field,
        scratch=(pltpu.VMEM((tiles, width + 2 * REACH, LANES), f32),),
        name="lon_back",
    )(far, close, landing, taps)
    far, close, _ = exchange(halved, halved, "lat", False)
    own_part = call(
        own_back_kernel,
        shape((height, levels, width), f32),
        [VMEM, VMEM],
        VMEM,
        conv_flops // 2,
        12 * field,
        name="lat_back_own",
    )(back, held)
    return call(
        lat_back_kernel,
        shape((height, levels, width), f32),
        [VMEM] * 3,
        HBM,
        conv_flops // 2,
        16 * field,
        scratch=(halos, band, pltpu.SemaphoreType.DMA((BAND_PIECES,))),
        name="lat_back",
    )(far, close, own_part)


def solution(mesh):
    return jax.shard_map(
        shards,
        mesh=mesh,
        in_specs=(
            P("lat", None, "lon"),
            P("lat", None, "lon"),
            P("lat"),
            P("lat", "lon"),
            P("lat", "lon"),
            P("lat", "lon"),
            P("lat", "lon"),
            P(),
            P(),
            P(),
            P(),
            P(),
            P(),
        ),
        out_specs=P("lat", None, "lon"),
        check_vma=False,
    )
```

```python
import functools

import jax
import jax.numpy as jnp
import numpy as np
from jax import lax
from jax.experimental import pallas as pl
from jax.experimental.pallas import tpu as pltpu
from jax.sharding import PartitionSpec as P

REACH = 16
BLOCK_COLS = 8
LANES = 128
LAT_SIGMA = 8.0
WEIGHT_PIECES = 4
BAND_PIECES = 4
SWAP_COVER = 10
VMEM_BYTES = 40 * 1024 * 1024

VMEM = pl.BlockSpec(memory_space=pltpu.VMEM)
SMEM = pl.BlockSpec(memory_space=pltpu.SMEM)
HBM = pl.BlockSpec(memory_space=pltpu.HBM)
ANY = pl.BlockSpec(memory_space=pl.ANY)


def lat_taps():
    offsets = np.arange(-REACH, REACH + 1, dtype=np.float64)
    raw = np.exp(-offsets * offsets / (2.0 * LAT_SIGMA * LAT_SIGMA))
    return [float(v) for v in (raw / np.sqrt(np.sum(raw * raw))).astype(np.float32)]


def call(kernel, out_shape, in_specs, out_specs, flops, bytes_moved, scratch=(), name=None):
    return pl.pallas_call(
        kernel,
        out_shape=out_shape,
        in_specs=in_specs,
        out_specs=out_specs,
        scratch_shapes=list(scratch),
        compiler_params=pltpu.CompilerParams(vmem_limit_bytes=VMEM_BYTES),
        cost_estimate=pl.CostEstimate(flops=flops, bytes_accessed=bytes_moved, transcendentals=0),
        name=name,
    )


def pinned(*values):
    return [pltpu.with_memory_space_constraint(value, pltpu.HBM) for value in values]


def lat_sum(parts, row, first, height, start=None):
    taps = lat_taps()
    acc = start
    for k in range(height):
        j = first + k - row
        if abs(j) <= REACH:
            term = taps[j + REACH] * parts[k]
            acc = term if acc is None else acc + term
    return acc


def lat_rims(row, part, halos, height):
    low = lat_sum(halos.at[0], row, -REACH, REACH, part)
    return lat_sum(halos.at[1], row, height, REACH, low)


def fill_padded(padded, far, own, close):
    width = own.shape[1]
    low, high = sides(far[...], close[...], "lon")
    padded[:, 0:REACH, :] = low
    padded[:, REACH : REACH + width, :] = own[...]
    padded[:, REACH + width :, :] = high


def lon_conv(padded, taps, tile, start, width):
    middle = REACH + start
    acc = taps[tile, 0:1, :] * padded[tile, pl.ds(middle, width), :]
    for j in range(1, REACH + 1):
        both = padded[tile, pl.ds(middle + j, width), :] + padded[tile, pl.ds(middle - j, width), :]
        acc = acc + taps[tile, j : j + 1, :] * both
    return acc


def rounded(value):
    return value.astype(jnp.bfloat16).astype(jnp.float32)


def halved_rows(rows, order):
    halves, carry = {}, None
    for row in order:
        value = rows[row] if carry is None else rows[row] + carry
        halves[row] = value.astype(jnp.bfloat16)
        carry = value - halves[row].astype(jnp.float32)
    return [halves[row] for row in sorted(halves)]


def halve_for_sides(rows, height, to_far, to_close):
    odd = odd_index("lat")
    upward = halved_rows(rows, range(height - 1, -1, -1))
    downward = halved_rows(rows, range(height))
    for row in range(height):
        to_far[row] = jnp.where(odd, upward[row], downward[row])
        to_close[row] = jnp.where(odd, downward[row], upward[row])


def first_kernel(
    radiance, block_owner, channel_count, control, slabs, to_far, to_close, owners, counts, rows, tables, held, sems
):
    recv_most = radiance.shape[0]
    moves = [
        pltpu.make_async_copy(radiance, slabs.at[pl.ds(0, recv_most)], sems.at[0]),
        pltpu.make_async_copy(block_owner, owners, sems.at[1]),
        pltpu.make_async_copy(channel_count, counts, sems.at[2]),
    ]
    piece = control.shape[0] // BAND_PIECES
    for k in range(BAND_PIECES):
        part = pl.ds(k * piece, piece)
        moves.append(pltpu.make_async_copy(control.at[part], held.at[part], sems.at[4 + k]))
    for move in moves[3:] + moves[:3]:
        move.start()
    rows[...] = jnp.full(rows.shape, -1.0, jnp.float32)
    moves[1].wait()
    moves[2].wait()
    rows[0:1, 0 : owners.shape[1]] = owners[...].astype(jnp.float32)
    rows[1:2, 0 : counts.shape[1]] = counts[...].astype(jnp.float32)
    tables[...] = rows[...].astype(jnp.bfloat16)
    last = pltpu.make_async_copy(tables, slabs.at[recv_most], sems.at[3])
    last.start()
    for move in moves[3:]:
        move.wait()
    halve_for_sides(held, held.shape[0], to_far, to_close)
    moves[0].wait()
    last.wait()


def prepare_kernel(
    lon_width,
    background,
    block_cells,
    block_owner,
    control,
    taps,
    turned,
    plan,
    own_part,
    widths,
    cells,
    owners,
    field,
    band,
    sems,
):
    moves = [
        pltpu.make_async_copy(lon_width, widths, sems.at[0]),
        pltpu.make_async_copy(block_cells, cells, sems.at[1]),
        pltpu.make_async_copy(block_owner, owners, sems.at[2]),
        pltpu.make_async_copy(background, field, sems.at[3]),
        pltpu.make_async_copy(control, band, sems.at[4]),
    ]
    tiles = turned.shape[0]
    height, levels, width = background.shape
    per_tile = height // tiles
    for move in moves:
        move.start()
    groups = width // BLOCK_COLS
    rim = REACH // BLOCK_COLS
    slot_count = cells.shape[1]

    lane_row = lax.broadcasted_iota(jnp.int32, (1, LANES), 1) // levels
    steps = lax.broadcasted_iota(jnp.int32, (taps.shape[1], LANES), 0)
    dist = steps.astype(jnp.float32)
    weight = jnp.where(steps == 0, 1.0, jnp.where(steps <= REACH, 2.0, 0.0))
    moves[0].wait()
    for tile in range(tiles):
        spread = jnp.zeros((1, LANES), jnp.int32)
        for sub in range(per_tile):
            spread = jnp.where(lane_row == sub, widths[tile * per_tile + sub], spread)
        spread = spread.astype(jnp.float32)
        raw = jnp.exp(-dist * dist / (2.0 * spread * spread))
        norm = jnp.sum(weight * raw * raw, axis=0, keepdims=True)
        taps[tile] = raw / jnp.sqrt(norm)

    moves[1].wait()
    moves[2].wait()
    rows = lax.broadcasted_iota(jnp.int32, (slot_count, slot_count), 0)
    lanes = lax.broadcasted_iota(jnp.int32, (slot_count, slot_count), 1)
    group = cells[...] % groups
    outer = ((group < rim) | (group >= groups - rim)) & (owners[...] >= 0)
    outer_here = jnp.where(outer, 1, 0)
    outer_count = jnp.sum(outer_here, axis=1, keepdims=True)
    earlier = jnp.sum(jnp.where(lanes < rows, outer_here, 0), axis=1, keepdims=True)
    here = jnp.sum(jnp.where(lanes == rows, outer_here, 0), axis=1, keepdims=True)
    cell = jnp.sum(jnp.where(lanes == rows, cells[...], 0), axis=1, keepdims=True)
    position = jnp.where(here == 1, earlier, outer_count + rows[:, 0:1] - earlier)
    at = lax.broadcasted_iota(jnp.int32, (slot_count, LANES), 1)
    hit = position == at
    slot = lax.broadcasted_iota(jnp.int32, (slot_count, LANES), 0)
    plan[...] = jnp.zeros_like(plan)
    plan[0:1, :] = jnp.sum(jnp.where(hit, cell, 0), axis=0, keepdims=True)
    plan[1:2, :] = jnp.sum(jnp.where(hit, slot, 0), axis=0, keepdims=True)
    plan[2:3, :] = jnp.broadcast_to(outer_count, (1, LANES))

    moves[3].wait()
    for tile in range(tiles):
        block = field[tile * per_tile : (tile + 1) * per_tile].reshape(per_tile * levels, width)
        turned[tile] = jnp.transpose(block)
    moves[4].wait()
    for row in range(height):
        own_part[row] = lat_sum(band, row, 0, height)


def swap_bits(count):
    return list(range(count.bit_length() - 2, 0, -1))


def routing(recv_most, slot_count, slabs, table):
    per_owner = recv_most + 1
    spans, count = [], 0
    for ref in slabs:
        spans.append((ref, count))
        count += ref.shape[0] // per_owner
    half = count // 2
    here = lax.axis_index("lat")
    rows = lax.broadcasted_iota(jnp.int32, (slot_count, LANES), 0)
    lanes = lax.broadcasted_iota(jnp.int32, (slot_count, LANES), 1)
    diagonal = rows == lanes
    zero = jnp.zeros((slot_count, LANES), jnp.int32)

    bits = swap_bits(count)

    def device_of(k):
        apart = jnp.where(k < half, 0, 1)
        for place, bit in enumerate(bits):
            apart = apart + (((k >> place) & 1) << bit)
        return here ^ apart

    def over_sets(step):
        acc = zero
        for ref, first in spans:

            def add(k, acc, ref=ref, first=first):
                lines = ref[k * per_owner + recv_most].astype(jnp.float32)
                owners, counts = lines[0:1].astype(jnp.int32), lines[1:2].astype(jnp.int32)
                return acc + step(device_of(first + k), owners, counts)

            acc = lax.fori_loop(0, ref.shape[0] // per_owner, add, acc, unroll=count <= 8)
        return jnp.sum(acc, axis=1, keepdims=True)

    mine = slabs[0][recv_most].astype(jnp.float32)[0:1].astype(jnp.int32)
    owner = jnp.sum(jnp.where(diagonal, mine, 0), axis=1, keepdims=True)

    def rank(device, owners, counts):
        before = (device < here) | ((device == here) & (lanes < rows))
        return jnp.where((owners == owner) & before, 1, 0)

    arrival = over_sets(rank)

    def counted(device, owners, counts):
        return jnp.where((owner == device) & (lanes == arrival), counts, 0)

    kept = over_sets(counted)
    apart = owner ^ here
    entry = (apart & 1) * half
    for place, bit in enumerate(bits):
        entry = entry + (((apart >> bit) & 1) << place)
    target = jnp.where(owner >= 0, entry * per_owner + arrival, 0)
    table[...] = jnp.zeros_like(table)
    for row, column in enumerate((target, kept)):
        table[row : row + 1, :] = jnp.sum(jnp.where(diagonal, column, 0), axis=0, keepdims=True)


def odd_index(axis):
    return lax.axis_index(axis) % 2 == 1


def sides(far, close, axis):
    odd = odd_index(axis)
    far, close = far.astype(jnp.float32), close.astype(jnp.float32)
    return jnp.where(odd, close, far), jnp.where(odd, far, close)


def split_sides(low, high, axis):
    odd = odd_index(axis)
    return jnp.where(odd, high, low), jnp.where(odd, low, high)


def lat_smooth_kernel(far, close, own_part, smoothed, to_far, to_close, halos):
    tiles = smoothed.shape[0]
    height, levels, width = own_part.shape
    per_tile = height // tiles
    halos[0], halos[1] = sides(far[...], close[...], "lat")
    for tile in range(tiles):
        rows = range(tile * per_tile, (tile + 1) * per_tile)
        rows = [lat_rims(row, own_part[row], halos, height) for row in rows]
        turned = jnp.transpose(jnp.concatenate(rows, axis=0))
        smoothed[tile] = turned
        to_far[tile], to_close[tile] = split_sides(turned[0:REACH], turned[width - REACH : width], "lon")


def block_place(plan, position, groups, per_tile, width):
    block = plan[0, position]
    row = block // groups
    start = (row // per_tile) * width + (block % groups) * BLOCK_COLS
    return pl.multiple_of(start, BLOCK_COLS), row % per_tile


def take_blocks(plan, profile, picked, first, count, per_tile, width):
    groups = width // BLOCK_COLS
    lane_row = lax.broadcasted_iota(jnp.int32, (BLOCK_COLS, LANES), 1) // (LANES // per_tile)
    for k in range(count):
        start, sub = block_place(plan, first + k, groups, per_tile, width)
        block = profile[pl.ds(start, BLOCK_COLS), :]
        picked[k * BLOCK_COLS : (k + 1) * BLOCK_COLS, :] = jnp.where(lane_row == sub, block, 0.0)


def land_blocks(plan, field, sens, first, count, per_tile, width):
    groups = width // BLOCK_COLS
    lane_row = lax.broadcasted_iota(jnp.int32, (BLOCK_COLS, LANES), 1) // (LANES // per_tile)
    for k in range(first, first + count):
        start, sub = block_place(plan, k, groups, per_tile, width)
        block = sens[k * BLOCK_COLS : (k + 1) * BLOCK_COLS, :]
        field[pl.ds(start, BLOCK_COLS), :] += jnp.where(lane_row == sub, block, 0.0)


def take_observed(plan, table, slabs, observed, first, count):
    channels = observed.shape[1]
    channel = lax.broadcasted_iota(jnp.int32, (BLOCK_COLS, LANES), 1)
    for k in range(count):
        slot = plan[1, first + k]
        at, kept = table[0, slot], table[1, slot]
        slab, start = None, 0
        for ref in slabs:
            size = ref.shape[0]
            found = ref[jnp.clip(at - start, 0, size - 1)].astype(jnp.float32)
            slab = found if slab is None else jnp.where(at >= start, found, slab)
            start += size
        for h in range(channels // LANES):
            part = slab[h * BLOCK_COLS : (h + 1) * BLOCK_COLS]
            part = jnp.where(channel + h * LANES < kept, part, jnp.inf)
            observed[k * BLOCK_COLS : (k + 1) * BLOCK_COLS, h * LANES : (h + 1) * LANES] = part


def dot(a, b):
    return jnp.dot(a, b, preferred_element_type=jnp.float32)


def dot_t(a, b):
    return lax.dot_general(a, b, (((1,), (1,)), ((), ())), preferred_element_type=jnp.float32)


def net_first(picked, weights, act_one):
    inputs = picked[...].astype(jnp.bfloat16)
    act_one[...] = jnp.tanh(dot(inputs, weights[0][...]) + weights[3][...]).astype(jnp.bfloat16)


def net_rest(weights, states):
    _, weight_two, weight_out, _, bias_two, bias_out = weights
    act_one, act_two, emitted = states
    act_two[...] = jnp.tanh(dot(act_one[...], weight_two[...]) + bias_two[...]).astype(jnp.bfloat16)
    emitted[...] = dot(act_two[...], weight_out[...]) + bias_out[...]


def net_forward(picked, weights, states):
    net_first(picked, weights, states[0])
    net_rest(weights, states)


def slopes(states, slope_one, slope_two):
    for act, slope in zip(states, (slope_one, slope_two)):
        value = act[...].astype(jnp.float32)
        slope[...] = 1.0 - value * value


def net_backward(observed, emitted, slope_one, slope_two, weights):
    wide_in, weight_two, weight_out = weights[:3]
    seen = observed[...]
    misfit = jnp.where(seen < jnp.inf, emitted[...] - seen, 0.0).astype(jnp.bfloat16)
    grad_two = (dot_t(misfit, weight_out[...]) * slope_two[...]).astype(jnp.bfloat16)
    grad_one = (dot_t(grad_two, weight_two[...]) * slope_one[...]).astype(jnp.bfloat16)
    return rounded(dot_t(grad_one, wide_in[...]))


def inner_forward_kernel(per_tile, outer_slots, plan, own, turned, taps, *refs):
    (in_weight, in_bias, mid_weight, mid_bias, out_weight, out_bias), refs = refs[:6], refs[6:]
    profile, states, weights, (rows, padded, picked, sems) = refs[0], refs[1:4], refs[4:10], refs[10:]
    wide_in, weight_two, weight_out, bias_one, bias_two, bias_out = weights
    tiles, width, _ = own.shape
    levels = in_weight.shape[0]
    count = picked.shape[0] // BLOCK_COLS
    piece = mid_weight.shape[0] // WEIGHT_PIECES
    pieces = [pl.ds(k * piece, piece) for k in range(WEIGHT_PIECES)]
    loads = [(plan, rows), (in_bias, bias_one)]
    loads += [(in_weight, wide_in.at[pl.ds(sub * levels, levels)]) for sub in range(per_tile)]
    early = len(loads)
    loads += [(mid_weight.at[part], weight_two.at[part]) for part in pieces] + [(mid_bias, bias_two)]
    loads += [(out_weight, weight_out), (out_bias, bias_out)]
    loads = [
        pltpu.make_async_copy(source, target, sems.at[k]) for k, (source, target) in enumerate(loads)
    ]
    for move in loads:
        move.start()
    zeros = jnp.zeros((tiles, REACH, LANES), jnp.float32)
    padded[:, 0:REACH, :] = zeros
    padded[:, REACH : REACH + width, :] = own[...]
    padded[:, REACH + width :, :] = zeros
    for tile in range(tiles):
        total = turned[tile] + lon_conv(padded, taps, tile, 0, width)
        profile[tile * width : (tile + 1) * width, :] = rounded(total)
    for move in loads[:early]:
        move.wait()
    take_blocks(rows, profile, picked, outer_slots, count, per_tile, width)
    act_one, act_two, emitted = states
    net_first(picked, weights, act_one)
    for move in loads[early:]:
        move.wait()

    @pl.when(rows[2, 0] <= outer_slots)
    def _():
        net_rest(weights, states)


def outer_forward_kernel(
    per_tile,
    plan,
    far,
    close,
    own,
    turned,
    taps,
    inner_profile,
    *refs,
):
    weights, states, late_states, (rows, padded, profile, picked, late_picked, sem) = (
        refs[:6],
        refs[6:9],
        refs[9:12],
        refs[12:],
    )
    tiles, width, _ = own.shape
    outer_slots = picked.shape[0] // BLOCK_COLS
    late_slots = late_picked.shape[0] // BLOCK_COLS
    plan_in = pltpu.make_async_copy(plan, rows, sem)
    plan_in.start()
    fill_padded(padded, far, own, close)
    profile[...] = inner_profile[...]
    for tile in range(tiles):
        for start in (0, width - REACH):
            total = turned[tile, start : start + REACH, :] + lon_conv(padded, taps, tile, start, REACH)
            profile[tile * width + start : tile * width + start + REACH, :] = rounded(total)
    plan_in.wait()
    take_blocks(rows, profile, picked, 0, outer_slots, per_tile, width)
    net_forward(picked, weights, states)

    @pl.when(rows[2, 0] > outer_slots)
    def _():
        take_blocks(rows, profile, late_picked, outer_slots, late_slots, per_tile, width)
        net_forward(late_picked, weights, late_states)


def outer_backward_kernel(per_tile, parts, recv_most, plan, *refs):
    slabs, refs = refs[:parts], refs[parts:]
    weights, states, late_states, refs = refs[:3], refs[3:6], refs[6:9], refs[9:]
    (table_rows, sens, to_far, to_close) = refs[:4]
    (rows, table, observed, late_observed, field, *slope, sems) = refs[4:]
    tiles = to_far.shape[0]
    width = field.shape[0] // tiles
    outer_slots = observed.shape[0] // BLOCK_COLS
    late_slots = late_observed.shape[0] // BLOCK_COLS

    plan_in = pltpu.make_async_copy(plan, rows, sems.at[0])
    plan_in.start()
    routing(recv_most, outer_slots + late_slots, slabs, table_rows)
    table_in = pltpu.make_async_copy(table_rows, table, sems.at[1])
    table_in.start()
    field[...] = jnp.zeros_like(field)
    slopes(states, *slope[:2])
    plan_in.wait()
    table_in.wait()

    take_observed(rows, table, slabs, observed, 0, outer_slots)
    sens[0 : outer_slots * BLOCK_COLS, :] = net_backward(observed, states[2], *slope[:2], weights)
    land_blocks(rows, field, sens, 0, outer_slots, per_tile, width)

    @pl.when(rows[2, 0] > outer_slots)
    def _():
        take_observed(rows, table, slabs, late_observed, outer_slots, late_slots)
        slopes(late_states, *slope[2:])
        sens[outer_slots * BLOCK_COLS :, :] = net_backward(
            late_observed, late_states[2], *slope[2:], weights
        )
        land_blocks(rows, field, sens, outer_slots, late_slots, per_tile, width)

    for tile in range(tiles):
        low = field[tile * width : tile * width + REACH, :]
        high = field[(tile + 1) * width - REACH : (tile + 1) * width, :]
        low, high = split_sides(low, high, "lon")
        to_far[tile], to_close[tile] = low.astype(jnp.bfloat16), high.astype(jnp.bfloat16)


def inner_backward_kernel(per_tile, parts, outer_slots, plan, table_rows, sens, *refs):
    slabs, refs = refs[:parts], refs[parts:]
    weights, states, refs = refs[:3], refs[3:6], refs[6:]
    landing, rows, table, observed, inner, field, *slope, sems = refs
    tiles, width, _ = landing.shape
    late_slots = observed.shape[0] // BLOCK_COLS
    split = outer_slots * BLOCK_COLS
    moves = [
        pltpu.make_async_copy(plan, rows, sems.at[0]),
        pltpu.make_async_copy(table_rows, table, sems.at[1]),
    ]
    for move in moves:
        move.start()
    field[...] = jnp.zeros_like(field)
    inner[...] = sens[...]
    slopes(states, *slope)
    for move in moves:
        move.wait()

    @pl.when(rows[2, 0] <= outer_slots)
    def _():
        take_observed(rows, table, slabs, observed, outer_slots, late_slots)
        inner[split:, :] = net_backward(observed, states[2], *slope, weights)

    land_blocks(rows, field, inner, 0, outer_slots + late_slots, per_tile, width)
    for tile in range(tiles):
        landing[tile] = field[tile * width : (tile + 1) * width, :]


def lon_back_kernel(far, close, own, taps, back, to_far, to_close, padded):
    tiles, width, _ = own.shape
    height, levels, _ = back.shape
    per_tile = height // tiles
    fill_padded(padded, far, own, close)
    for tile in range(tiles):
        rows = jnp.transpose(lon_conv(padded, taps, tile, 0, width))
        rows = rows.reshape(per_tile, levels, width)
        back[tile * per_tile : (tile + 1) * per_tile] = rows
    halve_for_sides(back, height, to_far, to_close)


def own_back_kernel(back, control, own_part, held, sem):
    control_in = pltpu.make_async_copy(control, held, sem)
    control_in.start()
    control_in.wait()
    height = back.shape[0]
    for row in range(height):
        own_part[row] = lat_sum(back, row, 0, height, held[row])


def lat_back_kernel(far, close, own_part, gradient, halos, done, sems):
    halos[0], halos[1] = sides(far[...], close[...], "lat")
    height = own_part.shape[0]
    piece = height // BAND_PIECES
    moves = []
    for k in range(BAND_PIECES):
        part = pl.ds(k * piece, piece)
        for row in range(k * piece, (k + 1) * piece):
            done[row] = lat_rims(row, own_part[row], halos, height)
        moves.append(pltpu.make_async_copy(done.at[part], gradient.at[part], sems.at[k]))
        moves[-1].start()
    for move in moves:
        move.wait()


def exchange(to_far, to_close, axis, periodic):
    count = lax.axis_size(axis)
    far = []
    for odd in range(1, count, 2):
        if odd + 1 < count or periodic:
            far += [(odd, (odd + 1) % count), ((odd + 1) % count, odd)]
    close = [(i, i ^ 1) for i in range(count)]
    to_close, _ = lax.optimization_barrier((to_close, to_far))
    from_far, from_close = lax.ppermute(to_far, axis, far), lax.ppermute(to_close, axis, close)
    from_far = lax.optimization_barrier(from_far)
    from_close, _ = lax.optimization_barrier((from_close, from_far))
    return from_far, from_close, to_close


def shards(
    control,
    background,
    lon_width,
    block_cells,
    block_owner,
    channel_count,
    radiance,
    in_weight,
    in_bias,
    mid_weight,
    mid_bias,
    out_weight,
    out_bias,
):
    height, levels, width = control.shape
    hidden = mid_weight.shape[0]
    channels, columns = radiance.shape
    slot_count = block_owner.shape[0]
    recv_most = channel_count.shape[0]
    per_tile = LANES // levels
    tiles = height // per_tile
    slab_rows = BLOCK_COLS * channels // LANES
    f32, bf16, i32 = jnp.float32, jnp.bfloat16, jnp.int32
    shape = jax.ShapeDtypeStruct
    field = height * levels * width
    conv_flops = 2 * 33 * field

    halves = channels // LANES
    radiance = radiance.T.reshape(recv_most, BLOCK_COLS, halves, LANES)
    radiance = jnp.swapaxes(radiance, 1, 2).reshape(recv_most, slab_rows, LANES)
    half_field = shape(control.shape, bf16)
    slabs, to_far, to_close = call(
        first_kernel,
        (shape((recv_most + 1, slab_rows, LANES), bf16), half_field, half_field),
        [HBM] * 4,
        (HBM, VMEM, VMEM),
        0,
        16 * field,
        scratch=(
            pltpu.VMEM((1, slot_count), i32),
            pltpu.VMEM((1, recv_most), i32),
            pltpu.VMEM((slab_rows, LANES), f32),
            pltpu.VMEM((slab_rows, LANES), bf16),
            pltpu.VMEM(control.shape, f32),
            pltpu.SemaphoreType.DMA((4 + BAND_PIECES,)),
        ),
        name="slabs_halves",
    )(*pinned(radiance, block_owner.reshape(1, slot_count), channel_count.reshape(1, recv_most), control))
    far, close, sent = exchange(to_far, to_close, "lat", False)

    band = pltpu.VMEM((height, levels, width), f32)
    taps, turned, plan, own_part = call(
        prepare_kernel,
        (
            shape((tiles, 24, LANES), f32),
            shape((tiles, width, LANES), f32),
            shape((8, LANES), i32),
            shape(control.shape, f32),
        ),
        [HBM] * 5,
        (VMEM,) * 4,
        conv_flops // 2,
        12 * field,
        scratch=(
            pltpu.SMEM((height,), i32),
            pltpu.VMEM((1, slot_count), i32),
            pltpu.VMEM((1, slot_count), i32),
            band,
            band,
            pltpu.SemaphoreType.DMA((5,)),
        ),
        name="taps_background",
    )(
        *pinned(
            lon_width,
            background,
            block_cells.reshape(1, slot_count),
            block_owner.reshape(1, slot_count),
            control,
        )
    )

    lat_count = lax.axis_size("lat")
    one, two, *others = swap_bits(lat_count)

    def swapped(part, apart):
        return lax.ppermute(part, "lat", [(i, i ^ apart) for i in range(lat_count)])

    slabs, _ = lax.optimization_barrier((slabs, sent))
    near = [slabs] + [swapped(slabs, apart) for apart in (1 << one, 1 << two, (1 << one) + (1 << two))]

    halos = pltpu.VMEM((2, REACH, levels, width), f32)
    smoothed, to_far, to_close = call(
        lat_smooth_kernel,
        (shape((tiles, width, LANES), f32),) + (shape((tiles, REACH, LANES), f32),) * 2,
        [VMEM] * 3,
        (VMEM,) * 3,
        conv_flops,
        16 * field,
        scratch=(halos,),
        name="lat_smooth",
    )(far, close, own_part)
    far, close, sent = exchange(to_far, to_close, "lon", True)
    outer_slots = 3 * slot_count // 8
    late_slots = slot_count - outer_slots
    x_rows = slot_count * BLOCK_COLS
    outer_rows, late_rows = outer_slots * BLOCK_COLS, late_slots * BLOCK_COLS
    row_flops = 2 * hidden * (LANES + hidden + channels)
    def state_shapes(rows):
        return (shape((rows, hidden), bf16), shape((rows, hidden), bf16), shape((rows, channels), f32))

    plan_rows = pltpu.SMEM((8, LANES), i32)
    padded = pltpu.VMEM((tiles, width + 2 * REACH, LANES), f32)
    flat = pltpu.VMEM((tiles * width, LANES), f32)

    profile, *rest = call(
        functools.partial(inner_forward_kernel, per_tile, outer_slots),
        (shape((tiles * width, LANES), f32),)
        + state_shapes(late_rows)
        + (
            shape((LANES, hidden), bf16),
            shape((hidden, hidden), bf16),
            shape((hidden, channels), bf16),
            shape((1, hidden), f32),
            shape((1, hidden), f32),
            shape((1, channels), f32),
        ),
        [ANY] + [VMEM] * 3 + [HBM] * 6,
        (VMEM,) * 10,
        late_rows * row_flops,
        4 * 1024 * 1024,
        scratch=(
            plan_rows,
            padded,
            pltpu.VMEM((late_rows, LANES), f32),
            pltpu.SemaphoreType.DMA((5 + per_tile + WEIGHT_PIECES,)),
        ),
        name="inner_forward",
    )(
        plan,
        smoothed,
        turned,
        taps,
        *pinned(
            in_weight,
            in_bias.reshape(1, hidden),
            mid_weight,
            mid_bias.reshape(1, hidden),
            out_weight,
            out_bias.reshape(1, channels),
        ),
    )
    inner_states, weights = rest[:3], rest[3:]
    *near, far, close, profile = lax.optimization_barrier((*near, far, close, profile))
    for bit in others:
        near = [jnp.concatenate(near, axis=0)]
        near.append(swapped(near[0], 1 << bit))
    near = [jnp.concatenate(near[:-1], axis=0), near[-1]]
    across = [swapped(part, 1) for part in near]

    states = call(
        functools.partial(outer_forward_kernel, per_tile),
        state_shapes(outer_rows) + state_shapes(late_rows),
        [ANY] + [VMEM] * 12,
        (VMEM,) * 6,
        SWAP_COVER * outer_rows * row_flops,
        SWAP_COVER * 4 * 1024 * 1024,
        scratch=(
            plan_rows,
            padded,
            flat,
            pltpu.VMEM((outer_rows, LANES), f32),
            pltpu.VMEM((late_rows, LANES), f32),
            pltpu.SemaphoreType.DMA,
        ),
        name="outer_forward",
    )(plan, far, close, smoothed, turned, taps, profile, *weights)

    slabs = [*near, *across]
    table, sens, to_far, to_close = call(
        functools.partial(outer_backward_kernel, per_tile, len(slabs), recv_most),
        (
            shape((8, LANES), i32),
            shape((x_rows, LANES), f32),
            shape((tiles, REACH, LANES), bf16),
            shape((tiles, REACH, LANES), bf16),
        ),
        [ANY] + [VMEM] * (len(slabs) + 9),
        (VMEM,) * 4,
        outer_rows * row_flops,
        4 * 1024 * 1024,
        scratch=(
            plan_rows,
            pltpu.SMEM((8, LANES), i32),
            pltpu.VMEM((outer_rows, channels), f32),
            pltpu.VMEM((late_rows, channels), f32),
            flat,
            pltpu.VMEM((outer_rows, hidden), f32),
            pltpu.VMEM((outer_rows, hidden), f32),
            pltpu.VMEM((late_rows, hidden), f32),
            pltpu.VMEM((late_rows, hidden), f32),
            pltpu.SemaphoreType.DMA((2,)),
        ),
        name="outer_backward",
    )(plan, *slabs, *weights[:3], *states)
    far, close, sent = exchange(to_far, to_close, "lon", True)

    landing = call(
        functools.partial(inner_backward_kernel, per_tile, len(slabs), outer_slots),
        shape((tiles, width, LANES), f32),
        [ANY, ANY] + [VMEM] * (len(slabs) + 7),
        VMEM,
        late_rows * row_flops,
        4 * 1024 * 1024,
        scratch=(
            plan_rows,
            pltpu.SMEM((8, LANES), i32),
            pltpu.VMEM((late_rows, channels), f32),
            pltpu.VMEM((x_rows, LANES), f32),
            flat,
            pltpu.VMEM((late_rows, hidden), f32),
            pltpu.VMEM((late_rows, hidden), f32),
            pltpu.SemaphoreType.DMA((2,)),
        ),
        name="inner_backward",
    )(plan, table, sens, *slabs, *weights[:3], *inner_states)

    back, to_far, to_close = call(
        lon_back_kernel,
        (shape((height, levels, width), f32), half_field, half_field),
        [VMEM] * 4,
        (VMEM,) * 3,
        conv_flops,
        8 * field,
        scratch=(pltpu.VMEM((tiles, width + 2 * REACH, LANES), f32),),
        name="lon_back",
    )(far, close, landing, taps)
    far, close, sent = exchange(to_far, to_close, "lat", False)
    own_part = call(
        own_back_kernel,
        shape((height, levels, width), f32),
        [VMEM, HBM],
        VMEM,
        conv_flops // 2,
        12 * field,
        scratch=(band, pltpu.SemaphoreType.DMA),
        name="lat_back_own",
    )(back, *pinned(control))

    return call(
        lat_back_kernel,
        shape((height, levels, width), f32),
        [VMEM] * 3,
        HBM,
        conv_flops // 2,
        16 * field,
        scratch=(halos, band, pltpu.SemaphoreType.DMA((BAND_PIECES,))),
        name="lat_back",
    )(far, close, own_part)


def solution(mesh):
    return jax.shard_map(
        shards,
        mesh=mesh,
        in_specs=(
            P("lat", None, "lon"),
            P("lat", None, "lon"),
            P("lat"),
            P("lat", "lon"),
            P("lat", "lon"),
            P("lat", "lon"),
            P("lat", "lon"),
            P(),
            P(),
            P(),
            P(),
            P(),
            P(),
        ),
        out_specs=P("lat", None, "lon"),
        check_vma=False,
    )
```
